32 devices in a mesh: items: 8 (over z, core), rows: 4 (over y, x).
Axes of the slice: x: 2, y: 2, z: 4, core: 2. Of those that a mesh axis runs over, the one named last changes fastest.
Arguments:
- tokens: bfloat16 [24, 1280, 768], P('items', 'rows'), may hold values from -6 to 6
- valid_rows: int32 [24], P('items'), may hold values from 16 to 30, as said below
- dataset_ids: int32 [24], P('items'), may hold values from 0 to 7
- shift_flags: int32 [24], P('items'), may hold values 0 or 1
- norm_gains: float32 [2, 768], replicated, may hold values from 0.5 to 1.5
- norm_biases: float32 [2, 768], replicated, may hold values from -4 to 4
- qkv_weight: bfloat16 [768, 2304], replicated, may hold values from -0.21875 to 0.21875
- qv_bias: float32 [1536], replicated, may hold values from -4 to 4
- out_weight: bfloat16 [768, 768], replicated, may hold values from -6 to 6
- out_bias: float32 [768], replicated, may hold values from -4 to 4
- fc1_weight: bfloat16 [768, 3072], replicated, may hold values from -0.21875 to 0.21875
- fc1_bias: float32 [3072], replicated, may hold values from -4 to 4
- fc2_weight: bfloat16 [3072, 768], replicated, may hold values from -0.109375 to 0.109375
- fc2_bias: float32 [768], replicated, may hold values from -4 to 4
- tap_weight: bfloat16 [768, 256], replicated, may hold values from -0.21875 to 0.21875
- tap_bias: float32 [256], replicated, may hold values from -4 to 4
- conv_weights: bfloat16 [4, 2304, 256], replicated, may hold values from -0.125 to 0.125
- conv_biases: float32 [4, 256], replicated, may hold values from -4 to 4
- table_gain: float32 [8, 256], replicated, may hold values from 0.1 to 1.9
- table_shift: float32 [8, 256], replicated, may hold values from -6 to 6
- token_cotangent: bfloat16 [24, 1280, 768], P('items', 'rows'), may hold values from -6 to 6
- joined_cotangent: bfloat16 [24, 64, 80, 256], P('items', 'rows'), may hold values from -6 to 6
Outputs:
- out_tokens: bfloat16 [24, 1280, 768], P('items', 'rows')
- joined: bfloat16 [24, 64, 80, 256], P('items', 'rows')
- grad_tokens: float32 [24, 1280, 768], P('items', 'rows')
- grad_norm_gains: float32 [2, 768], P(None, 'rows')
- grad_norm_biases: float32 [2, 768], P(None, 'rows')
- grad_qkv_weight: float32 [768, 2304], P('rows')
- grad_qv_bias: float32 [1536], P('rows')
- grad_out_weight: float32 [768, 768], P('rows')
- grad_out_bias: float32 [768], P('rows')
- grad_fc1_weight: float32 [768, 3072], P('rows')
- grad_fc1_bias: float32 [3072], P('rows')
- grad_fc2_weight: float32 [3072, 768], P('rows')
- grad_fc2_bias: float32 [768], P('rows')
- grad_tap_weight: float32 [768, 256], P('rows')
- grad_tap_bias: float32 [256], P('rows')
- grad_conv_weights: float32 [4, 2304, 256], P(None, 'rows')
- grad_conv_biases: float32 [4, 256], P(None, 'rows')
- grad_table_gain: float32 [8, 256], P(None, 'rows')
- grad_table_shift: float32 [8, 256], P(None, 'rows')
The draws below stay inside these ranges and needn't reach their ends.
Inputs may be any that keep to these rules, and one draw needn't show every extreme that they name: `valid_rows`: valid patch rows of each item, counted from the top of its grid; in each aligned block of 3 items one item has the most.
All inputs are finite; a program needn't handle non-finite values. No bound on the sum of `shift_flags` on one device may be relied on, other than what follows from the above.
Results may differ from the reference program's by a relative error of at most 0.022.
Values may be sent and summed in bfloat16 or wider, within the bound.
A program may use at most 384 MiB of HBM per device.

```python
import jax
import jax.numpy as jnp
from jax import lax

D = 768
HEADS = 12
HEAD_DIM = 64
FF = 3072
C = 256
NDATA = 8
PR = 32
PC = 40
ITEMS_DEV = 3
ITEMS = 24
TOKS = 1280


def draw_valid_rows(key, part):
    key = jax.random.fold_in(key, 11)
    rows_key, pick_key = jax.random.split(key)
    most_rows = PR - PR // 16
    drawn_rows = jax.random.randint(rows_key, (ITEMS,), PR // 2, most_rows + 1)
    picked = jax.random.randint(pick_key, (ITEMS // ITEMS_DEV,), 0, ITEMS_DEV)
    positions = jnp.arange(ITEMS)
    chosen = positions == positions // ITEMS_DEV * ITEMS_DEV + jnp.repeat(picked, ITEMS_DEV)
    return jnp.where(chosen, most_rows, drawn_rows).astype(jnp.int32)


def touch_ends(result, own_key, least, largest):
    dims = result.shape
    index_at = [jax.random.randint(jax.random.fold_in(own_key, axis), (), 0, dims[axis]) for axis in range(len(dims))]
    result = result.at[tuple(index_at)].set(least)
    longest = dims.index(max(dims))
    index_at[longest] = (index_at[longest] + 1) % dims[longest]
    return result.at[tuple(index_at)].set(largest)


def steps_of(rng, dims, shards, smallest, largest):
    def one(position, blocks):
        steps = jax.random.uniform(jax.random.fold_in(jax.random.fold_in(rng, 6), position), (blocks,), jnp.float32, smallest / len(shards), largest / len(shards))
        return jnp.repeat(jnp.exp(steps), dims[position] // blocks).reshape((-1,) + (1,) * (len(dims) - position - 1))

    loudness = one(*shards[0])
    for cut in shards[1:]:
        loudness = loudness * one(*cut)
    return loudness


def gaussian(rng, shape, deviation, bound, cuts=(), kind=jnp.bfloat16):
    array = deviation * jax.random.normal(rng, shape, jnp.float32)
    if cuts:
        array = array * steps_of(rng, shape, cuts, -0.22, 0.18)
    return jnp.clip(array, -bound, bound).astype(kind)


def setup_inputs(seed: int = 0) -> dict:
    seeds = jax.random.split(jax.random.key(seed), 23)
    return {
        "tokens": gaussian(seeds[0], (ITEMS, TOKS, D), 1.0, 6.0, ((0, 8), (1, 4))),
        "valid_rows": draw_valid_rows(jax.random.fold_in(seeds[22], 71), 0),
        "dataset_ids": touch_ends(jax.random.randint(seeds[2], (ITEMS,), 0, NDATA), jax.random.fold_in(seeds[2], 1), 0, NDATA - 1).astype(jnp.int32),
        "shift_flags": touch_ends((jax.random.randint(seeds[3], (ITEMS,), 0, 2) < 1).astype(jnp.int32), jax.random.fold_in(seeds[3], 1), 0, 1),
        "norm_gains": jnp.clip(1.0 + 0.1 * jax.random.normal(seeds[4], (2, D), jnp.float32), 0.5, 1.5),
        "norm_biases": gaussian(seeds[5], (2, D), 0.3, 4.0, (), jnp.float32),
        "qkv_weight": gaussian(seeds[6], (D, 3 * D), D ** -0.5, 0.21875),
        "qv_bias": gaussian(seeds[7], (2 * D,), 0.3, 4.0, (), jnp.float32),
        "out_weight": gaussian(seeds[8], (D, D), 1 ** -0.5, 6.0),
        "out_bias": gaussian(seeds[9], (D,), 0.3, 4.0, (), jnp.float32),
        "fc1_weight": gaussian(seeds[10], (D, FF), D ** -0.5, 0.21875),
        "fc1_bias": gaussian(seeds[11], (FF,), 0.3, 4.0, (), jnp.float32),
        "fc2_weight": gaussian(seeds[12], (FF, D), FF ** -0.5, 0.109375),
        "fc2_bias": gaussian(seeds[13], (D,), 0.3, 4.0, (), jnp.float32),
        "tap_weight": gaussian(seeds[14], (D, C), D ** -0.5, 0.21875),
        "tap_bias": gaussian(seeds[15], (C,), 0.3, 4.0, (), jnp.float32),
        "conv_weights": gaussian(seeds[16], (4, 9 * C, C), (9 * C) ** -0.5, 0.125),
        "conv_biases": gaussian(seeds[17], (4, C), 0.3, 4.0, (), jnp.float32),
        "table_gain": jnp.clip(1.0 + 0.18 * jax.random.normal(seeds[18], (NDATA, C), jnp.float32), 0.1, 1.9),
        "table_shift": gaussian(seeds[19], (NDATA, C), 0.5, 6.0, (), jnp.float32),
        "token_cotangent": gaussian(seeds[20], (ITEMS, TOKS, D), 1.0, 6.0, ((0, 8), (1, 4))),
        "joined_cotangent": gaussian(seeds[21], (ITEMS, 2 * PR, 2 * PC, C), 1.0, 6.0, ((0, 8), (1, 4))),
    }


@jax.custom_vjp
def low(v):
    return lax.optimization_barrier(v.astype(jnp.bfloat16)).astype(jnp.float32)

@jax.custom_vjp
def low_back(v):
    return v

def low_keep(v):
    return (low(v), None)

def low_pass(kept, grad):
    return (grad,)

def back_keep(v):
    return (v, None)

def back_low(kept, grad):
    return (low(grad),)
low.defvjp(low_keep, low_pass)
low_back.defvjp(back_keep, back_low)
epsilon = 1e-06
highest = lax.Precision.HIGHEST

def layer_norm(values, gain, shift):
    centre = lax.optimization_barrier(jnp.mean(values, axis=-1, keepdims=True))
    centred = values - centre
    spread = lax.optimization_barrier(jnp.mean(centred * centred, axis=-1, keepdims=True))
    return centred * lax.rsqrt(spread + epsilon) * gain + shift

def gelu_exact(values):
    return jax.nn.gelu(values, approximate=False)

def convolve(field, weight):
    channels = field.shape[-1]
    kernel = weight.reshape(3, 3, channels, weight.shape[-1])
    return lax.conv_general_dilated(field[None], kernel, (1, 1), 'SAME', dimension_numbers=('NHWC', 'HWIO', 'NHWC'), precision=highest)[0]

def double_along(field, which_dim):
    length = field.shape[which_dim]
    first_row = lax.slice_in_dim(field, 0, 1, axis=which_dim)
    last_row = lax.slice_in_dim(field, length - 1, length, axis=which_dim)
    before = jnp.concatenate([first_row, lax.slice_in_dim(field, 0, length - 1, axis=which_dim)], which_dim)
    after_rows = jnp.concatenate([lax.slice_in_dim(field, 1, length, axis=which_dim), last_row], which_dim)
    even_rows = 0.75 * field + 0.25 * before
    odd_rows = 0.75 * field + 0.25 * after_rows
    paired = jnp.stack([even_rows, odd_rows], which_dim + 1)
    new_shape = field.shape[:which_dim] + (2 * length,) + field.shape[which_dim + 1:]
    return paired.reshape(new_shape)

def item_forward(tokens, params, valid_count, dataset, flag):
    norm_gains, norm_biases, qkv_weight, qv_bias, out_weight, out_bias, fc1_weight, fc1_bias, fc2_weight, fc2_bias, tap_weight, tap_bias, conv_weights, conv_biases, table_gain, table_shift = params
    normed_one = low(layer_norm(tokens, norm_gains[0], norm_biases[0]))
    qkv_bias = jnp.concatenate([qv_bias[:D], jnp.zeros((D,), jnp.float32), qv_bias[D:]])
    qkv = low(low_back(jnp.dot(normed_one, qkv_weight, precision=highest) + qkv_bias))
    queries = qkv[:, :D].reshape(TOKS, HEADS, HEAD_DIM)
    key_rows = qkv[:, D:2 * D].reshape(TOKS, HEADS, HEAD_DIM)
    values = qkv[:, 2 * D:].reshape(TOKS, HEADS, HEAD_DIM)
    scores = low_back(jnp.einsum('thd,shd->hts', queries, key_rows, precision=highest) * HEAD_DIM ** (-0.5))
    token_valid = jnp.arange(TOKS) // PC < valid_count
    scores = jnp.where(token_valid[None, None, :], scores, -1e+30)
    probs = low(jax.nn.softmax(scores, axis=-1))
    attended = low(low_back(jnp.einsum('hts,shd->thd', probs, values, precision=highest).reshape(TOKS, D)))
    resid = tokens + low_back(jnp.dot(attended, out_weight, precision=highest) + out_bias)
    normed_two = low(layer_norm(resid, norm_gains[1], norm_biases[1]))
    hidden_pre = low_back(jnp.dot(normed_two, fc1_weight, precision=highest) + fc1_bias)
    hidden = low(gelu_exact(hidden_pre))
    output = resid + low_back(jnp.dot(hidden, fc2_weight, precision=highest) + fc2_bias)
    output_low = low(output)
    mask_column = token_valid.astype(jnp.float32)[:, None]
    field = low_back((jnp.dot(output_low, tap_weight, precision=highest) + tap_bias) * mask_column).reshape(PR, PC, C)
    for unit_index in range(2):
        act_one = low(gelu_exact(field))
        conv_one = low_back(convolve(act_one, conv_weights[2 * unit_index]) + conv_biases[2 * unit_index])
        act_two = low(gelu_exact(conv_one))
        field = field + low_back(convolve(act_two, conv_weights[2 * unit_index + 1]) + conv_biases[2 * unit_index + 1])
    wide = double_along(double_along(field, 0), 1)
    choose = (jnp.arange(NDATA) == dataset).astype(jnp.float32)
    gain_pick = jnp.dot(choose, table_gain, precision=highest)
    shift_pick = jnp.dot(choose, table_shift, precision=highest)
    flag_value = flag.astype(jnp.float32)
    joined = wide * (1.0 + flag_value * (gain_pick - 1.0)) + flag_value * shift_pick
    return (output, joined)

def reference(tokens, valid_rows, dataset_ids, shift_flags, norm_gains, norm_biases, qkv_weight, qv_bias, out_weight, out_bias, fc1_weight, fc1_bias, fc2_weight, fc2_bias, tap_weight, tap_bias, conv_weights, conv_biases, table_gain, table_shift, token_cotangent, joined_cotangent):
    params = (norm_gains.astype(jnp.float32), norm_biases.astype(jnp.float32), qkv_weight.astype(jnp.float32), qv_bias.astype(jnp.float32), out_weight.astype(jnp.float32), out_bias.astype(jnp.float32), fc1_weight.astype(jnp.float32), fc1_bias.astype(jnp.float32), fc2_weight.astype(jnp.float32), fc2_bias.astype(jnp.float32), tap_weight.astype(jnp.float32), tap_bias.astype(jnp.float32), conv_weights.astype(jnp.float32), conv_biases.astype(jnp.float32), table_gain.astype(jnp.float32), table_shift.astype(jnp.float32))
    totals = jax.tree.map(jnp.zeros_like, params)

    def one_item(running, packed):
        item_tokens, valid_count, dataset, flag, grad_tokens_in, grad_joined_in = packed

        def forward(tokens_in, params_in):
            return item_forward(tokens_in, params_in, valid_count, dataset, flag)
        (output, joined), pullback = jax.vjp(forward, item_tokens, params)
        grad_item, grad_params = pullback((grad_tokens_in, grad_joined_in))
        return (jax.tree.map(jnp.add, running, grad_params), (output.astype(jnp.bfloat16), joined.astype(jnp.bfloat16), grad_item))
    totals, stacked = lax.scan(one_item, totals, (tokens.astype(jnp.float32), valid_rows, dataset_ids, shift_flags, token_cotangent.astype(jnp.float32), joined_cotangent.astype(jnp.float32)))
    return (stacked[0], stacked[1], stacked[2], totals[0], totals[1], totals[2], totals[3], totals[4], totals[5], totals[6], totals[7], totals[8], totals[9], totals[10], totals[11], totals[12], totals[13], totals[14], totals[15])
```

```python
import functools

import jax
import jax.numpy as jnp
from jax import lax
from jax.experimental import pallas as pl
from jax.experimental.pallas import tpu as pltpu
from jax.sharding import PartitionSpec as P

HEAD_DIM = 64
PC = 40
GROUP = 256
HEADS_PER_GROUP = GROUP // HEAD_DIM

BF = jnp.bfloat16
F32 = jnp.float32
LOG2E = 1.4426950408889634
MASKED = -1e30
NN = (((1,), (0,)), ((), ()))
NT = (((1,), (1,)), ((), ()))
TN = (((0,), (0,)), ((), ()))

epsilon = 1e-06
highest = lax.Precision.HIGHEST


def mm(left, right, dims=NN):
    return lax.dot_general(left, right, dims, preferred_element_type=F32)


def normal_parts(values):
    bell = jnp.exp2(values * values * (-0.5 * LOG2E))
    t = 1.0 / (1.0 + (0.3275911 * 0.7071067811865476) * jnp.abs(values))
    poly = t * (
        0.5 * 0.254829592
        + t
        * (
            0.5 * -0.284496736
            + t * (0.5 * 1.421413741 + t * (0.5 * -1.453152027 + t * (0.5 * 1.061405429)))
        )
    )
    tail = poly * bell
    cdf = jnp.where(values >= 0.0, 1.0 - tail, tail)
    return cdf, values * bell * 0.3989422804014327


def gelu_exact(values):
    return values * normal_parts(values)[0]


def gelu_slope(values):
    cdf, slope = normal_parts(values)
    return cdf + slope


def gelu_back(values, grad_out):
    return gelu_slope(values) * grad_out


def norm_stats(values):
    centre = jnp.mean(values, axis=-1, keepdims=True)
    centred = values - centre
    spread = jnp.mean(centred * centred, axis=-1, keepdims=True)
    rstd = lax.rsqrt(spread + epsilon)
    return centred * rstd, rstd


def layer_norm(values, gain, shift):
    return norm_stats(values)[0] * gain + shift


def norm_back(values, gain, grad_out):
    unit, rstd = norm_stats(values)
    scaled = grad_out * gain
    mean_one = jnp.mean(scaled, axis=-1, keepdims=True)
    mean_two = jnp.mean(scaled * unit, axis=-1, keepdims=True)
    result = rstd * (scaled - mean_one - unit * mean_two)
    return result, jnp.sum(grad_out * unit, axis=0), jnp.sum(grad_out, axis=0)


def swap(block, axis, mask):
    count = lax.axis_size(axis)
    return lax.ppermute(block, axis, [(i, i ^ mask) for i in range(count)])


def axis_bits(axis):
    return (lax.axis_size(axis) - 1).bit_length()


def gather_blocks(block):
    bits = axis_bits("rows")
    half = block.shape[0] // 2
    halves = []
    for order, part in (
        (range(bits), block[:half]),
        (range(bits - 1, -1, -1), block[half:]),
    ):
        held = {0: part}
        for bit in order:
            keys = sorted(held)
            sent = jnp.concatenate([held[key] for key in keys]) if len(keys) > 1 else held[keys[0]]
            got = swap(sent, "rows", 1 << bit)
            for place, key in enumerate(keys):
                held[key | (1 << bit)] = got[place * half : (place + 1) * half]
        halves.append(held)
    blocks = []
    for j in range(1 << bits):
        blocks += [halves[0][j], halves[1][j]]
    return jnp.concatenate(blocks)


def scatter_blocks(whole):
    bits = axis_bits("rows")
    count = 1 << bits
    block = whole.shape[0] // count
    half = block // 2
    results = []
    for which, order in ((0, range(bits - 1, -1, -1)), (1, range(bits))):
        held = {
            j: whole[j * block + which * half : j * block + (which + 1) * half]
            for j in range(count)
        }
        for bit in order:
            sent_keys = sorted(key for key in held if key >> bit & 1)
            sent = (
                jnp.concatenate([held[key] for key in sent_keys])
                if len(sent_keys) > 1
                else held[sent_keys[0]]
            )
            got = swap(sent, "rows", 1 << bit)
            held = {
                key ^ (1 << bit): held[key ^ (1 << bit)].astype(F32)
                + got[place * half : (place + 1) * half].astype(F32)
                for place, key in enumerate(sent_keys)
            }
            if len(held) > 1:
                held = {key: value.astype(BF) for key, value in held.items()}
        results.append(held[0])
    return jnp.concatenate(results)


def add_low(first, second):
    return (first.astype(F32) + second.astype(F32)).astype(BF)


def head_mask(shape, head):
    lane = lax.broadcasted_iota(jnp.int32, shape, 1)
    return lane // HEAD_DIM == head


def spread_heads(block):
    zero = jnp.zeros_like(block)
    return jnp.concatenate(
        [jnp.where(head_mask(block.shape, h), block, zero) for h in range(HEADS_PER_GROUP)],
        axis=0,
    )


def key_bias(index, dim, length, block, info_ref):
    start = jnp.full_like(index, info_ref[1])
    for j in range(1, length // block):
        start = jnp.where(index >= j * block, info_ref[1 + j] - j * block, start)
    return jnp.where(index + start < info_ref[0], 0.0, MASKED).astype(F32)


def attention_forward_kernel(info_ref, q_ref, k_ref, v_ref, o_ref, lse_ref):
    t, n = q_ref.shape[0], k_ref.shape[0]
    bias = key_bias(lax.broadcasted_iota(jnp.int32, (1, n), 1), 1, n, t, info_ref)
    keys, values = k_ref[...], v_ref[...]
    queries = q_ref[...] * jnp.asarray(HEAD_DIM**-0.5, BF)
    out = jnp.zeros((t, GROUP), F32)
    for h in range(HEADS_PER_GROUP):
        mask = head_mask((t, GROUP), h)
        one = jnp.where(mask, queries, jnp.zeros_like(queries))
        scores = mm(one, keys, NT) + bias
        top = jnp.max(scores, axis=1, keepdims=True)
        probs = jnp.exp2((scores - top) * LOG2E)
        total = jnp.sum(probs, axis=1, keepdims=True)
        weighted = mm(probs.astype(BF), values)
        out = jnp.where(mask, weighted * (1.0 / total), out)
        lse = top * LOG2E + jnp.log2(total)
        lse_ref[0, :, pl.ds(h * t, t)] = jnp.transpose(jnp.broadcast_to(lse, (t, 128)))[:8]
    o_ref[...] = out.astype(BF)


def attention_forward(info, queries, keyvals):
    t, d = queries.shape
    n = keyvals.shape[0]
    groups = d // GROUP
    return pl.pallas_call(
        attention_forward_kernel,
        grid=(groups,),
        in_specs=[
            pl.BlockSpec(memory_space=pltpu.SMEM),
            pl.BlockSpec((t, GROUP), lambda i: (0, i)),
            pl.BlockSpec((n, GROUP), lambda i: (0, i)),
            pl.BlockSpec((n, GROUP), lambda i: (0, i + groups)),
        ],
        out_specs=[
            pl.BlockSpec((t, GROUP), lambda i: (0, i)),
            pl.BlockSpec((1, 8, HEADS_PER_GROUP * t), lambda i: (i, 0, 0)),
        ],
        out_shape=[
            jax.ShapeDtypeStruct((t, d), BF),
            jax.ShapeDtypeStruct((groups, 8, HEADS_PER_GROUP * t), F32),
        ],
        compiler_params=pltpu.CompilerParams(vmem_limit_bytes=40 << 20),
        cost_estimate=pl.CostEstimate(
            flops=16 * t * n * d, bytes_accessed=4 * t * d + 4 * n * d, transcendentals=12 * t * n
        ),
        name="attention_forward",
    )(info, queries, keyvals, keyvals)


def attention_backward_kernel(
    info_ref, q_ref, k_ref, v_ref, g_ref, o_ref, lse_ref, dq_ref, dk_ref, dv_ref, q4, g4, acc, *, kb
):
    t, n = q_ref.shape[0], k_ref.shape[0]
    q4[...] = spread_heads(q_ref[...] * jnp.asarray(HEAD_DIM**-0.5, BF))
    grads = spread_heads(g_ref[...])
    g4[...] = grads
    outs = jnp.concatenate([o_ref[...].astype(F32)] * HEADS_PER_GROUP, axis=0)
    product = grads.astype(F32) * outs
    high = product.astype(BF)
    low = (product - high.astype(F32)).astype(BF)
    ones = jnp.ones((8, GROUP), BF)
    dots = (mm(ones, high, NT) + mm(ones, low, NT))[:1]
    lse = lse_ref[0, :1, :]
    acc[...] = jnp.zeros_like(acc)

    def step(b, carry):
        at = pl.ds(pl.multiple_of(b * kb, kb), kb)
        keys, values = k_ref[at, :], v_ref[at, :]
        index = b * kb + lax.broadcasted_iota(jnp.int32, (kb, 1), 0)
        bias = key_bias(index, 0, n, t, info_ref)
        scores = mm(keys, q4[...], NT)
        probs = jnp.exp2((scores * LOG2E + bias) - lse)
        grad_probs = mm(values, g4[...], NT)
        grad_scores = (probs * (grad_probs - dots)).astype(BF)
        dv_ref[at, :] = mm(probs.astype(BF), g4[...]).astype(BF)
        dk_ref[at, :] = mm(grad_scores, q4[...]).astype(BF)
        acc[...] += mm(grad_scores, keys, TN)
        return carry

    lax.fori_loop(0, n // kb, step, 0)
    out = jnp.zeros((t, GROUP), F32)
    for h in range(HEADS_PER_GROUP):
        out = jnp.where(head_mask((t, GROUP), h), acc[pl.ds(h * t, t), :], out)
    dq_ref[...] = (out * HEAD_DIM**-0.5).astype(BF)


def attention_backward(info, queries, keyvals, grads, outs, lse):
    t, d = queries.shape
    n = keyvals.shape[0]
    groups = d // GROUP
    rows4 = HEADS_PER_GROUP * t
    query_spec = pl.BlockSpec((t, GROUP), lambda i: (0, i))
    key_spec = pl.BlockSpec((n, GROUP), lambda i: (0, i))
    return pl.pallas_call(
        functools.partial(attention_backward_kernel, kb=n // 2),
        grid=(groups,),
        in_specs=[
            pl.BlockSpec(memory_space=pltpu.SMEM),
            query_spec,
            key_spec,
            pl.BlockSpec((n, GROUP), lambda i: (0, i + groups)),
            query_spec,
            query_spec,
            pl.BlockSpec((1, 8, rows4), lambda i: (i, 0, 0)),
        ],
        out_specs=[query_spec, key_spec, key_spec],
        out_shape=[
            jax.ShapeDtypeStruct((t, d), BF),
            jax.ShapeDtypeStruct((n, d), BF),
            jax.ShapeDtypeStruct((n, d), BF),
        ],
        scratch_shapes=[
            pltpu.VMEM((rows4, GROUP), BF),
            pltpu.VMEM((rows4, GROUP), BF),
            pltpu.VMEM((rows4, GROUP), F32),
        ],
        compiler_params=pltpu.CompilerParams(vmem_limit_bytes=48 << 20),
        cost_estimate=pl.CostEstimate(
            flops=40 * t * n * d, bytes_accessed=8 * t * d + 8 * n * d, transcendentals=12 * t * n
        ),
        name="attention_backward",
    )(info, queries, keyvals, keyvals, grads, outs, lse)


WIDE = 48
EDGES = 10
FIELD_EDGE, TALL_EDGE = 4, 5


def refine_kernel(
    field_ref,
    weight_ref,
    bias_ref,
    factor_ref,
    offset_ref,
    cot_ref,
    joined_ref,
    grad_ref,
    dw_ref,
    db_ref,
    sums_ref,
    acts,
    slopes,
    grads3,
    work,
    frame,
    tall,
    lane2,
    edge,
    halo,
    send_sem,
    recv_sem,
    *,
    items,
    rows,
    count,
):
    me = lax.axis_index("rows")
    here = lax.axis_index("items")
    channels = field_ref.shape[-1]
    flat = items * rows * WIDE
    lanes = channels // 128
    column = lax.broadcasted_iota(jnp.int32, (WIDE, channels), 0)
    inside = column < PC

    barrier = pltpu.get_barrier_semaphore()
    for step in (-1, 1):

        @pl.when((me + step >= 0) & (me + step < count))
        def _():
            pl.semaphore_signal(
                barrier, inc=1, device_id=(here, me + step), device_id_type=pl.DeviceIdType.MESH
            )

    @pl.when((me > 0) & (me < count - 1))
    def _():
        pl.semaphore_wait(barrier, 2)

    @pl.when((me == 0) | (me == count - 1))
    def _():
        pl.semaphore_wait(barrier, 1)

    def each(side):
        return (me > 0) if side == 0 else (me < count - 1)

    def copy(e, side):
        return pltpu.make_async_remote_copy(
            src_ref=edge.at[e, side],
            dst_ref=halo.at[e, 1 - side],
            send_sem=send_sem.at[e, side],
            recv_sem=recv_sem.at[e, 1 - side],
            device_id=(here, me + (2 * side - 1)),
            device_id_type=pl.DeviceIdType.MESH,
        )

    def send(e):
        for side in (0, 1):

            @pl.when(each(side))
            def _():
                copy(e, side).start()

    def receive(e):
        for side in (0, 1):

            @pl.when(each(side))
            def _():
                pltpu.make_async_remote_copy(
                    src_ref=edge.at[e, side],
                    dst_ref=halo.at[e, side],
                    send_sem=send_sem.at[e, side],
                    recv_sem=recv_sem.at[e, side],
                    device_id=(here, me + (2 * side - 1)),
                    device_id_type=pl.DeviceIdType.MESH,
                ).wait_recv()

            @pl.when(jnp.logical_not(each(side)))
            def _():
                halo[e, side] = jnp.zeros(halo.shape[2:], BF)

    def shifted(values, flip):
        before = pltpu.roll(values, 1, 0)
        after = pltpu.roll(values, WIDE - 1, 0)
        parts = [after, values, before] if flip else [before, values, after]
        return jnp.concatenate([part.astype(BF) for part in parts], axis=1)

    def all_rows(body, e):
        for item in range(items):
            for row, side in ((0, 0), (rows - 1, 1)):
                body(item, row, (e, side))
        send(e)

        def step(row, carry):
            for item in range(items):
                body(item, row, None)
            return carry

        lax.fori_loop(1, rows - 1, step, 0)

    def spread_halo(target, e, flip):
        for side, row in ((0, 0), (1, rows + 1)):
            for item in range(items):
                target[item, row] = shifted(halo[e, side, item].astype(F32), flip)

    for item in range(items):
        factor = factor_ref[pl.ds(item, 1), :]

        def back(row, carry, item=item, factor=factor):
            whole = cot_ref[item, row].astype(F32) * factor
            for part in range(lanes):
                lane2[part, pl.ds(0, 2 * PC), :] = whole[:, part * 128 : (part + 1) * 128]
            even, odd = (
                jnp.concatenate(
                    [lane2[part, pl.ds(start, PC, stride=2), :] for part in range(lanes)], axis=1
                )
                for start in (0, 1)
            )
            place = lax.broadcasted_iota(jnp.int32, (PC, channels), 0)
            even_next = jnp.where(place == PC - 1, odd, pltpu.roll(even, PC - 1, 0))
            odd_prev = jnp.where(place == 0, even, pltpu.roll(odd, 1, 0))
            tall[item, row + 1, pl.ds(0, PC), :] = 0.75 * (even + odd) + 0.25 * (
                even_next + odd_prev
            )
            tall[item, row + 1, pl.ds(PC, WIDE - PC), :] = jnp.zeros((WIDE - PC, channels), F32)
            return carry

        lax.fori_loop(0, 2 * rows, back, 0)
        edge[TALL_EDGE, 0, item] = tall[item, 1].astype(BF)
        edge[TALL_EDGE, 1, item] = tall[item, 2 * rows].astype(BF)
    send(TALL_EDGE)

    def activate(source, which):
        def body(item, row, out):
            values = source[item, row]
            cdf, rest = normal_parts(values)
            act = jnp.where(inside, values * cdf, 0.0)
            slopes[which, item, row] = cdf + rest
            acts[which, item, row + 1] = shifted(act, False)
            if out is not None:
                edge[out[0], out[1], item] = act.astype(BF)

        all_rows(body, which)

    def weight_of(conv, kr):
        return weight_ref[conv, pl.ds(kr * 3 * channels, 3 * channels), :]

    def lhs(source, item, first, number):
        return source[item, pl.ds(first, number)].reshape(number * WIDE, -1)

    def forward(conv, add):
        bias = bias_ref[pl.ds(conv, 1), :]
        for item in range(items):
            centre = mm(lhs(acts.at[conv], item, 1, rows), weight_of(conv, 1)) + bias
            if add:
                centre = centre + frame[item, pl.ds(1, rows)].reshape(rows * WIDE, channels)
            work[item] = centre.reshape(rows, WIDE, channels)
            upper = mm(lhs(acts.at[conv], item, 1, rows - 1), weight_of(conv, 0))
            work[item, pl.ds(1, rows - 1)] += upper.reshape(rows - 1, WIDE, channels)
            lower = mm(lhs(acts.at[conv], item, 2, rows - 1), weight_of(conv, 2))
            work[item, pl.ds(0, rows - 1)] += lower.reshape(rows - 1, WIDE, channels)
        receive(conv)
        spread_halo(acts.at[conv], conv, False)
        for kr, source, row in ((0, 0, 0), (2, rows + 1, rows - 1)):
            block = jnp.concatenate([acts[conv, item, source] for item in range(items)], axis=0)
            extra = mm(block, weight_of(conv, kr))
            for item in range(items):
                work[item, row] += extra[item * WIDE : (item + 1) * WIDE]

    def keep_field(source):
        for item in range(items):
            frame[item, pl.ds(1, rows)] = source[item]

    keep_field(field_ref)
    for unit in (0, 1):
        activate(field_ref if unit == 0 else work, 2 * unit)
        forward(2 * unit, False)
        activate(work, 2 * unit + 1)
        forward(2 * unit + 1, True)
        keep_field(work)

    for item in range(items):
        edge[FIELD_EDGE, 0, item] = frame[item, 1].astype(BF)
        edge[FIELD_EDGE, 1, item] = frame[item, rows].astype(BF)
    send(FIELD_EDGE)

    receive(TALL_EDGE)
    for item in range(items):
        tall[item, 0] = jnp.where(me == 0, tall[item, 1], halo[TALL_EDGE, 0, item].astype(F32))
        tall[item, 2 * rows + 1] = jnp.where(
            me == count - 1, tall[item, 2 * rows], halo[TALL_EDGE, 1, item].astype(F32)
        )

        def fold(row, carry, item=item):
            grad_ref[item, row] = 0.75 * (
                tall[item, 2 * row + 1] + tall[item, 2 * row + 2]
            ) + 0.25 * (tall[item, 2 * row] + tall[item, 2 * row + 3])
            return carry

        lax.fori_loop(0, rows, fold, 0)

    receive(FIELD_EDGE)
    for item in range(items):
        frame[item, 0] = jnp.where(me == 0, frame[item, 1], halo[FIELD_EDGE, 0, item].astype(F32))
        frame[item, rows + 1] = jnp.where(
            me == count - 1, frame[item, rows], halo[FIELD_EDGE, 1, item].astype(F32)
        )
        factor = factor_ref[pl.ds(item, 1), :]
        offset = offset_ref[pl.ds(item, 1), :]

        def widen(row, carry, item=item, factor=factor, offset=offset):
            gain_sum, shift_sum = carry
            centre = frame[item, row + 1]
            for half in (0, 1):
                line = 0.75 * centre + 0.25 * frame[item, row + 2 * half]
                before = jnp.where(column == 0, line, pltpu.roll(line, 1, 0))
                after = jnp.where(column == PC - 1, line, pltpu.roll(line, WIDE - 1, 0))
                for start, side in ((0, before), (1, after)):
                    mixed = 0.75 * line + 0.25 * side
                    for part in range(lanes):
                        lane2[part, pl.ds(start, WIDE, stride=2), :] = mixed[
                            :, part * 128 : (part + 1) * 128
                        ]
                wide = jnp.concatenate(
                    [lane2[part, pl.ds(0, 2 * PC), :] for part in range(lanes)], axis=1
                )
                joined_ref[item, 2 * row + half] = (wide * factor + offset).astype(BF)
                cot = cot_ref[item, 2 * row + half].astype(F32)
                gain_sum = gain_sum + jnp.sum((cot * wide).reshape(-1, 8, channels), axis=0)
                shift_sum = shift_sum + jnp.sum(cot.reshape(-1, 8, channels), axis=0)
            return gain_sum, shift_sum

        zero = jnp.zeros((8, channels), F32)
        gain_sum, shift_sum = lax.fori_loop(0, rows, widen, (zero, zero))
        sums_ref[0, pl.ds(item, 1), :] = jnp.sum(gain_sum, axis=0, keepdims=True)
        sums_ref[1, pl.ds(item, 1), :] = jnp.sum(shift_sum, axis=0, keepdims=True)

    def grad_pass(conv, make):
        e = 6 + conv

        def body(item, row, out):
            values = jnp.where(inside, make(item, row), 0.0).astype(BF).astype(F32)
            grads3[item, row + 1] = shifted(values, True)
            if out is not None:
                edge[out[0], out[1], item] = values.astype(BF)

        all_rows(body, e)
        middle = jnp.concatenate(
            [
                grads3[item, pl.ds(1, rows), :, pl.ds(channels, channels)].reshape(
                    rows * WIDE, channels
                )
                for item in range(items)
            ],
            axis=0,
        )
        for kr in range(3):
            block = jnp.concatenate(
                [lhs(acts.at[conv], item, kr, rows) for item in range(items)], axis=0
            )
            dw_ref[conv, pl.ds(kr * 3 * channels, 3 * channels), :] = mm(block, middle, TN).astype(BF)
        ones = jnp.ones((8, flat), BF)
        db_ref[pl.ds(conv, 1), :] = mm(ones, middle)[:1]

        def product(block, kr):
            total = None
            for kc in range(3):
                part = mm(
                    block[:, kc * channels : (kc + 1) * channels],
                    weight_ref[conv, pl.ds((kr * 3 + kc) * channels, channels), :],
                    NT,
                )
                total = part if total is None else total + part
            return total

        for item in range(items):
            work[item] = product(lhs(grads3, item, 1, rows), 1).reshape(rows, WIDE, channels)
            work[item, pl.ds(1, rows - 1)] += product(lhs(grads3, item, 1, rows - 1), 2).reshape(
                rows - 1, WIDE, channels
            )
            work[item, pl.ds(0, rows - 1)] += product(lhs(grads3, item, 2, rows - 1), 0).reshape(
                rows - 1, WIDE, channels
            )
        receive(e)
        spread_halo(grads3, e, True)
        for kr, source, row in ((2, 0, 0), (0, rows + 1, rows - 1)):
            block = jnp.concatenate([grads3[item, source] for item in range(items)], axis=0)
            extra = product(block, kr)
            for item in range(items):
                work[item, row] += extra[item * WIDE : (item + 1) * WIDE]

    for unit in (1, 0):
        first, second = 2 * unit, 2 * unit + 1
        grad_pass(second, lambda item, row: grad_ref[item, row])
        grad_pass(first, lambda item, row: work[item, row] * slopes[second, item, row])

        def gather(row, carry, first=first):
            for item in range(items):
                grad_ref[item, row] += work[item, row] * slopes[first, item, row]
            return carry

        lax.fori_loop(0, rows, gather, 0)

    for e in range(EDGES):
        for side in (0, 1):

            @pl.when(each(side))
            def _():
                copy(e, side).wait_send()


def refine(field, conv_weights, conv_biases, factor, offset, cotangent):
    items, rows, _, channels = field.shape
    count = lax.axis_size("rows")
    padded = jnp.pad(field, ((0, 0), (0, 0), (0, WIDE - PC), (0, 0)))
    vmem = pl.BlockSpec(memory_space=pltpu.VMEM)
    pixels = items * rows * PC
    outs = pl.pallas_call(
        functools.partial(refine_kernel, items=items, rows=rows, count=count),
        in_specs=[vmem] * 6,
        out_specs=[vmem] * 5,
        out_shape=[
            jax.ShapeDtypeStruct((items, 2 * rows, 2 * PC, channels), BF),
            jax.ShapeDtypeStruct((items, rows, WIDE, channels), F32),
            jax.ShapeDtypeStruct(conv_weights.shape, BF),
            jax.ShapeDtypeStruct(conv_biases.shape, F32),
            jax.ShapeDtypeStruct((2, items, channels), F32),
        ],
        scratch_shapes=[
            pltpu.VMEM((4, items, rows + 2, WIDE, 3 * channels), BF),
            pltpu.VMEM((4, items, rows, WIDE, channels), F32),
            pltpu.VMEM((items, rows + 2, WIDE, 3 * channels), BF),
            pltpu.VMEM((items, rows, WIDE, channels), F32),
            pltpu.VMEM((items, rows + 2, WIDE, channels), F32),
            pltpu.VMEM((items, 2 * rows + 2, WIDE, channels), F32),
            pltpu.VMEM((channels // 128, 2 * WIDE, 128), F32),
            pltpu.VMEM((EDGES, 2, items, WIDE, channels), BF),
            pltpu.VMEM((EDGES, 2, items, WIDE, channels), BF),
            pltpu.SemaphoreType.DMA((EDGES, 2)),
            pltpu.SemaphoreType.DMA((EDGES, 2)),
        ],
        compiler_params=pltpu.CompilerParams(
            vmem_limit_bytes=56 << 20, collective_id=0, has_side_effects=True
        ),
        cost_estimate=pl.CostEstimate(
            flops=2 * 12 * pixels * 9 * channels * channels,
            bytes_accessed=20 << 20,
            transcendentals=8 * pixels * channels,
        ),
        name="refine",
    )(padded, conv_weights, conv_biases, factor, offset, cotangent)
    return outs


MESH = pl.DeviceIdType.MESH
STRIP = 256
LAG = 3


def flip(index, bit):
    return index + (1 - 2 * (index // (1 << bit) % 2)) * (1 << bit)


class Reducer:
    def __init__(self, chunks, depth, row_bits, item_bits):
        self.chunks, self.depth = chunks, depth
        self.row_bits, self.item_bits = row_bits, item_bits
        self.orders = (tuple(range(row_bits - 1, -1, -1)), tuple(range(row_bits)))
        self.far = max(item_bits - 2, 0)
        self.phases = 1 + row_bits + 1 + self.far + 1 + 1

    def scratch(self):
        c, half = self.chunks, self.depth // 2
        shares = (2,) * self.row_bits
        slots = [
            pltpu.VMEM((c,) + shares + (self.depth, 128), BF),
            pltpu.VMEM((c,) + shares + (self.depth, 128), BF),
        ]
        for stage in range(self.row_bits):
            for _ in (0, 1):
                slots.append(pltpu.VMEM((c,) + (2,) * (self.row_bits - 1 - stage) + (half, 128), BF))
        slots.append(pltpu.VMEM((c, half, 128), BF))
        for _ in range(self.far):
            slots.append(pltpu.VMEM((c, half, 128), BF))
            slots.append(pltpu.VMEM((c, half, 128), BF))
        arrivals = 1 + 1 + 2 * self.row_bits + 1 + self.far + 1 + 1
        sends = 1 + 2 * self.row_bits + 1 + self.far + 1 + 1
        return slots + [pltpu.SemaphoreType.DMA((arrivals, c)), pltpu.SemaphoreType.DMA((sends,))]

    def out_shape(self):
        return jax.ShapeDtypeStruct((2, self.chunks, self.depth, 128), BF)

    def bind(self, out_ref, slots):
        slots = list(slots)
        self.out = out_ref
        self.mine, self.core_in = slots[0], slots[1]
        self.row_in = [
            (slots[2 + 2 * stage], slots[3 + 2 * stage]) for stage in range(self.row_bits)
        ]
        rest = slots[2 + 2 * self.row_bits :]
        self.near_in = rest[0]
        self.far_out = [rest[1 + 2 * k] for k in range(self.far)]
        self.far_in = [rest[2 + 2 * k] for k in range(self.far)]
        self.recv_sem, self.send_sem = rest[-2], rest[-1]
        self.me = lax.axis_index("rows")
        self.at = lax.axis_index("items")
        self.core = self.at % 2
        self.near = self.at // 2 % 2

    def peers(self):
        found = [(flip(self.at, bit), self.me) for bit in range(self.item_bits)]
        return found + [(self.at, flip(self.me, bit)) for bit in range(self.row_bits)]

    def greet(self):
        barrier = pltpu.get_barrier_semaphore()
        for peer in self.peers():
            pl.semaphore_signal(barrier, inc=1, device_id=peer, device_id_type=MESH)
        pl.semaphore_wait(barrier, len(self.peers()))

    def remote(self, source, target, arrival, sent, chunk, peer):
        return pltpu.make_async_remote_copy(
            src_ref=source,
            dst_ref=target,
            send_sem=self.send_sem.at[sent],
            recv_sem=self.recv_sem.at[arrival, chunk],
            device_id=peer,
            device_id_type=MESH,
        )

    def first(self, view, column, chunk):
        lead = (slice(None),) * (self.row_bits + 1)
        theirs = view.at[lead + (pl.ds(pl.multiple_of(column + (1 - self.core) * 128, 128), 128),)]
        ours = view.at[lead + (pl.ds(pl.multiple_of(column + self.core * 128, 128), 128),)]
        self.remote(
            theirs, self.core_in.at[chunk], 0, 0, chunk, (flip(self.at, 0), self.me)
        ).start()
        pltpu.make_async_copy(ours, self.mine.at[chunk], self.recv_sem.at[1, chunk]).start()

    def bit(self, which):
        return self.me // (1 << which) % 2

    def shares(self, half, stage, sent):
        order = self.orders[half]
        index = [slice(None)] * self.row_bits
        for done in order[:stage]:
            index[self.row_bits - 1 - done] = self.bit(done)
        now = order[stage]
        index[self.row_bits - 1 - now] = 1 - self.bit(now) if sent else self.bit(now)
        return tuple(index)

    def rows(self, half):
        depth = self.depth // 2
        return pl.ds(half * depth, depth)

    def row_copy(self, stage, half, chunk):
        source = self.mine.at[(chunk,) + self.shares(half, stage, True) + (self.rows(half),)]
        return self.remote(
            source,
            self.row_in[stage][half].at[chunk],
            2 + 2 * stage + half,
            1 + 2 * stage + half,
            chunk,
            (self.at, flip(self.me, self.orders[half][stage])),
        )

    def own(self, chunk, rows):
        return (chunk,) + tuple(self.bit(b) for b in range(self.row_bits - 1, -1, -1)) + (rows,)

    def near_rows(self, mine):
        half = self.depth // 2
        place = self.near if mine else 1 - self.near
        return pl.ds(pl.multiple_of(place * half, half), half)

    def near_copy(self, chunk):
        return self.remote(
            self.mine.at[self.own(chunk, self.near_rows(False))],
            self.near_in.at[chunk],
            2 + 2 * self.row_bits,
            1 + 2 * self.row_bits,
            chunk,
            (flip(self.at, 1), self.me),
        )

    def far_copy(self, k, chunk):
        return self.remote(
            self.far_out[k].at[chunk],
            self.far_in[k].at[chunk],
            3 + 2 * self.row_bits + k,
            2 + 2 * self.row_bits + k,
            chunk,
            (flip(self.at, 2 + k), self.me),
        )

    def back_copy(self, chunk):
        place = self.out.at[self.core, chunk, self.near_rows(True)]
        return self.remote(
            place,
            place,
            3 + 2 * self.row_bits + self.far,
            2 + 2 * self.row_bits + self.far,
            chunk,
            (flip(self.at, 1), self.me),
        )

    def last_copy(self, chunk):
        place = self.out.at[self.core, chunk]
        return self.remote(
            place,
            place,
            4 + 2 * self.row_bits + self.far,
            3 + 2 * self.row_bits + self.far,
            chunk,
            (flip(self.at, 0), self.me),
        )

    def phase(self, number, chunk):
        bits, half = self.row_bits, self.depth // 2
        if number == 0:
            self.remote(
                self.core_in.at[chunk], self.core_in.at[chunk], 0, 0, chunk, (flip(self.at, 0), self.me)
            ).wait_recv()
            pltpu.make_async_copy(
                self.core_in.at[chunk], self.mine.at[chunk], self.recv_sem.at[1, chunk]
            ).wait()
            self.mine[chunk] = add_low(self.mine[chunk], self.core_in[chunk])
            for side in (0, 1):
                self.row_copy(0, side, chunk).start()
        elif number <= bits:
            stage = number - 1
            for side in (0, 1):
                self.row_copy(stage, side, chunk).wait_recv()
                at = (chunk,) + self.shares(side, stage, False) + (self.rows(side),)
                self.mine[at] = add_low(self.mine[at], self.row_in[stage][side][chunk])
                if stage + 1 < bits:
                    self.row_copy(stage + 1, side, chunk).start()
            if stage + 1 == bits:
                self.near_copy(chunk).start()
        elif number == bits + 1:
            self.near_copy(chunk).wait_recv()
            total = add_low(
                self.mine[self.own(chunk, self.near_rows(True))], self.near_in[chunk]
            )
            self.pass_on(0, chunk, total)
        elif number <= bits + 1 + self.far:
            k = number - bits - 2
            self.far_copy(k, chunk).wait_recv()
            self.pass_on(k + 1, chunk, add_low(self.far_out[k][chunk], self.far_in[k][chunk]))
        elif number == bits + 2 + self.far:
            self.back_copy_arrived(chunk)
            self.last_copy(chunk).start()
        else:
            self.last_arrived(chunk)

    def pass_on(self, k, chunk, total):
        if k < self.far:
            self.far_out[k][chunk] = total
            self.far_copy(k, chunk).start()
        else:
            self.out[self.core, chunk, self.near_rows(True)] = total
            self.back_copy(chunk).start()

    def back_copy_arrived(self, chunk):
        place = self.out.at[self.core, chunk, self.near_rows(False)]
        self.remote(
            place,
            place,
            3 + 2 * self.row_bits + self.far,
            2 + 2 * self.row_bits + self.far,
            chunk,
            (flip(self.at, 1), self.me),
        ).wait_recv()

    def last_arrived(self, chunk):
        place = self.out.at[1 - self.core, chunk]
        self.remote(
            place,
            place,
            4 + 2 * self.row_bits + self.far,
            3 + 2 * self.row_bits + self.far,
            chunk,
            (flip(self.at, 0), self.me),
        ).wait_recv()

    def step(self, t):
        for number in range(self.phases - 1, -1, -1):
            chunk = t - LAG * number

            @pl.when((chunk >= 0) & (chunk < self.chunks))
            def _():
                self.phase(number, jnp.clip(chunk, 0, self.chunks - 1))

    @property
    def steps(self):
        return self.chunks + LAG * (self.phases - 1)

    def finish(self):
        def drain(sem, ref):
            pltpu.make_async_copy(ref, ref, self.send_sem.at[sem]).wait()

        drain(0, self.core_in)
        for stage in range(self.row_bits):
            for side in (0, 1):
                drain(1 + 2 * stage + side, self.row_in[stage][side])
        base = 1 + 2 * self.row_bits
        drain(base, self.near_in)
        for k in range(self.far):
            drain(base + 1 + k, self.far_in[k])
        drain(base + 1 + self.far, self.near_in)
        drain(base + 2 + self.far, self.out.at[0])


def chunk_list(arrays, depth):
    found = []
    for number, array in enumerate(arrays):
        rows, columns = array.shape[-2:]
        lead = array.shape[0] if array.ndim == 3 else None
        for outer in range(lead or 1):
            for row in range(0, rows // lax.axis_size("rows"), depth):
                for column in range(0, columns, STRIP):
                    found.append((number, outer if lead else None, row, column))
    return found


def reduce_kernel(*refs, reducer, table, arrays):
    sources, out_ref, slots = refs[:arrays], refs[arrays], refs[arrays + 1 :]
    reducer.bind(out_ref, slots)
    reducer.greet()
    lead = (slice(None),) * reducer.row_bits
    for chunk, (number, outer, row, column) in enumerate(table):
        ref = sources[number] if outer is None else sources[number].at[outer]
        reducer.first(ref.at[lead + (pl.ds(row, reducer.depth), slice(None))], column, chunk)

    def step(t, carry):
        reducer.step(t)
        return carry

    lax.fori_loop(0, reducer.steps, step, 0)
    reducer.finish()


def share_views(arrays):
    bits = axis_bits("rows")
    views = []
    for array in arrays:
        lead = array.shape[:-2]
        views.append(
            array.reshape(lead + (2,) * bits + (array.shape[-2] >> bits, array.shape[-1]))
        )
    return views


def reduce_all(arrays, depth, collective_id):
    table = chunk_list(arrays, depth)
    reducer = Reducer(len(table), depth, axis_bits("rows"), axis_bits("items"))
    out = pl.pallas_call(
        functools.partial(reduce_kernel, reducer=reducer, table=table, arrays=len(arrays)),
        in_specs=[pl.BlockSpec(memory_space=pl.ANY)] * len(arrays),
        out_specs=pl.BlockSpec(memory_space=pltpu.VMEM),
        out_shape=reducer.out_shape(),
        scratch_shapes=reducer.scratch(),
        compiler_params=pltpu.CompilerParams(
            vmem_limit_bytes=58 << 20, collective_id=collective_id, has_side_effects=True
        ),
        name="reduce_weights",
    )(*share_views(arrays))
    return unpack(out, arrays, table, depth)


def unpack_kernel(held_ref, *refs, table, depth, outs):
    targets, (wide, sem) = refs[:outs], refs[outs:]

    def copy(chunk, number, outer, row, column):
        target = targets[number] if outer is None else targets[number].at[outer]
        return pltpu.make_async_copy(
            wide.at[chunk],
            target.at[pl.ds(row, depth), pl.ds(column, STRIP)],
            sem.at[chunk],
        )

    for chunk, entry in enumerate(table):
        wide[chunk] = jnp.concatenate(
            [held_ref[0, chunk].astype(F32), held_ref[1, chunk].astype(F32)], axis=1
        )
        copy(chunk, *entry).start()
    for chunk, entry in enumerate(table):
        copy(chunk, *entry).wait()


def unpack(out, arrays, table, depth):
    count = lax.axis_size("rows")
    shapes = [
        jax.ShapeDtypeStruct(
            array.shape[:-2] + (array.shape[-2] // count, array.shape[-1]), F32
        )
        for array in arrays
    ]
    return pl.pallas_call(
        functools.partial(unpack_kernel, table=table, depth=depth, outs=len(arrays)),
        in_specs=[pl.BlockSpec(memory_space=pltpu.VMEM)],
        out_specs=[pl.BlockSpec(memory_space=pl.ANY)] * len(arrays),
        out_shape=shapes,
        scratch_shapes=[
            pltpu.VMEM((len(table), depth, STRIP), F32),
            pltpu.SemaphoreType.DMA((len(table),)),
        ],
        compiler_params=pltpu.CompilerParams(vmem_limit_bytes=40 << 20),
        name="unpack",
    )(out)


def shards(
    tokens,
    valid_rows,
    dataset_ids,
    shift_flags,
    norm_gains,
    norm_biases,
    qkv_weight,
    qv_bias,
    out_weight,
    out_bias,
    fc1_weight,
    fc1_bias,
    fc2_weight,
    fc2_bias,
    tap_weight,
    tap_bias,
    conv_weights,
    conv_biases,
    table_gain,
    table_shift,
    token_cotangent,
    joined_cotangent,
):
    items_here, tok_here, width = tokens.shape
    rows_here = tok_here // PC
    channels = tap_weight.shape[1]
    row_index = lax.axis_index("rows")
    row_count = lax.axis_size("rows")
    last_index = row_count - 1

    flat_in = tokens.reshape(-1, width).astype(F32)
    normed_one = layer_norm(flat_in, norm_gains[0], norm_biases[0]).astype(BF)
    normed_all = [
        gather_blocks(normed_one[i * tok_here : (i + 1) * tok_here]) for i in range(items_here)
    ]
    starts = jnp.stack([(row_index ^ j) * tok_here for j in range(row_count)]).astype(jnp.int32)
    infos = [
        jnp.concatenate([valid_rows[i : i + 1] * PC, starts]) for i in range(items_here)
    ]
    key_weight = qkv_weight[:, width:]
    key_shift = jnp.concatenate([jnp.zeros((width,), F32), qv_bias[width:]])
    queries = (mm(normed_one, qkv_weight[:, :width]) + qv_bias[:width]).astype(BF)
    queries = [queries[i * tok_here : (i + 1) * tok_here] for i in range(items_here)]
    keyvals, attended, lses = [], [], []
    for i in range(items_here):
        keyvals.append((mm(normed_all[i], key_weight) + key_shift).astype(BF))
        out, lse = attention_forward(infos[i], queries[i], keyvals[i])
        attended.append(out)
        lses.append(lse)
    attended_flat = jnp.concatenate(attended)
    resid = flat_in + mm(attended_flat, out_weight) + out_bias
    normed_two = layer_norm(resid, norm_gains[1], norm_biases[1]).astype(BF)
    hidden_pre = mm(normed_two, fc1_weight) + fc1_bias
    hidden_cdf, hidden_rest = normal_parts(hidden_pre)
    hidden = (hidden_pre * hidden_cdf).astype(BF)
    hidden_slope = (hidden_cdf + hidden_rest).astype(BF)
    output = resid + mm(hidden, fc2_weight) + fc2_bias
    output_low = output.astype(BF)
    grid_rows = row_index * rows_here + jnp.arange(rows_here, dtype=jnp.int32)
    row_valid = (grid_rows[None, :] < valid_rows[:, None]).astype(F32)
    token_valid = jnp.broadcast_to(
        row_valid[:, :, None], (items_here, rows_here, PC)
    ).reshape(-1, 1)
    tap_pre = mm(output_low, tap_weight) + tap_bias
    field = (tap_pre * token_valid).reshape(items_here, rows_here, PC, channels)

    choose = (
        dataset_ids[:, None] == jnp.arange(table_gain.shape[0], dtype=jnp.int32)[None, :]
    ).astype(F32)
    flag_value = shift_flags.astype(F32)[:, None]
    gain_pick = jnp.dot(choose, table_gain, precision=highest)
    shift_pick = jnp.dot(choose, table_shift, precision=highest)
    factor = 1.0 + flag_value * (gain_pick - 1.0)
    offset = flag_value * shift_pick
    joined, grad_field, conv_grads, grad_conv_biases, table_sums = refine(
        field, conv_weights, conv_biases, factor, offset, joined_cotangent
    )
    grad_table_gain = jnp.dot(choose.T, flag_value * table_sums[0], precision=highest)
    grad_table_shift = jnp.dot(choose.T, flag_value * table_sums[1], precision=highest)
    grad_field = grad_field[:, :, :PC]
    grad_tap = (grad_field.reshape(-1, channels) * token_valid).astype(BF)
    tap_grad = mm(output_low, grad_tap, TN).astype(BF)
    grad_tap_bias = jnp.sum(grad_tap.astype(F32), axis=0)
    grad_output = token_cotangent.reshape(-1, width).astype(F32) + mm(grad_tap, tap_weight, NT)
    grad_mlp = grad_output.astype(BF)
    fc2_grad = mm(hidden, grad_mlp, TN).astype(BF)
    grad_fc2_bias = jnp.sum(grad_mlp.astype(F32), axis=0)
    grad_pre = (mm(grad_mlp, fc2_weight, NT) * hidden_slope.astype(F32)).astype(BF)
    fc1_grad = mm(normed_two, grad_pre, TN).astype(BF)
    grad_fc1_bias = jnp.sum(grad_pre.astype(F32), axis=0)
    grad_normed_two = mm(grad_pre, fc1_weight, NT)
    grad_resid_norm, grad_gain_two, grad_shift_two = norm_back(
        resid, norm_gains[1], grad_normed_two
    )
    grad_resid = grad_output + grad_resid_norm
    grad_branch = grad_resid.astype(BF)
    out_grad = mm(attended_flat, grad_branch, TN).astype(BF)
    grad_out_bias = jnp.sum(grad_branch.astype(F32), axis=0)
    grad_attended = mm(grad_branch, out_weight, NT).astype(BF)

    grads_q, grads_k, grads_v, grads_in = [], [], [], []
    for i in range(items_here):
        here = slice(i * tok_here, (i + 1) * tok_here)
        grad_q, grad_k, grad_v = attention_backward(
            infos[i], queries[i], keyvals[i], grad_attended[here], attended[i], lses[i]
        )
        partial = (
            mm(grad_k, qkv_weight[:, width : 2 * width], NT)
            + mm(grad_v, qkv_weight[:, 2 * width :], NT)
        ).astype(BF)
        own = mm(grad_q, qkv_weight[:, :width], NT)
        grads_in.append(scatter_blocks(partial) + own)
        grads_q.append(grad_q)
        grads_k.append(grad_k)
        grads_v.append(grad_v)
    grad_q = jnp.concatenate(grads_q)
    every_norm = jnp.concatenate(normed_all)
    every_k = jnp.concatenate(grads_k)
    every_v = jnp.concatenate(grads_v)
    q_grad = mm(normed_one, grad_q, TN).astype(BF)
    k_grad = mm(every_norm, every_k, TN).astype(BF)
    v_grad = mm(every_norm, every_v, TN).astype(BF)
    qkv_grad = jnp.concatenate([q_grad, k_grad, v_grad], axis=1)
    grad_q_bias = jnp.sum(grad_q.astype(F32), axis=0)
    grad_v_bias = jnp.sum(every_v.astype(F32), axis=0)
    grad_in_norm, grad_gain_one, grad_shift_one = norm_back(
        flat_in, norm_gains[0], jnp.concatenate(grads_in)
    )
    grad_tokens = (grad_resid + grad_in_norm).reshape(tokens.shape)

    small = [
        (jnp.stack([grad_gain_one, grad_gain_two]), 1),
        (jnp.stack([grad_shift_one, grad_shift_two]), 1),
        (jnp.concatenate([grad_q_bias, grad_v_bias]), 0),
        (grad_out_bias, 0),
        (grad_fc1_bias, 0),
        (grad_fc2_bias, 0),
        (grad_tap_bias, 0),
        (grad_conv_biases, 1),
        (grad_table_gain, 1),
        (grad_table_shift, 1),
    ]
    packed, shapes = [], []
    for array, dim in small:
        if array.ndim == 1:
            pieces = array.reshape(row_count, -1)
        else:
            pieces = jnp.swapaxes(
                array.reshape(array.shape[0], row_count, -1), 0, 1
            ).reshape(row_count, -1)
        shapes.append((array.ndim, array.shape[0], pieces.shape[1]))
        packed.append(pieces)
    packed = jnp.concatenate(packed, axis=1)
    depth = width // row_count
    size = packed.shape[1]
    packed = jnp.pad(packed, ((0, 0), (0, depth * STRIP - size))).astype(BF)
    packed = packed.reshape(row_count * depth, STRIP)
    (
        share_conv,
        share_tap,
        share_fc2,
        share_fc1,
        share_out,
        share_qkv,
        summed,
    ) = reduce_all(
        [conv_grads, tap_grad, fc2_grad, fc1_grad, out_grad, qkv_grad, packed], depth, 1
    )
    summed = summed.reshape(-1)
    outs, place = [], 0
    for ndim, lead, length in shapes:
        piece = summed[place : place + length]
        place += length
        outs.append(piece if ndim == 1 else piece.reshape(lead, -1))
    (
        out_gains,
        out_shifts,
        out_qv,
        out_out,
        out_fc1,
        out_fc2,
        out_tap,
        out_conv,
        out_table_gain,
        out_table_shift,
    ) = outs
    return (
        output_low.reshape(tokens.shape),
        joined,
        grad_tokens,
        out_gains,
        out_shifts,
        share_qkv,
        out_qv,
        share_out,
        out_out,
        share_fc1,
        out_fc1,
        share_fc2,
        out_fc2,
        share_tap,
        out_tap,
        share_conv,
        out_conv,
        out_table_gain,
        out_table_shift,
    )


def solution(mesh):
    return jax.shard_map(
        shards,
        mesh=mesh,
        in_specs=(P("items", "rows", None), P("items"), P("items"), P("items"))
        + (P(),) * 16
        + (P("items", "rows", None), P("items", "rows", None, None)),
        out_specs=(
            P("items", "rows", None),
            P("items", "rows", None, None),
            P("items", "rows", None),
            P(None, "rows"),
            P(None, "rows"),
            P("rows", None),
            P("rows"),
            P("rows", None),
            P("rows"),
            P("rows", None),
            P("rows"),
            P("rows", None),
            P("rows"),
            P("rows", None),
            P("rows"),
            P(None, "rows", None),
            P(None, "rows"),
            P(None, "rows"),
            P(None, "rows"),
        ),
        check_vma=False,
    )
```

```python
import functools

import jax
import jax.numpy as jnp
from jax import lax
from jax.experimental import pallas as pl
from jax.experimental.pallas import tpu as pltpu
from jax.sharding import PartitionSpec as P

HEAD_DIM = 64
PC = 40
GROUP = 256
HEADS_PER_GROUP = GROUP // HEAD_DIM

BF = jnp.bfloat16
F32 = jnp.float32
LOG2E = 1.4426950408889634
MASKED = -1e30
NN = (((1,), (0,)), ((), ()))
NT = (((1,), (1,)), ((), ()))
TN = (((0,), (0,)), ((), ()))

epsilon = 1e-06
highest = lax.Precision.HIGHEST


def mm(left, right, dims=NN):
    return lax.dot_general(left, right, dims, preferred_element_type=F32)


def normal_parts(values):
    bell = jnp.exp2(values * values * (-0.5 * LOG2E))
    t = 1.0 / (1.0 + (0.3275911 * 0.7071067811865476) * jnp.abs(values))
    poly = t * (
        0.5 * 0.254829592
        + t
        * (
            0.5 * -0.284496736
            + t * (0.5 * 1.421413741 + t * (0.5 * -1.453152027 + t * (0.5 * 1.061405429)))
        )
    )
    tail = poly * bell
    cdf = jnp.where(values >= 0.0, 1.0 - tail, tail)
    return cdf, values * bell * 0.3989422804014327


def gelu_exact(values):
    return values * normal_parts(values)[0]


def gelu_slope(values):
    cdf, slope = normal_parts(values)
    return cdf + slope


def gelu_back(values, grad_out):
    return gelu_slope(values) * grad_out


def norm_stats(values):
    centre = jnp.mean(values, axis=-1, keepdims=True)
    centred = values - centre
    spread = jnp.mean(centred * centred, axis=-1, keepdims=True)
    rstd = lax.rsqrt(spread + epsilon)
    return centred * rstd, rstd


def layer_norm(values, gain, shift):
    return norm_stats(values)[0] * gain + shift


def norm_back(values, gain, grad_out):
    unit, rstd = norm_stats(values)
    scaled = grad_out * gain
    mean_one = jnp.mean(scaled, axis=-1, keepdims=True)
    mean_two = jnp.mean(scaled * unit, axis=-1, keepdims=True)
    result = rstd * (scaled - mean_one - unit * mean_two)
    return result, jnp.sum(grad_out * unit, axis=0), jnp.sum(grad_out, axis=0)


def swap(block, axis, mask):
    count = lax.axis_size(axis)
    return lax.ppermute(block, axis, [(i, i ^ mask) for i in range(count)])


def axis_bits(axis):
    return (lax.axis_size(axis) - 1).bit_length()


def gather_blocks(block):
    bits = axis_bits("rows")
    half = block.shape[0] // 2
    halves = []
    for order, part in (
        (range(bits), block[:half]),
        (range(bits - 1, -1, -1), block[half:]),
    ):
        held = {0: part}
        for bit in order:
            keys = sorted(held)
            sent = jnp.concatenate([held[key] for key in keys]) if len(keys) > 1 else held[keys[0]]
            got = swap(sent, "rows", 1 << bit)
            for place, key in enumerate(keys):
                held[key | (1 << bit)] = got[place * half : (place + 1) * half]
        halves.append(held)
    blocks = []
    for j in range(1 << bits):
        blocks += [halves[0][j], halves[1][j]]
    return jnp.concatenate(blocks)


def add_low(first, second):
    return (first.astype(F32) + second.astype(F32)).astype(BF)


def head_mask(shape, head):
    lane = lax.broadcasted_iota(jnp.int32, shape, 1)
    return lane // HEAD_DIM == head


def spread_heads(block):
    zero = jnp.zeros_like(block)
    return jnp.concatenate(
        [jnp.where(head_mask(block.shape, h), block, zero) for h in range(HEADS_PER_GROUP)],
        axis=0,
    )


def key_bias(index, dim, length, block, info_ref):
    start = jnp.full_like(index, info_ref[1])
    for j in range(1, length // block):
        start = jnp.where(index >= j * block, info_ref[1 + j] - j * block, start)
    return jnp.where(index + start < info_ref[0], 0.0, MASKED).astype(F32)


def attention_forward_kernel(info_ref, q_ref, k_ref, v_ref, o_ref, lse_ref):
    t, n = q_ref.shape[0], k_ref.shape[0]
    bias = key_bias(lax.broadcasted_iota(jnp.int32, (1, n), 1), 1, n, t, info_ref)
    keys, values = k_ref[...], v_ref[...]
    queries = q_ref[...] * jnp.asarray(HEAD_DIM**-0.5, BF)
    out = jnp.zeros((t, GROUP), F32)
    for h in range(HEADS_PER_GROUP):
        mask = head_mask((t, GROUP), h)
        one = jnp.where(mask, queries, jnp.zeros_like(queries))
        scores = mm(one, keys, NT) + bias
        top = jnp.max(scores, axis=1, keepdims=True)
        probs = jnp.exp2((scores - top) * LOG2E)
        total = jnp.sum(probs, axis=1, keepdims=True)
        weighted = mm(probs.astype(BF), values)
        out = jnp.where(mask, weighted * (1.0 / total), out)
        lse = top * LOG2E + jnp.log2(total)
        lse_ref[0, :, pl.ds(h * t, t)] = jnp.transpose(jnp.broadcast_to(lse, (t, 128)))[:8]
    o_ref[...] = out.astype(BF)


def attention_forward(info, queries, keyvals):
    t, d = queries.shape
    n = keyvals.shape[0]
    groups = d // GROUP
    return pl.pallas_call(
        attention_forward_kernel,
        grid=(groups,),
        in_specs=[
            pl.BlockSpec(memory_space=pltpu.SMEM),
            pl.BlockSpec((t, GROUP), lambda i: (0, i)),
            pl.BlockSpec((n, GROUP), lambda i: (0, i)),
            pl.BlockSpec((n, GROUP), lambda i: (0, i + groups)),
        ],
        out_specs=[
            pl.BlockSpec((t, GROUP), lambda i: (0, i)),
            pl.BlockSpec((1, 8, HEADS_PER_GROUP * t), lambda i: (i, 0, 0)),
        ],
        out_shape=[
            jax.ShapeDtypeStruct((t, d), BF),
            jax.ShapeDtypeStruct((groups, 8, HEADS_PER_GROUP * t), F32),
        ],
        compiler_params=pltpu.CompilerParams(vmem_limit_bytes=40 << 20),
        cost_estimate=pl.CostEstimate(
            flops=16 * t * n * d, bytes_accessed=4 * t * d + 4 * n * d, transcendentals=12 * t * n
        ),
        name="attention_forward",
    )(info, queries, keyvals, keyvals)


WIDE = 48
EDGES = 10
FIELD_EDGE, TALL_EDGE = 4, 5


def refine_kernel(
    field_ref,
    weight_ref,
    bias_ref,
    factor_ref,
    offset_ref,
    cot_ref,
    joined_ref,
    grad_ref,
    dw_ref,
    db_ref,
    sums_ref,
    acts,
    slopes,
    grads3,
    work,
    frame,
    tall,
    lane2,
    edge,
    halo,
    send_sem,
    recv_sem,
    *,
    items,
    rows,
    count,
    depth,
):
    bits = (count - 1).bit_length()
    per_share = 9 * field_ref.shape[-1] // count // depth
    me = lax.axis_index("rows")
    here = lax.axis_index("items")
    channels = field_ref.shape[-1]
    flat = items * rows * WIDE
    lanes = channels // 128
    column = lax.broadcasted_iota(jnp.int32, (WIDE, channels), 0)
    inside = column < PC

    barrier = pltpu.get_barrier_semaphore()
    for step in (-1, 1):

        @pl.when((me + step >= 0) & (me + step < count))
        def _():
            pl.semaphore_signal(
                barrier, inc=1, device_id=(here, me + step), device_id_type=pl.DeviceIdType.MESH
            )

    @pl.when((me > 0) & (me < count - 1))
    def _():
        pl.semaphore_wait(barrier, 2)

    @pl.when((me == 0) | (me == count - 1))
    def _():
        pl.semaphore_wait(barrier, 1)

    def each(side):
        return (me > 0) if side == 0 else (me < count - 1)

    def copy(e, side):
        return pltpu.make_async_remote_copy(
            src_ref=edge.at[e, side],
            dst_ref=halo.at[e, 1 - side],
            send_sem=send_sem.at[e, side],
            recv_sem=recv_sem.at[e, 1 - side],
            device_id=(here, me + (2 * side - 1)),
            device_id_type=pl.DeviceIdType.MESH,
        )

    def send(e):
        for side in (0, 1):

            @pl.when(each(side))
            def _():
                copy(e, side).start()

    def receive(e):
        for side in (0, 1):

            @pl.when(each(side))
            def _():
                pltpu.make_async_remote_copy(
                    src_ref=edge.at[e, side],
                    dst_ref=halo.at[e, side],
                    send_sem=send_sem.at[e, side],
                    recv_sem=recv_sem.at[e, side],
                    device_id=(here, me + (2 * side - 1)),
                    device_id_type=pl.DeviceIdType.MESH,
                ).wait_recv()

            @pl.when(jnp.logical_not(each(side)))
            def _():
                halo[e, side] = jnp.zeros(halo.shape[2:], BF)

    def shifted(values, flip):
        before = pltpu.roll(values, 1, 0)
        after = pltpu.roll(values, WIDE - 1, 0)
        parts = [after, values, before] if flip else [before, values, after]
        return jnp.concatenate([part.astype(BF) for part in parts], axis=1)

    def all_rows(body, e):
        for item in range(items):
            for row, side in ((0, 0), (rows - 1, 1)):
                body(item, row, (e, side))
        send(e)

        def step(row, carry):
            for item in range(items):
                body(item, row, None)
            return carry

        lax.fori_loop(1, rows - 1, step, 0)

    def spread_halo(target, e, flip):
        for side, row in ((0, 0), (1, rows + 1)):
            for item in range(items):
                target[item, row] = shifted(halo[e, side, item].astype(F32), flip)

    for item in range(items):
        factor = factor_ref[pl.ds(item, 1), :]

        def back(row, carry, item=item, factor=factor):
            whole = cot_ref[item, row].astype(F32) * factor
            for part in range(lanes):
                lane2[part, pl.ds(0, 2 * PC), :] = whole[:, part * 128 : (part + 1) * 128]
            even, odd = (
                jnp.concatenate(
                    [lane2[part, pl.ds(start, PC, stride=2), :] for part in range(lanes)], axis=1
                )
                for start in (0, 1)
            )
            place = lax.broadcasted_iota(jnp.int32, (PC, channels), 0)
            even_next = jnp.where(place == PC - 1, odd, pltpu.roll(even, PC - 1, 0))
            odd_prev = jnp.where(place == 0, even, pltpu.roll(odd, 1, 0))
            tall[item, row + 1, pl.ds(0, PC), :] = 0.75 * (even + odd) + 0.25 * (
                even_next + odd_prev
            )
            tall[item, row + 1, pl.ds(PC, WIDE - PC), :] = jnp.zeros((WIDE - PC, channels), F32)
            return carry

        lax.fori_loop(0, 2 * rows, back, 0)
        edge[TALL_EDGE, 0, item] = tall[item, 1].astype(BF)
        edge[TALL_EDGE, 1, item] = tall[item, 2 * rows].astype(BF)
    send(TALL_EDGE)

    def activate(source, which):
        def body(item, row, out):
            values = source[item, row]
            cdf, rest = normal_parts(values)
            act = jnp.where(inside, values * cdf, 0.0)
            slopes[which, item, row] = cdf + rest
            acts[which, item, row + 1] = shifted(act, False)
            if out is not None:
                edge[out[0], out[1], item] = act.astype(BF)

        all_rows(body, which)

    def weight_of(conv, kr):
        return weight_ref[conv, pl.ds(kr * 3 * channels, 3 * channels), :]

    def lhs(source, item, first, number):
        return source[item, pl.ds(first, number)].reshape(number * WIDE, -1)

    def forward(conv, add):
        bias = bias_ref[pl.ds(conv, 1), :]
        for item in range(items):
            centre = mm(lhs(acts.at[conv], item, 1, rows), weight_of(conv, 1)) + bias
            if add:
                centre = centre + frame[item, pl.ds(1, rows)].reshape(rows * WIDE, channels)
            work[item] = centre.reshape(rows, WIDE, channels)
            upper = mm(lhs(acts.at[conv], item, 1, rows - 1), weight_of(conv, 0))
            work[item, pl.ds(1, rows - 1)] += upper.reshape(rows - 1, WIDE, channels)
            lower = mm(lhs(acts.at[conv], item, 2, rows - 1), weight_of(conv, 2))
            work[item, pl.ds(0, rows - 1)] += lower.reshape(rows - 1, WIDE, channels)
        receive(conv)
        spread_halo(acts.at[conv], conv, False)
        for kr, source, row in ((0, 0, 0), (2, rows + 1, rows - 1)):
            block = jnp.concatenate([acts[conv, item, source] for item in range(items)], axis=0)
            extra = mm(block, weight_of(conv, kr))
            for item in range(items):
                work[item, row] += extra[item * WIDE : (item + 1) * WIDE]

    def keep_field(source):
        for item in range(items):
            frame[item, pl.ds(1, rows)] = source[item]

    keep_field(field_ref)
    for unit in (0, 1):
        activate(field_ref if unit == 0 else work, 2 * unit)
        forward(2 * unit, False)
        activate(work, 2 * unit + 1)
        forward(2 * unit + 1, True)
        keep_field(work)

    for item in range(items):
        edge[FIELD_EDGE, 0, item] = frame[item, 1].astype(BF)
        edge[FIELD_EDGE, 1, item] = frame[item, rows].astype(BF)
    send(FIELD_EDGE)

    receive(TALL_EDGE)
    for item in range(items):
        tall[item, 0] = jnp.where(me == 0, tall[item, 1], halo[TALL_EDGE, 0, item].astype(F32))
        tall[item, 2 * rows + 1] = jnp.where(
            me == count - 1, tall[item, 2 * rows], halo[TALL_EDGE, 1, item].astype(F32)
        )

        def fold(row, carry, item=item):
            grad_ref[item, row] = 0.75 * (
                tall[item, 2 * row + 1] + tall[item, 2 * row + 2]
            ) + 0.25 * (tall[item, 2 * row] + tall[item, 2 * row + 3])
            return carry

        lax.fori_loop(0, rows, fold, 0)

    receive(FIELD_EDGE)
    for item in range(items):
        frame[item, 0] = jnp.where(me == 0, frame[item, 1], halo[FIELD_EDGE, 0, item].astype(F32))
        frame[item, rows + 1] = jnp.where(
            me == count - 1, frame[item, rows], halo[FIELD_EDGE, 1, item].astype(F32)
        )
        factor = factor_ref[pl.ds(item, 1), :]
        offset = offset_ref[pl.ds(item, 1), :]

        def widen(row, carry, item=item, factor=factor, offset=offset):
            gain_sum, shift_sum = carry
            centre = frame[item, row + 1]
            for half in (0, 1):
                line = 0.75 * centre + 0.25 * frame[item, row + 2 * half]
                before = jnp.where(column == 0, line, pltpu.roll(line, 1, 0))
                after = jnp.where(column == PC - 1, line, pltpu.roll(line, WIDE - 1, 0))
                for start, side in ((0, before), (1, after)):
                    mixed = 0.75 * line + 0.25 * side
                    for part in range(lanes):
                        lane2[part, pl.ds(start, WIDE, stride=2), :] = mixed[
                            :, part * 128 : (part + 1) * 128
                        ]
                wide = jnp.concatenate(
                    [lane2[part, pl.ds(0, 2 * PC), :] for part in range(lanes)], axis=1
                )
                joined_ref[item, 2 * row + half] = (wide * factor + offset).astype(BF)
                cot = cot_ref[item, 2 * row + half].astype(F32)
                gain_sum = gain_sum + jnp.sum((cot * wide).reshape(-1, 8, channels), axis=0)
                shift_sum = shift_sum + jnp.sum(cot.reshape(-1, 8, channels), axis=0)
            return gain_sum, shift_sum

        zero = jnp.zeros((8, channels), F32)
        gain_sum, shift_sum = lax.fori_loop(0, rows, widen, (zero, zero))
        sums_ref[0, pl.ds(item, 1), :] = jnp.sum(gain_sum, axis=0, keepdims=True)
        sums_ref[1, pl.ds(item, 1), :] = jnp.sum(shift_sum, axis=0, keepdims=True)

    def grad_pass(conv, make):
        e = 6 + conv

        def body(item, row, out):
            values = jnp.where(inside, make(item, row), 0.0).astype(BF).astype(F32)
            grads3[item, row + 1] = shifted(values, True)
            if out is not None:
                edge[out[0], out[1], item] = values.astype(BF)

        all_rows(body, e)
        middle = jnp.concatenate(
            [
                grads3[item, pl.ds(1, rows), :, pl.ds(channels, channels)].reshape(
                    rows * WIDE, channels
                )
                for item in range(items)
            ],
            axis=0,
        )
        for kr in range(3):
            block = jnp.concatenate(
                [lhs(acts.at[conv], item, kr, rows) for item in range(items)], axis=0
            )
            weight = mm(block, middle, TN).astype(BF)
            pieces = 3 * channels // depth
            for k in range(pieces):
                share, place = divmod(kr * pieces + k, per_share)
                at = tuple(share >> b & 1 for b in range(bits - 1, -1, -1))
                dw_ref[(conv,) + at + (slice(None), pl.ds(place * channels, channels))] = weight[
                    k * depth : (k + 1) * depth
                ]
        ones = jnp.ones((8, flat), BF)
        db_ref[pl.ds(conv, 1), :] = mm(ones, middle)[:1]

        def product(block, kr):
            total = None
            for kc in range(3):
                part = mm(
                    block[:, kc * channels : (kc + 1) * channels],
                    weight_ref[conv, pl.ds((kr * 3 + kc) * channels, channels), :],
                    NT,
                )
                total = part if total is None else total + part
            return total

        for item in range(items):
            work[item] = product(lhs(grads3, item, 1, rows), 1).reshape(rows, WIDE, channels)
            work[item, pl.ds(1, rows - 1)] += product(lhs(grads3, item, 1, rows - 1), 2).reshape(
                rows - 1, WIDE, channels
            )
            work[item, pl.ds(0, rows - 1)] += product(lhs(grads3, item, 2, rows - 1), 0).reshape(
                rows - 1, WIDE, channels
            )
        receive(e)
        spread_halo(grads3, e, True)
        for kr, source, row in ((2, 0, 0), (0, rows + 1, rows - 1)):
            block = jnp.concatenate([grads3[item, source] for item in range(items)], axis=0)
            extra = product(block, kr)
            for item in range(items):
                work[item, row] += extra[item * WIDE : (item + 1) * WIDE]

    for unit in (1, 0):
        first, second = 2 * unit, 2 * unit + 1
        grad_pass(second, lambda item, row: grad_ref[item, row])
        grad_pass(first, lambda item, row: work[item, row] * slopes[second, item, row])

        def gather(row, carry, first=first):
            for item in range(items):
                grad_ref[item, row] += work[item, row] * slopes[first, item, row]
            return carry

        lax.fori_loop(0, rows, gather, 0)

    for e in range(EDGES):
        for side in (0, 1):

            @pl.when(each(side))
            def _():
                copy(e, side).wait_send()


def refine(field, conv_weights, conv_biases, factor, offset, cotangent, depth):
    items, rows, _, channels = field.shape
    count = lax.axis_size("rows")
    padded = jnp.pad(field, ((0, 0), (0, 0), (0, WIDE - PC), (0, 0)))
    vmem = pl.BlockSpec(memory_space=pltpu.VMEM)
    pixels = items * rows * PC
    outs = pl.pallas_call(
        functools.partial(refine_kernel, items=items, rows=rows, count=count, depth=depth),
        in_specs=[vmem] * 6,
        out_specs=[vmem] * 5,
        out_shape=[
            jax.ShapeDtypeStruct((items, 2 * rows, 2 * PC, channels), BF),
            jax.ShapeDtypeStruct((items, rows, WIDE, channels), F32),
            jax.ShapeDtypeStruct(
                conv_weights.shape[:1]
                + (2,) * axis_bits("rows")
                + (depth, conv_weights.shape[1] // count // depth * channels),
                BF,
            ),
            jax.ShapeDtypeStruct(conv_biases.shape, F32),
            jax.ShapeDtypeStruct((2, items, channels), F32),
        ],
        scratch_shapes=[
            pltpu.VMEM((4, items, rows + 2, WIDE, 3 * channels), BF),
            pltpu.VMEM((4, items, rows, WIDE, channels), F32),
            pltpu.VMEM((items, rows + 2, WIDE, 3 * channels), BF),
            pltpu.VMEM((items, rows, WIDE, channels), F32),
            pltpu.VMEM((items, rows + 2, WIDE, channels), F32),
            pltpu.VMEM((items, 2 * rows + 2, WIDE, channels), F32),
            pltpu.VMEM((channels // 128, 2 * WIDE, 128), F32),
            pltpu.VMEM((EDGES, 2, items, WIDE, channels), BF),
            pltpu.VMEM((EDGES, 2, items, WIDE, channels), BF),
            pltpu.SemaphoreType.DMA((EDGES, 2)),
            pltpu.SemaphoreType.DMA((EDGES, 2)),
        ],
        compiler_params=pltpu.CompilerParams(
            vmem_limit_bytes=56 << 20, collective_id=0, has_side_effects=True
        ),
        cost_estimate=pl.CostEstimate(
            flops=2 * 12 * pixels * 9 * channels * channels,
            bytes_accessed=20 << 20,
            transcendentals=8 * pixels * channels,
        ),
        name="refine",
    )(padded, conv_weights, conv_biases, factor, offset, cotangent)
    return outs


MESH = pl.DeviceIdType.MESH


def flip(index, bit):
    return index + (1 - 2 * (index // (1 << bit) % 2)) * (1 << bit)


class Reducer:
    def __init__(self, chunks, depth, strip, row_bits, item_bits, space, lag):
        self.chunks, self.depth, self.lanes = chunks, depth, strip // 2
        self.space, self.lag = space, lag
        self.row_bits, self.item_bits = row_bits, item_bits
        self.orders = (tuple(range(row_bits - 1, -1, -1)), tuple(range(row_bits)))
        self.far = max(item_bits - 2, 0)
        self.phases = 1 + row_bits + 1 + self.far + 1 + 1

    def scratch(self):
        c, half = self.chunks, self.depth // 2
        shares = (2,) * self.row_bits
        slots = [
            pltpu.VMEM((c,) + shares + (self.depth, self.lanes), BF),
            pltpu.VMEM((2,) + shares + (self.depth, self.lanes), BF),
        ]
        for stage in range(self.row_bits):
            for _ in (0, 1):
                slots.append(pltpu.VMEM((c,) + (2,) * (self.row_bits - 1 - stage) + (half, self.lanes), BF))
        slots.append(pltpu.VMEM((c, half, self.lanes), BF))
        for _ in range(self.far):
            slots.append(pltpu.VMEM((c, half, self.lanes), BF))
            slots.append(pltpu.VMEM((c, half, self.lanes), BF))
        arrivals = 1 + 2 * self.row_bits + 1 + self.far + 1 + 1
        sends = 1 + 2 * self.row_bits + 1 + self.far + 1 + 1
        return slots + [
            pltpu.VMEM((2, c, self.depth, self.lanes), BF),
            pltpu.SemaphoreType.DMA((2,)),
            pltpu.SemaphoreType.DMA((arrivals, c)),
            pltpu.SemaphoreType.DMA((sends,)),
        ]

    def slots(self):
        return len(self.scratch())

    def out_shape(self):
        return jax.ShapeDtypeStruct((2, self.chunks, self.depth, self.lanes), BF)

    def bind(self, out_ref, slots, sources=None, held=None):
        slots = list(slots)
        self.result, self.sources, self.held = out_ref, sources, held
        self.total, self.ring = slots[0], slots[1]
        self.row_in = [
            (slots[2 + 2 * stage], slots[3 + 2 * stage]) for stage in range(self.row_bits)
        ]
        rest = slots[2 + 2 * self.row_bits :]
        self.near_in = rest[0]
        self.far_out = [rest[1 + 2 * k] for k in range(self.far)]
        self.far_in = [rest[2 + 2 * k] for k in range(self.far)]
        self.out, self.ring_sem, self.recv_sem, self.send_sem = rest[-4:]
        self.me = lax.axis_index("rows")
        self.at = lax.axis_index("items")
        self.core = self.at % 2
        self.near = self.at // 2 % 2

    def peers(self):
        found = [(flip(self.at, bit), self.me) for bit in range(self.item_bits)]
        return found + [(self.at, flip(self.me, bit)) for bit in range(self.row_bits)]

    def greet(self):
        barrier = pltpu.get_barrier_semaphore()
        for peer in self.peers():
            pl.semaphore_signal(barrier, inc=1, device_id=peer, device_id_type=MESH)
        pl.semaphore_wait(barrier, len(self.peers()))

    def remote(self, source, target, arrival, sent, chunk, peer):
        return pltpu.make_async_remote_copy(
            src_ref=source,
            dst_ref=target,
            send_sem=self.send_sem.at[sent],
            recv_sem=self.recv_sem.at[arrival, chunk],
            device_id=peer,
            device_id_type=MESH,
        )

    def strip(self, ref, index, mine):
        side = self.core if mine else 1 - self.core
        lanes = pl.ds(pl.multiple_of(side * self.lanes, self.lanes), self.lanes)
        return ref.at[(index,) + (slice(None),) * (self.row_bits + 1) + (lanes,)]

    def core_copy(self, source, chunk):
        return self.remote(
            source, self.total.at[chunk], 0, 0, chunk, (flip(self.at, 0), self.me)
        )

    def begin(self):
        base = 0
        for ref in self.sources:

            def go(index, carry, ref=ref, base=base):
                self.core_copy(self.strip(ref, index, False), base + index).start()
                return carry

            lax.fori_loop(0, ref.shape[0], go, 0)
            base += ref.shape[0]
        self.fetch(0)

    def begin_held(self, chunk):
        self.core_copy(self.strip(self.held, chunk, False), chunk).start()

    def fetch(self, chunk):
        base = 0
        for ref in self.sources:

            @pl.when((chunk >= base) & (chunk < base + ref.shape[0]))
            def _(ref=ref, base=base):
                index = jnp.clip(chunk - base, 0, ref.shape[0] - 1)
                pltpu.make_async_copy(
                    self.strip(ref, index, True),
                    self.ring.at[chunk % 2],
                    self.ring_sem.at[chunk % 2],
                ).start()

            base += ref.shape[0]

    def add_mine(self, chunk):
        if self.held is not None:
            block = self.held[chunk]
            side = (slice(None),) * (self.row_bits + 1)
            block = jnp.where(
                self.core == 0,
                block[side + (slice(0, self.lanes),)],
                block[side + (slice(self.lanes, None),)],
            )
        else:
            slot = chunk % 2
            pltpu.make_async_copy(
                self.total.at[chunk], self.ring.at[slot], self.ring_sem.at[slot]
            ).wait()
            block = self.ring[slot]
        self.total[chunk] = add_low(self.total[chunk], block)

    def bit(self, which):
        return self.me // (1 << which) % 2

    def shares(self, half, stage, sent):
        order = self.orders[half]
        index = [slice(None)] * self.row_bits
        for done in order[:stage]:
            index[self.row_bits - 1 - done] = self.bit(done)
        now = order[stage]
        index[self.row_bits - 1 - now] = 1 - self.bit(now) if sent else self.bit(now)
        return tuple(index)

    def rows(self, half):
        depth = self.depth // 2
        return pl.ds(half * depth, depth)

    def row_copy(self, stage, half, chunk):
        source = self.total.at[(chunk,) + self.shares(half, stage, True) + (self.rows(half),)]
        return self.remote(
            source,
            self.row_in[stage][half].at[chunk],
            1 + 2 * stage + half,
            1 + 2 * stage + half,
            chunk,
            (self.at, flip(self.me, self.orders[half][stage])),
        )

    def own(self, chunk, rows):
        return (chunk,) + tuple(self.bit(b) for b in range(self.row_bits - 1, -1, -1)) + (rows,)

    def near_rows(self, mine):
        half = self.depth // 2
        place = self.near if mine else 1 - self.near
        return pl.ds(pl.multiple_of(place * half, half), half)

    def near_copy(self, chunk):
        return self.remote(
            self.total.at[self.own(chunk, self.near_rows(False))],
            self.near_in.at[chunk],
            1 + 2 * self.row_bits,
            1 + 2 * self.row_bits,
            chunk,
            (flip(self.at, 1), self.me),
        )

    def far_copy(self, k, chunk):
        return self.remote(
            self.far_out[k].at[chunk],
            self.far_in[k].at[chunk],
            2 + 2 * self.row_bits + k,
            2 + 2 * self.row_bits + k,
            chunk,
            (flip(self.at, 2 + k), self.me),
        )

    def back_copy(self, chunk):
        place = self.out.at[self.core, chunk, self.near_rows(True)]
        return self.remote(
            place,
            place,
            2 + 2 * self.row_bits + self.far,
            2 + 2 * self.row_bits + self.far,
            chunk,
            (flip(self.at, 1), self.me),
        )

    def last_copy(self, chunk):
        place = self.out.at[self.core, chunk]
        return self.remote(
            place,
            place,
            3 + 2 * self.row_bits + self.far,
            3 + 2 * self.row_bits + self.far,
            chunk,
            (flip(self.at, 0), self.me),
        )

    def phase(self, number, chunk):
        bits, half = self.row_bits, self.depth // 2
        if number == 0:
            self.core_copy(self.total.at[chunk], chunk).wait_recv()
            self.add_mine(chunk)
            if self.sources is not None:

                @pl.when(chunk + 1 < self.chunks)
                def _():
                    self.fetch(chunk + 1)

            for side in (0, 1):
                self.row_copy(0, side, chunk).start()
        elif number <= bits:
            stage = number - 1
            for side in (0, 1):
                self.row_copy(stage, side, chunk).wait_recv()
                at = (chunk,) + self.shares(side, stage, False) + (self.rows(side),)
                self.total[at] = add_low(self.total[at], self.row_in[stage][side][chunk])
                if stage + 1 < bits:
                    self.row_copy(stage + 1, side, chunk).start()
            if stage + 1 == bits:
                self.near_copy(chunk).start()
        elif number == bits + 1:
            self.near_copy(chunk).wait_recv()
            total = add_low(
                self.total[self.own(chunk, self.near_rows(True))], self.near_in[chunk]
            )
            self.pass_on(0, chunk, total)
        elif number <= bits + 1 + self.far:
            k = number - bits - 2
            self.far_copy(k, chunk).wait_recv()
            self.pass_on(k + 1, chunk, add_low(self.far_out[k][chunk], self.far_in[k][chunk]))
        elif number == bits + 2 + self.far:
            self.back_copy_arrived(chunk)
            self.last_copy(chunk).start()
        else:
            self.last_arrived(chunk)

    def pass_on(self, k, chunk, total):
        if k < self.far:
            self.far_out[k][chunk] = total
            self.far_copy(k, chunk).start()
        else:
            self.out[self.core, chunk, self.near_rows(True)] = total
            self.back_copy(chunk).start()

    def back_copy_arrived(self, chunk):
        place = self.out.at[self.core, chunk, self.near_rows(False)]
        self.remote(
            place,
            place,
            2 + 2 * self.row_bits + self.far,
            2 + 2 * self.row_bits + self.far,
            chunk,
            (flip(self.at, 1), self.me),
        ).wait_recv()

    def last_arrived(self, chunk):
        place = self.out.at[1 - self.core, chunk]
        self.remote(
            place,
            place,
            3 + 2 * self.row_bits + self.far,
            3 + 2 * self.row_bits + self.far,
            chunk,
            (flip(self.at, 0), self.me),
        ).wait_recv()

    def step(self, t):
        for number in range(self.phases - 1, -1, -1):
            place = t - self.lag * number
            chunk = place // self.space

            @pl.when((place >= 0) & (place % self.space == 0) & (chunk < self.chunks))
            def _(number=number, chunk=chunk):
                self.phase(number, jnp.clip(chunk, 0, self.chunks - 1))

    @property
    def steps(self):
        return (self.chunks - 1) * self.space + self.lag * (self.phases - 1) + 1

    def finish(self):
        def drain(sem, ref):
            pltpu.make_async_copy(ref, ref, self.send_sem.at[sem]).wait()

        drain(0, self.total)
        for stage in range(self.row_bits):
            for side in (0, 1):
                drain(1 + 2 * stage + side, self.row_in[stage][side])
        base = 1 + 2 * self.row_bits
        drain(base, self.near_in)
        for k in range(self.far):
            drain(base + 1 + k, self.far_in[k])
        drain(base + 1 + self.far, self.near_in)
        drain(base + 2 + self.far, self.out.at[0])
        copy = pltpu.make_async_copy(self.out, self.result, self.ring_sem.at[0])
        copy.start()
        copy.wait()


def unpack_kernel(held_ref, *refs, table, outs):
    targets, (wide, sem) = refs[:outs], refs[outs:]
    depth = wide.shape[1]

    def copy(place, chunk, first, size, number, outer, row, column):
        target = targets[number] if outer is None else targets[number].at[outer]
        return pltpu.make_async_copy(
            wide.at[chunk, :, pl.ds(first, size)],
            target.at[pl.ds(row, depth), pl.ds(column, size)],
            sem.at[place],
        )

    done = set()
    for place, entry in enumerate(table):
        chunk = entry[0]
        if chunk not in done:
            done.add(chunk)
            wide[chunk] = jnp.concatenate(
                [held_ref[0, chunk].astype(F32), held_ref[1, chunk].astype(F32)], axis=1
            )
        copy(place, *entry).start()
    for place, entry in enumerate(table):
        copy(place, *entry).wait()


def unpack(out, table, shapes):
    chunks, depth, lanes = out.shape[1:]
    return pl.pallas_call(
        functools.partial(unpack_kernel, table=table, outs=len(shapes)),
        in_specs=[pl.BlockSpec(memory_space=pltpu.VMEM)],
        out_specs=[pl.BlockSpec(memory_space=pl.ANY)] * len(shapes),
        out_shape=[jax.ShapeDtypeStruct(shape, F32) for shape in shapes],
        scratch_shapes=[
            pltpu.VMEM((chunks, depth, 2 * lanes), F32),
            pltpu.SemaphoreType.DMA((len(table),)),
        ],
        compiler_params=pltpu.CompilerParams(vmem_limit_bytes=40 << 20),
        name="unpack",
    )(out)


def all_sum_kernel(value_ref, out_ref, piece, landed, over, send_sem, recv_sem, *, count, others):
    at, me = lax.axis_index("items"), lax.axis_index("rows")
    barrier = pltpu.get_barrier_semaphore()
    row_peers = [(at, (me + k) % count) for k in range(1, count)]
    item_peers = [((at + k) % others, me) for k in range(1, others)]
    for peer in row_peers + item_peers:
        pl.semaphore_signal(barrier, inc=1, device_id=peer, device_id_type=MESH)
    pl.semaphore_wait(barrier, count + others - 2)

    def row_copy(k):
        return pltpu.make_async_remote_copy(
            src_ref=value_ref.at[row_peers[k][1]],
            dst_ref=landed.at[k],
            send_sem=send_sem.at[k],
            recv_sem=recv_sem.at[k],
            device_id=row_peers[k],
            device_id_type=MESH,
        )

    def item_copy(k):
        return pltpu.make_async_remote_copy(
            src_ref=piece,
            dst_ref=over.at[k],
            send_sem=send_sem.at[count - 1 + k],
            recv_sem=recv_sem.at[count - 1 + k],
            device_id=item_peers[k],
            device_id_type=MESH,
        )

    for k in range(count - 1):
        row_copy(k).start()
    total = value_ref[me]
    for k in range(count - 1):
        row_copy(k).wait_recv()
        total = total + landed[k]
    piece[...] = total
    for k in range(others - 1):
        item_copy(k).start()
    for k in range(others - 1):
        item_copy(k).wait_recv()
        total = total + over[k]
    out_ref[...] = total
    for k in range(count - 1):
        row_copy(k).wait_send()
    for k in range(others - 1):
        item_copy(k).wait_send()


def all_sum(value, collective_id):
    count, others = lax.axis_size("rows"), lax.axis_size("items")
    vmem = pl.BlockSpec(memory_space=pltpu.VMEM)
    block = value.shape[1:]
    return pl.pallas_call(
        functools.partial(all_sum_kernel, count=count, others=others),
        in_specs=[vmem],
        out_specs=vmem,
        out_shape=jax.ShapeDtypeStruct(block, F32),
        scratch_shapes=[
            pltpu.VMEM(block, F32),
            pltpu.VMEM((count - 1,) + block, F32),
            pltpu.VMEM((others - 1,) + block, F32),
            pltpu.SemaphoreType.DMA((count + others - 2,)),
            pltpu.SemaphoreType.DMA((count + others - 2,)),
        ],
        compiler_params=pltpu.CompilerParams(collective_id=collective_id, has_side_effects=True),
        name="sum_small",
    )(value)


def shares_of(bits):
    return (2,) * bits


def mlp_backward_kernel(
    tap_grad_ref,
    cot_ref,
    out_tokens_ref,
    normed_ref,
    resid_ref,
    attended_ref,
    gain_ref,
    tap_w_ref,
    out_w_ref,
    hidden_ref,
    slope_ref,
    fc1_ref,
    fc2_ref,
    tap_dw_ref,
    out_dw_ref,
    fc1_dw_ref,
    fc2_dw_ref,
    resid_grad_ref,
    attended_grad_ref,
    wide_sums_ref,
    fc1_sums_ref,
    out_grad,
    low_grad,
    pre_grad,
    back,
    *,
    blocks,
    row_block,
    bits,
):
    step = pl.program_id(0)
    tokens, width = low_grad.shape
    count = 1 << bits
    depth = width // count
    shares = shares_of(bits)
    pieces = [pl.ds(k * row_block, row_block) for k in range(tokens // row_block)]

    @pl.when(step == 0)
    def _():
        total = jnp.zeros((1, width), F32)
        tap_total = jnp.zeros((1, tap_grad_ref.shape[1]), F32)
        for piece in pieces:
            tap_part = tap_grad_ref[piece, :]
            value = cot_ref[piece, :].astype(F32) + mm(tap_part, tap_w_ref[...], NT)
            out_grad[piece, :] = value
            low = value.astype(BF)
            low_grad[piece, :] = low
            back[piece, :] = jnp.zeros((row_block, width), F32)
            total = total + jnp.sum(low.astype(F32), axis=0, keepdims=True)
            tap_total = tap_total + jnp.sum(tap_part.astype(F32), axis=0, keepdims=True)
        wide_sums_ref[pl.ds(0, 1), :] = total
        wide_sums_ref[pl.ds(4, 1), :] = jnp.concatenate(
            [tap_total] * (width // tap_total.shape[1]), axis=1
        )
        weight = mm(out_tokens_ref[...], tap_grad_ref[...], TN).astype(BF)
        weight = jnp.concatenate(
            [weight, jnp.zeros((width, width - weight.shape[1]), BF)], axis=1
        )
        tap_dw_ref[0] = weight.reshape(shares + (depth, width))

    def rows_of(number):
        return pl.ds(pl.multiple_of(number * row_block, row_block), row_block)

    def inward(number, sums):
        piece = rows_of(number)
        grads = mm(low_grad[piece, :], fc2_ref[...], NT) * slope_ref[piece, :].astype(F32)
        low = grads.astype(BF)
        pre_grad[piece, :] = low
        return sums + jnp.sum(low.astype(F32), axis=0, keepdims=True)

    fc1_sums_ref[...] = lax.fori_loop(
        0, len(pieces), inward, jnp.zeros((1, pre_grad.shape[1]), F32)
    )
    weight = mm(hidden_ref[...], low_grad[...], TN).astype(BF)
    per_share = weight.shape[0] // depth * blocks // count
    for place in range(weight.shape[0] // depth):
        fc2_dw_ref[place % per_share, place // per_share] = weight[
            place * depth : (place + 1) * depth
        ]
    weight = mm(normed_ref[...], pre_grad[...], TN).astype(BF)
    fc1_dw_ref[0] = weight.reshape(shares + (depth, width))

    def outward(number, carry):
        piece = rows_of(number)
        back[piece, :] += mm(pre_grad[piece, :], fc1_ref[...], NT)
        return carry

    lax.fori_loop(0, len(pieces), outward, 0)

    @pl.when(step == blocks - 1)
    def _():
        gain = gain_ref[...]
        gain_total = jnp.zeros((1, width), F32)
        shift_total = jnp.zeros((1, width), F32)
        total = jnp.zeros((1, width), F32)
        for piece in pieces:
            grads = back[piece, :]
            unit, rstd = norm_stats(resid_ref[piece, :])
            scaled = grads * gain
            mean_one = jnp.mean(scaled, axis=-1, keepdims=True)
            mean_two = jnp.mean(scaled * unit, axis=-1, keepdims=True)
            value = out_grad[piece, :] + rstd * (scaled - mean_one - unit * mean_two)
            resid_grad_ref[piece, :] = value
            low = value.astype(BF)
            low_grad[piece, :] = low
            gain_total = gain_total + jnp.sum(grads * unit, axis=0, keepdims=True)
            shift_total = shift_total + jnp.sum(grads, axis=0, keepdims=True)
            total = total + jnp.sum(low.astype(F32), axis=0, keepdims=True)
            attended_grad_ref[piece, :] = mm(low, out_w_ref[...], NT).astype(BF)
        wide_sums_ref[pl.ds(1, 1), :] = gain_total
        wide_sums_ref[pl.ds(2, 1), :] = shift_total
        wide_sums_ref[pl.ds(3, 1), :] = total
        weight = mm(attended_ref[...], low_grad[...], TN).astype(BF)
        out_dw_ref[0] = weight.reshape(shares + (depth, width))


def mlp_backward(
    grad_tap,
    cotangent,
    out_tokens,
    normed,
    resid,
    attended,
    gain,
    tap_weight,
    out_weight,
    hidden,
    slope,
    fc1_weight,
    fc2_weight,
    row_block,
):
    tokens, width = resid.shape
    inner = hidden.shape[1]
    bits = axis_bits("rows")
    count = 1 << bits
    depth = width // count
    blocks = inner // width
    vmem = pl.BlockSpec(memory_space=pltpu.VMEM)
    column = pl.BlockSpec((tokens, width), lambda i: (0, i))
    fc2_chunks = inner // count // depth
    shares = shares_of(bits)
    share_step = count // blocks
    outs = pl.pallas_call(
        functools.partial(
            mlp_backward_kernel,
            blocks=blocks,
            row_block=row_block,
            bits=bits,
        ),
        grid=(blocks,),
        in_specs=[vmem] * 9
        + [
            column,
            column,
            pl.BlockSpec((width, width), lambda i: (0, i)),
            pl.BlockSpec((width, width), lambda i: (i, 0)),
        ],
        out_specs=[
            vmem,
            vmem,
            pl.BlockSpec((1,) + shares + (depth, width), lambda i: (i,) + (0,) * (bits + 2)),
            pl.BlockSpec((fc2_chunks, share_step, depth, width), lambda i: (0, i, 0, 0)),
            vmem,
            vmem,
            vmem,
            pl.BlockSpec((1, width), lambda i: (0, i)),
        ],
        out_shape=[
            jax.ShapeDtypeStruct((1,) + shares + (depth, width), BF),
            jax.ShapeDtypeStruct((1,) + shares + (depth, width), BF),
            jax.ShapeDtypeStruct((blocks,) + shares + (depth, width), BF),
            jax.ShapeDtypeStruct((fc2_chunks, count, depth, width), BF),
            jax.ShapeDtypeStruct((tokens, width), F32),
            jax.ShapeDtypeStruct((tokens, width), BF),
            jax.ShapeDtypeStruct((8, width), F32),
            jax.ShapeDtypeStruct((1, inner), F32),
        ],
        scratch_shapes=[
            pltpu.VMEM((tokens, width), F32),
            pltpu.VMEM((tokens, width), BF),
            pltpu.VMEM((tokens, width), BF),
            pltpu.VMEM((tokens, width), F32),
        ],
        compiler_params=pltpu.CompilerParams(vmem_limit_bytes=60 << 20),
        cost_estimate=pl.CostEstimate(
            flops=8 * tokens * width * inner, bytes_accessed=40 << 20, transcendentals=0
        ),
        name="mlp_backward",
    )(
        grad_tap,
        cotangent,
        out_tokens,
        normed,
        resid,
        attended,
        gain,
        tap_weight,
        out_weight,
        hidden,
        slope,
        fc1_weight,
        fc2_weight,
    )
    return outs


class Scatter:
    def __init__(self, bits, tokens, width, items):
        self.bits, self.tokens, self.width, self.items = bits, tokens, width, items
        self.orders = (tuple(range(bits - 1, -1, -1)), tuple(range(bits)))

    def scratch(self):
        slots = [pltpu.VMEM((2,) * self.bits + (self.tokens, self.width), BF)]
        for stage in range(self.bits):
            for _ in (0, 1):
                slots.append(
                    pltpu.VMEM(
                        (self.items,)
                        + (2,) * (self.bits - 1 - stage)
                        + (self.tokens // 2, self.width),
                        BF,
                    )
                )
        return slots + [
            pltpu.SemaphoreType.DMA((self.bits, 2)),
            pltpu.SemaphoreType.DMA((self.items, self.bits, 2)),
        ]

    def bind(self, slots):
        self.held = slots[0]
        self.landed = [(slots[1 + 2 * s], slots[2 + 2 * s]) for s in range(self.bits)]
        self.send_sem, self.recv_sem = slots[-2:]

    def place(self, half, stage, bit_value):
        index = [slice(None)] * self.bits
        for done in self.orders[half][:stage]:
            index[self.bits - 1 - done] = 0
        index[self.bits - 1 - self.orders[half][stage]] = bit_value
        size = self.tokens // 2
        return tuple(index) + (pl.ds(half * size, size),)

    def copy(self, item, stage, half):
        me, at = lax.axis_index("rows"), lax.axis_index("items")
        return pltpu.make_async_remote_copy(
            src_ref=self.held.at[self.place(half, stage, 1)],
            dst_ref=self.landed[stage][half].at[item],
            send_sem=self.send_sem.at[stage, half],
            recv_sem=self.recv_sem.at[item, stage, half],
            device_id=(at, flip(me, self.orders[half][stage])),
            device_id_type=MESH,
        )

    def start(self, item):
        for half in (0, 1):
            self.copy(item, 0, half).start()

    def advance(self, item, stage, finish):
        for half in (0, 1):
            self.copy(item, stage, half).wait_recv()
            at = self.place(half, stage, 0)
            if stage + 1 < self.bits:
                self.held[at] = add_low(self.held[at], self.landed[stage][half][item])
                self.copy(item, stage + 1, half).start()
            else:
                finish(
                    at[-1],
                    self.held[at].astype(F32) + self.landed[stage][half][item].astype(F32),
                )

    def drain(self, item):
        for stage in range(self.bits):
            for half in (0, 1):
                self.copy(item, stage, half).wait_send()


def attention_backward_kernel(
    valid_ref,
    q_ref,
    k_ref,
    v_ref,
    g_ref,
    o_ref,
    lse_ref,
    normed_ref,
    wq_ref,
    wk_ref,
    wv_ref,
    *refs,
    reducer,
    late,
    scatter,
    groups,
    items,
    kb,
    rounds,
    sources,
):
    early_sources = refs[:sources]
    grad_ref, sums_ref, early_out, late_out = refs[sources : sources + 4]
    slots = list(refs[sources + 4 :])
    q4, g4, acc, dkv, back, held = slots[:6]
    del slots[:6]
    early_slots = slots[: reducer.slots()]
    del slots[: reducer.slots()]
    late_slots = slots[: late.slots()]
    del slots[: late.slots()]
    reducer.bind(early_out, early_slots, sources=early_sources)
    late.bind(late_out, late_slots, held=held)
    scatter.bind(slots)
    step = pl.program_id(0)
    item, group = step // groups, step % groups
    t, n = q_ref.shape[1], k_ref.shape[1]
    width = back.shape[1]
    depth = width // (1 << reducer.row_bits)
    shares = shares_of(reducer.row_bits)
    me = lax.axis_index("rows")

    @pl.when(step == 0)
    def _():
        reducer.greet()
        reducer.begin()
        sums_ref[...] = jnp.zeros_like(sums_ref)

    q4[...] = spread_heads(q_ref[0] * jnp.asarray(HEAD_DIM**-0.5, BF))
    grads = spread_heads(g_ref[0])
    g4[...] = grads
    outs = jnp.concatenate([o_ref[0].astype(F32)] * HEADS_PER_GROUP, axis=0)
    product = grads.astype(F32) * outs
    high = product.astype(BF)
    low = (product - high.astype(F32)).astype(BF)
    ones = jnp.ones((8, GROUP), BF)
    dots = (mm(ones, high, NT) + mm(ones, low, NT))[:1]
    lse = lse_ref[0, 0, :1, :]
    acc[...] = jnp.zeros_like(acc)
    limit = valid_ref[item] * PC

    def turn(number):
        now = step * rounds + number
        reducer.step(now)
        late.step(now - ((items - 1) * groups + 1) * rounds)

    inner = n // kb
    each = rounds // inner

    def block_step(b, carry):
        at = pl.ds(pl.multiple_of(b * kb, kb), kb)
        keys, values = k_ref[0, at, :], v_ref[0, at, :]
        index = b * kb + lax.broadcasted_iota(jnp.int32, (kb, 1), 0)
        position = index + key_shift(index, n, t, me)
        bias = jnp.where(position < limit, 0.0, MASKED).astype(F32)
        scores = mm(keys, q4[...], NT)
        probs = jnp.exp2((scores * LOG2E + bias) - lse)
        grad_probs = mm(values, g4[...], NT)
        grad_scores = (probs * (grad_probs - dots)).astype(BF)
        dkv[at, pl.ds(GROUP, GROUP)] = mm(probs.astype(BF), g4[...]).astype(BF)
        dkv[at, pl.ds(0, GROUP)] = mm(grad_scores, q4[...]).astype(BF)
        acc[...] += mm(grad_scores, keys, TN)

        def rest(k, inner_carry):
            turn(b * each + k)
            return inner_carry

        lax.fori_loop(0, each, rest, 0)
        return carry

    lax.fori_loop(0, inner, block_step, 0)
    out = jnp.zeros((t, GROUP), F32)
    for h in range(HEADS_PER_GROUP):
        out = jnp.where(head_mask((t, GROUP), h), acc[pl.ds(h * t, t), :], out)
    dq = (out * HEAD_DIM**-0.5).astype(BF)

    for stage in range(scatter.bits):

        @pl.when((group == stage) & (item > 0))
        def _(stage=stage):
            def finish(rows, value):
                grad_ref[item - 1, rows, :] += value

            scatter.advance(item - 1, stage, finish)

    row_piece = n // 4
    both = jnp.concatenate([wk_ref[...], wv_ref[...]], axis=1)

    def project(k, carry):
        at = pl.ds(pl.multiple_of(k * row_piece, row_piece), row_piece)
        value = mm(dkv[at, :], both, NT)
        back[at, :] = jnp.where(group == 0, value, back[at, :] + value)
        return carry

    lax.fori_loop(0, 4, project, 0)
    value = mm(dq, wq_ref[...], NT)
    grad_ref[item] = jnp.where(group == 0, value, grad_ref[item] + value)

    part = jnp.concatenate(
        [mm(normed_ref[0, pl.ds(0, t), :], dq, TN), mm(normed_ref[0], dkv[...], TN)], axis=1
    ).reshape(shares + (depth, width))
    before = held[group].astype(F32)
    held[group] = jnp.where(item == 0, part, before + part).astype(BF)
    sums_ref[group, pl.ds(0, 1), :] += jnp.sum(dq.astype(F32), axis=0, keepdims=True)
    sums_ref[group, pl.ds(1, 1), :] += jnp.sum(
        dkv[:, pl.ds(GROUP, GROUP)].astype(F32), axis=0, keepdims=True
    )

    @pl.when(item == items - 1)
    def _():
        late.begin_held(group)

    @pl.when(group == groups - 1)
    def _():
        @pl.when(item > 0)
        def _():
            scatter.drain(item - 1)

        for j in range(1 << scatter.bits):
            index = tuple(j >> b & 1 for b in range(scatter.bits - 1, -1, -1))
            scatter.held[index] = back[pl.ds(j * t, t), :].astype(BF)
        scatter.start(item)

    @pl.when(step == items * groups - 1)
    def _():
        start = ((items - 1) * groups + 1) * rounds

        def rest(now, carry):
            @pl.when(now < reducer.steps)
            def _():
                reducer.step(now)

            late.step(now - start)
            return carry

        last = items * groups * rounds
        end = start + late.steps
        lax.fori_loop(last, last + late.lag, rest, 0)
        for stage in range(scatter.bits):

            def finish(rows, value):
                grad_ref[items - 1, rows, :] += value

            scatter.advance(items - 1, stage, finish)
        lax.fori_loop(last + late.lag, max(end, reducer.steps), rest, 0)
        scatter.drain(items - 1)
        reducer.finish()
        late.finish()


def key_shift(index, length, block, me):
    start = jnp.full_like(index, me * block)
    for j in range(1, length // block):
        other = me
        for bit in range(j.bit_length()):
            if j >> bit & 1:
                other = flip(other, bit)
        start = jnp.where(index >= j * block, (other - j) * block, start)
    return start


def attention_backward(
    valid_rows, queries, keyvals, grads, outs, lse, normed, qkv_weight, packed, collective_id
):
    items, t, d = queries.shape
    n = keyvals.shape[1]
    groups = d // GROUP
    bits = axis_bits("rows")
    depth = d >> bits
    rows4 = HEADS_PER_GROUP * t
    rounds = 8
    reducer = Reducer(
        sum(a.shape[0] for a in packed), depth, d, bits, axis_bits("items"), 4, 5
    )
    late = Reducer(groups, depth, d, bits, axis_bits("items"), rounds, 4)
    scatter = Scatter(bits, t, d, items)
    query_spec = pl.BlockSpec((1, t, GROUP), lambda i: (i // groups, 0, i % groups))
    vmem = pl.BlockSpec(memory_space=pltpu.VMEM)

    def weight_spec(kind):
        return pl.BlockSpec((d, GROUP), lambda i: (0, kind * groups + i % groups))

    def key_spec(kind):
        return pl.BlockSpec((1, n, GROUP), lambda i: (i // groups, 0, kind * groups + i % groups))

    outs = pl.pallas_call(
        functools.partial(
            attention_backward_kernel,
            reducer=reducer,
            late=late,
            scatter=scatter,
            groups=groups,
            items=items,
            kb=n // 4,
            rounds=rounds,
            sources=len(packed),
        ),
        grid=(items * groups,),
        in_specs=[
            pl.BlockSpec(memory_space=pltpu.SMEM),
            query_spec,
            key_spec(0),
            key_spec(1),
            query_spec,
            query_spec,
            pl.BlockSpec((1, 1, 8, rows4), lambda i: (i // groups, i % groups, 0, 0)),
            pl.BlockSpec((1, n, d), lambda i: (i // groups, 0, 0), pipeline_mode=pl.Buffered(1)),
            weight_spec(0),
            weight_spec(1),
            weight_spec(2),
        ]
        + [pl.BlockSpec(memory_space=pl.ANY)] * len(packed),
        out_specs=[vmem] * 2 + [pl.BlockSpec(memory_space=pl.ANY)] * 2,
        out_shape=[
            jax.ShapeDtypeStruct((items, t, d), F32),
            jax.ShapeDtypeStruct((groups, 8, GROUP), F32),
            reducer.out_shape(),
            late.out_shape(),
        ],
        scratch_shapes=[
            pltpu.VMEM((rows4, GROUP), BF),
            pltpu.VMEM((rows4, GROUP), BF),
            pltpu.VMEM((rows4, GROUP), F32),
            pltpu.VMEM((n, 2 * GROUP), BF),
            pltpu.VMEM((n, d), F32),
            pltpu.VMEM((groups,) + shares_of(bits) + (depth, d), BF),
        ]
        + reducer.scratch()
        + late.scratch()
        + scatter.scratch(),
        compiler_params=pltpu.CompilerParams(
            vmem_limit_bytes=63 << 20, collective_id=collective_id, has_side_effects=True
        ),
        cost_estimate=pl.CostEstimate(
            flops=100 * items * t * n * d,
            bytes_accessed=40 << 20,
            transcendentals=12 * items * t * n,
        ),
        name="attention_backward",
    )(
        valid_rows,
        queries,
        keyvals,
        keyvals,
        grads,
        outs,
        lse,
        normed,
        qkv_weight,
        qkv_weight,
        qkv_weight,
        *packed,
    )
    return outs


def shards(
    tokens,
    valid_rows,
    dataset_ids,
    shift_flags,
    norm_gains,
    norm_biases,
    qkv_weight,
    qv_bias,
    out_weight,
    out_bias,
    fc1_weight,
    fc1_bias,
    fc2_weight,
    fc2_bias,
    tap_weight,
    tap_bias,
    conv_weights,
    conv_biases,
    table_gain,
    table_shift,
    token_cotangent,
    joined_cotangent,
):
    items_here, tok_here, width = tokens.shape
    rows_here = tok_here // PC
    channels = tap_weight.shape[1]
    row_index = lax.axis_index("rows")
    row_count = lax.axis_size("rows")
    last_index = row_count - 1

    flat_in = tokens.reshape(-1, width).astype(F32)
    normed_one = layer_norm(flat_in, norm_gains[0], norm_biases[0]).astype(BF)
    normed_all = [
        gather_blocks(normed_one[i * tok_here : (i + 1) * tok_here]) for i in range(items_here)
    ]
    starts = jnp.stack([(row_index ^ j) * tok_here for j in range(row_count)]).astype(jnp.int32)
    infos = [
        jnp.concatenate([valid_rows[i : i + 1] * PC, starts]) for i in range(items_here)
    ]
    key_weight = qkv_weight[:, width:]
    key_shift = jnp.concatenate([jnp.zeros((width,), F32), qv_bias[width:]])
    queries = (mm(normed_one, qkv_weight[:, :width]) + qv_bias[:width]).astype(BF)
    queries = [queries[i * tok_here : (i + 1) * tok_here] for i in range(items_here)]
    keyvals, attended, lses = [], [], []
    for i in range(items_here):
        keyvals.append((mm(normed_all[i], key_weight) + key_shift).astype(BF))
        out, lse = attention_forward(infos[i], queries[i], keyvals[i])
        attended.append(out)
        lses.append(lse)
    attended_flat = jnp.concatenate(attended)
    resid = flat_in + mm(attended_flat, out_weight) + out_bias
    normed_two = layer_norm(resid, norm_gains[1], norm_biases[1]).astype(BF)
    hidden_pre = mm(normed_two, fc1_weight) + fc1_bias
    hidden_cdf, hidden_rest = normal_parts(hidden_pre)
    hidden = (hidden_pre * hidden_cdf).astype(BF)
    hidden_slope = (hidden_cdf + hidden_rest).astype(BF)
    output = resid + mm(hidden, fc2_weight) + fc2_bias
    output_low = output.astype(BF)
    grid_rows = row_index * rows_here + jnp.arange(rows_here, dtype=jnp.int32)
    row_valid = (grid_rows[None, :] < valid_rows[:, None]).astype(F32)
    token_valid = jnp.broadcast_to(
        row_valid[:, :, None], (items_here, rows_here, PC)
    ).reshape(-1, 1)
    tap_pre = mm(output_low, tap_weight) + tap_bias
    field = (tap_pre * token_valid).reshape(items_here, rows_here, PC, channels)

    choose = (
        dataset_ids[:, None] == jnp.arange(table_gain.shape[0], dtype=jnp.int32)[None, :]
    ).astype(F32)
    flag_value = shift_flags.astype(F32)[:, None]
    gain_pick = jnp.dot(choose, table_gain, precision=highest)
    shift_pick = jnp.dot(choose, table_shift, precision=highest)
    factor = 1.0 + flag_value * (gain_pick - 1.0)
    offset = flag_value * shift_pick
    depth = width // row_count
    joined, grad_field, conv_grads, grad_conv_biases, table_sums = refine(
        field, conv_weights, conv_biases, factor, offset, joined_cotangent, depth
    )
    grad_table_gain = jnp.dot(choose.T, flag_value * table_sums[0], precision=highest)
    grad_table_shift = jnp.dot(choose.T, flag_value * table_sums[1], precision=highest)

    grad_tap = (grad_field[:, :, :PC].reshape(-1, channels) * token_valid).astype(BF)
    (
        tap_grads,
        out_grads,
        fc1_grads,
        fc2_grads,
        grad_resid,
        grad_attended,
        wide_sums,
        fc1_sums,
    ) = mlp_backward(
        grad_tap,
        token_cotangent.reshape(-1, width),
        output_low,
        normed_two,
        resid,
        attended_flat,
        norm_gains[1:2],
        tap_weight,
        out_weight,
        hidden,
        hidden_slope,
        fc1_weight,
        fc2_weight,
        tok_here,
    )
    shares = shares_of(axis_bits("rows"))
    fc2_grads = fc2_grads.reshape(fc2_grads.shape[:1] + shares + fc2_grads.shape[2:])
    grads_in, qkv_sums, early_sum, late_sum = attention_backward(
        valid_rows,
        jnp.stack(queries),
        jnp.stack(keyvals),
        grad_attended.reshape(tokens.shape),
        attended_flat.reshape(tokens.shape),
        jnp.stack(lses),
        jnp.stack(normed_all),
        qkv_weight,
        [conv_grads, tap_grads, fc2_grads, fc1_grads, out_grads],
        3,
    )
    grad_in_norm, grad_gain_one, grad_shift_one = norm_back(
        flat_in, norm_gains[0], grads_in.reshape(-1, width)
    )
    grad_tokens = (grad_resid + grad_in_norm).reshape(tokens.shape)

    groups = width // GROUP
    inner = fc1_weight.shape[1]
    kernels = conv_weights.shape[1]
    convs = conv_weights.shape[0]
    places = kernels // row_count // depth
    fc2_chunks = inner // row_count // depth
    blocks = inner // width
    table = [
        (conv, place * channels, channels, 0, conv, place * depth, 0)
        for conv in range(convs)
        for place in range(places)
    ]
    table += [(convs, 0, channels, 1, None, 0, 0)]
    first = convs + 1
    table += [(first + k, 0, width, 2, None, k * depth, 0) for k in range(fc2_chunks)]
    first += fc2_chunks
    table += [(first + k, 0, width, 3, None, 0, k * width) for k in range(blocks)]
    table += [(first + blocks, 0, width, 4, None, 0, 0)]
    share_conv, share_tap, share_fc2, share_fc1, share_out = unpack(
        early_sum,
        table,
        [
            (convs, kernels // row_count, channels),
            (depth, channels),
            (inner // row_count, width),
            (depth, inner),
            (depth, width),
        ],
    )
    (share_qkv,) = unpack(
        late_sum,
        [
            (group, kind * GROUP, GROUP, 0, None, 0, (kind * groups + group) * GROUP)
            for group in range(groups)
            for kind in range(3)
        ],
        [(depth, 3 * width)],
    )

    small = [
        jnp.stack([grad_gain_one, wide_sums[1]]),
        jnp.stack([grad_shift_one, wide_sums[2]]),
        jnp.concatenate([qkv_sums[:, 0].reshape(-1), qkv_sums[:, 1].reshape(-1)]),
        wide_sums[3],
        fc1_sums[0],
        wide_sums[0],
        wide_sums[4, :channels],
        grad_conv_biases,
        grad_table_gain,
        grad_table_shift,
    ]
    packed = jnp.concatenate(
        [
            array.reshape(row_count, -1)
            if array.ndim == 1
            else jnp.swapaxes(array.reshape(array.shape[0], row_count, -1), 0, 1).reshape(
                row_count, -1
            )
            for array in small
        ],
        axis=1,
    )
    packed = jnp.pad(packed, ((0, 0), (0, -packed.shape[1] % 1024)))
    summed = all_sum(packed.reshape(row_count, -1, 128), 4).reshape(-1)
    outs, place = [], 0
    for array in small:
        size = array.size // row_count
        piece = summed[place : place + size]
        place += size
        outs.append(piece if array.ndim == 1 else piece.reshape(array.shape[0], -1))
    (
        out_gains,
        out_shifts,
        out_qv,
        out_out,
        out_fc1,
        out_fc2,
        out_tap,
        out_conv,
        out_table_gain,
        out_table_shift,
    ) = outs
    return (
        output_low.reshape(tokens.shape),
        joined,
        grad_tokens,
        out_gains,
        out_shifts,
        share_qkv,
        out_qv,
        share_out,
        out_out,
        share_fc1,
        out_fc1,
        share_fc2,
        out_fc2,
        share_tap,
        out_tap,
        share_conv,
        out_conv,
        out_table_gain,
        out_table_shift,
    )


def solution(mesh):
    return jax.shard_map(
        shards,
        mesh=mesh,
        in_specs=(P("items", "rows", None), P("items"), P("items"), P("items"))
        + (P(),) * 16
        + (P("items", "rows", None), P("items", "rows", None, None)),
        out_specs=(
            P("items", "rows", None),
            P("items", "rows", None, None),
            P("items", "rows", None),
            P(None, "rows"),
            P(None, "rows"),
            P("rows", None),
            P("rows"),
            P("rows", None),
            P("rows"),
            P("rows", None),
            P("rows"),
            P("rows", None),
            P("rows"),
            P("rows", None),
            P("rows"),
            P(None, "rows", None),
            P(None, "rows"),
            P(None, "rows"),
            P(None, "rows"),
        ),
        check_vma=False,
    )
```

```python
import functools

import jax
import jax.numpy as jnp
from jax import lax
from jax.experimental import pallas as pl
from jax.experimental.pallas import tpu as pltpu
from jax.sharding import PartitionSpec as P

HEAD_DIM = 64
PC = 40
GROUP = 256
HEADS_PER_GROUP = GROUP // HEAD_DIM

BF = jnp.bfloat16
F32 = jnp.float32
LOG2E = 1.4426950408889634
MASKED = -1e30
NN = (((1,), (0,)), ((), ()))
NT = (((1,), (1,)), ((), ()))
TN = (((0,), (0,)), ((), ()))

epsilon = 1e-06
highest = lax.Precision.HIGHEST


def mm(left, right, dims=NN):
    return lax.dot_general(left, right, dims, preferred_element_type=F32)


def normal_parts(values):
    bell = jnp.exp2(values * values * (-0.5 * LOG2E))
    t = 1.0 / (1.0 + (0.3275911 * 0.7071067811865476) * jnp.abs(values))
    poly = t * (
        0.5 * 0.254829592
        + t
        * (
            0.5 * -0.284496736
            + t * (0.5 * 1.421413741 + t * (0.5 * -1.453152027 + t * (0.5 * 1.061405429)))
        )
    )
    tail = poly * bell
    cdf = jnp.where(values >= 0.0, 1.0 - tail, tail)
    return cdf, values * bell * 0.3989422804014327


def gelu_exact(values):
    return values * normal_parts(values)[0]


def gelu_slope(values):
    cdf, slope = normal_parts(values)
    return cdf + slope


def gelu_back(values, grad_out):
    return gelu_slope(values) * grad_out


def norm_stats(values):
    centre = jnp.mean(values, axis=-1, keepdims=True)
    centred = values - centre
    spread = jnp.mean(centred * centred, axis=-1, keepdims=True)
    rstd = lax.rsqrt(spread + epsilon)
    return centred * rstd, rstd


def layer_norm(values, gain, shift):
    return norm_stats(values)[0] * gain + shift


def norm_back(values, gain, grad_out):
    unit, rstd = norm_stats(values)
    scaled = grad_out * gain
    mean_one = jnp.mean(scaled, axis=-1, keepdims=True)
    mean_two = jnp.mean(scaled * unit, axis=-1, keepdims=True)
    result = rstd * (scaled - mean_one - unit * mean_two)
    return result, jnp.sum(grad_out * unit, axis=0), jnp.sum(grad_out, axis=0)


def axis_bits(axis):
    return (lax.axis_size(axis) - 1).bit_length()


def add_low(first, second):
    return (first.astype(F32) + second.astype(F32)).astype(BF)


def head_mask(shape, head):
    lane = lax.broadcasted_iota(jnp.int32, shape, 1)
    return lane // HEAD_DIM == head


def spread_heads(block):
    zero = jnp.zeros_like(block)
    return jnp.concatenate(
        [jnp.where(head_mask(block.shape, h), block, zero) for h in range(HEADS_PER_GROUP)],
        axis=0,
    )


WIDE = 48
EDGES = 10
FIELD_EDGE, TALL_EDGE = 4, 5


def refine_kernel(
    field_ref,
    weight_ref,
    bias_ref,
    factor_ref,
    offset_ref,
    cot_ref,
    joined_ref,
    grad_ref,
    dw_ref,
    db_ref,
    sums_ref,
    acts,
    slopes,
    grads3,
    work,
    frame,
    tall,
    lane2,
    edge,
    halo,
    send_sem,
    recv_sem,
    *,
    items,
    rows,
    count,
    depth,
):
    bits = (count - 1).bit_length()
    per_share = 9 * field_ref.shape[-1] // count // depth
    me = lax.axis_index("rows")
    here = lax.axis_index("items")
    channels = field_ref.shape[-1]
    flat = items * rows * WIDE
    lanes = channels // 128
    column = lax.broadcasted_iota(jnp.int32, (WIDE, channels), 0)
    inside = column < PC

    barrier = pltpu.get_barrier_semaphore()
    for step in (-1, 1):

        @pl.when((me + step >= 0) & (me + step < count))
        def _():
            pl.semaphore_signal(
                barrier, inc=1, device_id=(here, me + step), device_id_type=pl.DeviceIdType.MESH
            )

    @pl.when((me > 0) & (me < count - 1))
    def _():
        pl.semaphore_wait(barrier, 2)

    @pl.when((me == 0) | (me == count - 1))
    def _():
        pl.semaphore_wait(barrier, 1)

    def each(side):
        return (me > 0) if side == 0 else (me < count - 1)

    def copy(e, side):
        return pltpu.make_async_remote_copy(
            src_ref=edge.at[e, side],
            dst_ref=halo.at[e, 1 - side],
            send_sem=send_sem.at[e, side],
            recv_sem=recv_sem.at[e, 1 - side],
            device_id=(here, me + (2 * side - 1)),
            device_id_type=pl.DeviceIdType.MESH,
        )

    def send(e):
        for side in (0, 1):

            @pl.when(each(side))
            def _():
                copy(e, side).start()

    def receive(e):
        for side in (0, 1):

            @pl.when(each(side))
            def _():
                pltpu.make_async_remote_copy(
                    src_ref=edge.at[e, side],
                    dst_ref=halo.at[e, side],
                    send_sem=send_sem.at[e, side],
                    recv_sem=recv_sem.at[e, side],
                    device_id=(here, me + (2 * side - 1)),
                    device_id_type=pl.DeviceIdType.MESH,
                ).wait_recv()

            @pl.when(jnp.logical_not(each(side)))
            def _():
                halo[e, side] = jnp.zeros(halo.shape[2:], BF)

    def shifted(values, flip):
        before = pltpu.roll(values, 1, 0)
        after = pltpu.roll(values, WIDE - 1, 0)
        parts = [after, values, before] if flip else [before, values, after]
        return jnp.concatenate([part.astype(BF) for part in parts], axis=1)

    def all_rows(body, e):
        for item in range(items):
            for row, side in ((0, 0), (rows - 1, 1)):
                body(item, row, (e, side))
        send(e)

        def step(row, carry):
            for item in range(items):
                body(item, row, None)
            return carry

        lax.fori_loop(1, rows - 1, step, 0)

    def spread_halo(target, e, flip):
        for side, row in ((0, 0), (1, rows + 1)):
            for item in range(items):
                target[item, row] = shifted(halo[e, side, item].astype(F32), flip)

    for item in range(items):
        factor = factor_ref[pl.ds(item, 1), :]

        def back(row, carry, item=item, factor=factor):
            whole = cot_ref[item, row].astype(F32) * factor
            for part in range(lanes):
                lane2[part, pl.ds(0, 2 * PC), :] = whole[:, part * 128 : (part + 1) * 128]
            even, odd = (
                jnp.concatenate(
                    [lane2[part, pl.ds(start, PC, stride=2), :] for part in range(lanes)], axis=1
                )
                for start in (0, 1)
            )
            place = lax.broadcasted_iota(jnp.int32, (PC, channels), 0)
            even_next = jnp.where(place == PC - 1, odd, pltpu.roll(even, PC - 1, 0))
            odd_prev = jnp.where(place == 0, even, pltpu.roll(odd, 1, 0))
            tall[item, row + 1, pl.ds(0, PC), :] = 0.75 * (even + odd) + 0.25 * (
                even_next + odd_prev
            )
            tall[item, row + 1, pl.ds(PC, WIDE - PC), :] = jnp.zeros((WIDE - PC, channels), F32)
            return carry

        lax.fori_loop(0, 2 * rows, back, 0)
        edge[TALL_EDGE, 0, item] = tall[item, 1].astype(BF)
        edge[TALL_EDGE, 1, item] = tall[item, 2 * rows].astype(BF)
    send(TALL_EDGE)

    def activate(source, which):
        def body(item, row, out):
            values = source[item, row]
            cdf, rest = normal_parts(values)
            act = jnp.where(inside, values * cdf, 0.0)
            slopes[which, item, row] = cdf + rest
            acts[which, item, row + 1] = shifted(act, False)
            if out is not None:
                edge[out[0], out[1], item] = act.astype(BF)

        all_rows(body, which)

    def weight_of(conv, kr):
        return weight_ref[conv, pl.ds(kr * 3 * channels, 3 * channels), :]

    def lhs(source, item, first, number):
        return source[item, pl.ds(first, number)].reshape(number * WIDE, -1)

    def forward(conv, add):
        bias = bias_ref[pl.ds(conv, 1), :]
        for item in range(items):
            centre = mm(lhs(acts.at[conv], item, 1, rows), weight_of(conv, 1)) + bias
            if add:
                centre = centre + frame[item, pl.ds(1, rows)].reshape(rows * WIDE, channels)
            work[item] = centre.reshape(rows, WIDE, channels)
            upper = mm(lhs(acts.at[conv], item, 1, rows - 1), weight_of(conv, 0))
            work[item, pl.ds(1, rows - 1)] += upper.reshape(rows - 1, WIDE, channels)
            lower = mm(lhs(acts.at[conv], item, 2, rows - 1), weight_of(conv, 2))
            work[item, pl.ds(0, rows - 1)] += lower.reshape(rows - 1, WIDE, channels)
        receive(conv)
        spread_halo(acts.at[conv], conv, False)
        for kr, source, row in ((0, 0, 0), (2, rows + 1, rows - 1)):
            block = jnp.concatenate([acts[conv, item, source] for item in range(items)], axis=0)
            extra = mm(block, weight_of(conv, kr))
            for item in range(items):
                work[item, row] += extra[item * WIDE : (item + 1) * WIDE]

    def keep_field(source):
        for item in range(items):
            frame[item, pl.ds(1, rows)] = source[item]

    keep_field(field_ref)
    for unit in (0, 1):
        activate(field_ref if unit == 0 else work, 2 * unit)
        forward(2 * unit, False)
        activate(work, 2 * unit + 1)
        forward(2 * unit + 1, True)
        keep_field(work)

    for item in range(items):
        edge[FIELD_EDGE, 0, item] = frame[item, 1].astype(BF)
        edge[FIELD_EDGE, 1, item] = frame[item, rows].astype(BF)
    send(FIELD_EDGE)

    receive(TALL_EDGE)
    for item in range(items):
        tall[item, 0] = jnp.where(me == 0, tall[item, 1], halo[TALL_EDGE, 0, item].astype(F32))
        tall[item, 2 * rows + 1] = jnp.where(
            me == count - 1, tall[item, 2 * rows], halo[TALL_EDGE, 1, item].astype(F32)
        )

        def fold(row, carry, item=item):
            grad_ref[item, row] = 0.75 * (
                tall[item, 2 * row + 1] + tall[item, 2 * row + 2]
            ) + 0.25 * (tall[item, 2 * row] + tall[item, 2 * row + 3])
            return carry

        lax.fori_loop(0, rows, fold, 0)

    receive(FIELD_EDGE)
    for item in range(items):
        frame[item, 0] = jnp.where(me == 0, frame[item, 1], halo[FIELD_EDGE, 0, item].astype(F32))
        frame[item, rows + 1] = jnp.where(
            me == count - 1, frame[item, rows], halo[FIELD_EDGE, 1, item].astype(F32)
        )
        factor = factor_ref[pl.ds(item, 1), :]
        offset = offset_ref[pl.ds(item, 1), :]

        def widen(row, carry, item=item, factor=factor, offset=offset):
            gain_sum, shift_sum = carry
            centre = frame[item, row + 1]
            for half in (0, 1):
                line = 0.75 * centre + 0.25 * frame[item, row + 2 * half]
                before = jnp.where(column == 0, line, pltpu.roll(line, 1, 0))
                after = jnp.where(column == PC - 1, line, pltpu.roll(line, WIDE - 1, 0))
                for start, side in ((0, before), (1, after)):
                    mixed = 0.75 * line + 0.25 * side
                    for part in range(lanes):
                        lane2[part, pl.ds(start, WIDE, stride=2), :] = mixed[
                            :, part * 128 : (part + 1) * 128
                        ]
                wide = jnp.concatenate(
                    [lane2[part, pl.ds(0, 2 * PC), :] for part in range(lanes)], axis=1
                )
                joined_ref[item, 2 * row + half] = (wide * factor + offset).astype(BF)
                cot = cot_ref[item, 2 * row + half].astype(F32)
                gain_sum = gain_sum + jnp.sum((cot * wide).reshape(-1, 8, channels), axis=0)
                shift_sum = shift_sum + jnp.sum(cot.reshape(-1, 8, channels), axis=0)
            return gain_sum, shift_sum

        zero = jnp.zeros((8, channels), F32)
        gain_sum, shift_sum = lax.fori_loop(0, rows, widen, (zero, zero))
        sums_ref[0, pl.ds(item, 1), :] = jnp.sum(gain_sum, axis=0, keepdims=True)
        sums_ref[1, pl.ds(item, 1), :] = jnp.sum(shift_sum, axis=0, keepdims=True)

    def grad_pass(conv, make):
        e = 6 + conv

        def body(item, row, out):
            values = jnp.where(inside, make(item, row), 0.0).astype(BF).astype(F32)
            grads3[item, row + 1] = shifted(values, True)
            if out is not None:
                edge[out[0], out[1], item] = values.astype(BF)

        all_rows(body, e)
        middle = jnp.concatenate(
            [
                grads3[item, pl.ds(1, rows), :, pl.ds(channels, channels)].reshape(
                    rows * WIDE, channels
                )
                for item in range(items)
            ],
            axis=0,
        )
        for kr in range(3):
            block = jnp.concatenate(
                [lhs(acts.at[conv], item, kr, rows) for item in range(items)], axis=0
            )
            weight = mm(block, middle, TN).astype(BF)
            pieces = 3 * channels // depth
            for k in range(pieces):
                share, place = divmod(kr * pieces + k, per_share)
                at = tuple(share >> b & 1 for b in range(bits - 1, -1, -1))
                dw_ref[(conv,) + at + (slice(None), pl.ds(place * channels, channels))] = weight[
                    k * depth : (k + 1) * depth
                ]
        ones = jnp.ones((8, flat), BF)
        db_ref[pl.ds(conv, 1), :] = mm(ones, middle)[:1]

        def product(block, kr):
            total = None
            for kc in range(3):
                part = mm(
                    block[:, kc * channels : (kc + 1) * channels],
                    weight_ref[conv, pl.ds((kr * 3 + kc) * channels, channels), :],
                    NT,
                )
                total = part if total is None else total + part
            return total

        for item in range(items):
            work[item] = product(lhs(grads3, item, 1, rows), 1).reshape(rows, WIDE, channels)
            work[item, pl.ds(1, rows - 1)] += product(lhs(grads3, item, 1, rows - 1), 2).reshape(
                rows - 1, WIDE, channels
            )
            work[item, pl.ds(0, rows - 1)] += product(lhs(grads3, item, 2, rows - 1), 0).reshape(
                rows - 1, WIDE, channels
            )
        receive(e)
        spread_halo(grads3, e, True)
        for kr, source, row in ((2, 0, 0), (0, rows + 1, rows - 1)):
            block = jnp.concatenate([grads3[item, source] for item in range(items)], axis=0)
            extra = product(block, kr)
            for item in range(items):
                work[item, row] += extra[item * WIDE : (item + 1) * WIDE]

    for unit in (1, 0):
        first, second = 2 * unit, 2 * unit + 1
        grad_pass(second, lambda item, row: grad_ref[item, row])
        grad_pass(first, lambda item, row: work[item, row] * slopes[second, item, row])

        def gather(row, carry, first=first):
            for item in range(items):
                grad_ref[item, row] += work[item, row] * slopes[first, item, row]
            return carry

        lax.fori_loop(0, rows, gather, 0)

    for e in range(EDGES):
        for side in (0, 1):

            @pl.when(each(side))
            def _():
                copy(e, side).wait_send()


def refine(field, conv_weights, conv_biases, factor, offset, cotangent, depth):
    items, rows, _, channels = field.shape
    count = lax.axis_size("rows")
    padded = jnp.pad(field, ((0, 0), (0, 0), (0, WIDE - PC), (0, 0)))
    vmem = pl.BlockSpec(memory_space=pltpu.VMEM)
    pixels = items * rows * PC
    outs = pl.pallas_call(
        functools.partial(refine_kernel, items=items, rows=rows, count=count, depth=depth),
        in_specs=[vmem] * 6,
        out_specs=[vmem] * 5,
        out_shape=[
            jax.ShapeDtypeStruct((items, 2 * rows, 2 * PC, channels), BF),
            jax.ShapeDtypeStruct((items, rows, WIDE, channels), F32),
            jax.ShapeDtypeStruct(
                conv_weights.shape[:1]
                + (2,) * axis_bits("rows")
                + (depth, conv_weights.shape[1] // count // depth * channels),
                BF,
            ),
            jax.ShapeDtypeStruct(conv_biases.shape, F32),
            jax.ShapeDtypeStruct((2, items, channels), F32),
        ],
        scratch_shapes=[
            pltpu.VMEM((4, items, rows + 2, WIDE, 3 * channels), BF),
            pltpu.VMEM((4, items, rows, WIDE, channels), F32),
            pltpu.VMEM((items, rows + 2, WIDE, 3 * channels), BF),
            pltpu.VMEM((items, rows, WIDE, channels), F32),
            pltpu.VMEM((items, rows + 2, WIDE, channels), F32),
            pltpu.VMEM((items, 2 * rows + 2, WIDE, channels), F32),
            pltpu.VMEM((channels // 128, 2 * WIDE, 128), F32),
            pltpu.VMEM((EDGES, 2, items, WIDE, channels), BF),
            pltpu.VMEM((EDGES, 2, items, WIDE, channels), BF),
            pltpu.SemaphoreType.DMA((EDGES, 2)),
            pltpu.SemaphoreType.DMA((EDGES, 2)),
        ],
        compiler_params=pltpu.CompilerParams(
            vmem_limit_bytes=56 << 20, collective_id=0, has_side_effects=True
        ),
        cost_estimate=pl.CostEstimate(
            flops=2 * 12 * pixels * 9 * channels * channels,
            bytes_accessed=20 << 20,
            transcendentals=8 * pixels * channels,
        ),
        name="refine",
    )(padded, conv_weights, conv_biases, factor, offset, cotangent)
    return outs


MESH = pl.DeviceIdType.MESH


def flip(index, bit):
    return index + (1 - 2 * (index // (1 << bit) % 2)) * (1 << bit)


class Reducer:
    def __init__(self, chunks, depth, strip, row_bits, item_bits, space, lag):
        self.chunks, self.depth, self.lanes = chunks, depth, strip // 2
        self.space, self.lag = space, lag
        self.row_bits, self.item_bits = row_bits, item_bits
        self.orders = (tuple(range(row_bits - 1, -1, -1)), tuple(range(row_bits)))
        self.far = max(item_bits - 2, 0)
        self.phases = 1 + row_bits + 1 + self.far + 1 + 1

    def scratch(self):
        c, half = self.chunks, self.depth // 2
        shares = (2,) * self.row_bits
        slots = [
            pltpu.VMEM((c,) + shares + (self.depth, self.lanes), BF),
            pltpu.VMEM((2,) + shares + (self.depth, self.lanes), BF),
        ]
        for stage in range(self.row_bits):
            for _ in (0, 1):
                slots.append(pltpu.VMEM((c,) + (2,) * (self.row_bits - 1 - stage) + (half, self.lanes), BF))
        slots.append(pltpu.VMEM((c, half, self.lanes), BF))
        for _ in range(self.far):
            slots.append(pltpu.VMEM((c, half, self.lanes), BF))
            slots.append(pltpu.VMEM((c, half, self.lanes), BF))
        arrivals = 1 + 2 * self.row_bits + 1 + self.far + 1 + 1
        sends = 1 + 2 * self.row_bits + 1 + self.far + 1 + 1
        return slots + [
            pltpu.VMEM((2, c, self.depth, self.lanes), BF),
            pltpu.SemaphoreType.DMA((2,)),
            pltpu.SemaphoreType.DMA((arrivals, c)),
            pltpu.SemaphoreType.DMA((sends,)),
        ]

    def slots(self):
        return len(self.scratch())

    def out_shape(self):
        return jax.ShapeDtypeStruct((2, self.chunks, self.depth, self.lanes), BF)

    def bind(self, out_ref, slots, sources=None, held=None):
        slots = list(slots)
        self.result, self.sources, self.held = out_ref, sources, held
        self.total, self.ring = slots[0], slots[1]
        self.row_in = [
            (slots[2 + 2 * stage], slots[3 + 2 * stage]) for stage in range(self.row_bits)
        ]
        rest = slots[2 + 2 * self.row_bits :]
        self.near_in = rest[0]
        self.far_out = [rest[1 + 2 * k] for k in range(self.far)]
        self.far_in = [rest[2 + 2 * k] for k in range(self.far)]
        self.out, self.ring_sem, self.recv_sem, self.send_sem = rest[-4:]
        self.me = lax.axis_index("rows")
        self.at = lax.axis_index("items")
        self.core = self.at % 2
        self.near = self.at // 2 % 2

    def peers(self):
        found = [(flip(self.at, bit), self.me) for bit in range(self.item_bits)]
        return found + [(self.at, flip(self.me, bit)) for bit in range(self.row_bits)]

    def greet(self):
        barrier = pltpu.get_barrier_semaphore()
        for peer in self.peers():
            pl.semaphore_signal(barrier, inc=1, device_id=peer, device_id_type=MESH)
        pl.semaphore_wait(barrier, len(self.peers()))

    def remote(self, source, target, arrival, sent, chunk, peer):
        return pltpu.make_async_remote_copy(
            src_ref=source,
            dst_ref=target,
            send_sem=self.send_sem.at[sent],
            recv_sem=self.recv_sem.at[arrival, chunk],
            device_id=peer,
            device_id_type=MESH,
        )

    def strip(self, ref, index, mine):
        side = self.core if mine else 1 - self.core
        lanes = pl.ds(pl.multiple_of(side * self.lanes, self.lanes), self.lanes)
        return ref.at[(index,) + (slice(None),) * (self.row_bits + 1) + (lanes,)]

    def core_copy(self, source, chunk):
        return self.remote(
            source, self.total.at[chunk], 0, 0, chunk, (flip(self.at, 0), self.me)
        )

    def begin(self):
        base = 0
        for ref in self.sources:

            def go(index, carry, ref=ref, base=base):
                self.core_copy(self.strip(ref, index, False), base + index).start()
                return carry

            lax.fori_loop(0, ref.shape[0], go, 0)
            base += ref.shape[0]
        self.fetch(0)

    def begin_held(self, chunk):
        self.core_copy(self.strip(self.held, chunk, False), chunk).start()

    def fetch(self, chunk):
        base = 0
        for ref in self.sources:

            @pl.when((chunk >= base) & (chunk < base + ref.shape[0]))
            def _(ref=ref, base=base):
                index = jnp.clip(chunk - base, 0, ref.shape[0] - 1)
                pltpu.make_async_copy(
                    self.strip(ref, index, True),
                    self.ring.at[chunk % 2],
                    self.ring_sem.at[chunk % 2],
                ).start()

            base += ref.shape[0]

    def add_mine(self, chunk):
        if self.held is not None:
            block = self.held[chunk]
            side = (slice(None),) * (self.row_bits + 1)
            block = jnp.where(
                self.core == 0,
                block[side + (slice(0, self.lanes),)],
                block[side + (slice(self.lanes, None),)],
            )
        else:
            slot = chunk % 2
            pltpu.make_async_copy(
                self.total.at[chunk], self.ring.at[slot], self.ring_sem.at[slot]
            ).wait()
            block = self.ring[slot]
        self.total[chunk] = add_low(self.total[chunk], block)

    def bit(self, which):
        return self.me // (1 << which) % 2

    def shares(self, half, stage, sent):
        order = self.orders[half]
        index = [slice(None)] * self.row_bits
        for done in order[:stage]:
            index[self.row_bits - 1 - done] = self.bit(done)
        now = order[stage]
        index[self.row_bits - 1 - now] = 1 - self.bit(now) if sent else self.bit(now)
        return tuple(index)

    def rows(self, half):
        depth = self.depth // 2
        return pl.ds(half * depth, depth)

    def row_copy(self, stage, half, chunk):
        source = self.total.at[(chunk,) + self.shares(half, stage, True) + (self.rows(half),)]
        return self.remote(
            source,
            self.row_in[stage][half].at[chunk],
            1 + 2 * stage + half,
            1 + 2 * stage + half,
            chunk,
            (self.at, flip(self.me, self.orders[half][stage])),
        )

    def own(self, chunk, rows):
        return (chunk,) + tuple(self.bit(b) for b in range(self.row_bits - 1, -1, -1)) + (rows,)

    def near_rows(self, mine):
        half = self.depth // 2
        place = self.near if mine else 1 - self.near
        return pl.ds(pl.multiple_of(place * half, half), half)

    def near_copy(self, chunk):
        return self.remote(
            self.total.at[self.own(chunk, self.near_rows(False))],
            self.near_in.at[chunk],
            1 + 2 * self.row_bits,
            1 + 2 * self.row_bits,
            chunk,
            (flip(self.at, 1), self.me),
        )

    def far_copy(self, k, chunk):
        return self.remote(
            self.far_out[k].at[chunk],
            self.far_in[k].at[chunk],
            2 + 2 * self.row_bits + k,
            2 + 2 * self.row_bits + k,
            chunk,
            (flip(self.at, 2 + k), self.me),
        )

    def back_copy(self, chunk):
        place = self.out.at[self.core, chunk, self.near_rows(True)]
        return self.remote(
            place,
            place,
            2 + 2 * self.row_bits + self.far,
            2 + 2 * self.row_bits + self.far,
            chunk,
            (flip(self.at, 1), self.me),
        )

    def last_copy(self, chunk):
        place = self.out.at[self.core, chunk]
        return self.remote(
            place,
            place,
            3 + 2 * self.row_bits + self.far,
            3 + 2 * self.row_bits + self.far,
            chunk,
            (flip(self.at, 0), self.me),
        )

    def phase(self, number, chunk):
        bits, half = self.row_bits, self.depth // 2
        if number == 0:
            self.core_copy(self.total.at[chunk], chunk).wait_recv()
            self.add_mine(chunk)
            if self.sources is not None:

                @pl.when(chunk + 1 < self.chunks)
                def _():
                    self.fetch(chunk + 1)

            for side in (0, 1):
                self.row_copy(0, side, chunk).start()
        elif number <= bits:
            stage = number - 1
            for side in (0, 1):
                self.row_copy(stage, side, chunk).wait_recv()
                at = (chunk,) + self.shares(side, stage, False) + (self.rows(side),)
                self.total[at] = add_low(self.total[at], self.row_in[stage][side][chunk])
                if stage + 1 < bits:
                    self.row_copy(stage + 1, side, chunk).start()
            if stage + 1 == bits:
                self.near_copy(chunk).start()
        elif number == bits + 1:
            self.near_copy(chunk).wait_recv()
            total = add_low(
                self.total[self.own(chunk, self.near_rows(True))], self.near_in[chunk]
            )
            self.pass_on(0, chunk, total)
        elif number <= bits + 1 + self.far:
            k = number - bits - 2
            self.far_copy(k, chunk).wait_recv()
            self.pass_on(k + 1, chunk, add_low(self.far_out[k][chunk], self.far_in[k][chunk]))
        elif number == bits + 2 + self.far:
            self.back_copy_arrived(chunk)
            self.last_copy(chunk).start()
        else:
            self.last_arrived(chunk)

    def pass_on(self, k, chunk, total):
        if k < self.far:
            self.far_out[k][chunk] = total
            self.far_copy(k, chunk).start()
        else:
            self.out[self.core, chunk, self.near_rows(True)] = total
            self.back_copy(chunk).start()

    def back_copy_arrived(self, chunk):
        place = self.out.at[self.core, chunk, self.near_rows(False)]
        self.remote(
            place,
            place,
            2 + 2 * self.row_bits + self.far,
            2 + 2 * self.row_bits + self.far,
            chunk,
            (flip(self.at, 1), self.me),
        ).wait_recv()

    def last_arrived(self, chunk):
        place = self.out.at[1 - self.core, chunk]
        self.remote(
            place,
            place,
            3 + 2 * self.row_bits + self.far,
            3 + 2 * self.row_bits + self.far,
            chunk,
            (flip(self.at, 0), self.me),
        ).wait_recv()

    def step(self, t):
        for number in range(self.phases - 1, -1, -1):
            place = t - self.lag * number
            chunk = place // self.space

            @pl.when((place >= 0) & (place % self.space == 0) & (chunk < self.chunks))
            def _(number=number, chunk=chunk):
                self.phase(number, jnp.clip(chunk, 0, self.chunks - 1))

    @property
    def steps(self):
        return (self.chunks - 1) * self.space + self.lag * (self.phases - 1) + 1

    def finish(self):
        def drain(sem, ref):
            pltpu.make_async_copy(ref, ref, self.send_sem.at[sem]).wait()

        drain(0, self.total)
        for stage in range(self.row_bits):
            for side in (0, 1):
                drain(1 + 2 * stage + side, self.row_in[stage][side])
        base = 1 + 2 * self.row_bits
        drain(base, self.near_in)
        for k in range(self.far):
            drain(base + 1 + k, self.far_in[k])
        drain(base + 1 + self.far, self.near_in)
        drain(base + 2 + self.far, self.out.at[0])
        copy = pltpu.make_async_copy(self.out, self.result, self.ring_sem.at[0])
        copy.start()
        copy.wait()


def unpack_kernel(held_ref, *refs, table, outs):
    targets, (wide, sem) = refs[:outs], refs[outs:]
    depth = wide.shape[1]

    def copy(place, chunk, first, size, number, outer, row, column):
        target = targets[number] if outer is None else targets[number].at[outer]
        return pltpu.make_async_copy(
            wide.at[chunk, :, pl.ds(first, size)],
            target.at[pl.ds(row, depth), pl.ds(column, size)],
            sem.at[place],
        )

    done = set()
    for place, entry in enumerate(table):
        chunk = entry[0]
        if chunk not in done:
            done.add(chunk)
            wide[chunk] = jnp.concatenate(
                [held_ref[0, chunk].astype(F32), held_ref[1, chunk].astype(F32)], axis=1
            )
        copy(place, *entry).start()
    for place, entry in enumerate(table):
        copy(place, *entry).wait()


def unpack(out, table, shapes):
    chunks, depth, lanes = out.shape[1:]
    return pl.pallas_call(
        functools.partial(unpack_kernel, table=table, outs=len(shapes)),
        in_specs=[pl.BlockSpec(memory_space=pltpu.VMEM)],
        out_specs=[pl.BlockSpec(memory_space=pl.ANY)] * len(shapes),
        out_shape=[jax.ShapeDtypeStruct(shape, F32) for shape in shapes],
        scratch_shapes=[
            pltpu.VMEM((chunks, depth, 2 * lanes), F32),
            pltpu.SemaphoreType.DMA((len(table),)),
        ],
        compiler_params=pltpu.CompilerParams(vmem_limit_bytes=40 << 20),
        name="unpack",
    )(out)


def all_sum_kernel(value_ref, out_ref, piece, landed, over, send_sem, recv_sem, *, count, others):
    at, me = lax.axis_index("items"), lax.axis_index("rows")
    barrier = pltpu.get_barrier_semaphore()
    row_peers = [(at, (me + k) % count) for k in range(1, count)]
    item_peers = [((at + k) % others, me) for k in range(1, others)]
    for peer in row_peers + item_peers:
        pl.semaphore_signal(barrier, inc=1, device_id=peer, device_id_type=MESH)
    pl.semaphore_wait(barrier, count + others - 2)

    def row_copy(k):
        return pltpu.make_async_remote_copy(
            src_ref=value_ref.at[row_peers[k][1]],
            dst_ref=landed.at[k],
            send_sem=send_sem.at[k],
            recv_sem=recv_sem.at[k],
            device_id=row_peers[k],
            device_id_type=MESH,
        )

    def item_copy(k):
        return pltpu.make_async_remote_copy(
            src_ref=piece,
            dst_ref=over.at[k],
            send_sem=send_sem.at[count - 1 + k],
            recv_sem=recv_sem.at[count - 1 + k],
            device_id=item_peers[k],
            device_id_type=MESH,
        )

    for k in range(count - 1):
        row_copy(k).start()
    total = value_ref[me]
    for k in range(count - 1):
        row_copy(k).wait_recv()
        total = total + landed[k]
    piece[...] = total
    for k in range(others - 1):
        item_copy(k).start()
    for k in range(others - 1):
        item_copy(k).wait_recv()
        total = total + over[k]
    out_ref[...] = total
    for k in range(count - 1):
        row_copy(k).wait_send()
    for k in range(others - 1):
        item_copy(k).wait_send()


def all_sum(value, collective_id):
    count, others = lax.axis_size("rows"), lax.axis_size("items")
    vmem = pl.BlockSpec(memory_space=pltpu.VMEM)
    block = value.shape[1:]
    return pl.pallas_call(
        functools.partial(all_sum_kernel, count=count, others=others),
        in_specs=[vmem],
        out_specs=vmem,
        out_shape=jax.ShapeDtypeStruct(block, F32),
        scratch_shapes=[
            pltpu.VMEM(block, F32),
            pltpu.VMEM((count - 1,) + block, F32),
            pltpu.VMEM((others - 1,) + block, F32),
            pltpu.SemaphoreType.DMA((count + others - 2,)),
            pltpu.SemaphoreType.DMA((count + others - 2,)),
        ],
        compiler_params=pltpu.CompilerParams(collective_id=collective_id, has_side_effects=True),
        name="sum_small",
    )(value)


class Gather:
    def __init__(self, bits, items):
        self.bits, self.items = bits, items
        self.orders = (tuple(range(bits)), tuple(range(bits - 1, -1, -1)))

    def bind(self, held, send_sem, recv_sem):
        self.held, self.send_sem, self.recv_sem = held, send_sem, recv_sem

    def place(self, item, half, stage, now):
        order = self.orders[half]
        index = [0] * self.bits
        for done in order[:stage]:
            index[self.bits - 1 - done] = slice(None)
        index[self.bits - 1 - order[stage]] = now
        size = self.held.shape[-2] // 2
        return (item,) + tuple(index) + (pl.ds(half * size, size),)

    def copy(self, item, stage, half):
        me, at = lax.axis_index("rows"), lax.axis_index("items")
        return pltpu.make_async_remote_copy(
            src_ref=self.held.at[self.place(item, half, stage, 0)],
            dst_ref=self.held.at[self.place(item, half, stage, 1)],
            send_sem=self.send_sem.at[item, stage, half],
            recv_sem=self.recv_sem.at[item, stage, half],
            device_id=(at, flip(me, self.orders[half][stage])),
            device_id_type=MESH,
        )

    def start(self, item, stage):
        for half in (0, 1):
            self.copy(item, stage, half).start()

    def arrived(self, item, stage):
        for half in (0, 1):
            self.copy(item, stage, half).wait_recv()

    def drain(self, item):
        for stage in range(self.bits):
            for half in (0, 1):
                self.copy(item, stage, half).wait_send()


def attention_forward_kernel(
    valid_ref,
    tokens_ref,
    gain_ref,
    shift_ref,
    q_bias_ref,
    v_bias_ref,
    wq_ref,
    wk_ref,
    wv_ref,
    q_ref,
    k_ref,
    v_ref,
    o_ref,
    lse_ref,
    normed_ref,
    held,
    send_sem,
    recv_sem,
    copy_sem,
    *,
    gather,
    groups,
    items,
):
    gather.bind(held, send_sem, recv_sem)
    step = pl.program_id(0)
    item, group = step // groups, step % groups
    t, width = held.shape[-2:]
    n = k_ref.shape[1]
    me, at = lax.axis_index("rows"), lax.axis_index("items")
    bits = gather.bits
    mine = (0,) * bits

    def store(which):
        held[(which,) + mine] = layer_norm(
            tokens_ref[which].astype(F32), gain_ref[...], shift_ref[...]
        ).astype(BF)

    def keep(which):
        return pltpu.make_async_copy(held.at[which], normed_ref.at[which], copy_sem.at[which])

    @pl.when(step == 0)
    def _():
        store(0)
        barrier = pltpu.get_barrier_semaphore()
        for bit in range(bits):
            pl.semaphore_signal(
                barrier, inc=1, device_id=(at, flip(me, bit)), device_id_type=MESH
            )
        pl.semaphore_wait(barrier, bits)
        gather.start(0, 0)
        for which in range(1, items):
            store(which)
        for stage in range(1, bits):
            gather.arrived(0, stage - 1)
            gather.start(0, stage)
        gather.start(1, 0)

    @pl.when(group == 0)
    def _():
        gather.arrived(item, bits - 1)
        keep(item).start()

    limit = valid_ref[item] * PC
    index = lax.broadcasted_iota(jnp.int32, (1, n), 1)
    bias = jnp.where(index + key_shift(index, n, t, me) < limit, 0.0, MASKED).astype(F32)
    every = held[item].reshape(n, width)
    keys = mm(every, wk_ref[...]).astype(BF)
    values = (mm(every, wv_ref[...]) + v_bias_ref[...]).astype(BF)
    queries = (mm(held[(item,) + mine], wq_ref[...]) + q_bias_ref[...]).astype(BF)
    k_ref[0] = keys
    v_ref[0] = values
    q_ref[0] = queries
    queries = queries * jnp.asarray(HEAD_DIM**-0.5, BF)
    out = jnp.zeros((t, GROUP), F32)
    for h in range(HEADS_PER_GROUP):
        mask = head_mask((t, GROUP), h)
        one = jnp.where(mask, queries, jnp.zeros_like(queries))
        scores = mm(one, keys, NT) + bias
        top = jnp.max(scores, axis=1, keepdims=True)
        probs = jnp.exp2((scores - top) * LOG2E)
        total = jnp.sum(probs, axis=1, keepdims=True)
        weighted = mm(probs.astype(BF), values)
        out = jnp.where(mask, weighted * (1.0 / total), out)
        lse = top * LOG2E + jnp.log2(total)
        lse_ref[0, 0, :, pl.ds(h * t, t)] = jnp.transpose(jnp.broadcast_to(lse, (t, 128)))[:8]
    o_ref[0] = out.astype(BF)

    for stage in range(1, bits):

        @pl.when((group == stage - 1) & (item + 1 < items))
        def _(stage=stage):
            gather.arrived(item + 1, stage - 1)
            gather.start(item + 1, stage)

    @pl.when((group == bits - 2) & (item + 2 < items))
    def _():
        gather.start(item + 2, 0)

    @pl.when(step == items * groups - 1)
    def _():
        for which in range(items):
            gather.drain(which)
            keep(which).wait()


def attention_forward(valid_rows, tokens, gain, shift, qkv_weight, q_bias, v_bias, collective_id):
    items, t, d = tokens.shape
    bits = axis_bits("rows")
    n = t << bits
    groups = d // GROUP
    rows4 = HEADS_PER_GROUP * t
    vmem = pl.BlockSpec(memory_space=pltpu.VMEM)

    def weight_spec(kind):
        return pl.BlockSpec((d, GROUP), lambda i: (0, kind * groups + i % groups))

    bias_spec = pl.BlockSpec((1, GROUP), lambda i: (0, i % groups))
    query_spec = pl.BlockSpec((1, t, GROUP), lambda i: (i // groups, 0, i % groups))
    key_spec = pl.BlockSpec((1, n, GROUP), lambda i: (i // groups, 0, i % groups))
    return pl.pallas_call(
        functools.partial(
            attention_forward_kernel, gather=Gather(bits, items), groups=groups, items=items
        ),
        grid=(items * groups,),
        in_specs=[
            pl.BlockSpec(memory_space=pltpu.SMEM),
            vmem,
            vmem,
            vmem,
            bias_spec,
            bias_spec,
            weight_spec(0),
            weight_spec(1),
            weight_spec(2),
        ],
        out_specs=[
            query_spec,
            key_spec,
            key_spec,
            query_spec,
            pl.BlockSpec((1, 1, 8, rows4), lambda i: (i // groups, i % groups, 0, 0)),
            pl.BlockSpec(memory_space=pl.ANY),
        ],
        out_shape=[
            jax.ShapeDtypeStruct((items, t, d), BF),
            jax.ShapeDtypeStruct((items, n, d), BF),
            jax.ShapeDtypeStruct((items, n, d), BF),
            jax.ShapeDtypeStruct((items, t, d), BF),
            jax.ShapeDtypeStruct((items, groups, 8, rows4), F32),
            jax.ShapeDtypeStruct((items,) + (2,) * bits + (t, d), BF),
        ],
        scratch_shapes=[
            pltpu.VMEM((items,) + (2,) * bits + (t, d), BF),
            pltpu.SemaphoreType.DMA((items, bits, 2)),
            pltpu.SemaphoreType.DMA((items, bits, 2)),
            pltpu.SemaphoreType.DMA((items,)),
        ],
        compiler_params=pltpu.CompilerParams(
            vmem_limit_bytes=52 << 20, collective_id=collective_id, has_side_effects=True
        ),
        cost_estimate=pl.CostEstimate(
            flops=60 * items * t * n * d,
            bytes_accessed=40 << 20,
            transcendentals=12 * items * t * n,
        ),
        name="attention_forward",
    )(
        valid_rows,
        tokens,
        gain,
        shift,
        q_bias,
        v_bias,
        qkv_weight,
        qkv_weight,
        qkv_weight,
    )


def key_shift(index, length, block, me):
    start = jnp.full_like(index, me * block)
    for j in range(1, length // block):
        other = me
        for bit in range(j.bit_length()):
            if j >> bit & 1:
                other = flip(other, bit)
        start = jnp.where(index >= j * block, (other - j) * block, start)
    return start


def shares_of(bits):
    return (2,) * bits


def mlp_backward_kernel(
    tap_grad_ref,
    cot_ref,
    out_tokens_ref,
    normed_ref,
    resid_ref,
    attended_ref,
    gain_ref,
    tap_w_ref,
    out_w_ref,
    hidden_ref,
    slope_ref,
    fc1_ref,
    fc2_ref,
    tap_dw_ref,
    out_dw_ref,
    fc1_dw_ref,
    fc2_dw_ref,
    resid_grad_ref,
    attended_grad_ref,
    wide_sums_ref,
    fc1_sums_ref,
    out_grad,
    low_grad,
    pre_grad,
    back,
    *,
    blocks,
    row_block,
    bits,
):
    step = pl.program_id(0)
    tokens, width = low_grad.shape
    count = 1 << bits
    depth = width // count
    shares = shares_of(bits)
    pieces = [pl.ds(k * row_block, row_block) for k in range(tokens // row_block)]

    @pl.when(step == 0)
    def _():
        total = jnp.zeros((1, width), F32)
        tap_total = jnp.zeros((1, tap_grad_ref.shape[1]), F32)
        for piece in pieces:
            tap_part = tap_grad_ref[piece, :]
            value = cot_ref[piece, :].astype(F32) + mm(tap_part, tap_w_ref[...], NT)
            out_grad[piece, :] = value
            low = value.astype(BF)
            low_grad[piece, :] = low
            back[piece, :] = jnp.zeros((row_block, width), F32)
            total = total + jnp.sum(low.astype(F32), axis=0, keepdims=True)
            tap_total = tap_total + jnp.sum(tap_part.astype(F32), axis=0, keepdims=True)
        wide_sums_ref[pl.ds(0, 1), :] = total
        wide_sums_ref[pl.ds(4, 1), :] = jnp.concatenate(
            [tap_total] * (width // tap_total.shape[1]), axis=1
        )
        weight = mm(out_tokens_ref[...], tap_grad_ref[...], TN).astype(BF)
        weight = jnp.concatenate(
            [weight, jnp.zeros((width, width - weight.shape[1]), BF)], axis=1
        )
        tap_dw_ref[0] = weight.reshape(shares + (depth, width))

    def rows_of(number):
        return pl.ds(pl.multiple_of(number * row_block, row_block), row_block)

    def inward(number, sums):
        piece = rows_of(number)
        grads = mm(low_grad[piece, :], fc2_ref[...], NT) * slope_ref[piece, :].astype(F32)
        low = grads.astype(BF)
        pre_grad[piece, :] = low
        return sums + jnp.sum(low.astype(F32), axis=0, keepdims=True)

    fc1_sums_ref[...] = lax.fori_loop(
        0, len(pieces), inward, jnp.zeros((1, pre_grad.shape[1]), F32)
    )
    weight = mm(hidden_ref[...], low_grad[...], TN).astype(BF)
    per_share = weight.shape[0] // depth * blocks // count
    for place in range(weight.shape[0] // depth):
        fc2_dw_ref[place % per_share, place // per_share] = weight[
            place * depth : (place + 1) * depth
        ]
    weight = mm(normed_ref[...], pre_grad[...], TN).astype(BF)
    fc1_dw_ref[0] = weight.reshape(shares + (depth, width))

    def outward(number, carry):
        piece = rows_of(number)
        back[piece, :] += mm(pre_grad[piece, :], fc1_ref[...], NT)
        return carry

    lax.fori_loop(0, len(pieces), outward, 0)

    @pl.when(step == blocks - 1)
    def _():
        gain = gain_ref[...]
        gain_total = jnp.zeros((1, width), F32)
        shift_total = jnp.zeros((1, width), F32)
        total = jnp.zeros((1, width), F32)
        for piece in pieces:
            grads = back[piece, :]
            unit, rstd = norm_stats(resid_ref[piece, :])
            scaled = grads * gain
            mean_one = jnp.mean(scaled, axis=-1, keepdims=True)
            mean_two = jnp.mean(scaled * unit, axis=-1, keepdims=True)
            value = out_grad[piece, :] + rstd * (scaled - mean_one - unit * mean_two)
            resid_grad_ref[piece, :] = value
            low = value.astype(BF)
            low_grad[piece, :] = low
            gain_total = gain_total + jnp.sum(grads * unit, axis=0, keepdims=True)
            shift_total = shift_total + jnp.sum(grads, axis=0, keepdims=True)
            total = total + jnp.sum(low.astype(F32), axis=0, keepdims=True)
            attended_grad_ref[piece, :] = mm(low, out_w_ref[...], NT).astype(BF)
        wide_sums_ref[pl.ds(1, 1), :] = gain_total
        wide_sums_ref[pl.ds(2, 1), :] = shift_total
        wide_sums_ref[pl.ds(3, 1), :] = total
        weight = mm(attended_ref[...], low_grad[...], TN).astype(BF)
        out_dw_ref[0] = weight.reshape(shares + (depth, width))


def mlp_backward(
    grad_tap,
    cotangent,
    out_tokens,
    normed,
    resid,
    attended,
    gain,
    tap_weight,
    out_weight,
    hidden,
    slope,
    fc1_weight,
    fc2_weight,
    row_block,
):
    tokens, width = resid.shape
    inner = hidden.shape[1]
    bits = axis_bits("rows")
    count = 1 << bits
    depth = width // count
    blocks = inner // width
    vmem = pl.BlockSpec(memory_space=pltpu.VMEM)
    column = pl.BlockSpec((tokens, width), lambda i: (0, i))
    fc2_chunks = inner // count // depth
    shares = shares_of(bits)
    share_step = count // blocks
    outs = pl.pallas_call(
        functools.partial(
            mlp_backward_kernel,
            blocks=blocks,
            row_block=row_block,
            bits=bits,
        ),
        grid=(blocks,),
        in_specs=[vmem] * 9
        + [
            column,
            column,
            pl.BlockSpec((width, width), lambda i: (0, i)),
            pl.BlockSpec((width, width), lambda i: (i, 0)),
        ],
        out_specs=[
            vmem,
            vmem,
            pl.BlockSpec((1,) + shares + (depth, width), lambda i: (i,) + (0,) * (bits + 2)),
            pl.BlockSpec((fc2_chunks, share_step, depth, width), lambda i: (0, i, 0, 0)),
            vmem,
            vmem,
            vmem,
            pl.BlockSpec((1, width), lambda i: (0, i)),
        ],
        out_shape=[
            jax.ShapeDtypeStruct((1,) + shares + (depth, width), BF),
            jax.ShapeDtypeStruct((1,) + shares + (depth, width), BF),
            jax.ShapeDtypeStruct((blocks,) + shares + (depth, width), BF),
            jax.ShapeDtypeStruct((fc2_chunks, count, depth, width), BF),
            jax.ShapeDtypeStruct((tokens, width), F32),
            jax.ShapeDtypeStruct((tokens, width), BF),
            jax.ShapeDtypeStruct((8, width), F32),
            jax.ShapeDtypeStruct((1, inner), F32),
        ],
        scratch_shapes=[
            pltpu.VMEM((tokens, width), F32),
            pltpu.VMEM((tokens, width), BF),
            pltpu.VMEM((tokens, width), BF),
            pltpu.VMEM((tokens, width), F32),
        ],
        compiler_params=pltpu.CompilerParams(vmem_limit_bytes=60 << 20),
        cost_estimate=pl.CostEstimate(
            flops=8 * tokens * width * inner, bytes_accessed=40 << 20, transcendentals=0
        ),
        name="mlp_backward",
    )(
        grad_tap,
        cotangent,
        out_tokens,
        normed,
        resid,
        attended,
        gain,
        tap_weight,
        out_weight,
        hidden,
        slope,
        fc1_weight,
        fc2_weight,
    )
    return outs


class Scatter:
    def __init__(self, bits, tokens, width, items):
        self.bits, self.tokens, self.width, self.items = bits, tokens, width, items
        self.orders = (tuple(range(bits - 1, -1, -1)), tuple(range(bits)))

    def scratch(self):
        slots = [pltpu.VMEM((2,) * self.bits + (self.tokens, self.width), BF)]
        for stage in range(self.bits):
            for _ in (0, 1):
                slots.append(
                    pltpu.VMEM(
                        (self.items,)
                        + (2,) * (self.bits - 1 - stage)
                        + (self.tokens // 2, self.width),
                        BF,
                    )
                )
        return slots + [
            pltpu.SemaphoreType.DMA((self.bits, 2)),
            pltpu.SemaphoreType.DMA((self.items, self.bits, 2)),
        ]

    def bind(self, slots):
        self.held = slots[0]
        self.landed = [(slots[1 + 2 * s], slots[2 + 2 * s]) for s in range(self.bits)]
        self.send_sem, self.recv_sem = slots[-2:]

    def place(self, half, stage, bit_value):
        index = [slice(None)] * self.bits
        for done in self.orders[half][:stage]:
            index[self.bits - 1 - done] = 0
        index[self.bits - 1 - self.orders[half][stage]] = bit_value
        size = self.tokens // 2
        return tuple(index) + (pl.ds(half * size, size),)

    def copy(self, item, stage, half):
        me, at = lax.axis_index("rows"), lax.axis_index("items")
        return pltpu.make_async_remote_copy(
            src_ref=self.held.at[self.place(half, stage, 1)],
            dst_ref=self.landed[stage][half].at[item],
            send_sem=self.send_sem.at[stage, half],
            recv_sem=self.recv_sem.at[item, stage, half],
            device_id=(at, flip(me, self.orders[half][stage])),
            device_id_type=MESH,
        )

    def start(self, item):
        for half in (0, 1):
            self.copy(item, 0, half).start()

    def advance(self, item, stage, finish):
        for half in (0, 1):
            self.copy(item, stage, half).wait_recv()
            at = self.place(half, stage, 0)
            if stage + 1 < self.bits:
                self.held[at] = add_low(self.held[at], self.landed[stage][half][item])
                self.copy(item, stage + 1, half).start()
            else:
                finish(
                    at[-1],
                    self.held[at].astype(F32) + self.landed[stage][half][item].astype(F32),
                )

    def drain(self, item):
        for stage in range(self.bits):
            for half in (0, 1):
                self.copy(item, stage, half).wait_send()


def attention_backward_kernel(
    valid_ref,
    q_ref,
    k_ref,
    v_ref,
    g_ref,
    o_ref,
    lse_ref,
    normed_ref,
    wq_ref,
    wk_ref,
    wv_ref,
    *refs,
    reducer,
    late,
    scatter,
    groups,
    items,
    kb,
    rounds,
    sources,
):
    early_sources = refs[:sources]
    grad_ref, sums_ref, early_out, late_out = refs[sources : sources + 4]
    slots = list(refs[sources + 4 :])
    q4, g4, acc, dkv, back, held = slots[:6]
    del slots[:6]
    early_slots = slots[: reducer.slots()]
    del slots[: reducer.slots()]
    late_slots = slots[: late.slots()]
    del slots[: late.slots()]
    reducer.bind(early_out, early_slots, sources=early_sources)
    late.bind(late_out, late_slots, held=held)
    scatter.bind(slots)
    step = pl.program_id(0)
    item, group = step // groups, step % groups
    t, n = q_ref.shape[1], k_ref.shape[1]
    width = back.shape[1]
    depth = width // (1 << reducer.row_bits)
    shares = shares_of(reducer.row_bits)
    me = lax.axis_index("rows")

    @pl.when(step == 0)
    def _():
        reducer.greet()
        reducer.begin()
        sums_ref[...] = jnp.zeros_like(sums_ref)

    q4[...] = spread_heads(q_ref[0] * jnp.asarray(HEAD_DIM**-0.5, BF))
    grads = spread_heads(g_ref[0])
    g4[...] = grads
    outs = jnp.concatenate([o_ref[0].astype(F32)] * HEADS_PER_GROUP, axis=0)
    product = grads.astype(F32) * outs
    high = product.astype(BF)
    low = (product - high.astype(F32)).astype(BF)
    ones = jnp.ones((8, GROUP), BF)
    dots = (mm(ones, high, NT) + mm(ones, low, NT))[:1]
    lse = lse_ref[0, 0, :1, :]
    acc[...] = jnp.zeros_like(acc)
    limit = valid_ref[item] * PC

    def turn(number):
        now = step * rounds + number
        reducer.step(now)
        late.step(now - ((items - 1) * groups + 1) * rounds)

    inner = n // kb
    each = rounds // inner

    def block_step(b, carry):
        at = pl.ds(pl.multiple_of(b * kb, kb), kb)
        keys, values = k_ref[0, at, :], v_ref[0, at, :]
        index = b * kb + lax.broadcasted_iota(jnp.int32, (kb, 1), 0)
        position = index + key_shift(index, n, t, me)
        bias = jnp.where(position < limit, 0.0, MASKED).astype(F32)
        scores = mm(keys, q4[...], NT)
        probs = jnp.exp2((scores * LOG2E + bias) - lse)
        grad_probs = mm(values, g4[...], NT)
        grad_scores = (probs * (grad_probs - dots)).astype(BF)
        dkv[at, pl.ds(GROUP, GROUP)] = mm(probs.astype(BF), g4[...]).astype(BF)
        dkv[at, pl.ds(0, GROUP)] = mm(grad_scores, q4[...]).astype(BF)
        acc[...] += mm(grad_scores, keys, TN)

        def rest(k, inner_carry):
            turn(b * each + k)
            return inner_carry

        lax.fori_loop(0, each, rest, 0)
        return carry

    lax.fori_loop(0, inner, block_step, 0)
    out = jnp.zeros((t, GROUP), F32)
    for h in range(HEADS_PER_GROUP):
        out = jnp.where(head_mask((t, GROUP), h), acc[pl.ds(h * t, t), :], out)
    dq = (out * HEAD_DIM**-0.5).astype(BF)

    for stage in range(scatter.bits):

        @pl.when((group == stage) & (item > 0))
        def _(stage=stage):
            def finish(rows, value):
                grad_ref[item - 1, rows, :] += value

            scatter.advance(item - 1, stage, finish)

    row_piece = n // 4
    both = jnp.concatenate([wk_ref[...], wv_ref[...]], axis=1)

    def project(k, carry):
        at = pl.ds(pl.multiple_of(k * row_piece, row_piece), row_piece)
        value = mm(dkv[at, :], both, NT)
        back[at, :] = jnp.where(group == 0, value, back[at, :] + value)
        return carry

    lax.fori_loop(0, 4, project, 0)
    value = mm(dq, wq_ref[...], NT)
    grad_ref[item] = jnp.where(group == 0, value, grad_ref[item] + value)

    part = jnp.concatenate(
        [mm(normed_ref[0, pl.ds(0, t), :], dq, TN), mm(normed_ref[0], dkv[...], TN)], axis=1
    ).reshape(shares + (depth, width))
    before = held[group].astype(F32)
    held[group] = jnp.where(item == 0, part, before + part).astype(BF)
    sums_ref[group, pl.ds(0, 1), :] += jnp.sum(dq.astype(F32), axis=0, keepdims=True)
    sums_ref[group, pl.ds(1, 1), :] += jnp.sum(
        dkv[:, pl.ds(GROUP, GROUP)].astype(F32), axis=0, keepdims=True
    )

    @pl.when(item == items - 1)
    def _():
        late.begin_held(group)

    @pl.when(group == groups - 1)
    def _():
        @pl.when(item > 0)
        def _():
            scatter.drain(item - 1)

        for j in range(1 << scatter.bits):
            index = tuple(j >> b & 1 for b in range(scatter.bits - 1, -1, -1))
            scatter.held[index] = back[pl.ds(j * t, t), :].astype(BF)
        scatter.start(item)

    @pl.when(step == items * groups - 1)
    def _():
        start = ((items - 1) * groups + 1) * rounds

        def rest(now, carry):
            @pl.when(now < reducer.steps)
            def _():
                reducer.step(now)

            late.step(now - start)
            return carry

        last = items * groups * rounds
        end = start + late.steps
        lax.fori_loop(last, last + late.lag, rest, 0)
        for stage in range(scatter.bits):

            def finish(rows, value):
                grad_ref[items - 1, rows, :] += value

            scatter.advance(items - 1, stage, finish)
        lax.fori_loop(last + late.lag, max(end, reducer.steps), rest, 0)
        scatter.drain(items - 1)
        reducer.finish()
        late.finish()


def attention_backward(
    valid_rows, queries, keys, values, grads, outs, lse, normed, qkv_weight, packed, collective_id
):
    items, t, d = queries.shape
    n = keys.shape[1]
    groups = d // GROUP
    bits = axis_bits("rows")
    depth = d >> bits
    rows4 = HEADS_PER_GROUP * t
    rounds = 8
    reducer = Reducer(
        sum(a.shape[0] for a in packed), depth, d, bits, axis_bits("items"), 4, 5
    )
    late = Reducer(groups, depth, d, bits, axis_bits("items"), rounds, 4)
    scatter = Scatter(bits, t, d, items)
    query_spec = pl.BlockSpec((1, t, GROUP), lambda i: (i // groups, 0, i % groups))
    vmem = pl.BlockSpec(memory_space=pltpu.VMEM)

    def weight_spec(kind):
        return pl.BlockSpec((d, GROUP), lambda i: (0, kind * groups + i % groups))

    key_spec = pl.BlockSpec((1, n, GROUP), lambda i: (i // groups, 0, i % groups))

    outs = pl.pallas_call(
        functools.partial(
            attention_backward_kernel,
            reducer=reducer,
            late=late,
            scatter=scatter,
            groups=groups,
            items=items,
            kb=n // 4,
            rounds=rounds,
            sources=len(packed),
        ),
        grid=(items * groups,),
        in_specs=[
            pl.BlockSpec(memory_space=pltpu.SMEM),
            query_spec,
            key_spec,
            key_spec,
            query_spec,
            query_spec,
            pl.BlockSpec((1, 1, 8, rows4), lambda i: (i // groups, i % groups, 0, 0)),
            pl.BlockSpec((1, n, d), lambda i: (i // groups, 0, 0), pipeline_mode=pl.Buffered(1)),
            weight_spec(0),
            weight_spec(1),
            weight_spec(2),
        ]
        + [pl.BlockSpec(memory_space=pl.ANY)] * len(packed),
        out_specs=[vmem] * 2 + [pl.BlockSpec(memory_space=pl.ANY)] * 2,
        out_shape=[
            jax.ShapeDtypeStruct((items, t, d), F32),
            jax.ShapeDtypeStruct((groups, 8, GROUP), F32),
            reducer.out_shape(),
            late.out_shape(),
        ],
        scratch_shapes=[
            pltpu.VMEM((rows4, GROUP), BF),
            pltpu.VMEM((rows4, GROUP), BF),
            pltpu.VMEM((rows4, GROUP), F32),
            pltpu.VMEM((n, 2 * GROUP), BF),
            pltpu.VMEM((n, d), F32),
            pltpu.VMEM((groups,) + shares_of(bits) + (depth, d), BF),
        ]
        + reducer.scratch()
        + late.scratch()
        + scatter.scratch(),
        compiler_params=pltpu.CompilerParams(
            vmem_limit_bytes=63 << 20, collective_id=collective_id, has_side_effects=True
        ),
        cost_estimate=pl.CostEstimate(
            flops=100 * items * t * n * d,
            bytes_accessed=40 << 20,
            transcendentals=12 * items * t * n,
        ),
        name="attention_backward",
    )(
        valid_rows,
        queries,
        keys,
        values,
        grads,
        outs,
        lse,
        normed,
        qkv_weight,
        qkv_weight,
        qkv_weight,
        *packed,
    )
    return outs


def shards(
    tokens,
    valid_rows,
    dataset_ids,
    shift_flags,
    norm_gains,
    norm_biases,
    qkv_weight,
    qv_bias,
    out_weight,
    out_bias,
    fc1_weight,
    fc1_bias,
    fc2_weight,
    fc2_bias,
    tap_weight,
    tap_bias,
    conv_weights,
    conv_biases,
    table_gain,
    table_shift,
    token_cotangent,
    joined_cotangent,
):
    items_here, tok_here, width = tokens.shape
    rows_here = tok_here // PC
    channels = tap_weight.shape[1]
    row_index = lax.axis_index("rows")
    row_count = lax.axis_size("rows")
    last_index = row_count - 1

    flat_in = tokens.reshape(-1, width).astype(F32)
    queries, keys, values, attended, lses, normed_all = attention_forward(
        valid_rows,
        tokens,
        norm_gains[:1],
        norm_biases[:1],
        qkv_weight,
        qv_bias[None, :width],
        qv_bias[None, width:],
        5,
    )
    attended_flat = attended.reshape(-1, width)
    resid = flat_in + mm(attended_flat, out_weight) + out_bias
    normed_two = layer_norm(resid, norm_gains[1], norm_biases[1]).astype(BF)
    hidden_pre = mm(normed_two, fc1_weight) + fc1_bias
    hidden_cdf, hidden_rest = normal_parts(hidden_pre)
    hidden = (hidden_pre * hidden_cdf).astype(BF)
    hidden_slope = (hidden_cdf + hidden_rest).astype(BF)
    output = resid + mm(hidden, fc2_weight) + fc2_bias
    output_low = output.astype(BF)
    grid_rows = row_index * rows_here + jnp.arange(rows_here, dtype=jnp.int32)
    row_valid = (grid_rows[None, :] < valid_rows[:, None]).astype(F32)
    token_valid = jnp.broadcast_to(
        row_valid[:, :, None], (items_here, rows_here, PC)
    ).reshape(-1, 1)
    tap_pre = mm(output_low, tap_weight) + tap_bias
    field = (tap_pre * token_valid).reshape(items_here, rows_here, PC, channels)

    choose = (
        dataset_ids[:, None] == jnp.arange(table_gain.shape[0], dtype=jnp.int32)[None, :]
    ).astype(F32)
    flag_value = shift_flags.astype(F32)[:, None]
    gain_pick = jnp.dot(choose, table_gain, precision=highest)
    shift_pick = jnp.dot(choose, table_shift, precision=highest)
    factor = 1.0 + flag_value * (gain_pick - 1.0)
    offset = flag_value * shift_pick
    depth = width // row_count
    joined, grad_field, conv_grads, grad_conv_biases, table_sums = refine(
        field, conv_weights, conv_biases, factor, offset, joined_cotangent, depth
    )
    grad_table_gain = jnp.dot(choose.T, flag_value * table_sums[0], precision=highest)
    grad_table_shift = jnp.dot(choose.T, flag_value * table_sums[1], precision=highest)

    grad_tap = (grad_field[:, :, :PC].reshape(-1, channels) * token_valid).astype(BF)
    (
        tap_grads,
        out_grads,
        fc1_grads,
        fc2_grads,
        grad_resid,
        grad_attended,
        wide_sums,
        fc1_sums,
    ) = mlp_backward(
        grad_tap,
        token_cotangent.reshape(-1, width),
        output_low,
        normed_two,
        resid,
        attended_flat,
        norm_gains[1:2],
        tap_weight,
        out_weight,
        hidden,
        hidden_slope,
        fc1_weight,
        fc2_weight,
        tok_here,
    )
    shares = shares_of(axis_bits("rows"))
    fc2_grads = fc2_grads.reshape(fc2_grads.shape[:1] + shares + fc2_grads.shape[2:])
    grads_in, qkv_sums, early_sum, late_sum = attention_backward(
        valid_rows,
        queries,
        keys,
        values,
        grad_attended.reshape(tokens.shape),
        attended,
        lses,
        normed_all.reshape(keys.shape),
        qkv_weight,
        [conv_grads, tap_grads, fc2_grads, fc1_grads, out_grads],
        3,
    )
    grad_in_norm, grad_gain_one, grad_shift_one = norm_back(
        flat_in, norm_gains[0], grads_in.reshape(-1, width)
    )
    grad_tokens = (grad_resid + grad_in_norm).reshape(tokens.shape)

    groups = width // GROUP
    inner = fc1_weight.shape[1]
    kernels = conv_weights.shape[1]
    convs = conv_weights.shape[0]
    places = kernels // row_count // depth
    fc2_chunks = inner // row_count // depth
    blocks = inner // width
    table = [
        (conv, place * channels, channels, 0, conv, place * depth, 0)
        for conv in range(convs)
        for place in range(places)
    ]
    table += [(convs, 0, channels, 1, None, 0, 0)]
    first = convs + 1
    table += [(first + k, 0, width, 2, None, k * depth, 0) for k in range(fc2_chunks)]
    first += fc2_chunks
    table += [(first + k, 0, width, 3, None, 0, k * width) for k in range(blocks)]
    table += [(first + blocks, 0, width, 4, None, 0, 0)]
    share_conv, share_tap, share_fc2, share_fc1, share_out = unpack(
        early_sum,
        table,
        [
            (convs, kernels // row_count, channels),
            (depth, channels),
            (inner // row_count, width),
            (depth, inner),
            (depth, width),
        ],
    )
    (share_qkv,) = unpack(
        late_sum,
        [
            (group, kind * GROUP, GROUP, 0, None, 0, (kind * groups + group) * GROUP)
            for group in range(groups)
            for kind in range(3)
        ],
        [(depth, 3 * width)],
    )

    small = [
        jnp.stack([grad_gain_one, wide_sums[1]]),
        jnp.stack([grad_shift_one, wide_sums[2]]),
        jnp.concatenate([qkv_sums[:, 0].reshape(-1), qkv_sums[:, 1].reshape(-1)]),
        wide_sums[3],
        fc1_sums[0],
        wide_sums[0],
        wide_sums[4, :channels],
        grad_conv_biases,
        grad_table_gain,
        grad_table_shift,
    ]
    packed = jnp.concatenate(
        [
            array.reshape(row_count, -1)
            if array.ndim == 1
            else jnp.swapaxes(array.reshape(array.shape[0], row_count, -1), 0, 1).reshape(
                row_count, -1
            )
            for array in small
        ],
        axis=1,
    )
    packed = jnp.pad(packed, ((0, 0), (0, -packed.shape[1] % 1024)))
    summed = all_sum(packed.reshape(row_count, -1, 128), 4).reshape(-1)
    outs, place = [], 0
    for array in small:
        size = array.size // row_count
        piece = summed[place : place + size]
        place += size
        outs.append(piece if array.ndim == 1 else piece.reshape(array.shape[0], -1))
    (
        out_gains,
        out_shifts,
        out_qv,
        out_out,
        out_fc1,
        out_fc2,
        out_tap,
        out_conv,
        out_table_gain,
        out_table_shift,
    ) = outs
    return (
        output_low.reshape(tokens.shape),
        joined,
        grad_tokens,
        out_gains,
        out_shifts,
        share_qkv,
        out_qv,
        share_out,
        out_out,
        share_fc1,
        out_fc1,
        share_fc2,
        out_fc2,
        share_tap,
        out_tap,
        share_conv,
        out_conv,
        out_table_gain,
        out_table_shift,
    )


def solution(mesh):
    return jax.shard_map(
        shards,
        mesh=mesh,
        in_specs=(P("items", "rows", None), P("items"), P("items"), P("items"))
        + (P(),) * 16
        + (P("items", "rows", None), P("items", "rows", None, None)),
        out_specs=(
            P("items", "rows", None),
            P("items", "rows", None, None),
            P("items", "rows", None),
            P(None, "rows"),
            P(None, "rows"),
            P("rows", None),
            P("rows"),
            P("rows", None),
            P("rows"),
            P("rows", None),
            P("rows"),
            P("rows", None),
            P("rows"),
            P("rows", None),
            P("rows"),
            P(None, "rows", None),
            P(None, "rows"),
            P(None, "rows"),
            P(None, "rows"),
        ),
        check_vma=False,
    )
```

```python
import functools

import jax
import jax.numpy as jnp
from jax import lax
from jax.experimental import pallas as pl
from jax.experimental.pallas import tpu as pltpu
from jax.sharding import PartitionSpec as P

HEAD_DIM = 64
PC = 40
GROUP = 256
HEADS_PER_GROUP = GROUP // HEAD_DIM

BF = jnp.bfloat16
F32 = jnp.float32
LOG2E = 1.4426950408889634
MASKED = -1e30
NN = (((1,), (0,)), ((), ()))
NT = (((1,), (1,)), ((), ()))
TN = (((0,), (0,)), ((), ()))

epsilon = 1e-06
highest = lax.Precision.HIGHEST


def mm(left, right, dims=NN):
    return lax.dot_general(left, right, dims, preferred_element_type=F32)


def normal_parts(values):
    bell = jnp.exp2(values * values * (-0.5 * LOG2E))
    t = 1.0 / (1.0 + (0.3275911 * 0.7071067811865476) * jnp.abs(values))
    poly = t * (
        0.5 * 0.254829592
        + t
        * (
            0.5 * -0.284496736
            + t * (0.5 * 1.421413741 + t * (0.5 * -1.453152027 + t * (0.5 * 1.061405429)))
        )
    )
    tail = poly * bell
    cdf = jnp.where(values >= 0.0, 1.0 - tail, tail)
    return cdf, values * bell * 0.3989422804014327


def gelu_exact(values):
    return values * normal_parts(values)[0]


def gelu_slope(values):
    cdf, slope = normal_parts(values)
    return cdf + slope


def gelu_back(values, grad_out):
    return gelu_slope(values) * grad_out


def norm_stats(values):
    centre = jnp.mean(values, axis=-1, keepdims=True)
    centred = values - centre
    spread = jnp.mean(centred * centred, axis=-1, keepdims=True)
    rstd = lax.rsqrt(spread + epsilon)
    return centred * rstd, rstd


def layer_norm(values, gain, shift):
    return norm_stats(values)[0] * gain + shift


def norm_back(values, gain, grad_out):
    unit, rstd = norm_stats(values)
    scaled = grad_out * gain
    mean_one = jnp.mean(scaled, axis=-1, keepdims=True)
    mean_two = jnp.mean(scaled * unit, axis=-1, keepdims=True)
    result = rstd * (scaled - mean_one - unit * mean_two)
    return result, jnp.sum(grad_out * unit, axis=0), jnp.sum(grad_out, axis=0)


def axis_bits(axis):
    return (lax.axis_size(axis) - 1).bit_length()


def add_low(first, second):
    return (first.astype(F32) + second.astype(F32)).astype(BF)


def head_mask(shape, head):
    lane = lax.broadcasted_iota(jnp.int32, shape, 1)
    return lane // HEAD_DIM == head


def spread_heads(block):
    zero = jnp.zeros_like(block)
    return jnp.concatenate(
        [jnp.where(head_mask(block.shape, h), block, zero) for h in range(HEADS_PER_GROUP)],
        axis=0,
    )


WIDE = 48
EDGES = 10
FIELD_EDGE, TALL_EDGE = 4, 5


def refine_kernel(
    field_ref,
    weight_ref,
    bias_ref,
    factor_ref,
    offset_ref,
    cot_ref,
    joined_ref,
    grad_ref,
    dw_ref,
    db_ref,
    sums_ref,
    acts,
    slopes,
    grads3,
    work,
    frame,
    tall,
    lane2,
    edge,
    halo,
    send_sem,
    recv_sem,
    *,
    items,
    rows,
    count,
    depth,
):
    bits = (count - 1).bit_length()
    per_share = 9 * field_ref.shape[-1] // count // depth
    me = lax.axis_index("rows")
    here = lax.axis_index("items")
    channels = field_ref.shape[-1]
    flat = items * rows * WIDE
    lanes = channels // 128
    column = lax.broadcasted_iota(jnp.int32, (WIDE, channels), 0)
    inside = column < PC

    barrier = pltpu.get_barrier_semaphore()
    for step in (-1, 1):

        @pl.when((me + step >= 0) & (me + step < count))
        def _():
            pl.semaphore_signal(
                barrier, inc=1, device_id=(here, me + step), device_id_type=pl.DeviceIdType.MESH
            )

    @pl.when((me > 0) & (me < count - 1))
    def _():
        pl.semaphore_wait(barrier, 2)

    @pl.when((me == 0) | (me == count - 1))
    def _():
        pl.semaphore_wait(barrier, 1)

    def each(side):
        return (me > 0) if side == 0 else (me < count - 1)

    def copy(e, side):
        return pltpu.make_async_remote_copy(
            src_ref=edge.at[e, side],
            dst_ref=halo.at[e, 1 - side],
            send_sem=send_sem.at[e, side],
            recv_sem=recv_sem.at[e, 1 - side],
            device_id=(here, me + (2 * side - 1)),
            device_id_type=pl.DeviceIdType.MESH,
        )

    def send(e):
        for side in (0, 1):

            @pl.when(each(side))
            def _():
                copy(e, side).start()

    def receive(e):
        for side in (0, 1):

            @pl.when(each(side))
            def _():
                pltpu.make_async_remote_copy(
                    src_ref=edge.at[e, side],
                    dst_ref=halo.at[e, side],
                    send_sem=send_sem.at[e, side],
                    recv_sem=recv_sem.at[e, side],
                    device_id=(here, me + (2 * side - 1)),
                    device_id_type=pl.DeviceIdType.MESH,
                ).wait_recv()

            @pl.when(jnp.logical_not(each(side)))
            def _():
                halo[e, side] = jnp.zeros(halo.shape[2:], BF)

    def shifted(values, flip):
        before = pltpu.roll(values, 1, 0)
        after = pltpu.roll(values, WIDE - 1, 0)
        parts = [after, values, before] if flip else [before, values, after]
        return jnp.concatenate([part.astype(BF) for part in parts], axis=1)

    def all_rows(body, e):
        for item in range(items):
            for row, side in ((0, 0), (rows - 1, 1)):
                body(item, row, (e, side))
        send(e)

        def step(row, carry):
            for item in range(items):
                body(item, row, None)
            return carry

        lax.fori_loop(1, rows - 1, step, 0)

    def spread_halo(target, e, flip):
        for side, row in ((0, 0), (1, rows + 1)):
            for item in range(items):
                target[item, row] = shifted(halo[e, side, item].astype(F32), flip)

    for item in range(items):
        factor = factor_ref[pl.ds(item, 1), :]

        def back(row, carry, item=item, factor=factor):
            whole = cot_ref[item, row].astype(F32) * factor
            for part in range(lanes):
                lane2[part, pl.ds(0, 2 * PC), :] = whole[:, part * 128 : (part + 1) * 128]
            even, odd = (
                jnp.concatenate(
                    [lane2[part, pl.ds(start, PC, stride=2), :] for part in range(lanes)], axis=1
                )
                for start in (0, 1)
            )
            place = lax.broadcasted_iota(jnp.int32, (PC, channels), 0)
            even_next = jnp.where(place == PC - 1, odd, pltpu.roll(even, PC - 1, 0))
            odd_prev = jnp.where(place == 0, even, pltpu.roll(odd, 1, 0))
            tall[item, row + 1, pl.ds(0, PC), :] = 0.75 * (even + odd) + 0.25 * (
                even_next + odd_prev
            )
            tall[item, row + 1, pl.ds(PC, WIDE - PC), :] = jnp.zeros((WIDE - PC, channels), F32)
            return carry

        lax.fori_loop(0, 2 * rows, back, 0)
        edge[TALL_EDGE, 0, item] = tall[item, 1].astype(BF)
        edge[TALL_EDGE, 1, item] = tall[item, 2 * rows].astype(BF)
    send(TALL_EDGE)

    def activate(source, which):
        def body(item, row, out):
            values = source[item, row]
            cdf, rest = normal_parts(values)
            act = jnp.where(inside, values * cdf, 0.0)
            slopes[which, item, row] = cdf + rest
            acts[which, item, row + 1] = shifted(act, False)
            if out is not None:
                edge[out[0], out[1], item] = act.astype(BF)

        all_rows(body, which)

    def weight_of(conv, kr):
        return weight_ref[conv, pl.ds(kr * 3 * channels, 3 * channels), :]

    def lhs(source, item, first, number):
        return source[item, pl.ds(first, number)].reshape(number * WIDE, -1)

    def forward(conv, add):
        bias = bias_ref[pl.ds(conv, 1), :]
        for item in range(items):
            centre = mm(lhs(acts.at[conv], item, 1, rows), weight_of(conv, 1)) + bias
            if add:
                centre = centre + frame[item, pl.ds(1, rows)].reshape(rows * WIDE, channels)
            work[item] = centre.reshape(rows, WIDE, channels)
            upper = mm(lhs(acts.at[conv], item, 1, rows - 1), weight_of(conv, 0))
            work[item, pl.ds(1, rows - 1)] += upper.reshape(rows - 1, WIDE, channels)
            lower = mm(lhs(acts.at[conv], item, 2, rows - 1), weight_of(conv, 2))
            work[item, pl.ds(0, rows - 1)] += lower.reshape(rows - 1, WIDE, channels)
        receive(conv)
        spread_halo(acts.at[conv], conv, False)
        for kr, source, row in ((0, 0, 0), (2, rows + 1, rows - 1)):
            block = jnp.concatenate([acts[conv, item, source] for item in range(items)], axis=0)
            extra = mm(block, weight_of(conv, kr))
            for item in range(items):
                work[item, row] += extra[item * WIDE : (item + 1) * WIDE]

    def keep_field(source):
        for item in range(items):
            frame[item, pl.ds(1, rows)] = source[item]

    keep_field(field_ref)
    for unit in (0, 1):
        activate(field_ref if unit == 0 else work, 2 * unit)
        forward(2 * unit, False)
        activate(work, 2 * unit + 1)
        forward(2 * unit + 1, True)
        keep_field(work)

    for item in range(items):
        edge[FIELD_EDGE, 0, item] = frame[item, 1].astype(BF)
        edge[FIELD_EDGE, 1, item] = frame[item, rows].astype(BF)
    send(FIELD_EDGE)

    receive(TALL_EDGE)
    for item in range(items):
        tall[item, 0] = jnp.where(me == 0, tall[item, 1], halo[TALL_EDGE, 0, item].astype(F32))
        tall[item, 2 * rows + 1] = jnp.where(
            me == count - 1, tall[item, 2 * rows], halo[TALL_EDGE, 1, item].astype(F32)
        )

        def fold(row, carry, item=item):
            grad_ref[item, row] = 0.75 * (
                tall[item, 2 * row + 1] + tall[item, 2 * row + 2]
            ) + 0.25 * (tall[item, 2 * row] + tall[item, 2 * row + 3])
            return carry

        lax.fori_loop(0, rows, fold, 0)

    receive(FIELD_EDGE)
    for item in range(items):
        frame[item, 0] = jnp.where(me == 0, frame[item, 1], halo[FIELD_EDGE, 0, item].astype(F32))
        frame[item, rows + 1] = jnp.where(
            me == count - 1, frame[item, rows], halo[FIELD_EDGE, 1, item].astype(F32)
        )
        factor = factor_ref[pl.ds(item, 1), :]
        offset = offset_ref[pl.ds(item, 1), :]

        def widen(row, carry, item=item, factor=factor, offset=offset):
            gain_sum, shift_sum = carry
            centre = frame[item, row + 1]
            for half in (0, 1):
                line = 0.75 * centre + 0.25 * frame[item, row + 2 * half]
                before = jnp.where(column == 0, line, pltpu.roll(line, 1, 0))
                after = jnp.where(column == PC - 1, line, pltpu.roll(line, WIDE - 1, 0))
                for start, side in ((0, before), (1, after)):
                    mixed = 0.75 * line + 0.25 * side
                    for part in range(lanes):
                        lane2[part, pl.ds(start, WIDE, stride=2), :] = mixed[
                            :, part * 128 : (part + 1) * 128
                        ]
                wide = jnp.concatenate(
                    [lane2[part, pl.ds(0, 2 * PC), :] for part in range(lanes)], axis=1
                )
                joined_ref[item, 2 * row + half] = (wide * factor + offset).astype(BF)
                cot = cot_ref[item, 2 * row + half].astype(F32)
                gain_sum = gain_sum + jnp.sum((cot * wide).reshape(-1, 8, channels), axis=0)
                shift_sum = shift_sum + jnp.sum(cot.reshape(-1, 8, channels), axis=0)
            return gain_sum, shift_sum

        zero = jnp.zeros((8, channels), F32)
        gain_sum, shift_sum = lax.fori_loop(0, rows, widen, (zero, zero))
        sums_ref[0, pl.ds(item, 1), :] = jnp.sum(gain_sum, axis=0, keepdims=True)
        sums_ref[1, pl.ds(item, 1), :] = jnp.sum(shift_sum, axis=0, keepdims=True)

    def grad_pass(conv, make):
        e = 6 + conv

        def body(item, row, out):
            values = jnp.where(inside, make(item, row), 0.0).astype(BF).astype(F32)
            grads3[item, row + 1] = shifted(values, True)
            if out is not None:
                edge[out[0], out[1], item] = values.astype(BF)

        all_rows(body, e)
        middle = jnp.concatenate(
            [
                grads3[item, pl.ds(1, rows), :, pl.ds(channels, channels)].reshape(
                    rows * WIDE, channels
                )
                for item in range(items)
            ],
            axis=0,
        )
        for kr in range(3):
            block = jnp.concatenate(
                [lhs(acts.at[conv], item, kr, rows) for item in range(items)], axis=0
            )
            weight = mm(block, middle, TN).astype(BF)
            pieces = 3 * channels // depth
            for k in range(pieces):
                share, place = divmod(kr * pieces + k, per_share)
                at = tuple(share >> b & 1 for b in range(bits - 1, -1, -1))
                dw_ref[(conv,) + at + (slice(None), pl.ds(place * channels, channels))] = weight[
                    k * depth : (k + 1) * depth
                ]
        ones = jnp.ones((8, flat), BF)
        db_ref[pl.ds(conv, 1), :] = mm(ones, middle)[:1]

        def product(block, kr):
            total = None
            for kc in range(3):
                part = mm(
                    block[:, kc * channels : (kc + 1) * channels],
                    weight_ref[conv, pl.ds((kr * 3 + kc) * channels, channels), :],
                    NT,
                )
                total = part if total is None else total + part
            return total

        for item in range(items):
            work[item] = product(lhs(grads3, item, 1, rows), 1).reshape(rows, WIDE, channels)
            work[item, pl.ds(1, rows - 1)] += product(lhs(grads3, item, 1, rows - 1), 2).reshape(
                rows - 1, WIDE, channels
            )
            work[item, pl.ds(0, rows - 1)] += product(lhs(grads3, item, 2, rows - 1), 0).reshape(
                rows - 1, WIDE, channels
            )
        receive(e)
        spread_halo(grads3, e, True)
        for kr, source, row in ((2, 0, 0), (0, rows + 1, rows - 1)):
            block = jnp.concatenate([grads3[item, source] for item in range(items)], axis=0)
            extra = product(block, kr)
            for item in range(items):
                work[item, row] += extra[item * WIDE : (item + 1) * WIDE]

    for unit in (1, 0):
        first, second = 2 * unit, 2 * unit + 1
        grad_pass(second, lambda item, row: grad_ref[item, row])
        grad_pass(first, lambda item, row: work[item, row] * slopes[second, item, row])

        def gather(row, carry, first=first):
            for item in range(items):
                grad_ref[item, row] += work[item, row] * slopes[first, item, row]
            return carry

        lax.fori_loop(0, rows, gather, 0)

    for e in range(EDGES):
        for side in (0, 1):

            @pl.when(each(side))
            def _():
                copy(e, side).wait_send()


def refine(field, conv_weights, conv_biases, factor, offset, cotangent, depth):
    items, rows, _, channels = field.shape
    count = lax.axis_size("rows")
    padded = jnp.pad(field, ((0, 0), (0, 0), (0, WIDE - PC), (0, 0)))
    vmem = pl.BlockSpec(memory_space=pltpu.VMEM)
    pixels = items * rows * PC
    outs = pl.pallas_call(
        functools.partial(refine_kernel, items=items, rows=rows, count=count, depth=depth),
        in_specs=[vmem] * 6,
        out_specs=[vmem] * 5,
        out_shape=[
            jax.ShapeDtypeStruct((items, 2 * rows, 2 * PC, channels), BF),
            jax.ShapeDtypeStruct((items, rows, WIDE, channels), F32),
            jax.ShapeDtypeStruct(
                conv_weights.shape[:1]
                + (2,) * axis_bits("rows")
                + (depth, conv_weights.shape[1] // count // depth * channels),
                BF,
            ),
            jax.ShapeDtypeStruct(conv_biases.shape, F32),
            jax.ShapeDtypeStruct((2, items, channels), F32),
        ],
        scratch_shapes=[
            pltpu.VMEM((4, items, rows + 2, WIDE, 3 * channels), BF),
            pltpu.VMEM((4, items, rows, WIDE, channels), F32),
            pltpu.VMEM((items, rows + 2, WIDE, 3 * channels), BF),
            pltpu.VMEM((items, rows, WIDE, channels), F32),
            pltpu.VMEM((items, rows + 2, WIDE, channels), F32),
            pltpu.VMEM((items, 2 * rows + 2, WIDE, channels), F32),
            pltpu.VMEM((channels // 128, 2 * WIDE, 128), F32),
            pltpu.VMEM((EDGES, 2, items, WIDE, channels), BF),
            pltpu.VMEM((EDGES, 2, items, WIDE, channels), BF),
            pltpu.SemaphoreType.DMA((EDGES, 2)),
            pltpu.SemaphoreType.DMA((EDGES, 2)),
        ],
        compiler_params=pltpu.CompilerParams(
            vmem_limit_bytes=56 << 20, collective_id=0, has_side_effects=True
        ),
        cost_estimate=pl.CostEstimate(
            flops=2 * 12 * pixels * 9 * channels * channels,
            bytes_accessed=20 << 20,
            transcendentals=8 * pixels * channels,
        ),
        name="refine",
    )(padded, conv_weights, conv_biases, factor, offset, cotangent)
    return outs


MESH = pl.DeviceIdType.MESH


def flip(index, bit):
    return index + (1 - 2 * (index // (1 << bit) % 2)) * (1 << bit)


class Reducer:
    def __init__(self, chunks, depth, strip, row_bits, item_bits, space, lag):
        self.chunks, self.depth, self.lanes = chunks, depth, strip // 2
        self.space, self.lag = space, lag
        self.row_bits, self.item_bits = row_bits, item_bits
        self.orders = (tuple(range(row_bits - 1, -1, -1)), tuple(range(row_bits)))
        self.far = max(item_bits - 2, 0)
        self.phases = 1 + row_bits + 1 + self.far + 1 + 1

    def scratch(self):
        c, half = self.chunks, self.depth // 2
        shares = (2,) * self.row_bits
        slots = [
            pltpu.VMEM((c,) + shares + (self.depth, self.lanes), BF),
            pltpu.VMEM((2,) + shares + (self.depth, self.lanes), BF),
        ]
        for stage in range(self.row_bits):
            for _ in (0, 1):
                slots.append(pltpu.VMEM((c,) + (2,) * (self.row_bits - 1 - stage) + (half, self.lanes), BF))
        slots.append(pltpu.VMEM((c, half, self.lanes), BF))
        for _ in range(self.far):
            slots.append(pltpu.VMEM((c, half, self.lanes), BF))
            slots.append(pltpu.VMEM((c, half, self.lanes), BF))
        arrivals = 1 + 2 * self.row_bits + 1 + self.far + 1 + 1
        sends = 1 + 2 * self.row_bits + 1 + self.far + 1 + 1
        return slots + [
            pltpu.VMEM((2, c, self.depth, self.lanes), BF),
            pltpu.SemaphoreType.DMA((2,)),
            pltpu.SemaphoreType.DMA((arrivals, c)),
            pltpu.SemaphoreType.DMA((sends,)),
        ]

    def slots(self):
        return len(self.scratch())

    def out_shape(self):
        return jax.ShapeDtypeStruct((2, self.chunks, self.depth, self.lanes), BF)

    def bind(self, out_ref, slots, sources=None, held=None):
        slots = list(slots)
        self.result, self.sources, self.held = out_ref, sources, held
        self.total, self.ring = slots[0], slots[1]
        self.row_in = [
            (slots[2 + 2 * stage], slots[3 + 2 * stage]) for stage in range(self.row_bits)
        ]
        rest = slots[2 + 2 * self.row_bits :]
        self.near_in = rest[0]
        self.far_out = [rest[1 + 2 * k] for k in range(self.far)]
        self.far_in = [rest[2 + 2 * k] for k in range(self.far)]
        self.out, self.ring_sem, self.recv_sem, self.send_sem = rest[-4:]
        self.me = lax.axis_index("rows")
        self.at = lax.axis_index("items")
        self.core = self.at % 2
        self.near = self.at // 2 % 2

    def peers(self):
        found = [(flip(self.at, bit), self.me) for bit in range(self.item_bits)]
        return found + [(self.at, flip(self.me, bit)) for bit in range(self.row_bits)]

    def greet(self):
        barrier = pltpu.get_barrier_semaphore()
        for peer in self.peers():
            pl.semaphore_signal(barrier, inc=1, device_id=peer, device_id_type=MESH)
        pl.semaphore_wait(barrier, len(self.peers()))

    def remote(self, source, target, arrival, sent, chunk, peer):
        return pltpu.make_async_remote_copy(
            src_ref=source,
            dst_ref=target,
            send_sem=self.send_sem.at[sent],
            recv_sem=self.recv_sem.at[arrival, chunk],
            device_id=peer,
            device_id_type=MESH,
        )

    def strip(self, ref, index, mine):
        side = self.core if mine else 1 - self.core
        lanes = pl.ds(pl.multiple_of(side * self.lanes, self.lanes), self.lanes)
        return ref.at[(index,) + (slice(None),) * (self.row_bits + 1) + (lanes,)]

    def core_copy(self, source, chunk):
        return self.remote(
            source, self.total.at[chunk], 0, 0, chunk, (flip(self.at, 0), self.me)
        )

    def begin(self):
        base = 0
        for ref in self.sources:

            def go(index, carry, ref=ref, base=base):
                self.core_copy(self.strip(ref, index, False), base + index).start()
                return carry

            lax.fori_loop(0, ref.shape[0], go, 0)
            base += ref.shape[0]
        self.fetch(0)

    def begin_held(self, chunk):
        self.core_copy(self.strip(self.held, chunk, False), chunk).start()

    def fetch(self, chunk):
        base = 0
        for ref in self.sources:

            @pl.when((chunk >= base) & (chunk < base + ref.shape[0]))
            def _(ref=ref, base=base):
                index = jnp.clip(chunk - base, 0, ref.shape[0] - 1)
                pltpu.make_async_copy(
                    self.strip(ref, index, True),
                    self.ring.at[chunk % 2],
                    self.ring_sem.at[chunk % 2],
                ).start()

            base += ref.shape[0]

    def add_mine(self, chunk):
        if self.held is not None:
            block = self.held[chunk]
            side = (slice(None),) * (self.row_bits + 1)
            block = jnp.where(
                self.core == 0,
                block[side + (slice(0, self.lanes),)],
                block[side + (slice(self.lanes, None),)],
            )
        else:
            slot = chunk % 2
            pltpu.make_async_copy(
                self.total.at[chunk], self.ring.at[slot], self.ring_sem.at[slot]
            ).wait()
            block = self.ring[slot]
        self.total[chunk] = add_low(self.total[chunk], block)

    def bit(self, which):
        return self.me // (1 << which) % 2

    def shares(self, half, stage, sent):
        order = self.orders[half]
        index = [slice(None)] * self.row_bits
        for done in order[:stage]:
            index[self.row_bits - 1 - done] = self.bit(done)
        now = order[stage]
        index[self.row_bits - 1 - now] = 1 - self.bit(now) if sent else self.bit(now)
        return tuple(index)

    def rows(self, half):
        depth = self.depth // 2
        return pl.ds(half * depth, depth)

    def row_copy(self, stage, half, chunk):
        source = self.total.at[(chunk,) + self.shares(half, stage, True) + (self.rows(half),)]
        return self.remote(
            source,
            self.row_in[stage][half].at[chunk],
            1 + 2 * stage + half,
            1 + 2 * stage + half,
            chunk,
            (self.at, flip(self.me, self.orders[half][stage])),
        )

    def own(self, chunk, rows):
        return (chunk,) + tuple(self.bit(b) for b in range(self.row_bits - 1, -1, -1)) + (rows,)

    def near_rows(self, mine):
        half = self.depth // 2
        place = self.near if mine else 1 - self.near
        return pl.ds(pl.multiple_of(place * half, half), half)

    def near_copy(self, chunk):
        return self.remote(
            self.total.at[self.own(chunk, self.near_rows(False))],
            self.near_in.at[chunk],
            1 + 2 * self.row_bits,
            1 + 2 * self.row_bits,
            chunk,
            (flip(self.at, 1), self.me),
        )

    def far_copy(self, k, chunk):
        return self.remote(
            self.far_out[k].at[chunk],
            self.far_in[k].at[chunk],
            2 + 2 * self.row_bits + k,
            2 + 2 * self.row_bits + k,
            chunk,
            (flip(self.at, 2 + k), self.me),
        )

    def back_copy(self, chunk):
        place = self.out.at[self.core, chunk, self.near_rows(True)]
        return self.remote(
            place,
            place,
            2 + 2 * self.row_bits + self.far,
            2 + 2 * self.row_bits + self.far,
            chunk,
            (flip(self.at, 1), self.me),
        )

    def last_copy(self, chunk):
        place = self.out.at[self.core, chunk]
        return self.remote(
            place,
            place,
            3 + 2 * self.row_bits + self.far,
            3 + 2 * self.row_bits + self.far,
            chunk,
            (flip(self.at, 0), self.me),
        )

    def phase(self, number, chunk):
        bits, half = self.row_bits, self.depth // 2
        if number == 0:
            self.core_copy(self.total.at[chunk], chunk).wait_recv()
            self.add_mine(chunk)
            if self.sources is not None:

                @pl.when(chunk + 1 < self.chunks)
                def _():
                    self.fetch(chunk + 1)

            for side in (0, 1):
                self.row_copy(0, side, chunk).start()
        elif number <= bits:
            stage = number - 1
            for side in (0, 1):
                self.row_copy(stage, side, chunk).wait_recv()
                at = (chunk,) + self.shares(side, stage, False) + (self.rows(side),)
                self.total[at] = add_low(self.total[at], self.row_in[stage][side][chunk])
                if stage + 1 < bits:
                    self.row_copy(stage + 1, side, chunk).start()
            if stage + 1 == bits:
                self.near_copy(chunk).start()
        elif number == bits + 1:
            self.near_copy(chunk).wait_recv()
            total = add_low(
                self.total[self.own(chunk, self.near_rows(True))], self.near_in[chunk]
            )
            self.pass_on(0, chunk, total)
        elif number <= bits + 1 + self.far:
            k = number - bits - 2
            self.far_copy(k, chunk).wait_recv()
            self.pass_on(k + 1, chunk, add_low(self.far_out[k][chunk], self.far_in[k][chunk]))
        elif number == bits + 2 + self.far:
            self.back_copy_arrived(chunk)
            self.last_copy(chunk).start()
        else:
            self.last_arrived(chunk)

    def pass_on(self, k, chunk, total):
        if k < self.far:
            self.far_out[k][chunk] = total
            self.far_copy(k, chunk).start()
        else:
            self.out[self.core, chunk, self.near_rows(True)] = total
            self.back_copy(chunk).start()

    def back_copy_arrived(self, chunk):
        place = self.out.at[self.core, chunk, self.near_rows(False)]
        self.remote(
            place,
            place,
            2 + 2 * self.row_bits + self.far,
            2 + 2 * self.row_bits + self.far,
            chunk,
            (flip(self.at, 1), self.me),
        ).wait_recv()

    def last_arrived(self, chunk):
        place = self.out.at[1 - self.core, chunk]
        self.remote(
            place,
            place,
            3 + 2 * self.row_bits + self.far,
            3 + 2 * self.row_bits + self.far,
            chunk,
            (flip(self.at, 0), self.me),
        ).wait_recv()

    def step(self, t):
        for number in range(self.phases - 1, -1, -1):
            place = t - self.lag * number
            chunk = place // self.space

            @pl.when((place >= 0) & (place % self.space == 0) & (chunk < self.chunks))
            def _(number=number, chunk=chunk):
                self.phase(number, jnp.clip(chunk, 0, self.chunks - 1))

    @property
    def steps(self):
        return (self.chunks - 1) * self.space + self.lag * (self.phases - 1) + 1

    def finish(self):
        def drain(sem, ref):
            pltpu.make_async_copy(ref, ref, self.send_sem.at[sem]).wait()

        drain(0, self.total)
        for stage in range(self.row_bits):
            for side in (0, 1):
                drain(1 + 2 * stage + side, self.row_in[stage][side])
        base = 1 + 2 * self.row_bits
        drain(base, self.near_in)
        for k in range(self.far):
            drain(base + 1 + k, self.far_in[k])
        drain(base + 1 + self.far, self.near_in)
        drain(base + 2 + self.far, self.out.at[0])
        copy = pltpu.make_async_copy(self.out, self.result, self.ring_sem.at[0])
        copy.start()
        copy.wait()


def unpack_kernel(held_ref, *refs, table, outs):
    targets, (wide, sem) = refs[:outs], refs[outs:]
    depth = wide.shape[1]

    def copy(place, chunk, first, size, number, outer, row, column):
        target = targets[number] if outer is None else targets[number].at[outer]
        return pltpu.make_async_copy(
            wide.at[chunk, :, pl.ds(first, size)],
            target.at[pl.ds(row, depth), pl.ds(column, size)],
            sem.at[place],
        )

    done = set()
    for place, entry in enumerate(table):
        chunk = entry[0]
        if chunk not in done:
            done.add(chunk)
            wide[chunk] = jnp.concatenate(
                [held_ref[0, chunk].astype(F32), held_ref[1, chunk].astype(F32)], axis=1
            )
        copy(place, *entry).start()
    for place, entry in enumerate(table):
        copy(place, *entry).wait()


def unpack(out, table, shapes):
    chunks, depth, lanes = out.shape[1:]
    return pl.pallas_call(
        functools.partial(unpack_kernel, table=table, outs=len(shapes)),
        in_specs=[pl.BlockSpec(memory_space=pltpu.VMEM)],
        out_specs=[pl.BlockSpec(memory_space=pl.ANY)] * len(shapes),
        out_shape=[jax.ShapeDtypeStruct(shape, F32) for shape in shapes],
        scratch_shapes=[
            pltpu.VMEM((chunks, depth, 2 * lanes), F32),
            pltpu.SemaphoreType.DMA((len(table),)),
        ],
        compiler_params=pltpu.CompilerParams(vmem_limit_bytes=40 << 20),
        name="unpack",
    )(out)


def all_sum_kernel(value_ref, out_ref, piece, landed, over, send_sem, recv_sem, *, count, others):
    at, me = lax.axis_index("items"), lax.axis_index("rows")
    barrier = pltpu.get_barrier_semaphore()
    row_peers = [(at, (me + k) % count) for k in range(1, count)]
    item_peers = [((at + k) % others, me) for k in range(1, others)]
    for peer in row_peers + item_peers:
        pl.semaphore_signal(barrier, inc=1, device_id=peer, device_id_type=MESH)
    pl.semaphore_wait(barrier, count + others - 2)

    def row_copy(k):
        return pltpu.make_async_remote_copy(
            src_ref=value_ref.at[row_peers[k][1]],
            dst_ref=landed.at[k],
            send_sem=send_sem.at[k],
            recv_sem=recv_sem.at[k],
            device_id=row_peers[k],
            device_id_type=MESH,
        )

    def item_copy(k):
        return pltpu.make_async_remote_copy(
            src_ref=piece,
            dst_ref=over.at[k],
            send_sem=send_sem.at[count - 1 + k],
            recv_sem=recv_sem.at[count - 1 + k],
            device_id=item_peers[k],
            device_id_type=MESH,
        )

    for k in range(count - 1):
        row_copy(k).start()
    total = value_ref[me]
    for k in range(count - 1):
        row_copy(k).wait_recv()
        total = total + landed[k]
    piece[...] = total
    for k in range(others - 1):
        item_copy(k).start()
    for k in range(others - 1):
        item_copy(k).wait_recv()
        total = total + over[k]
    out_ref[...] = total
    for k in range(count - 1):
        row_copy(k).wait_send()
    for k in range(others - 1):
        item_copy(k).wait_send()


def all_sum(value, collective_id):
    count, others = lax.axis_size("rows"), lax.axis_size("items")
    vmem = pl.BlockSpec(memory_space=pltpu.VMEM)
    block = value.shape[1:]
    return pl.pallas_call(
        functools.partial(all_sum_kernel, count=count, others=others),
        in_specs=[vmem],
        out_specs=vmem,
        out_shape=jax.ShapeDtypeStruct(block, F32),
        scratch_shapes=[
            pltpu.VMEM(block, F32),
            pltpu.VMEM((count - 1,) + block, F32),
            pltpu.VMEM((others - 1,) + block, F32),
            pltpu.SemaphoreType.DMA((count + others - 2,)),
            pltpu.SemaphoreType.DMA((count + others - 2,)),
        ],
        compiler_params=pltpu.CompilerParams(collective_id=collective_id, has_side_effects=True),
        name="sum_small",
    )(value)


class Gather:
    def __init__(self, bits, items):
        self.bits, self.items = bits, items
        self.orders = (tuple(range(bits)), tuple(range(bits - 1, -1, -1)))

    def bind(self, held, send_sem, recv_sem):
        self.held, self.send_sem, self.recv_sem = held, send_sem, recv_sem

    def place(self, item, half, stage, now):
        order = self.orders[half]
        index = [0] * self.bits
        for done in order[:stage]:
            index[self.bits - 1 - done] = slice(None)
        index[self.bits - 1 - order[stage]] = now
        size = self.held.shape[-2] // 2
        return (item,) + tuple(index) + (pl.ds(half * size, size),)

    def copy(self, item, stage, half):
        me, at = lax.axis_index("rows"), lax.axis_index("items")
        return pltpu.make_async_remote_copy(
            src_ref=self.held.at[self.place(item, half, stage, 0)],
            dst_ref=self.held.at[self.place(item, half, stage, 1)],
            send_sem=self.send_sem.at[item, stage, half],
            recv_sem=self.recv_sem.at[item, stage, half],
            device_id=(at, flip(me, self.orders[half][stage])),
            device_id_type=MESH,
        )

    def start(self, item, stage):
        for half in (0, 1):
            self.copy(item, stage, half).start()

    def arrived(self, item, stage):
        for half in (0, 1):
            self.copy(item, stage, half).wait_recv()

    def drain(self, item):
        for stage in range(self.bits):
            for half in (0, 1):
                self.copy(item, stage, half).wait_send()


def attention_forward_kernel(
    valid_ref,
    tokens_ref,
    gain_ref,
    shift_ref,
    q_bias_ref,
    v_bias_ref,
    wq_ref,
    wk_ref,
    wv_ref,
    q_ref,
    k_ref,
    v_ref,
    o_ref,
    lse_ref,
    normed_ref,
    held,
    send_sem,
    recv_sem,
    copy_sem,
    *,
    gather,
    groups,
    items,
):
    gather.bind(held, send_sem, recv_sem)
    step = pl.program_id(0)
    item, group = step // groups, step % groups
    t, width = held.shape[-2:]
    n = k_ref.shape[1]
    me, at = lax.axis_index("rows"), lax.axis_index("items")
    bits = gather.bits
    mine = (0,) * bits

    def store(which):
        held[(which,) + mine] = layer_norm(
            tokens_ref[which].astype(F32), gain_ref[...], shift_ref[...]
        ).astype(BF)

    def keep(which):
        return pltpu.make_async_copy(held.at[which], normed_ref.at[which], copy_sem.at[which])

    @pl.when(step == 0)
    def _():
        store(0)
        barrier = pltpu.get_barrier_semaphore()
        for bit in range(bits):
            pl.semaphore_signal(
                barrier, inc=1, device_id=(at, flip(me, bit)), device_id_type=MESH
            )
        pl.semaphore_wait(barrier, bits)
        gather.start(0, 0)
        for which in range(1, items):
            store(which)
        for stage in range(1, bits):
            gather.arrived(0, stage - 1)
            gather.start(0, stage)
        gather.start(1, 0)

    @pl.when(group == 0)
    def _():
        gather.arrived(item, bits - 1)
        keep(item).start()

    limit = valid_ref[item] * PC
    index = lax.broadcasted_iota(jnp.int32, (1, n), 1)
    bias = jnp.where(index + key_shift(index, n, t, me) < limit, 0.0, MASKED).astype(F32)
    every = held[item].reshape(n, width)
    keys = mm(every, wk_ref[...]).astype(BF)
    values = (mm(every, wv_ref[...]) + v_bias_ref[...]).astype(BF)
    queries = (mm(held[(item,) + mine], wq_ref[...]) + q_bias_ref[...]).astype(BF)
    k_ref[0] = keys
    v_ref[0] = values
    q_ref[0] = queries
    queries = queries * jnp.asarray(HEAD_DIM**-0.5, BF)
    out = jnp.zeros((t, GROUP), F32)
    for h in range(HEADS_PER_GROUP):
        mask = head_mask((t, GROUP), h)
        one = jnp.where(mask, queries, jnp.zeros_like(queries))
        scores = mm(one, keys, NT) + bias
        top = jnp.max(scores, axis=1, keepdims=True)
        probs = jnp.exp2((scores - top) * LOG2E)
        total = jnp.sum(probs, axis=1, keepdims=True)
        weighted = mm(probs.astype(BF), values)
        out = jnp.where(mask, weighted * (1.0 / total), out)
        lse = top * LOG2E + jnp.log2(total)
        lse_ref[0, 0, :, pl.ds(h * t, t)] = jnp.transpose(jnp.broadcast_to(lse, (t, 128)))[:8]
    o_ref[0] = out.astype(BF)

    for stage in range(1, bits):

        @pl.when((group == stage - 1) & (item + 1 < items))
        def _(stage=stage):
            gather.arrived(item + 1, stage - 1)
            gather.start(item + 1, stage)

    @pl.when((group == bits - 2) & (item + 2 < items))
    def _():
        gather.start(item + 2, 0)

    @pl.when(step == items * groups - 1)
    def _():
        for which in range(items):
            gather.drain(which)
            keep(which).wait()


def attention_forward(valid_rows, tokens, gain, shift, qkv_weight, q_bias, v_bias, collective_id):
    items, t, d = tokens.shape
    bits = axis_bits("rows")
    n = t << bits
    groups = d // GROUP
    rows4 = HEADS_PER_GROUP * t
    vmem = pl.BlockSpec(memory_space=pltpu.VMEM)

    def weight_spec(kind):
        return pl.BlockSpec((d, GROUP), lambda i: (0, kind * groups + i % groups))

    bias_spec = pl.BlockSpec((1, GROUP), lambda i: (0, i % groups))
    query_spec = pl.BlockSpec((1, t, GROUP), lambda i: (i // groups, 0, i % groups))
    key_spec = pl.BlockSpec((1, n, GROUP), lambda i: (i // groups, 0, i % groups))
    return pl.pallas_call(
        functools.partial(
            attention_forward_kernel, gather=Gather(bits, items), groups=groups, items=items
        ),
        grid=(items * groups,),
        in_specs=[
            pl.BlockSpec(memory_space=pltpu.SMEM),
            vmem,
            vmem,
            vmem,
            bias_spec,
            bias_spec,
            weight_spec(0),
            weight_spec(1),
            weight_spec(2),
        ],
        out_specs=[
            query_spec,
            key_spec,
            key_spec,
            query_spec,
            pl.BlockSpec((1, 1, 8, rows4), lambda i: (i // groups, i % groups, 0, 0)),
            pl.BlockSpec(memory_space=pl.ANY),
        ],
        out_shape=[
            jax.ShapeDtypeStruct((items, t, d), BF),
            jax.ShapeDtypeStruct((items, n, d), BF),
            jax.ShapeDtypeStruct((items, n, d), BF),
            jax.ShapeDtypeStruct((items, t, d), BF),
            jax.ShapeDtypeStruct((items, groups, 8, rows4), F32),
            jax.ShapeDtypeStruct((items,) + (2,) * bits + (t, d), BF),
        ],
        scratch_shapes=[
            pltpu.VMEM((items,) + (2,) * bits + (t, d), BF),
            pltpu.SemaphoreType.DMA((items, bits, 2)),
            pltpu.SemaphoreType.DMA((items, bits, 2)),
            pltpu.SemaphoreType.DMA((items,)),
        ],
        compiler_params=pltpu.CompilerParams(
            vmem_limit_bytes=52 << 20, collective_id=collective_id, has_side_effects=True
        ),
        cost_estimate=pl.CostEstimate(
            flops=60 * items * t * n * d,
            bytes_accessed=40 << 20,
            transcendentals=12 * items * t * n,
        ),
        name="attention_forward",
    )(
        valid_rows,
        tokens,
        gain,
        shift,
        q_bias,
        v_bias,
        qkv_weight,
        qkv_weight,
        qkv_weight,
    )


def key_shift(index, length, block, me):
    start = jnp.full_like(index, me * block)
    for j in range(1, length // block):
        other = me
        for bit in range(j.bit_length()):
            if j >> bit & 1:
                other = flip(other, bit)
        start = jnp.where(index >= j * block, (other - j) * block, start)
    return start


def shares_of(bits):
    return (2,) * bits


def mlp_backward_kernel(
    tap_grad_ref,
    cot_ref,
    out_tokens_ref,
    normed_ref,
    resid_ref,
    attended_ref,
    gain_ref,
    tap_w_ref,
    out_w_ref,
    hidden_ref,
    slope_ref,
    fc1_ref,
    fc2_ref,
    tap_dw_ref,
    out_dw_ref,
    fc1_dw_ref,
    fc2_dw_ref,
    resid_grad_ref,
    attended_grad_ref,
    wide_sums_ref,
    fc1_sums_ref,
    out_grad,
    low_grad,
    pre_grad,
    back,
    *,
    blocks,
    row_block,
    bits,
):
    step = pl.program_id(0)
    tokens, width = low_grad.shape
    count = 1 << bits
    depth = width // count
    shares = shares_of(bits)
    pieces = [pl.ds(k * row_block, row_block) for k in range(tokens // row_block)]

    @pl.when(step == 0)
    def _():
        total = jnp.zeros((1, width), F32)
        tap_total = jnp.zeros((1, tap_grad_ref.shape[1]), F32)
        for piece in pieces:
            tap_part = tap_grad_ref[piece, :]
            value = cot_ref[piece, :].astype(F32) + mm(tap_part, tap_w_ref[...], NT)
            out_grad[piece, :] = value
            low = value.astype(BF)
            low_grad[piece, :] = low
            back[piece, :] = jnp.zeros((row_block, width), F32)
            total = total + jnp.sum(low.astype(F32), axis=0, keepdims=True)
            tap_total = tap_total + jnp.sum(tap_part.astype(F32), axis=0, keepdims=True)
        wide_sums_ref[pl.ds(0, 1), :] = total
        wide_sums_ref[pl.ds(4, 1), :] = jnp.concatenate(
            [tap_total] * (width // tap_total.shape[1]), axis=1
        )
        weight = mm(out_tokens_ref[...], tap_grad_ref[...], TN).astype(BF)
        weight = jnp.concatenate(
            [weight, jnp.zeros((width, width - weight.shape[1]), BF)], axis=1
        )
        tap_dw_ref[0] = weight.reshape(shares + (depth, width))

    def rows_of(number):
        return pl.ds(pl.multiple_of(number * row_block, row_block), row_block)

    def inward(number, sums):
        piece = rows_of(number)
        grads = mm(low_grad[piece, :], fc2_ref[...], NT) * slope_ref[piece, :].astype(F32)
        low = grads.astype(BF)
        pre_grad[piece, :] = low
        return sums + jnp.sum(low.astype(F32), axis=0, keepdims=True)

    fc1_sums_ref[...] = lax.fori_loop(
        0, len(pieces), inward, jnp.zeros((1, pre_grad.shape[1]), F32)
    )
    weight = mm(hidden_ref[...], low_grad[...], TN).astype(BF)
    per_share = weight.shape[0] // depth * blocks // count
    for place in range(weight.shape[0] // depth):
        fc2_dw_ref[place % per_share, place // per_share] = weight[
            place * depth : (place + 1) * depth
        ]
    weight = mm(normed_ref[...], pre_grad[...], TN).astype(BF)
    fc1_dw_ref[0] = weight.reshape(shares + (depth, width))

    def outward(number, carry):
        piece = rows_of(number)
        back[piece, :] += mm(pre_grad[piece, :], fc1_ref[...], NT)
        return carry

    lax.fori_loop(0, len(pieces), outward, 0)

    @pl.when(step == blocks - 1)
    def _():
        gain = gain_ref[...]
        gain_total = jnp.zeros((1, width), F32)
        shift_total = jnp.zeros((1, width), F32)
        total = jnp.zeros((1, width), F32)
        for piece in pieces:
            grads = back[piece, :]
            unit, rstd = norm_stats(resid_ref[piece, :])
            scaled = grads * gain
            mean_one = jnp.mean(scaled, axis=-1, keepdims=True)
            mean_two = jnp.mean(scaled * unit, axis=-1, keepdims=True)
            value = out_grad[piece, :] + rstd * (scaled - mean_one - unit * mean_two)
            resid_grad_ref[piece, :] = value
            low = value.astype(BF)
            low_grad[piece, :] = low
            gain_total = gain_total + jnp.sum(grads * unit, axis=0, keepdims=True)
            shift_total = shift_total + jnp.sum(grads, axis=0, keepdims=True)
            total = total + jnp.sum(low.astype(F32), axis=0, keepdims=True)
            attended_grad_ref[piece, :] = mm(low, out_w_ref[...], NT).astype(BF)
        wide_sums_ref[pl.ds(1, 1), :] = gain_total
        wide_sums_ref[pl.ds(2, 1), :] = shift_total
        wide_sums_ref[pl.ds(3, 1), :] = total
        weight = mm(attended_ref[...], low_grad[...], TN).astype(BF)
        out_dw_ref[0] = weight.reshape(shares + (depth, width))


def mlp_backward(
    grad_tap,
    cotangent,
    out_tokens,
    normed,
    resid,
    attended,
    gain,
    tap_weight,
    out_weight,
    hidden,
    slope,
    fc1_weight,
    fc2_weight,
    row_block,
):
    tokens, width = resid.shape
    inner = hidden.shape[1]
    bits = axis_bits("rows")
    count = 1 << bits
    depth = width // count
    blocks = inner // width
    vmem = pl.BlockSpec(memory_space=pltpu.VMEM)
    column = pl.BlockSpec((tokens, width), lambda i: (0, i))
    fc2_chunks = inner // count // depth
    shares = shares_of(bits)
    share_step = count // blocks
    outs = pl.pallas_call(
        functools.partial(
            mlp_backward_kernel,
            blocks=blocks,
            row_block=row_block,
            bits=bits,
        ),
        grid=(blocks,),
        in_specs=[vmem] * 9
        + [
            column,
            column,
            pl.BlockSpec((width, width), lambda i: (0, i)),
            pl.BlockSpec((width, width), lambda i: (i, 0)),
        ],
        out_specs=[
            vmem,
            vmem,
            pl.BlockSpec((1,) + shares + (depth, width), lambda i: (i,) + (0,) * (bits + 2)),
            pl.BlockSpec((fc2_chunks, share_step, depth, width), lambda i: (0, i, 0, 0)),
            vmem,
            vmem,
            vmem,
            pl.BlockSpec((1, width), lambda i: (0, i)),
        ],
        out_shape=[
            jax.ShapeDtypeStruct((1,) + shares + (depth, width), BF),
            jax.ShapeDtypeStruct((1,) + shares + (depth, width), BF),
            jax.ShapeDtypeStruct((blocks,) + shares + (depth, width), BF),
            jax.ShapeDtypeStruct((fc2_chunks, count, depth, width), BF),
            jax.ShapeDtypeStruct((tokens, width), F32),
            jax.ShapeDtypeStruct((tokens, width), BF),
            jax.ShapeDtypeStruct((8, width), F32),
            jax.ShapeDtypeStruct((1, inner), F32),
        ],
        scratch_shapes=[
            pltpu.VMEM((tokens, width), F32),
            pltpu.VMEM((tokens, width), BF),
            pltpu.VMEM((tokens, width), BF),
            pltpu.VMEM((tokens, width), F32),
        ],
        compiler_params=pltpu.CompilerParams(vmem_limit_bytes=60 << 20),
        cost_estimate=pl.CostEstimate(
            flops=8 * tokens * width * inner, bytes_accessed=40 << 20, transcendentals=0
        ),
        name="mlp_backward",
    )(
        grad_tap,
        cotangent,
        out_tokens,
        normed,
        resid,
        attended,
        gain,
        tap_weight,
        out_weight,
        hidden,
        slope,
        fc1_weight,
        fc2_weight,
    )
    return outs


class Scatter:
    def __init__(self, bits, tokens, width, items):
        self.bits, self.tokens, self.width, self.items = bits, tokens, width, items
        self.orders = (tuple(range(bits - 1, -1, -1)), tuple(range(bits)))

    def scratch(self):
        slots = [pltpu.VMEM((2,) * self.bits + (self.tokens, self.width), BF)]
        for stage in range(self.bits):
            for _ in (0, 1):
                slots.append(
                    pltpu.VMEM(
                        (self.items,)
                        + (2,) * (self.bits - 1 - stage)
                        + (self.tokens // 2, self.width),
                        BF,
                    )
                )
        return slots + [
            pltpu.SemaphoreType.DMA((self.bits, 2)),
            pltpu.SemaphoreType.DMA((self.items, self.bits, 2)),
        ]

    def bind(self, slots):
        self.held = slots[0]
        self.landed = [(slots[1 + 2 * s], slots[2 + 2 * s]) for s in range(self.bits)]
        self.send_sem, self.recv_sem = slots[-2:]

    def place(self, half, stage, bit_value):
        index = [slice(None)] * self.bits
        for done in self.orders[half][:stage]:
            index[self.bits - 1 - done] = 0
        index[self.bits - 1 - self.orders[half][stage]] = bit_value
        size = self.tokens // 2
        return tuple(index) + (pl.ds(half * size, size),)

    def copy(self, item, stage, half):
        me, at = lax.axis_index("rows"), lax.axis_index("items")
        return pltpu.make_async_remote_copy(
            src_ref=self.held.at[self.place(half, stage, 1)],
            dst_ref=self.landed[stage][half].at[item],
            send_sem=self.send_sem.at[stage, half],
            recv_sem=self.recv_sem.at[item, stage, half],
            device_id=(at, flip(me, self.orders[half][stage])),
            device_id_type=MESH,
        )

    def start(self, item):
        for half in (0, 1):
            self.copy(item, 0, half).start()

    def advance(self, item, stage, finish):
        for half in (0, 1):
            self.copy(item, stage, half).wait_recv()
            at = self.place(half, stage, 0)
            if stage + 1 < self.bits:
                self.held[at] = add_low(self.held[at], self.landed[stage][half][item])
                self.copy(item, stage + 1, half).start()
            else:
                finish(
                    at[-1],
                    self.held[at].astype(F32) + self.landed[stage][half][item].astype(F32),
                )

    def drain(self, item):
        for stage in range(self.bits):
            for half in (0, 1):
                self.copy(item, stage, half).wait_send()


def attention_backward_kernel(
    valid_ref,
    q_ref,
    k_ref,
    v_ref,
    g_ref,
    o_ref,
    lse_ref,
    normed_ref,
    wq_ref,
    wk_ref,
    wv_ref,
    *refs,
    reducer,
    late,
    scatter,
    groups,
    items,
    kb,
    rounds,
    sources,
):
    early_sources = refs[:sources]
    grad_ref, sums_ref, early_out, late_out = refs[sources : sources + 4]
    slots = list(refs[sources + 4 :])
    q4, g4, acc, dkv, back, held = slots[:6]
    del slots[:6]
    early_slots = slots[: reducer.slots()]
    del slots[: reducer.slots()]
    late_slots = slots[: late.slots()]
    del slots[: late.slots()]
    reducer.bind(early_out, early_slots, sources=early_sources)
    late.bind(late_out, late_slots, held=held)
    scatter.bind(slots)
    step = pl.program_id(0)
    item, group = step // groups, step % groups
    t, n = q_ref.shape[1], k_ref.shape[1]
    width = back.shape[1]
    depth = width // (1 << reducer.row_bits)
    shares = shares_of(reducer.row_bits)
    me = lax.axis_index("rows")

    @pl.when(step == 0)
    def _():
        reducer.greet()
        reducer.begin()
        sums_ref[...] = jnp.zeros_like(sums_ref)

    q4[...] = spread_heads(q_ref[0] * jnp.asarray(HEAD_DIM**-0.5, BF))
    grads = spread_heads(g_ref[0])
    g4[...] = grads
    outs = jnp.concatenate([o_ref[0].astype(F32)] * HEADS_PER_GROUP, axis=0)
    product = grads.astype(F32) * outs
    high = product.astype(BF)
    low = (product - high.astype(F32)).astype(BF)
    ones = jnp.ones((8, GROUP), BF)
    dots = (mm(ones, high, NT) + mm(ones, low, NT))[:1]
    lse = lse_ref[0, 0, :1, :]
    acc[...] = jnp.zeros_like(acc)
    limit = valid_ref[item] * PC

    def turn(number):
        now = step * rounds + number
        reducer.step(now)
        late.step(now - ((items - 1) * groups + 1) * rounds)

    inner = n // kb
    each = rounds // inner

    def block_step(b, carry):
        at = pl.ds(pl.multiple_of(b * kb, kb), kb)
        keys, values = k_ref[0, at, :], v_ref[0, at, :]
        index = b * kb + lax.broadcasted_iota(jnp.int32, (kb, 1), 0)
        position = index + key_shift(index, n, t, me)
        bias = jnp.where(position < limit, 0.0, MASKED).astype(F32)
        scores = mm(keys, q4[...], NT)
        probs = jnp.exp2((scores * LOG2E + bias) - lse)
        grad_probs = mm(values, g4[...], NT)
        grad_scores = (probs * (grad_probs - dots)).astype(BF)
        dkv[at, pl.ds(GROUP, GROUP)] = mm(probs.astype(BF), g4[...]).astype(BF)
        dkv[at, pl.ds(0, GROUP)] = mm(grad_scores, q4[...]).astype(BF)
        acc[...] += mm(grad_scores, keys, TN)

        def rest(k, inner_carry):
            turn(b * each + k)
            return inner_carry

        lax.fori_loop(0, each, rest, 0)
        return carry

    lax.fori_loop(0, inner, block_step, 0)
    out = jnp.zeros((t, GROUP), F32)
    for h in range(HEADS_PER_GROUP):
        out = jnp.where(head_mask((t, GROUP), h), acc[pl.ds(h * t, t), :], out)
    dq = (out * HEAD_DIM**-0.5).astype(BF)

    for stage in range(scatter.bits):

        @pl.when((group == stage) & (item > 0))
        def _(stage=stage):
            def finish(rows, value):
                grad_ref[item - 1, rows, :] += value

            scatter.advance(item - 1, stage, finish)

    part = jnp.concatenate(
        [mm(normed_ref[0, pl.ds(0, t), :], dq, TN), mm(normed_ref[0], dkv[...], TN)], axis=1
    ).reshape(shares + (depth, width))
    before = held[group].astype(F32)
    held[group] = jnp.where(item == 0, part, before + part).astype(BF)
    sums_ref[group, pl.ds(0, 1), :] += jnp.sum(dq.astype(F32), axis=0, keepdims=True)
    sums_ref[group, pl.ds(1, 1), :] += jnp.sum(
        dkv[:, pl.ds(GROUP, GROUP)].astype(F32), axis=0, keepdims=True
    )

    @pl.when(item == items - 1)
    def _():
        late.begin_held(group)

    row_piece = n // 4
    both = jnp.concatenate([wk_ref[...], wv_ref[...]], axis=1)

    def project(k, carry):
        at = pl.ds(pl.multiple_of(k * row_piece, row_piece), row_piece)
        value = mm(dkv[at, :], both, NT)
        back[at, :] = jnp.where(group == 0, value, back[at, :] + value)
        return carry

    lax.fori_loop(0, 2, project, 0)

    @pl.when(step == items * groups - 1)
    def _():
        late.step((groups - 1) * rounds)

    lax.fori_loop(2, 4, project, 0)
    value = mm(dq, wq_ref[...], NT)
    grad_ref[item] = jnp.where(group == 0, value, grad_ref[item] + value)

    @pl.when(group == groups - 1)
    def _():
        @pl.when(item > 0)
        def _():
            scatter.drain(item - 1)

        for j in range(1 << scatter.bits):
            index = tuple(j >> b & 1 for b in range(scatter.bits - 1, -1, -1))
            scatter.held[index] = back[pl.ds(j * t, t), :].astype(BF)
        scatter.start(item)

    @pl.when(step == items * groups - 1)
    def _():
        start = ((items - 1) * groups + 1) * rounds

        last = items * groups * rounds

        def rest(now, carry):
            reducer.step(now)
            return carry

        def late_turn(k, carry):
            late.step(last - start + k * late.lag)
            return carry

        lax.fori_loop(last, max(last, reducer.steps), rest, 0)
        mark = 1

        for stage in range(scatter.bits):

            def finish(rows, value):
                grad_ref[items - 1, rows, :] += value

            lax.fori_loop(mark, 2 + 2 * stage, late_turn, 0)
            mark = 2 + 2 * stage
            scatter.advance(items - 1, stage, finish)
        lax.fori_loop(mark, late.phases, late_turn, 0)
        scatter.drain(items - 1)
        reducer.finish()
        late.finish()


def attention_backward(
    valid_rows, queries, keys, values, grads, outs, lse, normed, qkv_weight, packed, collective_id
):
    items, t, d = queries.shape
    n = keys.shape[1]
    groups = d // GROUP
    bits = axis_bits("rows")
    depth = d >> bits
    rows4 = HEADS_PER_GROUP * t
    rounds = 8
    reducer = Reducer(
        sum(a.shape[0] for a in packed), depth, d, bits, axis_bits("items"), 3, 7
    )
    late = Reducer(groups, depth, d, bits, axis_bits("items"), rounds, 8)
    scatter = Scatter(bits, t, d, items)
    query_spec = pl.BlockSpec((1, t, GROUP), lambda i: (i // groups, 0, i % groups))
    vmem = pl.BlockSpec(memory_space=pltpu.VMEM)

    def weight_spec(kind):
        return pl.BlockSpec((d, GROUP), lambda i: (0, kind * groups + i % groups))

    key_spec = pl.BlockSpec((1, n, GROUP), lambda i: (i // groups, 0, i % groups))

    outs = pl.pallas_call(
        functools.partial(
            attention_backward_kernel,
            reducer=reducer,
            late=late,
            scatter=scatter,
            groups=groups,
            items=items,
            kb=n // 4,
            rounds=rounds,
            sources=len(packed),
        ),
        grid=(items * groups,),
        in_specs=[
            pl.BlockSpec(memory_space=pltpu.SMEM),
            query_spec,
            key_spec,
            key_spec,
            query_spec,
            query_spec,
            pl.BlockSpec((1, 1, 8, rows4), lambda i: (i // groups, i % groups, 0, 0)),
            pl.BlockSpec((1, n, d), lambda i: (i // groups, 0, 0), pipeline_mode=pl.Buffered(1)),
            weight_spec(0),
            weight_spec(1),
            weight_spec(2),
        ]
        + [pl.BlockSpec(memory_space=pl.ANY)] * len(packed),
        out_specs=[vmem] * 2 + [pl.BlockSpec(memory_space=pl.ANY)] * 2,
        out_shape=[
            jax.ShapeDtypeStruct((items, t, d), F32),
            jax.ShapeDtypeStruct((groups, 8, GROUP), F32),
            reducer.out_shape(),
            late.out_shape(),
        ],
        scratch_shapes=[
            pltpu.VMEM((rows4, GROUP), BF),
            pltpu.VMEM((rows4, GROUP), BF),
            pltpu.VMEM((rows4, GROUP), F32),
            pltpu.VMEM((n, 2 * GROUP), BF),
            pltpu.VMEM((n, d), F32),
            pltpu.VMEM((groups,) + shares_of(bits) + (depth, d), BF),
        ]
        + reducer.scratch()
        + late.scratch()
        + scatter.scratch(),
        compiler_params=pltpu.CompilerParams(
            vmem_limit_bytes=63 << 20, collective_id=collective_id, has_side_effects=True
        ),
        cost_estimate=pl.CostEstimate(
            flops=100 * items * t * n * d,
            bytes_accessed=40 << 20,
            transcendentals=12 * items * t * n,
        ),
        name="attention_backward",
    )(
        valid_rows,
        queries,
        keys,
        values,
        grads,
        outs,
        lse,
        normed,
        qkv_weight,
        qkv_weight,
        qkv_weight,
        *packed,
    )
    return outs


def shards(
    tokens,
    valid_rows,
    dataset_ids,
    shift_flags,
    norm_gains,
    norm_biases,
    qkv_weight,
    qv_bias,
    out_weight,
    out_bias,
    fc1_weight,
    fc1_bias,
    fc2_weight,
    fc2_bias,
    tap_weight,
    tap_bias,
    conv_weights,
    conv_biases,
    table_gain,
    table_shift,
    token_cotangent,
    joined_cotangent,
):
    items_here, tok_here, width = tokens.shape
    rows_here = tok_here // PC
    channels = tap_weight.shape[1]
    row_index = lax.axis_index("rows")
    row_count = lax.axis_size("rows")
    last_index = row_count - 1

    flat_in = tokens.reshape(-1, width).astype(F32)
    queries, keys, values, attended, lses, normed_all = attention_forward(
        valid_rows,
        tokens,
        norm_gains[:1],
        norm_biases[:1],
        qkv_weight,
        qv_bias[None, :width],
        qv_bias[None, width:],
        5,
    )
    attended_flat = attended.reshape(-1, width)
    resid = flat_in + mm(attended_flat, out_weight) + out_bias
    normed_two = layer_norm(resid, norm_gains[1], norm_biases[1]).astype(BF)
    hidden_pre = mm(normed_two, fc1_weight) + fc1_bias
    hidden_cdf, hidden_rest = normal_parts(hidden_pre)
    hidden = (hidden_pre * hidden_cdf).astype(BF)
    hidden_slope = (hidden_cdf + hidden_rest).astype(BF)
    output = resid + mm(hidden, fc2_weight) + fc2_bias
    output_low = output.astype(BF)
    grid_rows = row_index * rows_here + jnp.arange(rows_here, dtype=jnp.int32)
    row_valid = (grid_rows[None, :] < valid_rows[:, None]).astype(F32)
    token_valid = jnp.broadcast_to(
        row_valid[:, :, None], (items_here, rows_here, PC)
    ).reshape(-1, 1)
    tap_pre = mm(output_low, tap_weight) + tap_bias
    field = (tap_pre * token_valid).reshape(items_here, rows_here, PC, channels)

    choose = (
        dataset_ids[:, None] == jnp.arange(table_gain.shape[0], dtype=jnp.int32)[None, :]
    ).astype(F32)
    flag_value = shift_flags.astype(F32)[:, None]
    gain_pick = jnp.dot(choose, table_gain, precision=highest)
    shift_pick = jnp.dot(choose, table_shift, precision=highest)
    factor = 1.0 + flag_value * (gain_pick - 1.0)
    offset = flag_value * shift_pick
    depth = width // row_count
    joined, grad_field, conv_grads, grad_conv_biases, table_sums = refine(
        field, conv_weights, conv_biases, factor, offset, joined_cotangent, depth
    )
    grad_table_gain = jnp.dot(choose.T, flag_value * table_sums[0], precision=highest)
    grad_table_shift = jnp.dot(choose.T, flag_value * table_sums[1], precision=highest)

    grad_tap = (grad_field[:, :, :PC].reshape(-1, channels) * token_valid).astype(BF)
    (
        tap_grads,
        out_grads,
        fc1_grads,
        fc2_grads,
        grad_resid,
        grad_attended,
        wide_sums,
        fc1_sums,
    ) = mlp_backward(
        grad_tap,
        token_cotangent.reshape(-1, width),
        output_low,
        normed_two,
        resid,
        attended_flat,
        norm_gains[1:2],
        tap_weight,
        out_weight,
        hidden,
        hidden_slope,
        fc1_weight,
        fc2_weight,
        tok_here,
    )
    shares = shares_of(axis_bits("rows"))
    fc2_grads = fc2_grads.reshape(fc2_grads.shape[:1] + shares + fc2_grads.shape[2:])
    grads_in, qkv_sums, early_sum, late_sum = attention_backward(
        valid_rows,
        queries,
        keys,
        values,
        grad_attended.reshape(tokens.shape),
        attended,
        lses,
        normed_all.reshape(keys.shape),
        qkv_weight,
        [conv_grads, tap_grads, fc2_grads, fc1_grads, out_grads],
        3,
    )
    grad_in_norm, grad_gain_one, grad_shift_one = norm_back(
        flat_in, norm_gains[0], grads_in.reshape(-1, width)
    )
    grad_tokens = (grad_resid + grad_in_norm).reshape(tokens.shape)

    groups = width // GROUP
    inner = fc1_weight.shape[1]
    kernels = conv_weights.shape[1]
    convs = conv_weights.shape[0]
    places = kernels // row_count // depth
    fc2_chunks = inner // row_count // depth
    blocks = inner // width
    table = [
        (conv, place * channels, channels, 0, conv, place * depth, 0)
        for conv in range(convs)
        for place in range(places)
    ]
    table += [(convs, 0, channels, 1, None, 0, 0)]
    first = convs + 1
    table += [(first + k, 0, width, 2, None, k * depth, 0) for k in range(fc2_chunks)]
    first += fc2_chunks
    table += [(first + k, 0, width, 3, None, 0, k * width) for k in range(blocks)]
    table += [(first + blocks, 0, width, 4, None, 0, 0)]
    share_conv, share_tap, share_fc2, share_fc1, share_out = unpack(
        early_sum,
        table,
        [
            (convs, kernels // row_count, channels),
            (depth, channels),
            (inner // row_count, width),
            (depth, inner),
            (depth, width),
        ],
    )
    (share_qkv,) = unpack(
        late_sum,
        [
            (group, kind * GROUP, GROUP, 0, None, 0, (kind * groups + group) * GROUP)
            for group in range(groups)
            for kind in range(3)
        ],
        [(depth, 3 * width)],
    )

    small = [
        jnp.stack([grad_gain_one, wide_sums[1]]),
        jnp.stack([grad_shift_one, wide_sums[2]]),
        jnp.concatenate([qkv_sums[:, 0].reshape(-1), qkv_sums[:, 1].reshape(-1)]),
        wide_sums[3],
        fc1_sums[0],
        wide_sums[0],
        wide_sums[4, :channels],
        grad_conv_biases,
        grad_table_gain,
        grad_table_shift,
    ]
    packed = jnp.concatenate(
        [
            array.reshape(row_count, -1)
            if array.ndim == 1
            else jnp.swapaxes(array.reshape(array.shape[0], row_count, -1), 0, 1).reshape(
                row_count, -1
            )
            for array in small
        ],
        axis=1,
    )
    packed = jnp.pad(packed, ((0, 0), (0, -packed.shape[1] % 1024)))
    summed = all_sum(packed.reshape(row_count, -1, 128), 4).reshape(-1)
    outs, place = [], 0
    for array in small:
        size = array.size // row_count
        piece = summed[place : place + size]
        place += size
        outs.append(piece if array.ndim == 1 else piece.reshape(array.shape[0], -1))
    (
        out_gains,
        out_shifts,
        out_qv,
        out_out,
        out_fc1,
        out_fc2,
        out_tap,
        out_conv,
        out_table_gain,
        out_table_shift,
    ) = outs
    return (
        output_low.reshape(tokens.shape),
        joined,
        grad_tokens,
        out_gains,
        out_shifts,
        share_qkv,
        out_qv,
        share_out,
        out_out,
        share_fc1,
        out_fc1,
        share_fc2,
        out_fc2,
        share_tap,
        out_tap,
        share_conv,
        out_conv,
        out_table_gain,
        out_table_shift,
    )


def solution(mesh):
    return jax.shard_map(
        shards,
        mesh=mesh,
        in_specs=(P("items", "rows", None), P("items"), P("items"), P("items"))
        + (P(),) * 16
        + (P("items", "rows", None), P("items", "rows", None, None)),
        out_specs=(
            P("items", "rows", None),
            P("items", "rows", None, None),
            P("items", "rows", None),
            P(None, "rows"),
            P(None, "rows"),
            P("rows", None),
            P("rows"),
            P("rows", None),
            P("rows"),
            P("rows", None),
            P("rows"),
            P("rows", None),
            P("rows"),
            P("rows", None),
            P("rows"),
            P(None, "rows", None),
            P(None, "rows"),
            P(None, "rows"),
            P(None, "rows"),
        ),
        check_vma=False,
    )
```

```python
import functools

import jax
import jax.numpy as jnp
from jax import lax
from jax.experimental import pallas as pl
from jax.experimental.pallas import tpu as pltpu
from jax.sharding import PartitionSpec as P

HEAD_DIM = 64
PC = 40
GROUP = 256
HEADS_PER_GROUP = GROUP // HEAD_DIM

BF = jnp.bfloat16
F32 = jnp.float32
LOG2E = 1.4426950408889634
MASKED = -1e30
NN = (((1,), (0,)), ((), ()))
NT = (((1,), (1,)), ((), ()))
TN = (((0,), (0,)), ((), ()))

epsilon = 1e-06
highest = lax.Precision.HIGHEST


def mm(left, right, dims=NN):
    return lax.dot_general(left, right, dims, preferred_element_type=F32)


def normal_parts(values):
    bell = jnp.exp2(values * values * (-0.5 * LOG2E))
    t = 1.0 / (1.0 + (0.3275911 * 0.7071067811865476) * jnp.abs(values))
    poly = t * (
        0.5 * 0.254829592
        + t
        * (
            0.5 * -0.284496736
            + t * (0.5 * 1.421413741 + t * (0.5 * -1.453152027 + t * (0.5 * 1.061405429)))
        )
    )
    tail = poly * bell
    cdf = jnp.where(values >= 0.0, 1.0 - tail, tail)
    return cdf, values * bell * 0.3989422804014327


def gelu_exact(values):
    return values * normal_parts(values)[0]


def gelu_slope(values):
    cdf, slope = normal_parts(values)
    return cdf + slope


def gelu_back(values, grad_out):
    return gelu_slope(values) * grad_out


def norm_stats(values):
    centre = jnp.mean(values, axis=-1, keepdims=True)
    centred = values - centre
    spread = jnp.mean(centred * centred, axis=-1, keepdims=True)
    rstd = lax.rsqrt(spread + epsilon)
    return centred * rstd, rstd


def layer_norm(values, gain, shift):
    return norm_stats(values)[0] * gain + shift


def norm_back(values, gain, grad_out):
    unit, rstd = norm_stats(values)
    scaled = grad_out * gain
    mean_one = jnp.mean(scaled, axis=-1, keepdims=True)
    mean_two = jnp.mean(scaled * unit, axis=-1, keepdims=True)
    result = rstd * (scaled - mean_one - unit * mean_two)
    return result, jnp.sum(grad_out * unit, axis=0), jnp.sum(grad_out, axis=0)


def axis_bits(axis):
    return (lax.axis_size(axis) - 1).bit_length()


def add_low(first, second):
    return (first.astype(F32) + second.astype(F32)).astype(BF)


def head_mask(shape, head):
    lane = lax.broadcasted_iota(jnp.int32, shape, 1)
    return lane // HEAD_DIM == head


def spread_heads(block):
    zero = jnp.zeros_like(block)
    return jnp.concatenate(
        [jnp.where(head_mask(block.shape, h), block, zero) for h in range(HEADS_PER_GROUP)],
        axis=0,
    )


WIDE = 48
EDGES = 10
FIELD_EDGE, TALL_EDGE = 4, 5


def refine_kernel(
    field_ref,
    weight_ref,
    bias_ref,
    factor_ref,
    offset_ref,
    cot_ref,
    joined_ref,
    grad_ref,
    dw_ref,
    db_ref,
    sums_ref,
    acts,
    slopes,
    grads3,
    work,
    frame,
    tall,
    lane2,
    edge,
    halo,
    send_sem,
    recv_sem,
    *,
    items,
    rows,
    count,
    depth,
):
    bits = (count - 1).bit_length()
    per_share = 9 * field_ref.shape[-1] // count // depth
    me = lax.axis_index("rows")
    here = lax.axis_index("items")
    channels = field_ref.shape[-1]
    flat = items * rows * WIDE
    lanes = channels // 128
    column = lax.broadcasted_iota(jnp.int32, (WIDE, channels), 0)
    inside = column < PC

    barrier = pltpu.get_barrier_semaphore()
    for step in (-1, 1):

        @pl.when((me + step >= 0) & (me + step < count))
        def _():
            pl.semaphore_signal(
                barrier, inc=1, device_id=(here, me + step), device_id_type=pl.DeviceIdType.MESH
            )

    @pl.when((me > 0) & (me < count - 1))
    def _():
        pl.semaphore_wait(barrier, 2)

    @pl.when((me == 0) | (me == count - 1))
    def _():
        pl.semaphore_wait(barrier, 1)

    def each(side):
        return (me > 0) if side == 0 else (me < count - 1)

    def copy(e, side):
        return pltpu.make_async_remote_copy(
            src_ref=edge.at[e, side],
            dst_ref=halo.at[e, 1 - side],
            send_sem=send_sem.at[e, side],
            recv_sem=recv_sem.at[e, 1 - side],
            device_id=(here, me + (2 * side - 1)),
            device_id_type=pl.DeviceIdType.MESH,
        )

    def send(e):
        for side in (0, 1):

            @pl.when(each(side))
            def _():
                copy(e, side).start()

    def receive(e):
        for side in (0, 1):

            @pl.when(each(side))
            def _():
                pltpu.make_async_remote_copy(
                    src_ref=edge.at[e, side],
                    dst_ref=halo.at[e, side],
                    send_sem=send_sem.at[e, side],
                    recv_sem=recv_sem.at[e, side],
                    device_id=(here, me + (2 * side - 1)),
                    device_id_type=pl.DeviceIdType.MESH,
                ).wait_recv()

            @pl.when(jnp.logical_not(each(side)))
            def _():
                halo[e, side] = jnp.zeros(halo.shape[2:], BF)

    def shifted(values, flip):
        before = pltpu.roll(values, 1, 0)
        after = pltpu.roll(values, WIDE - 1, 0)
        parts = [after, values, before] if flip else [before, values, after]
        return jnp.concatenate([part.astype(BF) for part in parts], axis=1)

    def all_rows(body, e):
        for item in range(items):
            for row, side in ((0, 0), (rows - 1, 1)):
                body(item, row, (e, side))
        send(e)

        def step(row, carry):
            for item in range(items):
                body(item, row, None)
            return carry

        lax.fori_loop(1, rows - 1, step, 0)

    def spread_halo(target, e, flip):
        for side, row in ((0, 0), (1, rows + 1)):
            for item in range(items):
                target[item, row] = shifted(halo[e, side, item].astype(F32), flip)

    for item in range(items):
        factor = factor_ref[pl.ds(item, 1), :]

        def back(row, carry, item=item, factor=factor):
            whole = cot_ref[item, row].astype(F32) * factor
            for part in range(lanes):
                lane2[part, pl.ds(0, 2 * PC), :] = whole[:, part * 128 : (part + 1) * 128]
            even, odd = (
                jnp.concatenate(
                    [lane2[part, pl.ds(start, PC, stride=2), :] for part in range(lanes)], axis=1
                )
                for start in (0, 1)
            )
            place = lax.broadcasted_iota(jnp.int32, (PC, channels), 0)
            even_next = jnp.where(place == PC - 1, odd, pltpu.roll(even, PC - 1, 0))
            odd_prev = jnp.where(place == 0, even, pltpu.roll(odd, 1, 0))
            tall[item, row + 1, pl.ds(0, PC), :] = 0.75 * (even + odd) + 0.25 * (
                even_next + odd_prev
            )
            tall[item, row + 1, pl.ds(PC, WIDE - PC), :] = jnp.zeros((WIDE - PC, channels), F32)
            return carry

        lax.fori_loop(0, 2 * rows, back, 0)
        edge[TALL_EDGE, 0, item] = tall[item, 1].astype(BF)
        edge[TALL_EDGE, 1, item] = tall[item, 2 * rows].astype(BF)
    send(TALL_EDGE)

    def activate(source, which):
        def body(item, row, out):
            values = source[item, row]
            cdf, rest = normal_parts(values)
            act = jnp.where(inside, values * cdf, 0.0)
            slopes[which, item, row] = cdf + rest
            acts[which, item, row + 1] = shifted(act, False)
            if out is not None:
                edge[out[0], out[1], item] = act.astype(BF)

        all_rows(body, which)

    def weight_of(conv, kr):
        return weight_ref[conv, pl.ds(kr * 3 * channels, 3 * channels), :]

    def lhs(source, item, first, number):
        return source[item, pl.ds(first, number)].reshape(number * WIDE, -1)

    def forward(conv, add):
        bias = bias_ref[pl.ds(conv, 1), :]
        for item in range(items):
            centre = mm(lhs(acts.at[conv], item, 1, rows), weight_of(conv, 1)) + bias
            if add:
                centre = centre + frame[item, pl.ds(1, rows)].reshape(rows * WIDE, channels)
            work[item] = centre.reshape(rows, WIDE, channels)
            upper = mm(lhs(acts.at[conv], item, 1, rows - 1), weight_of(conv, 0))
            work[item, pl.ds(1, rows - 1)] += upper.reshape(rows - 1, WIDE, channels)
            lower = mm(lhs(acts.at[conv], item, 2, rows - 1), weight_of(conv, 2))
            work[item, pl.ds(0, rows - 1)] += lower.reshape(rows - 1, WIDE, channels)
        receive(conv)
        spread_halo(acts.at[conv], conv, False)
        for kr, source, row in ((0, 0, 0), (2, rows + 1, rows - 1)):
            block = jnp.concatenate([acts[conv, item, source] for item in range(items)], axis=0)
            extra = mm(block, weight_of(conv, kr))
            for item in range(items):
                work[item, row] += extra[item * WIDE : (item + 1) * WIDE]

    def keep_field(source):
        for item in range(items):
            frame[item, pl.ds(1, rows)] = source[item]

    keep_field(field_ref)
    for unit in (0, 1):
        activate(field_ref if unit == 0 else work, 2 * unit)
        forward(2 * unit, False)
        activate(work, 2 * unit + 1)
        forward(2 * unit + 1, True)
        keep_field(work)

    for item in range(items):
        edge[FIELD_EDGE, 0, item] = frame[item, 1].astype(BF)
        edge[FIELD_EDGE, 1, item] = frame[item, rows].astype(BF)
    send(FIELD_EDGE)

    receive(TALL_EDGE)
    for item in range(items):
        tall[item, 0] = jnp.where(me == 0, tall[item, 1], halo[TALL_EDGE, 0, item].astype(F32))
        tall[item, 2 * rows + 1] = jnp.where(
            me == count - 1, tall[item, 2 * rows], halo[TALL_EDGE, 1, item].astype(F32)
        )

        def fold(row, carry, item=item):
            grad_ref[item, row] = 0.75 * (
                tall[item, 2 * row + 1] + tall[item, 2 * row + 2]
            ) + 0.25 * (tall[item, 2 * row] + tall[item, 2 * row + 3])
            return carry

        lax.fori_loop(0, rows, fold, 0)

    receive(FIELD_EDGE)
    for item in range(items):
        frame[item, 0] = jnp.where(me == 0, frame[item, 1], halo[FIELD_EDGE, 0, item].astype(F32))
        frame[item, rows + 1] = jnp.where(
            me == count - 1, frame[item, rows], halo[FIELD_EDGE, 1, item].astype(F32)
        )
        factor = factor_ref[pl.ds(item, 1), :]
        offset = offset_ref[pl.ds(item, 1), :]

        def widen(row, carry, item=item, factor=factor, offset=offset):
            gain_sum, shift_sum = carry
            centre = frame[item, row + 1]
            for half in (0, 1):
                line = 0.75 * centre + 0.25 * frame[item, row + 2 * half]
                before = jnp.where(column == 0, line, pltpu.roll(line, 1, 0))
                after = jnp.where(column == PC - 1, line, pltpu.roll(line, WIDE - 1, 0))
                for start, side in ((0, before), (1, after)):
                    mixed = 0.75 * line + 0.25 * side
                    for part in range(lanes):
                        lane2[part, pl.ds(start, WIDE, stride=2), :] = mixed[
                            :, part * 128 : (part + 1) * 128
                        ]
                wide = jnp.concatenate(
                    [lane2[part, pl.ds(0, 2 * PC), :] for part in range(lanes)], axis=1
                )
                joined_ref[item, 2 * row + half] = (wide * factor + offset).astype(BF)
                cot = cot_ref[item, 2 * row + half].astype(F32)
                gain_sum = gain_sum + jnp.sum((cot * wide).reshape(-1, 8, channels), axis=0)
                shift_sum = shift_sum + jnp.sum(cot.reshape(-1, 8, channels), axis=0)
            return gain_sum, shift_sum

        zero = jnp.zeros((8, channels), F32)
        gain_sum, shift_sum = lax.fori_loop(0, rows, widen, (zero, zero))
        sums_ref[0, pl.ds(item, 1), :] = jnp.sum(gain_sum, axis=0, keepdims=True)
        sums_ref[1, pl.ds(item, 1), :] = jnp.sum(shift_sum, axis=0, keepdims=True)

    def grad_pass(conv, make):
        e = 6 + conv

        def body(item, row, out):
            values = jnp.where(inside, make(item, row), 0.0).astype(BF).astype(F32)
            grads3[item, row + 1] = shifted(values, True)
            if out is not None:
                edge[out[0], out[1], item] = values.astype(BF)

        all_rows(body, e)
        middle = jnp.concatenate(
            [
                grads3[item, pl.ds(1, rows), :, pl.ds(channels, channels)].reshape(
                    rows * WIDE, channels
                )
                for item in range(items)
            ],
            axis=0,
        )
        for kr in range(3):
            block = jnp.concatenate(
                [lhs(acts.at[conv], item, kr, rows) for item in range(items)], axis=0
            )
            weight = mm(block, middle, TN).astype(BF)
            pieces = 3 * channels // depth
            for k in range(pieces):
                share, place = divmod(kr * pieces + k, per_share)
                at = tuple(share >> b & 1 for b in range(bits - 1, -1, -1))
                dw_ref[(conv,) + at + (slice(None), pl.ds(place * channels, channels))] = weight[
                    k * depth : (k + 1) * depth
                ]
        ones = jnp.ones((8, flat), BF)
        db_ref[pl.ds(conv, 1), :] = mm(ones, middle)[:1]

        def product(block, kr):
            total = None
            for kc in range(3):
                part = mm(
                    block[:, kc * channels : (kc + 1) * channels],
                    weight_ref[conv, pl.ds((kr * 3 + kc) * channels, channels), :],
                    NT,
                )
                total = part if total is None else total + part
            return total

        for item in range(items):
            work[item] = product(lhs(grads3, item, 1, rows), 1).reshape(rows, WIDE, channels)
            work[item, pl.ds(1, rows - 1)] += product(lhs(grads3, item, 1, rows - 1), 2).reshape(
                rows - 1, WIDE, channels
            )
            work[item, pl.ds(0, rows - 1)] += product(lhs(grads3, item, 2, rows - 1), 0).reshape(
                rows - 1, WIDE, channels
            )
        receive(e)
        spread_halo(grads3, e, True)
        for kr, source, row in ((2, 0, 0), (0, rows + 1, rows - 1)):
            block = jnp.concatenate([grads3[item, source] for item in range(items)], axis=0)
            extra = product(block, kr)
            for item in range(items):
                work[item, row] += extra[item * WIDE : (item + 1) * WIDE]

    for unit in (1, 0):
        first, second = 2 * unit, 2 * unit + 1
        grad_pass(second, lambda item, row: grad_ref[item, row])
        grad_pass(first, lambda item, row: work[item, row] * slopes[second, item, row])

        def gather(row, carry, first=first):
            for item in range(items):
                grad_ref[item, row] += work[item, row] * slopes[first, item, row]
            return carry

        lax.fori_loop(0, rows, gather, 0)

    for e in range(EDGES):
        for side in (0, 1):

            @pl.when(each(side))
            def _():
                copy(e, side).wait_send()


def refine(field, conv_weights, conv_biases, factor, offset, cotangent, depth):
    items, rows, _, channels = field.shape
    count = lax.axis_size("rows")
    padded = jnp.pad(field, ((0, 0), (0, 0), (0, WIDE - PC), (0, 0)))
    vmem = pl.BlockSpec(memory_space=pltpu.VMEM)
    pixels = items * rows * PC
    outs = pl.pallas_call(
        functools.partial(refine_kernel, items=items, rows=rows, count=count, depth=depth),
        in_specs=[vmem] * 6,
        out_specs=[vmem] * 5,
        out_shape=[
            jax.ShapeDtypeStruct((items, 2 * rows, 2 * PC, channels), BF),
            jax.ShapeDtypeStruct((items, rows, WIDE, channels), F32),
            jax.ShapeDtypeStruct(
                conv_weights.shape[:1]
                + (2,) * axis_bits("rows")
                + (depth, conv_weights.shape[1] // count // depth * channels),
                BF,
            ),
            jax.ShapeDtypeStruct(conv_biases.shape, F32),
            jax.ShapeDtypeStruct((2, items, channels), F32),
        ],
        scratch_shapes=[
            pltpu.VMEM((4, items, rows + 2, WIDE, 3 * channels), BF),
            pltpu.VMEM((4, items, rows, WIDE, channels), F32),
            pltpu.VMEM((items, rows + 2, WIDE, 3 * channels), BF),
            pltpu.VMEM((items, rows, WIDE, channels), F32),
            pltpu.VMEM((items, rows + 2, WIDE, channels), F32),
            pltpu.VMEM((items, 2 * rows + 2, WIDE, channels), F32),
            pltpu.VMEM((channels // 128, 2 * WIDE, 128), F32),
            pltpu.VMEM((EDGES, 2, items, WIDE, channels), BF),
            pltpu.VMEM((EDGES, 2, items, WIDE, channels), BF),
            pltpu.SemaphoreType.DMA((EDGES, 2)),
            pltpu.SemaphoreType.DMA((EDGES, 2)),
        ],
        compiler_params=pltpu.CompilerParams(
            vmem_limit_bytes=56 << 20, collective_id=0, has_side_effects=True
        ),
        cost_estimate=pl.CostEstimate(
            flops=2 * 12 * pixels * 9 * channels * channels,
            bytes_accessed=20 << 20,
            transcendentals=8 * pixels * channels,
        ),
        name="refine",
    )(padded, conv_weights, conv_biases, factor, offset, cotangent)
    return outs


MESH = pl.DeviceIdType.MESH


def flip(index, bit):
    return index + (1 - 2 * (index // (1 << bit) % 2)) * (1 << bit)


class Reducer:
    def __init__(self, chunks, depth, strip, row_bits, item_bits, space, lag):
        self.chunks, self.depth, self.lanes = chunks, depth, strip // 2
        self.space, self.lag = space, lag
        self.row_bits, self.item_bits = row_bits, item_bits
        self.orders = (tuple(range(row_bits - 1, -1, -1)), tuple(range(row_bits)))
        self.far = max(item_bits - 2, 0)
        self.phases = 1 + row_bits + 1 + self.far + 1 + 1

    def scratch(self):
        c, half = self.chunks, self.depth // 2
        shares = (2,) * self.row_bits
        slots = [
            pltpu.VMEM((c,) + shares + (self.depth, self.lanes), BF),
            pltpu.VMEM((2,) + shares + (self.depth, self.lanes), BF),
        ]
        for stage in range(self.row_bits):
            for _ in (0, 1):
                slots.append(pltpu.VMEM((c,) + (2,) * (self.row_bits - 1 - stage) + (half, self.lanes), BF))
        slots.append(pltpu.VMEM((c, half, self.lanes), BF))
        for _ in range(self.far):
            slots.append(pltpu.VMEM((c, half, self.lanes), BF))
            slots.append(pltpu.VMEM((c, half, self.lanes), BF))
        arrivals = 1 + 2 * self.row_bits + 1 + self.far + 1 + 1
        sends = 1 + 2 * self.row_bits + 1 + self.far + 1 + 1
        return slots + [
            pltpu.VMEM((2, c, self.depth, self.lanes), BF),
            pltpu.SemaphoreType.DMA((2,)),
            pltpu.SemaphoreType.DMA((arrivals, c)),
            pltpu.SemaphoreType.DMA((sends,)),
        ]

    def slots(self):
        return len(self.scratch())

    def out_shape(self):
        return jax.ShapeDtypeStruct((2, self.chunks, self.depth, self.lanes), BF)

    def bind(self, out_ref, slots, sources=None, held=None):
        slots = list(slots)
        self.result, self.sources, self.held = out_ref, sources, held
        self.total, self.ring = slots[0], slots[1]
        self.row_in = [
            (slots[2 + 2 * stage], slots[3 + 2 * stage]) for stage in range(self.row_bits)
        ]
        rest = slots[2 + 2 * self.row_bits :]
        self.near_in = rest[0]
        self.far_out = [rest[1 + 2 * k] for k in range(self.far)]
        self.far_in = [rest[2 + 2 * k] for k in range(self.far)]
        self.out, self.ring_sem, self.recv_sem, self.send_sem = rest[-4:]
        self.me = lax.axis_index("rows")
        self.at = lax.axis_index("items")
        self.core = self.at % 2
        self.near = self.at // 2 % 2

    def peers(self):
        found = [(flip(self.at, bit), self.me) for bit in range(self.item_bits)]
        return found + [(self.at, flip(self.me, bit)) for bit in range(self.row_bits)]

    def greet(self):
        barrier = pltpu.get_barrier_semaphore()
        for peer in self.peers():
            pl.semaphore_signal(barrier, inc=1, device_id=peer, device_id_type=MESH)
        pl.semaphore_wait(barrier, len(self.peers()))

    def remote(self, source, target, arrival, sent, chunk, peer):
        return pltpu.make_async_remote_copy(
            src_ref=source,
            dst_ref=target,
            send_sem=self.send_sem.at[sent],
            recv_sem=self.recv_sem.at[arrival, chunk],
            device_id=peer,
            device_id_type=MESH,
        )

    def strip(self, ref, index, mine):
        side = self.core if mine else 1 - self.core
        lanes = pl.ds(pl.multiple_of(side * self.lanes, self.lanes), self.lanes)
        return ref.at[(index,) + (slice(None),) * (self.row_bits + 1) + (lanes,)]

    def core_copy(self, source, chunk):
        return self.remote(
            source, self.total.at[chunk], 0, 0, chunk, (flip(self.at, 0), self.me)
        )

    def begin(self):
        base = 0
        for ref in self.sources:

            def go(index, carry, ref=ref, base=base):
                self.core_copy(self.strip(ref, index, False), base + index).start()
                return carry

            lax.fori_loop(0, ref.shape[0], go, 0)
            base += ref.shape[0]
        self.fetch(0)

    def begin_held(self, chunk):
        self.core_copy(self.strip(self.held, chunk, False), chunk).start()

    def fetch(self, chunk):
        base = 0
        for ref in self.sources:

            @pl.when((chunk >= base) & (chunk < base + ref.shape[0]))
            def _(ref=ref, base=base):
                index = jnp.clip(chunk - base, 0, ref.shape[0] - 1)
                pltpu.make_async_copy(
                    self.strip(ref, index, True),
                    self.ring.at[chunk % 2],
                    self.ring_sem.at[chunk % 2],
                ).start()

            base += ref.shape[0]

    def add_mine(self, chunk):
        if self.held is not None:
            block = self.held[chunk]
            side = (slice(None),) * (self.row_bits + 1)
            block = jnp.where(
                self.core == 0,
                block[side + (slice(0, self.lanes),)],
                block[side + (slice(self.lanes, None),)],
            )
        else:
            slot = chunk % 2
            pltpu.make_async_copy(
                self.total.at[chunk], self.ring.at[slot], self.ring_sem.at[slot]
            ).wait()
            block = self.ring[slot]
        self.total[chunk] = add_low(self.total[chunk], block)

    def bit(self, which):
        return self.me // (1 << which) % 2

    def shares(self, half, stage, sent):
        order = self.orders[half]
        index = [slice(None)] * self.row_bits
        for done in order[:stage]:
            index[self.row_bits - 1 - done] = self.bit(done)
        now = order[stage]
        index[self.row_bits - 1 - now] = 1 - self.bit(now) if sent else self.bit(now)
        return tuple(index)

    def rows(self, half):
        depth = self.depth // 2
        return pl.ds(half * depth, depth)

    def row_copy(self, stage, half, chunk):
        source = self.total.at[(chunk,) + self.shares(half, stage, True) + (self.rows(half),)]
        return self.remote(
            source,
            self.row_in[stage][half].at[chunk],
            1 + 2 * stage + half,
            1 + 2 * stage + half,
            chunk,
            (self.at, flip(self.me, self.orders[half][stage])),
        )

    def own(self, chunk, rows):
        return (chunk,) + tuple(self.bit(b) for b in range(self.row_bits - 1, -1, -1)) + (rows,)

    def near_rows(self, mine):
        half = self.depth // 2
        place = self.near if mine else 1 - self.near
        return pl.ds(pl.multiple_of(place * half, half), half)

    def near_copy(self, chunk):
        return self.remote(
            self.total.at[self.own(chunk, self.near_rows(False))],
            self.near_in.at[chunk],
            1 + 2 * self.row_bits,
            1 + 2 * self.row_bits,
            chunk,
            (flip(self.at, 1), self.me),
        )

    def far_copy(self, k, chunk):
        return self.remote(
            self.far_out[k].at[chunk],
            self.far_in[k].at[chunk],
            2 + 2 * self.row_bits + k,
            2 + 2 * self.row_bits + k,
            chunk,
            (flip(self.at, 2 + k), self.me),
        )

    def back_copy(self, chunk):
        place = self.out.at[self.core, chunk, self.near_rows(True)]
        return self.remote(
            place,
            place,
            2 + 2 * self.row_bits + self.far,
            2 + 2 * self.row_bits + self.far,
            chunk,
            (flip(self.at, 1), self.me),
        )

    def last_copy(self, chunk):
        place = self.out.at[self.core, chunk]
        return self.remote(
            place,
            place,
            3 + 2 * self.row_bits + self.far,
            3 + 2 * self.row_bits + self.far,
            chunk,
            (flip(self.at, 0), self.me),
        )

    def phase(self, number, chunk):
        bits, half = self.row_bits, self.depth // 2
        if number == 0:
            self.core_copy(self.total.at[chunk], chunk).wait_recv()
            self.add_mine(chunk)
            if self.sources is not None:

                @pl.when(chunk + 1 < self.chunks)
                def _():
                    self.fetch(chunk + 1)

            for side in (0, 1):
                self.row_copy(0, side, chunk).start()
        elif number <= bits:
            stage = number - 1
            for side in (0, 1):
                self.row_copy(stage, side, chunk).wait_recv()
                at = (chunk,) + self.shares(side, stage, False) + (self.rows(side),)
                self.total[at] = add_low(self.total[at], self.row_in[stage][side][chunk])
                if stage + 1 < bits:
                    self.row_copy(stage + 1, side, chunk).start()
            if stage + 1 == bits:
                self.near_copy(chunk).start()
        elif number == bits + 1:
            self.near_copy(chunk).wait_recv()
            total = add_low(
                self.total[self.own(chunk, self.near_rows(True))], self.near_in[chunk]
            )
            self.pass_on(0, chunk, total)
        elif number <= bits + 1 + self.far:
            k = number - bits - 2
            self.far_copy(k, chunk).wait_recv()
            self.pass_on(k + 1, chunk, add_low(self.far_out[k][chunk], self.far_in[k][chunk]))
        elif number == bits + 2 + self.far:
            self.back_copy_arrived(chunk)
            self.last_copy(chunk).start()
        else:
            self.last_arrived(chunk)

    def pass_on(self, k, chunk, total):
        if k < self.far:
            self.far_out[k][chunk] = total
            self.far_copy(k, chunk).start()
        else:
            self.out[self.core, chunk, self.near_rows(True)] = total
            self.back_copy(chunk).start()

    def back_copy_arrived(self, chunk):
        place = self.out.at[self.core, chunk, self.near_rows(False)]
        self.remote(
            place,
            place,
            2 + 2 * self.row_bits + self.far,
            2 + 2 * self.row_bits + self.far,
            chunk,
            (flip(self.at, 1), self.me),
        ).wait_recv()

    def last_arrived(self, chunk):
        place = self.out.at[1 - self.core, chunk]
        self.remote(
            place,
            place,
            3 + 2 * self.row_bits + self.far,
            3 + 2 * self.row_bits + self.far,
            chunk,
            (flip(self.at, 0), self.me),
        ).wait_recv()

    def step(self, t):
        for number in range(self.phases - 1, -1, -1):
            place = t - self.lag * number
            chunk = place // self.space

            @pl.when((place >= 0) & (place % self.space == 0) & (chunk < self.chunks))
            def _(number=number, chunk=chunk):
                self.phase(number, jnp.clip(chunk, 0, self.chunks - 1))

    @property
    def steps(self):
        return (self.chunks - 1) * self.space + self.lag * (self.phases - 1) + 1

    def finish(self):
        def drain(sem, ref):
            pltpu.make_async_copy(ref, ref, self.send_sem.at[sem]).wait()

        drain(0, self.total)
        for stage in range(self.row_bits):
            for side in (0, 1):
                drain(1 + 2 * stage + side, self.row_in[stage][side])
        base = 1 + 2 * self.row_bits
        drain(base, self.near_in)
        for k in range(self.far):
            drain(base + 1 + k, self.far_in[k])
        drain(base + 1 + self.far, self.near_in)
        drain(base + 2 + self.far, self.out.at[0])
        copy = pltpu.make_async_copy(self.out, self.result, self.ring_sem.at[0])
        copy.start()
        copy.wait()


def unpack_kernel(held_ref, *refs, table, outs):
    targets, (wide, sem) = refs[:outs], refs[outs:]
    depth = wide.shape[1]

    def copy(place, chunk, first, size, number, outer, row, column):
        target = targets[number] if outer is None else targets[number].at[outer]
        return pltpu.make_async_copy(
            wide.at[chunk, :, pl.ds(first, size)],
            target.at[pl.ds(row, depth), pl.ds(column, size)],
            sem.at[place],
        )

    done = set()
    for place, entry in enumerate(table):
        chunk = entry[0]
        if chunk not in done:
            done.add(chunk)
            wide[chunk] = jnp.concatenate(
                [held_ref[0, chunk].astype(F32), held_ref[1, chunk].astype(F32)], axis=1
            )
        copy(place, *entry).start()
    for place, entry in enumerate(table):
        copy(place, *entry).wait()


def unpack(out, table, shapes):
    chunks, depth, lanes = out.shape[1:]
    return pl.pallas_call(
        functools.partial(unpack_kernel, table=table, outs=len(shapes)),
        in_specs=[pl.BlockSpec(memory_space=pltpu.VMEM)],
        out_specs=[pl.BlockSpec(memory_space=pl.ANY)] * len(shapes),
        out_shape=[jax.ShapeDtypeStruct(shape, F32) for shape in shapes],
        scratch_shapes=[
            pltpu.VMEM((chunks, depth, 2 * lanes), F32),
            pltpu.SemaphoreType.DMA((len(table),)),
        ],
        compiler_params=pltpu.CompilerParams(vmem_limit_bytes=40 << 20),
        name="unpack",
    )(out)


def all_sum_kernel(value_ref, out_ref, piece, landed, over, send_sem, recv_sem, *, count, others):
    at, me = lax.axis_index("items"), lax.axis_index("rows")
    barrier = pltpu.get_barrier_semaphore()
    row_peers = [(at, (me + k) % count) for k in range(1, count)]
    item_peers = [((at + k) % others, me) for k in range(1, others)]
    for peer in row_peers + item_peers:
        pl.semaphore_signal(barrier, inc=1, device_id=peer, device_id_type=MESH)
    pl.semaphore_wait(barrier, count + others - 2)

    def row_copy(k):
        return pltpu.make_async_remote_copy(
            src_ref=value_ref.at[row_peers[k][1]],
            dst_ref=landed.at[k],
            send_sem=send_sem.at[k],
            recv_sem=recv_sem.at[k],
            device_id=row_peers[k],
            device_id_type=MESH,
        )

    def item_copy(k):
        return pltpu.make_async_remote_copy(
            src_ref=piece,
            dst_ref=over.at[k],
            send_sem=send_sem.at[count - 1 + k],
            recv_sem=recv_sem.at[count - 1 + k],
            device_id=item_peers[k],
            device_id_type=MESH,
        )

    for k in range(count - 1):
        row_copy(k).start()
    total = value_ref[me]
    for k in range(count - 1):
        row_copy(k).wait_recv()
        total = total + landed[k]
    piece[...] = total
    for k in range(others - 1):
        item_copy(k).start()
    for k in range(others - 1):
        item_copy(k).wait_recv()
        total = total + over[k]
    out_ref[...] = total
    for k in range(count - 1):
        row_copy(k).wait_send()
    for k in range(others - 1):
        item_copy(k).wait_send()


def all_sum(value, collective_id):
    count, others = lax.axis_size("rows"), lax.axis_size("items")
    vmem = pl.BlockSpec(memory_space=pltpu.VMEM)
    block = value.shape[1:]
    return pl.pallas_call(
        functools.partial(all_sum_kernel, count=count, others=others),
        in_specs=[vmem],
        out_specs=vmem,
        out_shape=jax.ShapeDtypeStruct(block, F32),
        scratch_shapes=[
            pltpu.VMEM(block, F32),
            pltpu.VMEM((count - 1,) + block, F32),
            pltpu.VMEM((others - 1,) + block, F32),
            pltpu.SemaphoreType.DMA((count + others - 2,)),
            pltpu.SemaphoreType.DMA((count + others - 2,)),
        ],
        compiler_params=pltpu.CompilerParams(collective_id=collective_id, has_side_effects=True),
        name="sum_small",
    )(value)


class Gather:
    def __init__(self, bits, items):
        self.bits, self.items = bits, items
        self.orders = (tuple(range(bits)), tuple(range(bits - 1, -1, -1)))

    def bind(self, held, send_sem, recv_sem):
        self.held, self.send_sem, self.recv_sem = held, send_sem, recv_sem

    def place(self, item, half, stage, now):
        order = self.orders[half]
        index = [0] * self.bits
        for done in order[:stage]:
            index[self.bits - 1 - done] = slice(None)
        index[self.bits - 1 - order[stage]] = now
        size = self.held.shape[-2] // 2
        return (item,) + tuple(index) + (pl.ds(half * size, size),)

    def copy(self, item, stage, half):
        me, at = lax.axis_index("rows"), lax.axis_index("items")
        return pltpu.make_async_remote_copy(
            src_ref=self.held.at[self.place(item, half, stage, 0)],
            dst_ref=self.held.at[self.place(item, half, stage, 1)],
            send_sem=self.send_sem.at[item, stage, half],
            recv_sem=self.recv_sem.at[item, stage, half],
            device_id=(at, flip(me, self.orders[half][stage])),
            device_id_type=MESH,
        )

    def start(self, item, stage):
        for half in (0, 1):
            self.copy(item, stage, half).start()

    def arrived(self, item, stage):
        for half in (0, 1):
            self.copy(item, stage, half).wait_recv()

    def drain(self, item):
        for stage in range(self.bits):
            for half in (0, 1):
                self.copy(item, stage, half).wait_send()


def attention_forward_kernel(
    valid_ref,
    tokens_ref,
    gain_ref,
    shift_ref,
    q_bias_ref,
    v_bias_ref,
    wq_ref,
    wk_ref,
    wv_ref,
    q_ref,
    k_ref,
    v_ref,
    o_ref,
    lse_ref,
    normed_ref,
    held,
    send_sem,
    recv_sem,
    copy_sem,
    *,
    gather,
    groups,
    items,
):
    gather.bind(held, send_sem, recv_sem)
    step = pl.program_id(0)
    item, group = step // groups, step % groups
    t, width = held.shape[-2:]
    n = k_ref.shape[1]
    me, at = lax.axis_index("rows"), lax.axis_index("items")
    bits = gather.bits
    mine = (0,) * bits

    def store(which):
        held[(which,) + mine] = layer_norm(
            tokens_ref[which].astype(F32), gain_ref[...], shift_ref[...]
        ).astype(BF)

    def keep(which):
        return pltpu.make_async_copy(held.at[which], normed_ref.at[which], copy_sem.at[which])

    @pl.when(step == 0)
    def _():
        store(0)
        barrier = pltpu.get_barrier_semaphore()
        for bit in range(bits):
            pl.semaphore_signal(
                barrier, inc=1, device_id=(at, flip(me, bit)), device_id_type=MESH
            )
        pl.semaphore_wait(barrier, bits)
        gather.start(0, 0)
        for which in range(1, items):
            store(which)
        for stage in range(1, bits):
            gather.arrived(0, stage - 1)
            gather.start(0, stage)
        gather.start(1, 0)

    @pl.when(group == 0)
    def _():
        gather.arrived(item, bits - 1)
        keep(item).start()

    limit = valid_ref[item] * PC
    index = lax.broadcasted_iota(jnp.int32, (1, n), 1)
    bias = jnp.where(index + key_shift(index, n, t, me) < limit, 0.0, MASKED).astype(F32)
    every = held[item].reshape(n, width)
    keys = mm(every, wk_ref[...]).astype(BF)
    values = (mm(every, wv_ref[...]) + v_bias_ref[...]).astype(BF)
    queries = (mm(held[(item,) + mine], wq_ref[...]) + q_bias_ref[...]).astype(BF)
    k_ref[0] = keys
    v_ref[0] = values
    q_ref[0] = queries
    queries = queries * jnp.asarray(HEAD_DIM**-0.5, BF)
    out = jnp.zeros((t, GROUP), F32)
    for h in range(HEADS_PER_GROUP):
        mask = head_mask((t, GROUP), h)
        one = jnp.where(mask, queries, jnp.zeros_like(queries))
        scores = mm(one, keys, NT) + bias
        top = jnp.max(scores, axis=1, keepdims=True)
        probs = jnp.exp2((scores - top) * LOG2E)
        total = jnp.sum(probs, axis=1, keepdims=True)
        weighted = mm(probs.astype(BF), values)
        out = jnp.where(mask, weighted * (1.0 / total), out)
        lse = top * LOG2E + jnp.log2(total)
        lse_ref[0, 0, :, pl.ds(h * t, t)] = jnp.transpose(jnp.broadcast_to(lse, (t, 128)))[:8]
    o_ref[0] = out.astype(BF)

    for stage in range(1, bits):

        @pl.when((group == stage - 1) & (item + 1 < items))
        def _(stage=stage):
            gather.arrived(item + 1, stage - 1)
            gather.start(item + 1, stage)

    @pl.when((group == bits - 2) & (item + 2 < items))
    def _():
        gather.start(item + 2, 0)

    @pl.when(step == items * groups - 1)
    def _():
        for which in range(items):
            gather.drain(which)
            keep(which).wait()


def attention_forward(valid_rows, tokens, gain, shift, qkv_weight, q_bias, v_bias, collective_id):
    items, t, d = tokens.shape
    bits = axis_bits("rows")
    n = t << bits
    groups = d // GROUP
    rows4 = HEADS_PER_GROUP * t
    vmem = pl.BlockSpec(memory_space=pltpu.VMEM)

    def weight_spec(kind):
        return pl.BlockSpec((d, GROUP), lambda i: (0, kind * groups + i % groups))

    bias_spec = pl.BlockSpec((1, GROUP), lambda i: (0, i % groups))
    query_spec = pl.BlockSpec((1, t, GROUP), lambda i: (i // groups, 0, i % groups))
    key_spec = pl.BlockSpec((1, n, GROUP), lambda i: (i // groups, 0, i % groups))
    return pl.pallas_call(
        functools.partial(
            attention_forward_kernel, gather=Gather(bits, items), groups=groups, items=items
        ),
        grid=(items * groups,),
        in_specs=[
            pl.BlockSpec(memory_space=pltpu.SMEM),
            vmem,
            vmem,
            vmem,
            bias_spec,
            bias_spec,
            weight_spec(0),
            weight_spec(1),
            weight_spec(2),
        ],
        out_specs=[
            query_spec,
            key_spec,
            key_spec,
            query_spec,
            pl.BlockSpec((1, 1, 8, rows4), lambda i: (i // groups, i % groups, 0, 0)),
            pl.BlockSpec(memory_space=pl.ANY),
        ],
        out_shape=[
            jax.ShapeDtypeStruct((items, t, d), BF),
            jax.ShapeDtypeStruct((items, n, d), BF),
            jax.ShapeDtypeStruct((items, n, d), BF),
            jax.ShapeDtypeStruct((items, t, d), BF),
            jax.ShapeDtypeStruct((items, groups, 8, rows4), F32),
            jax.ShapeDtypeStruct((items,) + (2,) * bits + (t, d), BF),
        ],
        scratch_shapes=[
            pltpu.VMEM((items,) + (2,) * bits + (t, d), BF),
            pltpu.SemaphoreType.DMA((items, bits, 2)),
            pltpu.SemaphoreType.DMA((items, bits, 2)),
            pltpu.SemaphoreType.DMA((items,)),
        ],
        compiler_params=pltpu.CompilerParams(
            vmem_limit_bytes=52 << 20, collective_id=collective_id, has_side_effects=True
        ),
        cost_estimate=pl.CostEstimate(
            flops=60 * items * t * n * d,
            bytes_accessed=40 << 20,
            transcendentals=12 * items * t * n,
        ),
        name="attention_forward",
    )(
        valid_rows,
        tokens,
        gain,
        shift,
        q_bias,
        v_bias,
        qkv_weight,
        qkv_weight,
        qkv_weight,
    )


def key_shift(index, length, block, me):
    start = jnp.full_like(index, me * block)
    for j in range(1, length // block):
        other = me
        for bit in range(j.bit_length()):
            if j >> bit & 1:
                other = flip(other, bit)
        start = jnp.where(index >= j * block, (other - j) * block, start)
    return start


def mlp_forward_kernel(
    tokens_ref,
    attended_ref,
    out_w_ref,
    out_bias_ref,
    gain_ref,
    shift_ref,
    fc2_bias_ref,
    tap_w_ref,
    tap_bias_ref,
    fc1_ref,
    fc1_bias_ref,
    fc2_ref,
    resid_ref,
    normed_ref,
    hidden_ref,
    slope_ref,
    out_ref,
    tap_ref,
    total,
    *,
    blocks,
    row_block,
):
    step = pl.program_id(0)
    count = total.shape[0] // row_block

    def rows_of(number):
        return pl.ds(number * row_block, row_block)

    @pl.when(step == 0)
    def _():
        def enter(number):
            piece = rows_of(number)
            resid = (
                tokens_ref[piece, :].astype(F32)
                + mm(attended_ref[piece, :], out_w_ref[...])
                + out_bias_ref[...]
            )
            resid_ref[piece, :] = resid
            total[piece, :] = resid + fc2_bias_ref[...]
            normed_ref[piece, :] = layer_norm(resid, gain_ref[...], shift_ref[...]).astype(BF)

        for number in range(count):
            enter(number)

    def middle(number):
        piece = rows_of(number)
        pre = mm(normed_ref[piece, :], fc1_ref[...]) + fc1_bias_ref[...]
        cdf, rest = normal_parts(pre)
        hidden = (pre * cdf).astype(BF)
        hidden_ref[piece, :] = hidden
        slope_ref[piece, :] = (cdf + rest).astype(BF)
        total[piece, :] += mm(hidden, fc2_ref[...])

    for number in range(count):
        middle(number)

    @pl.when(step == blocks - 1)
    def _():
        def leave(number):
            piece = rows_of(number)
            low = total[piece, :].astype(BF)
            out_ref[piece, :] = low
            tap_ref[piece, :] = mm(low, tap_w_ref[...]) + tap_bias_ref[...]

        for number in range(count):
            leave(number)


def mlp_forward(
    tokens,
    attended,
    out_weight,
    out_bias,
    gain,
    shift,
    fc1_weight,
    fc1_bias,
    fc2_weight,
    fc2_bias,
    tap_weight,
    tap_bias,
    row_block,
):
    count, width = tokens.shape
    inner, channels = fc1_weight.shape[1], tap_weight.shape[1]
    blocks = inner // width
    vmem = pl.BlockSpec(memory_space=pltpu.VMEM)
    column = pl.BlockSpec((count, width), lambda i: (0, i))
    return pl.pallas_call(
        functools.partial(mlp_forward_kernel, blocks=blocks, row_block=row_block),
        grid=(blocks,),
        in_specs=[vmem] * 9
        + [
            pl.BlockSpec((width, width), lambda i: (0, i)),
            pl.BlockSpec((1, width), lambda i: (0, i)),
            pl.BlockSpec((width, width), lambda i: (i, 0)),
        ],
        out_specs=[vmem, vmem, column, column, vmem, vmem],
        out_shape=[
            jax.ShapeDtypeStruct((count, width), F32),
            jax.ShapeDtypeStruct((count, width), BF),
            jax.ShapeDtypeStruct((count, inner), BF),
            jax.ShapeDtypeStruct((count, inner), BF),
            jax.ShapeDtypeStruct((count, width), BF),
            jax.ShapeDtypeStruct((count, channels), F32),
        ],
        scratch_shapes=[pltpu.VMEM((count, width), F32)],
        compiler_params=pltpu.CompilerParams(vmem_limit_bytes=48 << 20),
        cost_estimate=pl.CostEstimate(
            flops=5 * count * width * inner,
            bytes_accessed=40 << 20,
            transcendentals=2 * count * inner,
        ),
        name="mlp_forward",
    )(
        tokens,
        attended,
        out_weight,
        out_bias,
        gain,
        shift,
        fc2_bias,
        tap_weight,
        tap_bias,
        fc1_weight,
        fc1_bias,
        fc2_weight,
    )


def shares_of(bits):
    return (2,) * bits


def mlp_backward_kernel(
    tap_grad_ref,
    cot_ref,
    out_tokens_ref,
    normed_ref,
    resid_ref,
    attended_ref,
    gain_ref,
    tap_w_ref,
    out_w_ref,
    hidden_ref,
    slope_ref,
    fc1_ref,
    fc2_ref,
    tap_dw_ref,
    out_dw_ref,
    fc1_dw_ref,
    fc2_dw_ref,
    resid_grad_ref,
    attended_grad_ref,
    wide_sums_ref,
    fc1_sums_ref,
    out_grad,
    low_grad,
    pre_grad,
    back,
    *,
    blocks,
    row_block,
    bits,
):
    step = pl.program_id(0)
    tokens, width = low_grad.shape
    count = 1 << bits
    depth = width // count
    shares = shares_of(bits)
    pieces = [pl.ds(k * row_block, row_block) for k in range(tokens // row_block)]

    @pl.when(step == 0)
    def _():
        total = jnp.zeros((1, width), F32)
        tap_total = jnp.zeros((1, tap_grad_ref.shape[1]), F32)
        for piece in pieces:
            tap_part = tap_grad_ref[piece, :]
            value = cot_ref[piece, :].astype(F32) + mm(tap_part, tap_w_ref[...], NT)
            out_grad[piece, :] = value
            low = value.astype(BF)
            low_grad[piece, :] = low
            back[piece, :] = jnp.zeros((row_block, width), F32)
            total = total + jnp.sum(low.astype(F32), axis=0, keepdims=True)
            tap_total = tap_total + jnp.sum(tap_part.astype(F32), axis=0, keepdims=True)
        wide_sums_ref[pl.ds(0, 1), :] = total
        wide_sums_ref[pl.ds(4, 1), :] = jnp.concatenate(
            [tap_total] * (width // tap_total.shape[1]), axis=1
        )
        weight = mm(out_tokens_ref[...], tap_grad_ref[...], TN).astype(BF)
        weight = jnp.concatenate(
            [weight, jnp.zeros((width, width - weight.shape[1]), BF)], axis=1
        )
        tap_dw_ref[0] = weight.reshape(shares + (depth, width))

    sums = jnp.zeros((1, pre_grad.shape[1]), F32)
    for piece in pieces:
        grads = mm(low_grad[piece, :], fc2_ref[...], NT) * slope_ref[piece, :].astype(F32)
        low = grads.astype(BF)
        pre_grad[piece, :] = low
        sums = sums + jnp.sum(low.astype(F32), axis=0, keepdims=True)
    fc1_sums_ref[...] = sums
    weight = mm(hidden_ref[...], low_grad[...], TN).astype(BF)
    per_share = weight.shape[0] // depth * blocks // count
    for place in range(weight.shape[0] // depth):
        fc2_dw_ref[place % per_share, place // per_share] = weight[
            place * depth : (place + 1) * depth
        ]
    weight = mm(normed_ref[...], pre_grad[...], TN).astype(BF)
    fc1_dw_ref[0] = weight.reshape(shares + (depth, width))

    for piece in pieces:
        back[piece, :] += mm(pre_grad[piece, :], fc1_ref[...], NT)

    @pl.when(step == blocks - 1)
    def _():
        gain = gain_ref[...]
        gain_total = jnp.zeros((1, width), F32)
        shift_total = jnp.zeros((1, width), F32)
        total = jnp.zeros((1, width), F32)
        for piece in pieces:
            grads = back[piece, :]
            unit, rstd = norm_stats(resid_ref[piece, :])
            scaled = grads * gain
            mean_one = jnp.mean(scaled, axis=-1, keepdims=True)
            mean_two = jnp.mean(scaled * unit, axis=-1, keepdims=True)
            value = out_grad[piece, :] + rstd * (scaled - mean_one - unit * mean_two)
            resid_grad_ref[piece, :] = value
            low = value.astype(BF)
            low_grad[piece, :] = low
            gain_total = gain_total + jnp.sum(grads * unit, axis=0, keepdims=True)
            shift_total = shift_total + jnp.sum(grads, axis=0, keepdims=True)
            total = total + jnp.sum(low.astype(F32), axis=0, keepdims=True)
            attended_grad_ref[piece, :] = mm(low, out_w_ref[...], NT).astype(BF)
        wide_sums_ref[pl.ds(1, 1), :] = gain_total
        wide_sums_ref[pl.ds(2, 1), :] = shift_total
        wide_sums_ref[pl.ds(3, 1), :] = total
        weight = mm(attended_ref[...], low_grad[...], TN).astype(BF)
        out_dw_ref[0] = weight.reshape(shares + (depth, width))


def mlp_backward(
    grad_tap,
    cotangent,
    out_tokens,
    normed,
    resid,
    attended,
    gain,
    tap_weight,
    out_weight,
    hidden,
    slope,
    fc1_weight,
    fc2_weight,
    row_block,
):
    tokens, width = resid.shape
    inner = hidden.shape[1]
    bits = axis_bits("rows")
    count = 1 << bits
    depth = width // count
    blocks = inner // width
    vmem = pl.BlockSpec(memory_space=pltpu.VMEM)
    column = pl.BlockSpec((tokens, width), lambda i: (0, i))
    fc2_chunks = inner // count // depth
    shares = shares_of(bits)
    share_step = count // blocks
    outs = pl.pallas_call(
        functools.partial(
            mlp_backward_kernel,
            blocks=blocks,
            row_block=row_block,
            bits=bits,
        ),
        grid=(blocks,),
        in_specs=[vmem] * 9
        + [
            column,
            column,
            pl.BlockSpec((width, width), lambda i: (0, i)),
            pl.BlockSpec((width, width), lambda i: (i, 0)),
        ],
        out_specs=[
            vmem,
            vmem,
            pl.BlockSpec((1,) + shares + (depth, width), lambda i: (i,) + (0,) * (bits + 2)),
            pl.BlockSpec((fc2_chunks, share_step, depth, width), lambda i: (0, i, 0, 0)),
            vmem,
            vmem,
            vmem,
            pl.BlockSpec((1, width), lambda i: (0, i)),
        ],
        out_shape=[
            jax.ShapeDtypeStruct((1,) + shares + (depth, width), BF),
            jax.ShapeDtypeStruct((1,) + shares + (depth, width), BF),
            jax.ShapeDtypeStruct((blocks,) + shares + (depth, width), BF),
            jax.ShapeDtypeStruct((fc2_chunks, count, depth, width), BF),
            jax.ShapeDtypeStruct((tokens, width), F32),
            jax.ShapeDtypeStruct((tokens, width), BF),
            jax.ShapeDtypeStruct((8, width), F32),
            jax.ShapeDtypeStruct((1, inner), F32),
        ],
        scratch_shapes=[
            pltpu.VMEM((tokens, width), F32),
            pltpu.VMEM((tokens, width), BF),
            pltpu.VMEM((tokens, width), BF),
            pltpu.VMEM((tokens, width), F32),
        ],
        compiler_params=pltpu.CompilerParams(vmem_limit_bytes=60 << 20),
        cost_estimate=pl.CostEstimate(
            flops=8 * tokens * width * inner, bytes_accessed=40 << 20, transcendentals=0
        ),
        name="mlp_backward",
    )(
        grad_tap,
        cotangent,
        out_tokens,
        normed,
        resid,
        attended,
        gain,
        tap_weight,
        out_weight,
        hidden,
        slope,
        fc1_weight,
        fc2_weight,
    )
    return outs


class Scatter:
    def __init__(self, bits, tokens, width, items):
        self.bits, self.tokens, self.width, self.items = bits, tokens, width, items
        self.orders = (tuple(range(bits - 1, -1, -1)), tuple(range(bits)))

    def scratch(self):
        slots = [pltpu.VMEM((2,) * self.bits + (self.tokens, self.width), BF)]
        for stage in range(self.bits):
            for _ in (0, 1):
                slots.append(
                    pltpu.VMEM(
                        (self.items,)
                        + (2,) * (self.bits - 1 - stage)
                        + (self.tokens // 2, self.width),
                        BF,
                    )
                )
        return slots + [
            pltpu.SemaphoreType.DMA((self.bits, 2)),
            pltpu.SemaphoreType.DMA((self.items, self.bits, 2)),
        ]

    def bind(self, slots):
        self.held = slots[0]
        self.landed = [(slots[1 + 2 * s], slots[2 + 2 * s]) for s in range(self.bits)]
        self.send_sem, self.recv_sem = slots[-2:]

    def place(self, half, stage, bit_value):
        index = [slice(None)] * self.bits
        for done in self.orders[half][:stage]:
            index[self.bits - 1 - done] = 0
        index[self.bits - 1 - self.orders[half][stage]] = bit_value
        size = self.tokens // 2
        return tuple(index) + (pl.ds(half * size, size),)

    def copy(self, item, stage, half):
        me, at = lax.axis_index("rows"), lax.axis_index("items")
        return pltpu.make_async_remote_copy(
            src_ref=self.held.at[self.place(half, stage, 1)],
            dst_ref=self.landed[stage][half].at[item],
            send_sem=self.send_sem.at[stage, half],
            recv_sem=self.recv_sem.at[item, stage, half],
            device_id=(at, flip(me, self.orders[half][stage])),
            device_id_type=MESH,
        )

    def start(self, item):
        for half in (0, 1):
            self.copy(item, 0, half).start()

    def advance(self, item, stage, finish):
        for half in (0, 1):
            self.copy(item, stage, half).wait_recv()
            at = self.place(half, stage, 0)
            if stage + 1 < self.bits:
                self.held[at] = add_low(self.held[at], self.landed[stage][half][item])
                self.copy(item, stage + 1, half).start()
            else:
                finish(
                    at[-1],
                    self.held[at].astype(F32) + self.landed[stage][half][item].astype(F32),
                )

    def drain(self, item):
        for stage in range(self.bits):
            for half in (0, 1):
                self.copy(item, stage, half).wait_send()


def attention_backward_kernel(
    valid_ref,
    q_ref,
    k_ref,
    v_ref,
    g_ref,
    o_ref,
    lse_ref,
    normed_ref,
    wq_ref,
    wk_ref,
    wv_ref,
    *refs,
    reducer,
    late,
    scatter,
    groups,
    items,
    kb,
    rounds,
    sources,
):
    early_sources = refs[:sources]
    grad_ref, sums_ref, early_out, late_out = refs[sources : sources + 4]
    slots = list(refs[sources + 4 :])
    q4, g4, acc, dkv, back, held = slots[:6]
    del slots[:6]
    early_slots = slots[: reducer.slots()]
    del slots[: reducer.slots()]
    late_slots = slots[: late.slots()]
    del slots[: late.slots()]
    reducer.bind(early_out, early_slots, sources=early_sources)
    late.bind(late_out, late_slots, held=held)
    scatter.bind(slots)
    step = pl.program_id(0)
    item, group = step // groups, step % groups
    t, n = q_ref.shape[1], k_ref.shape[1]
    width = back.shape[1]
    depth = width // (1 << reducer.row_bits)
    shares = shares_of(reducer.row_bits)
    me = lax.axis_index("rows")

    @pl.when(step == 0)
    def _():
        reducer.greet()
        reducer.begin()
        sums_ref[...] = jnp.zeros_like(sums_ref)

    q4[...] = spread_heads(q_ref[0] * jnp.asarray(HEAD_DIM**-0.5, BF))
    grads = spread_heads(g_ref[0])
    g4[...] = grads
    outs = jnp.concatenate([o_ref[0].astype(F32)] * HEADS_PER_GROUP, axis=0)
    product = grads.astype(F32) * outs
    high = product.astype(BF)
    low = (product - high.astype(F32)).astype(BF)
    ones = jnp.ones((8, GROUP), BF)
    dots = (mm(ones, high, NT) + mm(ones, low, NT))[:1]
    lse = lse_ref[0, 0, :1, :]
    acc[...] = jnp.zeros_like(acc)
    limit = valid_ref[item] * PC

    def turn(number):
        now = step * rounds + number
        reducer.step(now)
        late.step(now - ((items - 1) * groups + 1) * rounds)

    inner = n // kb
    each = rounds // inner

    def block_step(b, carry):
        at = pl.ds(pl.multiple_of(b * kb, kb), kb)
        keys, values = k_ref[0, at, :], v_ref[0, at, :]
        index = b * kb + lax.broadcasted_iota(jnp.int32, (kb, 1), 0)
        position = index + key_shift(index, n, t, me)
        bias = jnp.where(position < limit, 0.0, MASKED).astype(F32)
        scores = mm(keys, q4[...], NT)
        probs = jnp.exp2((scores * LOG2E + bias) - lse)
        grad_probs = mm(values, g4[...], NT)
        grad_scores = (probs * (grad_probs - dots)).astype(BF)
        dkv[at, pl.ds(GROUP, GROUP)] = mm(probs.astype(BF), g4[...]).astype(BF)
        dkv[at, pl.ds(0, GROUP)] = mm(grad_scores, q4[...]).astype(BF)
        acc[...] += mm(grad_scores, keys, TN)

        def rest(k, inner_carry):
            turn(b * each + k)
            return inner_carry

        lax.fori_loop(0, each, rest, 0)
        return carry

    lax.fori_loop(0, inner, block_step, 0)
    out = jnp.zeros((t, GROUP), F32)
    for h in range(HEADS_PER_GROUP):
        out = jnp.where(head_mask((t, GROUP), h), acc[pl.ds(h * t, t), :], out)
    dq = (out * HEAD_DIM**-0.5).astype(BF)

    for stage in range(scatter.bits):

        @pl.when((group == stage) & (item > 0))
        def _(stage=stage):
            def finish(rows, value):
                grad_ref[item - 1, rows, :] += value

            scatter.advance(item - 1, stage, finish)

    part = jnp.concatenate(
        [mm(normed_ref[0, pl.ds(0, t), :], dq, TN), mm(normed_ref[0], dkv[...], TN)], axis=1
    ).reshape(shares + (depth, width))
    before = held[group].astype(F32)
    held[group] = jnp.where(item == 0, part, before + part).astype(BF)
    sums_ref[group, pl.ds(0, 1), :] += jnp.sum(dq.astype(F32), axis=0, keepdims=True)
    sums_ref[group, pl.ds(1, 1), :] += jnp.sum(
        dkv[:, pl.ds(GROUP, GROUP)].astype(F32), axis=0, keepdims=True
    )

    @pl.when(item == items - 1)
    def _():
        late.begin_held(group)

    row_piece = n // 4
    both = jnp.concatenate([wk_ref[...], wv_ref[...]], axis=1)

    def project(k, carry):
        at = pl.ds(pl.multiple_of(k * row_piece, row_piece), row_piece)
        value = mm(dkv[at, :], both, NT)
        back[at, :] = jnp.where(group == 0, value, back[at, :] + value)
        return carry

    lax.fori_loop(0, 2, project, 0)

    @pl.when(step == items * groups - 1)
    def _():
        late.step((groups - 1) * rounds)

    lax.fori_loop(2, 4, project, 0)
    value = mm(dq, wq_ref[...], NT)
    grad_ref[item] = jnp.where(group == 0, value, grad_ref[item] + value)

    @pl.when(group == groups - 1)
    def _():
        @pl.when(item > 0)
        def _():
            scatter.drain(item - 1)

        for j in range(1 << scatter.bits):
            index = tuple(j >> b & 1 for b in range(scatter.bits - 1, -1, -1))
            scatter.held[index] = back[pl.ds(j * t, t), :].astype(BF)
        scatter.start(item)

    @pl.when(step == items * groups - 1)
    def _():
        start = ((items - 1) * groups + 1) * rounds

        last = items * groups * rounds

        def rest(now, carry):
            reducer.step(now)
            return carry

        def late_turn(k, carry):
            late.step(last - start + k * late.lag)
            return carry

        lax.fori_loop(last, max(last, reducer.steps), rest, 0)
        mark = 1

        for stage in range(scatter.bits):

            def finish(rows, value):
                grad_ref[items - 1, rows, :] += value

            lax.fori_loop(mark, 2 + 2 * stage, late_turn, 0)
            mark = 2 + 2 * stage
            scatter.advance(items - 1, stage, finish)
        lax.fori_loop(mark, late.phases, late_turn, 0)
        scatter.drain(items - 1)
        reducer.finish()
        late.finish()


def attention_backward(
    valid_rows, queries, keys, values, grads, outs, lse, normed, qkv_weight, packed, collective_id
):
    items, t, d = queries.shape
    n = keys.shape[1]
    groups = d // GROUP
    bits = axis_bits("rows")
    depth = d >> bits
    rows4 = HEADS_PER_GROUP * t
    rounds = 8
    reducer = Reducer(
        sum(a.shape[0] for a in packed), depth, d, bits, axis_bits("items"), 3, 7
    )
    late = Reducer(groups, depth, d, bits, axis_bits("items"), rounds, 8)
    scatter = Scatter(bits, t, d, items)
    query_spec = pl.BlockSpec((1, t, GROUP), lambda i: (i // groups, 0, i % groups))
    vmem = pl.BlockSpec(memory_space=pltpu.VMEM)

    def weight_spec(kind):
        return pl.BlockSpec((d, GROUP), lambda i: (0, kind * groups + i % groups))

    key_spec = pl.BlockSpec((1, n, GROUP), lambda i: (i // groups, 0, i % groups))

    outs = pl.pallas_call(
        functools.partial(
            attention_backward_kernel,
            reducer=reducer,
            late=late,
            scatter=scatter,
            groups=groups,
            items=items,
            kb=n // 4,
            rounds=rounds,
            sources=len(packed),
        ),
        grid=(items * groups,),
        in_specs=[
            pl.BlockSpec(memory_space=pltpu.SMEM),
            query_spec,
            key_spec,
            key_spec,
            query_spec,
            query_spec,
            pl.BlockSpec((1, 1, 8, rows4), lambda i: (i // groups, i % groups, 0, 0)),
            pl.BlockSpec((1, n, d), lambda i: (i // groups, 0, 0), pipeline_mode=pl.Buffered(1)),
            weight_spec(0),
            weight_spec(1),
            weight_spec(2),
        ]
        + [pl.BlockSpec(memory_space=pl.ANY)] * len(packed),
        out_specs=[vmem] * 2 + [pl.BlockSpec(memory_space=pl.ANY)] * 2,
        out_shape=[
            jax.ShapeDtypeStruct((items, t, d), F32),
            jax.ShapeDtypeStruct((groups, 8, GROUP), F32),
            reducer.out_shape(),
            late.out_shape(),
        ],
        scratch_shapes=[
            pltpu.VMEM((rows4, GROUP), BF),
            pltpu.VMEM((rows4, GROUP), BF),
            pltpu.VMEM((rows4, GROUP), F32),
            pltpu.VMEM((n, 2 * GROUP), BF),
            pltpu.VMEM((n, d), F32),
            pltpu.VMEM((groups,) + shares_of(bits) + (depth, d), BF),
        ]
        + reducer.scratch()
        + late.scratch()
        + scatter.scratch(),
        compiler_params=pltpu.CompilerParams(
            vmem_limit_bytes=63 << 20, collective_id=collective_id, has_side_effects=True
        ),
        cost_estimate=pl.CostEstimate(
            flops=100 * items * t * n * d,
            bytes_accessed=40 << 20,
            transcendentals=12 * items * t * n,
        ),
        name="attention_backward",
    )(
        valid_rows,
        queries,
        keys,
        values,
        grads,
        outs,
        lse,
        normed,
        qkv_weight,
        qkv_weight,
        qkv_weight,
        *packed,
    )
    return outs


def shards(
    tokens,
    valid_rows,
    dataset_ids,
    shift_flags,
    norm_gains,
    norm_biases,
    qkv_weight,
    qv_bias,
    out_weight,
    out_bias,
    fc1_weight,
    fc1_bias,
    fc2_weight,
    fc2_bias,
    tap_weight,
    tap_bias,
    conv_weights,
    conv_biases,
    table_gain,
    table_shift,
    token_cotangent,
    joined_cotangent,
):
    items_here, tok_here, width = tokens.shape
    rows_here = tok_here // PC
    channels = tap_weight.shape[1]
    row_index = lax.axis_index("rows")
    row_count = lax.axis_size("rows")
    last_index = row_count - 1

    flat_in = tokens.reshape(-1, width).astype(F32)
    queries, keys, values, attended, lses, normed_all = attention_forward(
        valid_rows,
        tokens,
        norm_gains[:1],
        norm_biases[:1],
        qkv_weight,
        qv_bias[None, :width],
        qv_bias[None, width:],
        5,
    )
    attended_flat = attended.reshape(-1, width)
    resid, normed_two, hidden, hidden_slope, output_low, tap_pre = mlp_forward(
        tokens.reshape(-1, width),
        attended_flat,
        out_weight,
        out_bias[None],
        norm_gains[1:2],
        norm_biases[1:2],
        fc1_weight,
        fc1_bias[None],
        fc2_weight,
        fc2_bias[None],
        tap_weight,
        tap_bias[None],
        tok_here,
    )
    grid_rows = row_index * rows_here + jnp.arange(rows_here, dtype=jnp.int32)
    row_valid = (grid_rows[None, :] < valid_rows[:, None]).astype(F32)
    token_valid = jnp.broadcast_to(
        row_valid[:, :, None], (items_here, rows_here, PC)
    ).reshape(-1, 1)
    field = (tap_pre * token_valid).reshape(items_here, rows_here, PC, channels)

    choose = (
        dataset_ids[:, None] == jnp.arange(table_gain.shape[0], dtype=jnp.int32)[None, :]
    ).astype(F32)
    flag_value = shift_flags.astype(F32)[:, None]
    gain_pick = jnp.dot(choose, table_gain, precision=highest)
    shift_pick = jnp.dot(choose, table_shift, precision=highest)
    factor = 1.0 + flag_value * (gain_pick - 1.0)
    offset = flag_value * shift_pick
    depth = width // row_count
    joined, grad_field, conv_grads, grad_conv_biases, table_sums = refine(
        field, conv_weights, conv_biases, factor, offset, joined_cotangent, depth
    )
    grad_table_gain = jnp.dot(choose.T, flag_value * table_sums[0], precision=highest)
    grad_table_shift = jnp.dot(choose.T, flag_value * table_sums[1], precision=highest)

    grad_tap = (grad_field[:, :, :PC].reshape(-1, channels) * token_valid).astype(BF)
    (
        tap_grads,
        out_grads,
        fc1_grads,
        fc2_grads,
        grad_resid,
        grad_attended,
        wide_sums,
        fc1_sums,
    ) = mlp_backward(
        grad_tap,
        token_cotangent.reshape(-1, width),
        output_low,
        normed_two,
        resid,
        attended_flat,
        norm_gains[1:2],
        tap_weight,
        out_weight,
        hidden,
        hidden_slope,
        fc1_weight,
        fc2_weight,
        tok_here,
    )
    shares = shares_of(axis_bits("rows"))
    fc2_grads = fc2_grads.reshape(fc2_grads.shape[:1] + shares + fc2_grads.shape[2:])
    grads_in, qkv_sums, early_sum, late_sum = attention_backward(
        valid_rows,
        queries,
        keys,
        values,
        grad_attended.reshape(tokens.shape),
        attended,
        lses,
        normed_all.reshape(keys.shape),
        qkv_weight,
        [conv_grads, tap_grads, fc2_grads, fc1_grads, out_grads],
        3,
    )
    grad_in_norm, grad_gain_one, grad_shift_one = norm_back(
        flat_in, norm_gains[0], grads_in.reshape(-1, width)
    )
    grad_tokens = (grad_resid + grad_in_norm).reshape(tokens.shape)

    groups = width // GROUP
    inner = fc1_weight.shape[1]
    kernels = conv_weights.shape[1]
    convs = conv_weights.shape[0]
    places = kernels // row_count // depth
    fc2_chunks = inner // row_count // depth
    blocks = inner // width
    table = [
        (conv, place * channels, channels, 0, conv, place * depth, 0)
        for conv in range(convs)
        for place in range(places)
    ]
    table += [(convs, 0, channels, 1, None, 0, 0)]
    first = convs + 1
    table += [(first + k, 0, width, 2, None, k * depth, 0) for k in range(fc2_chunks)]
    first += fc2_chunks
    table += [(first + k, 0, width, 3, None, 0, k * width) for k in range(blocks)]
    table += [(first + blocks, 0, width, 4, None, 0, 0)]
    share_conv, share_tap, share_fc2, share_fc1, share_out = unpack(
        early_sum,
        table,
        [
            (convs, kernels // row_count, channels),
            (depth, channels),
            (inner // row_count, width),
            (depth, inner),
            (depth, width),
        ],
    )
    (share_qkv,) = unpack(
        late_sum,
        [
            (group, kind * GROUP, GROUP, 0, None, 0, (kind * groups + group) * GROUP)
            for group in range(groups)
            for kind in range(3)
        ],
        [(depth, 3 * width)],
    )

    small = [
        jnp.stack([grad_gain_one, wide_sums[1]]),
        jnp.stack([grad_shift_one, wide_sums[2]]),
        jnp.concatenate([qkv_sums[:, 0].reshape(-1), qkv_sums[:, 1].reshape(-1)]),
        wide_sums[3],
        fc1_sums[0],
        wide_sums[0],
        wide_sums[4, :channels],
        grad_conv_biases,
        grad_table_gain,
        grad_table_shift,
    ]
    packed = jnp.concatenate(
        [
            array.reshape(row_count, -1)
            if array.ndim == 1
            else jnp.swapaxes(array.reshape(array.shape[0], row_count, -1), 0, 1).reshape(
                row_count, -1
            )
            for array in small
        ],
        axis=1,
    )
    packed = jnp.pad(packed, ((0, 0), (0, -packed.shape[1] % 1024)))
    summed = all_sum(packed.reshape(row_count, -1, 128), 4).reshape(-1)
    outs, place = [], 0
    for array in small:
        size = array.size // row_count
        piece = summed[place : place + size]
        place += size
        outs.append(piece if array.ndim == 1 else piece.reshape(array.shape[0], -1))
    (
        out_gains,
        out_shifts,
        out_qv,
        out_out,
        out_fc1,
        out_fc2,
        out_tap,
        out_conv,
        out_table_gain,
        out_table_shift,
    ) = outs
    return (
        output_low.reshape(tokens.shape),
        joined,
        grad_tokens,
        out_gains,
        out_shifts,
        share_qkv,
        out_qv,
        share_out,
        out_out,
        share_fc1,
        out_fc1,
        share_fc2,
        out_fc2,
        share_tap,
        out_tap,
        share_conv,
        out_conv,
        out_table_gain,
        out_table_shift,
    )


def solution(mesh):
    return jax.shard_map(
        shards,
        mesh=mesh,
        in_specs=(P("items", "rows", None), P("items"), P("items"), P("items"))
        + (P(),) * 16
        + (P("items", "rows", None), P("items", "rows", None, None)),
        out_specs=(
            P("items", "rows", None),
            P("items", "rows", None, None),
            P("items", "rows", None),
            P(None, "rows"),
            P(None, "rows"),
            P("rows", None),
            P("rows"),
            P("rows", None),
            P("rows"),
            P("rows", None),
            P("rows"),
            P("rows", None),
            P("rows"),
            P("rows", None),
            P("rows"),
            P(None, "rows", None),
            P(None, "rows"),
            P(None, "rows"),
            P(None, "rows"),
        ),
        check_vma=False,
    )
```

```python
import functools

import jax
import jax.numpy as jnp
from jax import lax
from jax.experimental import pallas as pl
from jax.experimental.pallas import tpu as pltpu
from jax.sharding import PartitionSpec as P

HEAD_DIM = 64
PC = 40
GROUP = 256
HEADS_PER_GROUP = GROUP // HEAD_DIM

BF = jnp.bfloat16
F32 = jnp.float32
LOG2E = 1.4426950408889634
MASKED = -1e30
NN = (((1,), (0,)), ((), ()))
NT = (((1,), (1,)), ((), ()))
TN = (((0,), (0,)), ((), ()))

epsilon = 1e-06
highest = lax.Precision.HIGHEST


def mm(left, right, dims=NN):
    return lax.dot_general(left, right, dims, preferred_element_type=F32)


def normal_parts(values):
    bell = jnp.exp2(values * values * (-0.5 * LOG2E))
    t = 1.0 / (1.0 + (0.3275911 * 0.7071067811865476) * jnp.abs(values))
    poly = t * (
        0.5 * 0.254829592
        + t
        * (
            0.5 * -0.284496736
            + t * (0.5 * 1.421413741 + t * (0.5 * -1.453152027 + t * (0.5 * 1.061405429)))
        )
    )
    tail = poly * bell
    cdf = jnp.where(values >= 0.0, 1.0 - tail, tail)
    return cdf, values * bell * 0.3989422804014327


def gelu_exact(values):
    return values * normal_parts(values)[0]


def gelu_slope(values):
    cdf, slope = normal_parts(values)
    return cdf + slope


def gelu_back(values, grad_out):
    return gelu_slope(values) * grad_out


def norm_stats(values):
    centre = jnp.mean(values, axis=-1, keepdims=True)
    centred = values - centre
    spread = jnp.mean(centred * centred, axis=-1, keepdims=True)
    rstd = lax.rsqrt(spread + epsilon)
    return centred * rstd, rstd


def layer_norm(values, gain, shift):
    return norm_stats(values)[0] * gain + shift


def norm_back(values, gain, grad_out):
    unit, rstd = norm_stats(values)
    scaled = grad_out * gain
    mean_one = jnp.mean(scaled, axis=-1, keepdims=True)
    mean_two = jnp.mean(scaled * unit, axis=-1, keepdims=True)
    result = rstd * (scaled - mean_one - unit * mean_two)
    return result, jnp.sum(grad_out * unit, axis=0), jnp.sum(grad_out, axis=0)


def axis_bits(axis):
    return (lax.axis_size(axis) - 1).bit_length()


def add_low(first, second):
    return (first.astype(F32) + second.astype(F32)).astype(BF)


def head_mask(shape, head):
    lane = lax.broadcasted_iota(jnp.int32, shape, 1)
    return lane // HEAD_DIM == head


def spread_heads(block):
    zero = jnp.zeros_like(block)
    return jnp.concatenate(
        [jnp.where(head_mask(block.shape, h), block, zero) for h in range(HEADS_PER_GROUP)],
        axis=0,
    )


WIDE = 48
EDGES = 10
FIELD_EDGE, TALL_EDGE = 4, 5


def refine_kernel(
    field_ref,
    weight_ref,
    bias_ref,
    factor_ref,
    offset_ref,
    cot_ref,
    joined_ref,
    grad_ref,
    dw_ref,
    db_ref,
    sums_ref,
    acts,
    slopes,
    grads3,
    work,
    frame,
    tall,
    lane2,
    edge,
    halo,
    send_sem,
    recv_sem,
    *,
    items,
    rows,
    count,
    depth,
):
    bits = (count - 1).bit_length()
    per_share = 9 * field_ref.shape[-1] // count // depth
    me = lax.axis_index("rows")
    here = lax.axis_index("items")
    channels = field_ref.shape[-1]
    flat = items * rows * WIDE
    lanes = channels // 128
    column = lax.broadcasted_iota(jnp.int32, (WIDE, channels), 0)
    inside = column < PC

    barrier = pltpu.get_barrier_semaphore()
    for step in (-1, 1):

        @pl.when((me + step >= 0) & (me + step < count))
        def _():
            pl.semaphore_signal(
                barrier, inc=1, device_id=(here, me + step), device_id_type=pl.DeviceIdType.MESH
            )

    @pl.when((me > 0) & (me < count - 1))
    def _():
        pl.semaphore_wait(barrier, 2)

    @pl.when((me == 0) | (me == count - 1))
    def _():
        pl.semaphore_wait(barrier, 1)

    def each(side):
        return (me > 0) if side == 0 else (me < count - 1)

    def copy(e, side):
        return pltpu.make_async_remote_copy(
            src_ref=edge.at[e, side],
            dst_ref=halo.at[e, 1 - side],
            send_sem=send_sem.at[e, side],
            recv_sem=recv_sem.at[e, 1 - side],
            device_id=(here, me + (2 * side - 1)),
            device_id_type=pl.DeviceIdType.MESH,
        )

    def send(e):
        for side in (0, 1):

            @pl.when(each(side))
            def _():
                copy(e, side).start()

    def receive(e):
        for side in (0, 1):

            @pl.when(each(side))
            def _():
                pltpu.make_async_remote_copy(
                    src_ref=edge.at[e, side],
                    dst_ref=halo.at[e, side],
                    send_sem=send_sem.at[e, side],
                    recv_sem=recv_sem.at[e, side],
                    device_id=(here, me + (2 * side - 1)),
                    device_id_type=pl.DeviceIdType.MESH,
                ).wait_recv()

            @pl.when(jnp.logical_not(each(side)))
            def _():
                halo[e, side] = jnp.zeros(halo.shape[2:], BF)

    def shifted(values, flip):
        before = pltpu.roll(values, 1, 0)
        after = pltpu.roll(values, WIDE - 1, 0)
        parts = [after, values, before] if flip else [before, values, after]
        return jnp.concatenate([part.astype(BF) for part in parts], axis=1)

    def all_rows(body, e):
        for item in range(items):
            for row, side in ((0, 0), (rows - 1, 1)):
                body(item, row, (e, side))
        send(e)

        def step(row, carry):
            for item in range(items):
                body(item, row, None)
            return carry

        lax.fori_loop(1, rows - 1, step, 0)

    def spread_halo(target, e, flip):
        for side, row in ((0, 0), (1, rows + 1)):
            for item in range(items):
                target[item, row] = shifted(halo[e, side, item].astype(F32), flip)

    for item in range(items):
        factor = factor_ref[pl.ds(item, 1), :]

        def back(row, carry, item=item, factor=factor):
            whole = cot_ref[item, row].astype(F32) * factor
            for part in range(lanes):
                lane2[part, pl.ds(0, 2 * PC), :] = whole[:, part * 128 : (part + 1) * 128]
            even, odd = (
                jnp.concatenate(
                    [lane2[part, pl.ds(start, PC, stride=2), :] for part in range(lanes)], axis=1
                )
                for start in (0, 1)
            )
            place = lax.broadcasted_iota(jnp.int32, (PC, channels), 0)
            even_next = jnp.where(place == PC - 1, odd, pltpu.roll(even, PC - 1, 0))
            odd_prev = jnp.where(place == 0, even, pltpu.roll(odd, 1, 0))
            tall[item, row + 1, pl.ds(0, PC), :] = 0.75 * (even + odd) + 0.25 * (
                even_next + odd_prev
            )
            tall[item, row + 1, pl.ds(PC, WIDE - PC), :] = jnp.zeros((WIDE - PC, channels), F32)
            return carry

        lax.fori_loop(0, 2 * rows, back, 0)
        edge[TALL_EDGE, 0, item] = tall[item, 1].astype(BF)
        edge[TALL_EDGE, 1, item] = tall[item, 2 * rows].astype(BF)
    send(TALL_EDGE)

    def activate(source, which):
        def body(item, row, out):
            values = source[item, row]
            cdf, rest = normal_parts(values)
            act = jnp.where(inside, values * cdf, 0.0)
            slopes[which, item, row] = cdf + rest
            acts[which, item, row + 1] = shifted(act, False)
            if out is not None:
                edge[out[0], out[1], item] = act.astype(BF)

        all_rows(body, which)

    def weight_of(conv, kr):
        return weight_ref[conv, pl.ds(kr * 3 * channels, 3 * channels), :]

    def lhs(source, item, first, number):
        return source[item, pl.ds(first, number)].reshape(number * WIDE, -1)

    def forward(conv, add):
        bias = bias_ref[pl.ds(conv, 1), :]
        for item in range(items):
            centre = mm(lhs(acts.at[conv], item, 1, rows), weight_of(conv, 1)) + bias
            if add:
                centre = centre + frame[item, pl.ds(1, rows)].reshape(rows * WIDE, channels)
            work[item] = centre.reshape(rows, WIDE, channels)
            upper = mm(lhs(acts.at[conv], item, 1, rows - 1), weight_of(conv, 0))
            work[item, pl.ds(1, rows - 1)] += upper.reshape(rows - 1, WIDE, channels)
            lower = mm(lhs(acts.at[conv], item, 2, rows - 1), weight_of(conv, 2))
            work[item, pl.ds(0, rows - 1)] += lower.reshape(rows - 1, WIDE, channels)
        receive(conv)
        spread_halo(acts.at[conv], conv, False)
        for kr, source, row in ((0, 0, 0), (2, rows + 1, rows - 1)):
            block = jnp.concatenate([acts[conv, item, source] for item in range(items)], axis=0)
            extra = mm(block, weight_of(conv, kr))
            for item in range(items):
                work[item, row] += extra[item * WIDE : (item + 1) * WIDE]

    def keep_field(source):
        for item in range(items):
            frame[item, pl.ds(1, rows)] = source[item]

    keep_field(field_ref)
    for unit in (0, 1):
        activate(field_ref if unit == 0 else work, 2 * unit)
        forward(2 * unit, False)
        activate(work, 2 * unit + 1)
        forward(2 * unit + 1, True)
        keep_field(work)

    for item in range(items):
        edge[FIELD_EDGE, 0, item] = frame[item, 1].astype(BF)
        edge[FIELD_EDGE, 1, item] = frame[item, rows].astype(BF)
    send(FIELD_EDGE)

    receive(TALL_EDGE)
    for item in range(items):
        tall[item, 0] = jnp.where(me == 0, tall[item, 1], halo[TALL_EDGE, 0, item].astype(F32))
        tall[item, 2 * rows + 1] = jnp.where(
            me == count - 1, tall[item, 2 * rows], halo[TALL_EDGE, 1, item].astype(F32)
        )

        def fold(row, carry, item=item):
            grad_ref[item, row] = 0.75 * (
                tall[item, 2 * row + 1] + tall[item, 2 * row + 2]
            ) + 0.25 * (tall[item, 2 * row] + tall[item, 2 * row + 3])
            return carry

        lax.fori_loop(0, rows, fold, 0)

    receive(FIELD_EDGE)
    for item in range(items):
        frame[item, 0] = jnp.where(me == 0, frame[item, 1], halo[FIELD_EDGE, 0, item].astype(F32))
        frame[item, rows + 1] = jnp.where(
            me == count - 1, frame[item, rows], halo[FIELD_EDGE, 1, item].astype(F32)
        )
        factor = factor_ref[pl.ds(item, 1), :]
        offset = offset_ref[pl.ds(item, 1), :]

        def widen(row, carry, item=item, factor=factor, offset=offset):
            gain_sum, shift_sum = carry
            centre = frame[item, row + 1]
            for half in (0, 1):
                line = 0.75 * centre + 0.25 * frame[item, row + 2 * half]
                before = jnp.where(column == 0, line, pltpu.roll(line, 1, 0))
                after = jnp.where(column == PC - 1, line, pltpu.roll(line, WIDE - 1, 0))
                for start, side in ((0, before), (1, after)):
                    mixed = 0.75 * line + 0.25 * side
                    for part in range(lanes):
                        lane2[part, pl.ds(start, WIDE, stride=2), :] = mixed[
                            :, part * 128 : (part + 1) * 128
                        ]
                wide = jnp.concatenate(
                    [lane2[part, pl.ds(0, 2 * PC), :] for part in range(lanes)], axis=1
                )
                joined_ref[item, 2 * row + half] = (wide * factor + offset).astype(BF)
                cot = cot_ref[item, 2 * row + half].astype(F32)
                gain_sum = gain_sum + jnp.sum((cot * wide).reshape(-1, 8, channels), axis=0)
                shift_sum = shift_sum + jnp.sum(cot.reshape(-1, 8, channels), axis=0)
            return gain_sum, shift_sum

        zero = jnp.zeros((8, channels), F32)
        gain_sum, shift_sum = lax.fori_loop(0, rows, widen, (zero, zero))
        sums_ref[0, pl.ds(item, 1), :] = jnp.sum(gain_sum, axis=0, keepdims=True)
        sums_ref[1, pl.ds(item, 1), :] = jnp.sum(shift_sum, axis=0, keepdims=True)

    def grad_pass(conv, make):
        e = 6 + conv

        def body(item, row, out):
            values = jnp.where(inside, make(item, row), 0.0).astype(BF).astype(F32)
            grads3[item, row + 1] = shifted(values, True)
            if out is not None:
                edge[out[0], out[1], item] = values.astype(BF)

        all_rows(body, e)
        middle = jnp.concatenate(
            [
                grads3[item, pl.ds(1, rows), :, pl.ds(channels, channels)].reshape(
                    rows * WIDE, channels
                )
                for item in range(items)
            ],
            axis=0,
        )
        for kr in range(3):
            block = jnp.concatenate(
                [lhs(acts.at[conv], item, kr, rows) for item in range(items)], axis=0
            )
            weight = mm(block, middle, TN).astype(BF)
            pieces = 3 * channels // depth
            for k in range(pieces):
                share, place = divmod(kr * pieces + k, per_share)
                at = tuple(share >> b & 1 for b in range(bits - 1, -1, -1))
                dw_ref[(conv,) + at + (slice(None), pl.ds(place * channels, channels))] = weight[
                    k * depth : (k + 1) * depth
                ]
        ones = jnp.ones((8, flat), BF)
        db_ref[pl.ds(conv, 1), :] = mm(ones, middle)[:1]

        def product(block, kr):
            total = None
            for kc in range(3):
                part = mm(
                    block[:, kc * channels : (kc + 1) * channels],
                    weight_ref[conv, pl.ds((kr * 3 + kc) * channels, channels), :],
                    NT,
                )
                total = part if total is None else total + part
            return total

        for item in range(items):
            work[item] = product(lhs(grads3, item, 1, rows), 1).reshape(rows, WIDE, channels)
            work[item, pl.ds(1, rows - 1)] += product(lhs(grads3, item, 1, rows - 1), 2).reshape(
                rows - 1, WIDE, channels
            )
            work[item, pl.ds(0, rows - 1)] += product(lhs(grads3, item, 2, rows - 1), 0).reshape(
                rows - 1, WIDE, channels
            )
        receive(e)
        spread_halo(grads3, e, True)
        for kr, source, row in ((2, 0, 0), (0, rows + 1, rows - 1)):
            block = jnp.concatenate([grads3[item, source] for item in range(items)], axis=0)
            extra = product(block, kr)
            for item in range(items):
                work[item, row] += extra[item * WIDE : (item + 1) * WIDE]

    for unit in (1, 0):
        first, second = 2 * unit, 2 * unit + 1
        grad_pass(second, lambda item, row: grad_ref[item, row])
        grad_pass(first, lambda item, row: work[item, row] * slopes[second, item, row])

        def gather(row, carry, first=first):
            for item in range(items):
                grad_ref[item, row] += work[item, row] * slopes[first, item, row]
            return carry

        lax.fori_loop(0, rows, gather, 0)

    for e in range(EDGES):
        for side in (0, 1):

            @pl.when(each(side))
            def _():
                copy(e, side).wait_send()


def refine(field, conv_weights, conv_biases, factor, offset, cotangent, depth):
    items, rows, _, channels = field.shape
    count = lax.axis_size("rows")
    padded = jnp.pad(field, ((0, 0), (0, 0), (0, WIDE - PC), (0, 0)))
    vmem = pl.BlockSpec(memory_space=pltpu.VMEM)
    pixels = items * rows * PC
    outs = pl.pallas_call(
        functools.partial(refine_kernel, items=items, rows=rows, count=count, depth=depth),
        in_specs=[vmem] * 6,
        out_specs=[vmem] * 5,
        out_shape=[
            jax.ShapeDtypeStruct((items, 2 * rows, 2 * PC, channels), BF),
            jax.ShapeDtypeStruct((items, rows, WIDE, channels), F32),
            jax.ShapeDtypeStruct(
                conv_weights.shape[:1]
                + (2,) * axis_bits("rows")
                + (depth, conv_weights.shape[1] // count // depth * channels),
                BF,
            ),
            jax.ShapeDtypeStruct(conv_biases.shape, F32),
            jax.ShapeDtypeStruct((2, items, channels), F32),
        ],
        scratch_shapes=[
            pltpu.VMEM((4, items, rows + 2, WIDE, 3 * channels), BF),
            pltpu.VMEM((4, items, rows, WIDE, channels), F32),
            pltpu.VMEM((items, rows + 2, WIDE, 3 * channels), BF),
            pltpu.VMEM((items, rows, WIDE, channels), F32),
            pltpu.VMEM((items, rows + 2, WIDE, channels), F32),
            pltpu.VMEM((items, 2 * rows + 2, WIDE, channels), F32),
            pltpu.VMEM((channels // 128, 2 * WIDE, 128), F32),
            pltpu.VMEM((EDGES, 2, items, WIDE, channels), BF),
            pltpu.VMEM((EDGES, 2, items, WIDE, channels), BF),
            pltpu.SemaphoreType.DMA((EDGES, 2)),
            pltpu.SemaphoreType.DMA((EDGES, 2)),
        ],
        compiler_params=pltpu.CompilerParams(
            vmem_limit_bytes=56 << 20, collective_id=0, has_side_effects=True
        ),
        cost_estimate=pl.CostEstimate(
            flops=2 * 12 * pixels * 9 * channels * channels,
            bytes_accessed=20 << 20,
            transcendentals=8 * pixels * channels,
        ),
        name="refine",
    )(padded, conv_weights, conv_biases, factor, offset, cotangent)
    return outs


MESH = pl.DeviceIdType.MESH


def flip(index, bit):
    return index + (1 - 2 * (index // (1 << bit) % 2)) * (1 << bit)


class Reducer:
    def __init__(self, chunks, depth, strip, row_bits, item_bits, space, lag):
        self.chunks, self.depth, self.lanes = chunks, depth, strip // 2
        self.space, self.lag = space, lag
        self.row_bits, self.item_bits = row_bits, item_bits
        self.orders = (tuple(range(row_bits - 1, -1, -1)), tuple(range(row_bits)))
        self.far = max(item_bits - 2, 0)
        self.phases = 1 + row_bits + 1 + self.far + 1 + 1

    def scratch(self):
        c, half = self.chunks, self.depth // 2
        shares = (2,) * self.row_bits
        slots = [
            pltpu.VMEM((c,) + shares + (self.depth, self.lanes), BF),
            pltpu.VMEM((2,) + shares + (self.depth, self.lanes), BF),
        ]
        for stage in range(self.row_bits):
            for _ in (0, 1):
                slots.append(pltpu.VMEM((c,) + (2,) * (self.row_bits - 1 - stage) + (half, self.lanes), BF))
        slots.append(pltpu.VMEM((c, half, self.lanes), BF))
        for _ in range(self.far):
            slots.append(pltpu.VMEM((c, half, self.lanes), BF))
            slots.append(pltpu.VMEM((c, half, self.lanes), BF))
        arrivals = 1 + 2 * self.row_bits + 1 + self.far + 1 + 1
        sends = 1 + 2 * self.row_bits + 1 + self.far + 1 + 1
        return slots + [
            pltpu.VMEM((2, c, self.depth, self.lanes), BF),
            pltpu.SemaphoreType.DMA((2,)),
            pltpu.SemaphoreType.DMA((arrivals, c)),
            pltpu.SemaphoreType.DMA((sends,)),
        ]

    def slots(self):
        return len(self.scratch())

    def out_shape(self):
        return jax.ShapeDtypeStruct((2, self.chunks, self.depth, self.lanes), BF)

    def bind(self, out_ref, slots, sources=None, held=None):
        slots = list(slots)
        self.result, self.sources, self.held = out_ref, sources, held
        self.total, self.ring = slots[0], slots[1]
        self.row_in = [
            (slots[2 + 2 * stage], slots[3 + 2 * stage]) for stage in range(self.row_bits)
        ]
        rest = slots[2 + 2 * self.row_bits :]
        self.near_in = rest[0]
        self.far_out = [rest[1 + 2 * k] for k in range(self.far)]
        self.far_in = [rest[2 + 2 * k] for k in range(self.far)]
        self.out, self.ring_sem, self.recv_sem, self.send_sem = rest[-4:]
        self.me = lax.axis_index("rows")
        self.at = lax.axis_index("items")
        self.core = self.at % 2
        self.near = self.at // 2 % 2

    def peers(self):
        found = [(flip(self.at, bit), self.me) for bit in range(self.item_bits)]
        return found + [(self.at, flip(self.me, bit)) for bit in range(self.row_bits)]

    def greet(self):
        barrier = pltpu.get_barrier_semaphore()
        for peer in self.peers():
            pl.semaphore_signal(barrier, inc=1, device_id=peer, device_id_type=MESH)
        pl.semaphore_wait(barrier, len(self.peers()))

    def remote(self, source, target, arrival, sent, chunk, peer):
        return pltpu.make_async_remote_copy(
            src_ref=source,
            dst_ref=target,
            send_sem=self.send_sem.at[sent],
            recv_sem=self.recv_sem.at[arrival, chunk],
            device_id=peer,
            device_id_type=MESH,
        )

    def strip(self, ref, index, mine):
        side = self.core if mine else 1 - self.core
        lanes = pl.ds(pl.multiple_of(side * self.lanes, self.lanes), self.lanes)
        return ref.at[(index,) + (slice(None),) * (self.row_bits + 1) + (lanes,)]

    def core_copy(self, source, chunk):
        return self.remote(
            source, self.total.at[chunk], 0, 0, chunk, (flip(self.at, 0), self.me)
        )

    def begin(self):
        base = 0
        for ref in self.sources:

            def go(index, carry, ref=ref, base=base):
                self.core_copy(self.strip(ref, index, False), base + index).start()
                return carry

            lax.fori_loop(0, ref.shape[0], go, 0)
            base += ref.shape[0]
        self.fetch(0)

    def begin_held(self, chunk):
        self.core_copy(self.strip(self.held, chunk, False), chunk).start()

    def fetch(self, chunk):
        base = 0
        for ref in self.sources:

            @pl.when((chunk >= base) & (chunk < base + ref.shape[0]))
            def _(ref=ref, base=base):
                index = jnp.clip(chunk - base, 0, ref.shape[0] - 1)
                pltpu.make_async_copy(
                    self.strip(ref, index, True),
                    self.ring.at[chunk % 2],
                    self.ring_sem.at[chunk % 2],
                ).start()

            base += ref.shape[0]

    def add_mine(self, chunk):
        if self.held is not None:
            block = self.held[chunk]
            side = (slice(None),) * (self.row_bits + 1)
            block = jnp.where(
                self.core == 0,
                block[side + (slice(0, self.lanes),)],
                block[side + (slice(self.lanes, None),)],
            )
        else:
            slot = chunk % 2
            pltpu.make_async_copy(
                self.total.at[chunk], self.ring.at[slot], self.ring_sem.at[slot]
            ).wait()
            block = self.ring[slot]
        self.total[chunk] = add_low(self.total[chunk], block)

    def bit(self, which):
        return self.me // (1 << which) % 2

    def shares(self, half, stage, sent):
        order = self.orders[half]
        index = [slice(None)] * self.row_bits
        for done in order[:stage]:
            index[self.row_bits - 1 - done] = self.bit(done)
        now = order[stage]
        index[self.row_bits - 1 - now] = 1 - self.bit(now) if sent else self.bit(now)
        return tuple(index)

    def rows(self, half):
        depth = self.depth // 2
        return pl.ds(half * depth, depth)

    def row_copy(self, stage, half, chunk):
        source = self.total.at[(chunk,) + self.shares(half, stage, True) + (self.rows(half),)]
        return self.remote(
            source,
            self.row_in[stage][half].at[chunk],
            1 + 2 * stage + half,
            1 + 2 * stage + half,
            chunk,
            (self.at, flip(self.me, self.orders[half][stage])),
        )

    def own(self, chunk, rows):
        return (chunk,) + tuple(self.bit(b) for b in range(self.row_bits - 1, -1, -1)) + (rows,)

    def near_rows(self, mine):
        half = self.depth // 2
        place = self.near if mine else 1 - self.near
        return pl.ds(pl.multiple_of(place * half, half), half)

    def near_copy(self, chunk):
        return self.remote(
            self.total.at[self.own(chunk, self.near_rows(False))],
            self.near_in.at[chunk],
            1 + 2 * self.row_bits,
            1 + 2 * self.row_bits,
            chunk,
            (flip(self.at, 1), self.me),
        )

    def far_copy(self, k, chunk):
        return self.remote(
            self.far_out[k].at[chunk],
            self.far_in[k].at[chunk],
            2 + 2 * self.row_bits + k,
            2 + 2 * self.row_bits + k,
            chunk,
            (flip(self.at, 2 + k), self.me),
        )

    def back_copy(self, chunk):
        place = self.out.at[self.core, chunk, self.near_rows(True)]
        return self.remote(
            place,
            place,
            2 + 2 * self.row_bits + self.far,
            2 + 2 * self.row_bits + self.far,
            chunk,
            (flip(self.at, 1), self.me),
        )

    def last_copy(self, chunk):
        place = self.out.at[self.core, chunk]
        return self.remote(
            place,
            place,
            3 + 2 * self.row_bits + self.far,
            3 + 2 * self.row_bits + self.far,
            chunk,
            (flip(self.at, 0), self.me),
        )

    def phase(self, number, chunk):
        bits, half = self.row_bits, self.depth // 2
        if number == 0:
            self.core_copy(self.total.at[chunk], chunk).wait_recv()
            self.add_mine(chunk)
            if self.sources is not None:

                @pl.when(chunk + 1 < self.chunks)
                def _():
                    self.fetch(chunk + 1)

            for side in (0, 1):
                self.row_copy(0, side, chunk).start()
        elif number <= bits:
            stage = number - 1
            for side in (0, 1):
                self.row_copy(stage, side, chunk).wait_recv()
                at = (chunk,) + self.shares(side, stage, False) + (self.rows(side),)
                self.total[at] = add_low(self.total[at], self.row_in[stage][side][chunk])
                if stage + 1 < bits:
                    self.row_copy(stage + 1, side, chunk).start()
            if stage + 1 == bits:
                self.near_copy(chunk).start()
        elif number == bits + 1:
            self.near_copy(chunk).wait_recv()
            total = add_low(
                self.total[self.own(chunk, self.near_rows(True))], self.near_in[chunk]
            )
            self.pass_on(0, chunk, total)
        elif number <= bits + 1 + self.far:
            k = number - bits - 2
            self.far_copy(k, chunk).wait_recv()
            self.pass_on(k + 1, chunk, add_low(self.far_out[k][chunk], self.far_in[k][chunk]))
        elif number == bits + 2 + self.far:
            self.back_copy_arrived(chunk)
            self.last_copy(chunk).start()
        else:
            self.last_arrived(chunk)

    def pass_on(self, k, chunk, total):
        if k < self.far:
            self.far_out[k][chunk] = total
            self.far_copy(k, chunk).start()
        else:
            self.out[self.core, chunk, self.near_rows(True)] = total
            self.back_copy(chunk).start()

    def back_copy_arrived(self, chunk):
        place = self.out.at[self.core, chunk, self.near_rows(False)]
        self.remote(
            place,
            place,
            2 + 2 * self.row_bits + self.far,
            2 + 2 * self.row_bits + self.far,
            chunk,
            (flip(self.at, 1), self.me),
        ).wait_recv()

    def last_arrived(self, chunk):
        place = self.out.at[1 - self.core, chunk]
        self.remote(
            place,
            place,
            3 + 2 * self.row_bits + self.far,
            3 + 2 * self.row_bits + self.far,
            chunk,
            (flip(self.at, 0), self.me),
        ).wait_recv()

    def step(self, t):
        for number in range(self.phases - 1, -1, -1):
            place = t - self.lag * number
            chunk = place // self.space

            @pl.when((place >= 0) & (place % self.space == 0) & (chunk < self.chunks))
            def _(number=number, chunk=chunk):
                self.phase(number, jnp.clip(chunk, 0, self.chunks - 1))

    @property
    def steps(self):
        return (self.chunks - 1) * self.space + self.lag * (self.phases - 1) + 1

    def finish(self):
        def drain(sem, ref):
            pltpu.make_async_copy(ref, ref, self.send_sem.at[sem]).wait()

        drain(0, self.total)
        for stage in range(self.row_bits):
            for side in (0, 1):
                drain(1 + 2 * stage + side, self.row_in[stage][side])
        base = 1 + 2 * self.row_bits
        drain(base, self.near_in)
        for k in range(self.far):
            drain(base + 1 + k, self.far_in[k])
        drain(base + 1 + self.far, self.near_in)
        drain(base + 2 + self.far, self.out.at[0])
        copy = pltpu.make_async_copy(self.out, self.result, self.ring_sem.at[0])
        copy.start()
        copy.wait()


def unpack_kernel(held_ref, *refs, table, outs):
    targets, (wide, sem) = refs[:outs], refs[outs:]
    depth = wide.shape[1]

    def copy(place, chunk, first, size, number, outer, row, column):
        target = targets[number] if outer is None else targets[number].at[outer]
        return pltpu.make_async_copy(
            wide.at[chunk, :, pl.ds(first, size)],
            target.at[pl.ds(row, depth), pl.ds(column, size)],
            sem.at[place],
        )

    done = set()
    for place, entry in enumerate(table):
        chunk = entry[0]
        if chunk not in done:
            done.add(chunk)
            wide[chunk] = jnp.concatenate(
                [held_ref[0, chunk].astype(F32), held_ref[1, chunk].astype(F32)], axis=1
            )
        copy(place, *entry).start()
    for place, entry in enumerate(table):
        copy(place, *entry).wait()


def unpack(out, table, shapes):
    chunks, depth, lanes = out.shape[1:]
    return pl.pallas_call(
        functools.partial(unpack_kernel, table=table, outs=len(shapes)),
        in_specs=[pl.BlockSpec(memory_space=pltpu.VMEM)],
        out_specs=[pl.BlockSpec(memory_space=pl.ANY)] * len(shapes),
        out_shape=[jax.ShapeDtypeStruct(shape, F32) for shape in shapes],
        scratch_shapes=[
            pltpu.VMEM((chunks, depth, 2 * lanes), F32),
            pltpu.SemaphoreType.DMA((len(table),)),
        ],
        compiler_params=pltpu.CompilerParams(vmem_limit_bytes=40 << 20),
        name="unpack",
    )(out)


def all_sum_kernel(value_ref, out_ref, piece, landed, over, send_sem, recv_sem, *, count, others):
    at, me = lax.axis_index("items"), lax.axis_index("rows")
    barrier = pltpu.get_barrier_semaphore()
    row_peers = [(at, (me + k) % count) for k in range(1, count)]
    item_peers = [((at + k) % others, me) for k in range(1, others)]
    for peer in row_peers + item_peers:
        pl.semaphore_signal(barrier, inc=1, device_id=peer, device_id_type=MESH)
    pl.semaphore_wait(barrier, count + others - 2)

    def row_copy(k):
        return pltpu.make_async_remote_copy(
            src_ref=value_ref.at[row_peers[k][1]],
            dst_ref=landed.at[k],
            send_sem=send_sem.at[k],
            recv_sem=recv_sem.at[k],
            device_id=row_peers[k],
            device_id_type=MESH,
        )

    def item_copy(k):
        return pltpu.make_async_remote_copy(
            src_ref=piece,
            dst_ref=over.at[k],
            send_sem=send_sem.at[count - 1 + k],
            recv_sem=recv_sem.at[count - 1 + k],
            device_id=item_peers[k],
            device_id_type=MESH,
        )

    for k in range(count - 1):
        row_copy(k).start()
    total = value_ref[me]
    for k in range(count - 1):
        row_copy(k).wait_recv()
        total = total + landed[k]
    piece[...] = total
    for k in range(others - 1):
        item_copy(k).start()
    for k in range(others - 1):
        item_copy(k).wait_recv()
        total = total + over[k]
    out_ref[...] = total
    for k in range(count - 1):
        row_copy(k).wait_send()
    for k in range(others - 1):
        item_copy(k).wait_send()


def all_sum(value, collective_id):
    count, others = lax.axis_size("rows"), lax.axis_size("items")
    vmem = pl.BlockSpec(memory_space=pltpu.VMEM)
    block = value.shape[1:]
    return pl.pallas_call(
        functools.partial(all_sum_kernel, count=count, others=others),
        in_specs=[vmem],
        out_specs=vmem,
        out_shape=jax.ShapeDtypeStruct(block, F32),
        scratch_shapes=[
            pltpu.VMEM(block, F32),
            pltpu.VMEM((count - 1,) + block, F32),
            pltpu.VMEM((others - 1,) + block, F32),
            pltpu.SemaphoreType.DMA((count + others - 2,)),
            pltpu.SemaphoreType.DMA((count + others - 2,)),
        ],
        compiler_params=pltpu.CompilerParams(collective_id=collective_id, has_side_effects=True),
        name="sum_small",
    )(value)


class Gather:
    def __init__(self, bits, items):
        self.bits, self.items = bits, items
        self.orders = (tuple(range(bits)), tuple(range(bits - 1, -1, -1)))

    def bind(self, held, send_sem, recv_sem):
        self.held, self.send_sem, self.recv_sem = held, send_sem, recv_sem

    def place(self, item, half, stage, now):
        order = self.orders[half]
        index = [0] * self.bits
        for done in order[:stage]:
            index[self.bits - 1 - done] = slice(None)
        index[self.bits - 1 - order[stage]] = now
        size = self.held.shape[-2] // 2
        return (item,) + tuple(index) + (pl.ds(half * size, size),)

    def copy(self, item, stage, half):
        me, at = lax.axis_index("rows"), lax.axis_index("items")
        return pltpu.make_async_remote_copy(
            src_ref=self.held.at[self.place(item, half, stage, 0)],
            dst_ref=self.held.at[self.place(item, half, stage, 1)],
            send_sem=self.send_sem.at[item, stage, half],
            recv_sem=self.recv_sem.at[item, stage, half],
            device_id=(at, flip(me, self.orders[half][stage])),
            device_id_type=MESH,
        )

    def start(self, item, stage):
        for half in (0, 1):
            self.copy(item, stage, half).start()

    def arrived(self, item, stage):
        for half in (0, 1):
            self.copy(item, stage, half).wait_recv()

    def drain(self, item):
        for stage in range(self.bits):
            for half in (0, 1):
                self.copy(item, stage, half).wait_send()


def attention_forward_kernel(
    valid_ref,
    tokens_ref,
    gain_ref,
    shift_ref,
    q_bias_ref,
    v_bias_ref,
    wq_ref,
    wk_ref,
    wv_ref,
    q_ref,
    k_ref,
    v_ref,
    o_ref,
    lse_ref,
    normed_ref,
    held,
    send_sem,
    recv_sem,
    copy_sem,
    *,
    gather,
    groups,
    items,
):
    gather.bind(held, send_sem, recv_sem)
    step = pl.program_id(0)
    item, group = step // groups, step % groups
    t, width = held.shape[-2:]
    n = k_ref.shape[1]
    me, at = lax.axis_index("rows"), lax.axis_index("items")
    bits = gather.bits
    mine = (0,) * bits

    def store(which):
        held[(which,) + mine] = layer_norm(
            tokens_ref[which].astype(F32), gain_ref[...], shift_ref[...]
        ).astype(BF)

    def keep(which):
        return pltpu.make_async_copy(held.at[which], normed_ref.at[which], copy_sem.at[which])

    @pl.when(step == 0)
    def _():
        store(0)
        barrier = pltpu.get_barrier_semaphore()
        for bit in range(bits):
            pl.semaphore_signal(
                barrier, inc=1, device_id=(at, flip(me, bit)), device_id_type=MESH
            )
        pl.semaphore_wait(barrier, bits)
        gather.start(0, 0)
        for which in range(1, items):
            store(which)
        for stage in range(1, bits):
            gather.arrived(0, stage - 1)
            gather.start(0, stage)
        gather.start(1, 0)

    @pl.when(group == 0)
    def _():
        gather.arrived(item, bits - 1)
        keep(item).start()

    limit = valid_ref[item] * PC
    index = lax.broadcasted_iota(jnp.int32, (1, n), 1)
    bias = jnp.where(index + key_shift(index, n, t, me) < limit, 0.0, MASKED).astype(F32)
    every = held[item].reshape(n, width)
    keys = mm(every, wk_ref[...]).astype(BF)
    values = (mm(every, wv_ref[...]) + v_bias_ref[...]).astype(BF)
    queries = (mm(held[(item,) + mine], wq_ref[...]) + q_bias_ref[...]).astype(BF)
    k_ref[0] = keys
    v_ref[0] = values
    q_ref[0] = queries
    queries = queries * jnp.asarray(HEAD_DIM**-0.5, BF)
    out = jnp.zeros((t, GROUP), F32)
    for h in range(HEADS_PER_GROUP):
        mask = head_mask((t, GROUP), h)
        one = jnp.where(mask, queries, jnp.zeros_like(queries))
        scores = mm(one, keys, NT) + bias
        top = jnp.max(scores, axis=1, keepdims=True)
        probs = jnp.exp2((scores - top) * LOG2E)
        total = jnp.sum(probs, axis=1, keepdims=True)
        weighted = mm(probs.astype(BF), values)
        out = jnp.where(mask, weighted * (1.0 / total), out)
        lse = top * LOG2E + jnp.log2(total)
        lse_ref[0, 0, :, pl.ds(h * t, t)] = jnp.transpose(jnp.broadcast_to(lse, (t, 128)))[:8]
    o_ref[0] = out.astype(BF)

    for stage in range(1, bits):

        @pl.when((group == stage - 1) & (item + 1 < items))
        def _(stage=stage):
            gather.arrived(item + 1, stage - 1)
            gather.start(item + 1, stage)

    @pl.when((group == bits - 2) & (item + 2 < items))
    def _():
        gather.start(item + 2, 0)

    @pl.when(step == items * groups - 1)
    def _():
        for which in range(items):
            gather.drain(which)
            keep(which).wait()


def attention_forward(valid_rows, tokens, gain, shift, qkv_weight, q_bias, v_bias, collective_id):
    items, t, d = tokens.shape
    bits = axis_bits("rows")
    n = t << bits
    groups = d // GROUP
    rows4 = HEADS_PER_GROUP * t
    vmem = pl.BlockSpec(memory_space=pltpu.VMEM)

    def weight_spec(kind):
        return pl.BlockSpec((d, GROUP), lambda i: (0, kind * groups + i % groups))

    bias_spec = pl.BlockSpec((1, GROUP), lambda i: (0, i % groups))
    query_spec = pl.BlockSpec((1, t, GROUP), lambda i: (i // groups, 0, i % groups))
    key_spec = pl.BlockSpec((1, n, GROUP), lambda i: (i // groups, 0, i % groups))
    return pl.pallas_call(
        functools.partial(
            attention_forward_kernel, gather=Gather(bits, items), groups=groups, items=items
        ),
        grid=(items * groups,),
        in_specs=[
            pl.BlockSpec(memory_space=pltpu.SMEM),
            vmem,
            vmem,
            vmem,
            bias_spec,
            bias_spec,
            weight_spec(0),
            weight_spec(1),
            weight_spec(2),
        ],
        out_specs=[
            query_spec,
            key_spec,
            key_spec,
            query_spec,
            pl.BlockSpec((1, 1, 8, rows4), lambda i: (i // groups, i % groups, 0, 0)),
            pl.BlockSpec(memory_space=pl.ANY),
        ],
        out_shape=[
            jax.ShapeDtypeStruct((items, t, d), BF),
            jax.ShapeDtypeStruct((items, n, d), BF),
            jax.ShapeDtypeStruct((items, n, d), BF),
            jax.ShapeDtypeStruct((items, t, d), BF),
            jax.ShapeDtypeStruct((items, groups, 8, rows4), F32),
            jax.ShapeDtypeStruct((items,) + (2,) * bits + (t, d), BF),
        ],
        scratch_shapes=[
            pltpu.VMEM((items,) + (2,) * bits + (t, d), BF),
            pltpu.SemaphoreType.DMA((items, bits, 2)),
            pltpu.SemaphoreType.DMA((items, bits, 2)),
            pltpu.SemaphoreType.DMA((items,)),
        ],
        compiler_params=pltpu.CompilerParams(
            vmem_limit_bytes=52 << 20, collective_id=collective_id, has_side_effects=True
        ),
        cost_estimate=pl.CostEstimate(
            flops=60 * items * t * n * d,
            bytes_accessed=40 << 20,
            transcendentals=12 * items * t * n,
        ),
        name="attention_forward",
    )(
        valid_rows,
        tokens,
        gain,
        shift,
        q_bias,
        v_bias,
        qkv_weight,
        qkv_weight,
        qkv_weight,
    )


def key_shift(index, length, block, me):
    start = jnp.full_like(index, me * block)
    for j in range(1, length // block):
        other = me
        for bit in range(j.bit_length()):
            if j >> bit & 1:
                other = flip(other, bit)
        start = jnp.where(index >= j * block, (other - j) * block, start)
    return start


def mlp_forward_kernel(
    tokens_ref,
    attended_ref,
    out_w_ref,
    out_bias_ref,
    gain_ref,
    shift_ref,
    fc2_bias_ref,
    tap_w_ref,
    tap_bias_ref,
    fc1_ref,
    fc1_bias_ref,
    fc2_ref,
    resid_ref,
    normed_ref,
    hidden_ref,
    slope_ref,
    out_ref,
    tap_ref,
    total,
    *,
    blocks,
    row_block,
):
    step = pl.program_id(0)
    count = total.shape[0] // row_block

    def rows_of(number):
        return pl.ds(number * row_block, row_block)

    @pl.when(step == 0)
    def _():
        def enter(number):
            piece = rows_of(number)
            resid = (
                tokens_ref[piece, :].astype(F32)
                + mm(attended_ref[piece, :], out_w_ref[...])
                + out_bias_ref[...]
            )
            resid_ref[piece, :] = resid
            total[piece, :] = resid + fc2_bias_ref[...]
            normed_ref[piece, :] = layer_norm(resid, gain_ref[...], shift_ref[...]).astype(BF)

        for number in range(count):
            enter(number)

    def middle(number):
        piece = rows_of(number)
        pre = mm(normed_ref[piece, :], fc1_ref[...]) + fc1_bias_ref[...]
        cdf, rest = normal_parts(pre)
        hidden = (pre * cdf).astype(BF)
        hidden_ref[piece, :] = hidden
        slope_ref[piece, :] = (cdf + rest).astype(BF)
        total[piece, :] += mm(hidden, fc2_ref[...])

    for number in range(count):
        middle(number)

    @pl.when(step == blocks - 1)
    def _():
        def leave(number):
            piece = rows_of(number)
            low = total[piece, :].astype(BF)
            out_ref[piece, :] = low
            tap_ref[piece, :] = mm(low, tap_w_ref[...]) + tap_bias_ref[...]

        for number in range(count):
            leave(number)


def mlp_forward(
    tokens,
    attended,
    out_weight,
    out_bias,
    gain,
    shift,
    fc1_weight,
    fc1_bias,
    fc2_weight,
    fc2_bias,
    tap_weight,
    tap_bias,
    row_block,
):
    count, width = tokens.shape
    inner, channels = fc1_weight.shape[1], tap_weight.shape[1]
    blocks = inner // width
    vmem = pl.BlockSpec(memory_space=pltpu.VMEM)
    column = pl.BlockSpec((count, width), lambda i: (0, i))
    return pl.pallas_call(
        functools.partial(mlp_forward_kernel, blocks=blocks, row_block=row_block),
        grid=(blocks,),
        in_specs=[vmem] * 9
        + [
            pl.BlockSpec((width, width), lambda i: (0, i)),
            pl.BlockSpec((1, width), lambda i: (0, i)),
            pl.BlockSpec((width, width), lambda i: (i, 0)),
        ],
        out_specs=[vmem, vmem, column, column, vmem, vmem],
        out_shape=[
            jax.ShapeDtypeStruct((count, width), F32),
            jax.ShapeDtypeStruct((count, width), BF),
            jax.ShapeDtypeStruct((count, inner), BF),
            jax.ShapeDtypeStruct((count, inner), BF),
            jax.ShapeDtypeStruct((count, width), BF),
            jax.ShapeDtypeStruct((count, channels), F32),
        ],
        scratch_shapes=[pltpu.VMEM((count, width), F32)],
        compiler_params=pltpu.CompilerParams(vmem_limit_bytes=48 << 20),
        cost_estimate=pl.CostEstimate(
            flops=5 * count * width * inner,
            bytes_accessed=40 << 20,
            transcendentals=2 * count * inner,
        ),
        name="mlp_forward",
    )(
        tokens,
        attended,
        out_weight,
        out_bias,
        gain,
        shift,
        fc2_bias,
        tap_weight,
        tap_bias,
        fc1_weight,
        fc1_bias,
        fc2_weight,
    )


def shares_of(bits):
    return (2,) * bits


def mlp_backward_kernel(
    tap_grad_ref,
    cot_ref,
    out_tokens_ref,
    normed_ref,
    resid_ref,
    attended_ref,
    gain_ref,
    tap_w_ref,
    out_w_ref,
    hidden_ref,
    slope_ref,
    fc1_ref,
    fc2_ref,
    tap_dw_ref,
    out_dw_ref,
    fc1_dw_ref,
    fc2_dw_ref,
    resid_grad_ref,
    attended_grad_ref,
    wide_sums_ref,
    fc1_sums_ref,
    out_grad,
    low_grad,
    pre_grad,
    back,
    *,
    blocks,
    row_block,
    bits,
):
    step = pl.program_id(0)
    tokens, width = low_grad.shape
    count = 1 << bits
    depth = width // count
    shares = shares_of(bits)
    pieces = [pl.ds(k * row_block, row_block) for k in range(tokens // row_block)]

    @pl.when(step == 0)
    def _():
        total = jnp.zeros((1, width), F32)
        tap_total = jnp.zeros((1, tap_grad_ref.shape[1]), F32)
        for piece in pieces:
            tap_part = tap_grad_ref[piece, :]
            value = cot_ref[piece, :].astype(F32) + mm(tap_part, tap_w_ref[...], NT)
            out_grad[piece, :] = value
            low = value.astype(BF)
            low_grad[piece, :] = low
            back[piece, :] = jnp.zeros((row_block, width), F32)
            total = total + jnp.sum(low.astype(F32), axis=0, keepdims=True)
            tap_total = tap_total + jnp.sum(tap_part.astype(F32), axis=0, keepdims=True)
        wide_sums_ref[pl.ds(0, 1), :] = total
        wide_sums_ref[pl.ds(4, 1), :] = jnp.concatenate(
            [tap_total] * (width // tap_total.shape[1]), axis=1
        )
        weight = mm(out_tokens_ref[...], tap_grad_ref[...], TN).astype(BF)
        weight = jnp.concatenate(
            [weight, jnp.zeros((width, width - weight.shape[1]), BF)], axis=1
        )
        tap_dw_ref[0] = weight.reshape(shares + (depth, width))

    sums = jnp.zeros((1, pre_grad.shape[1]), F32)
    for piece in pieces:
        grads = mm(low_grad[piece, :], fc2_ref[...], NT) * slope_ref[piece, :].astype(F32)
        low = grads.astype(BF)
        pre_grad[piece, :] = low
        sums = sums + jnp.sum(low.astype(F32), axis=0, keepdims=True)
    fc1_sums_ref[...] = sums
    weight = mm(hidden_ref[...], low_grad[...], TN).astype(BF)
    per_share = weight.shape[0] // depth * blocks // count
    for place in range(weight.shape[0] // depth):
        fc2_dw_ref[place % per_share, place // per_share] = weight[
            place * depth : (place + 1) * depth
        ]
    weight = mm(normed_ref[...], pre_grad[...], TN).astype(BF)
    fc1_dw_ref[0] = weight.reshape(shares + (depth, width))

    for piece in pieces:
        back[piece, :] += mm(pre_grad[piece, :], fc1_ref[...], NT)

    @pl.when(step == blocks - 1)
    def _():
        gain = gain_ref[...]
        gain_total = jnp.zeros((1, width), F32)
        shift_total = jnp.zeros((1, width), F32)
        total = jnp.zeros((1, width), F32)
        for piece in pieces:
            grads = back[piece, :]
            unit, rstd = norm_stats(resid_ref[piece, :])
            scaled = grads * gain
            mean_one = jnp.mean(scaled, axis=-1, keepdims=True)
            mean_two = jnp.mean(scaled * unit, axis=-1, keepdims=True)
            value = out_grad[piece, :] + rstd * (scaled - mean_one - unit * mean_two)
            resid_grad_ref[piece, :] = value
            low = value.astype(BF)
            low_grad[piece, :] = low
            gain_total = gain_total + jnp.sum(grads * unit, axis=0, keepdims=True)
            shift_total = shift_total + jnp.sum(grads, axis=0, keepdims=True)
            total = total + jnp.sum(low.astype(F32), axis=0, keepdims=True)
            attended_grad_ref[piece, :] = mm(low, out_w_ref[...], NT).astype(BF)
        wide_sums_ref[pl.ds(1, 1), :] = gain_total
        wide_sums_ref[pl.ds(2, 1), :] = shift_total
        wide_sums_ref[pl.ds(3, 1), :] = total
        weight = mm(attended_ref[...], low_grad[...], TN).astype(BF)
        out_dw_ref[0] = weight.reshape(shares + (depth, width))


def mlp_backward(
    grad_tap,
    cotangent,
    out_tokens,
    normed,
    resid,
    attended,
    gain,
    tap_weight,
    out_weight,
    hidden,
    slope,
    fc1_weight,
    fc2_weight,
    row_block,
):
    tokens, width = resid.shape
    inner = hidden.shape[1]
    bits = axis_bits("rows")
    count = 1 << bits
    depth = width // count
    blocks = inner // width
    vmem = pl.BlockSpec(memory_space=pltpu.VMEM)
    column = pl.BlockSpec((tokens, width), lambda i: (0, i))
    fc2_chunks = inner // count // depth
    shares = shares_of(bits)
    share_step = count // blocks
    outs = pl.pallas_call(
        functools.partial(
            mlp_backward_kernel,
            blocks=blocks,
            row_block=row_block,
            bits=bits,
        ),
        grid=(blocks,),
        in_specs=[vmem] * 9
        + [
            column,
            column,
            pl.BlockSpec((width, width), lambda i: (0, i)),
            pl.BlockSpec((width, width), lambda i: (i, 0)),
        ],
        out_specs=[
            vmem,
            vmem,
            pl.BlockSpec((1,) + shares + (depth, width), lambda i: (i,) + (0,) * (bits + 2)),
            pl.BlockSpec((fc2_chunks, share_step, depth, width), lambda i: (0, i, 0, 0)),
            vmem,
            vmem,
            vmem,
            pl.BlockSpec((1, width), lambda i: (0, i)),
        ],
        out_shape=[
            jax.ShapeDtypeStruct((1,) + shares + (depth, width), BF),
            jax.ShapeDtypeStruct((1,) + shares + (depth, width), BF),
            jax.ShapeDtypeStruct((blocks,) + shares + (depth, width), BF),
            jax.ShapeDtypeStruct((fc2_chunks, count, depth, width), BF),
            jax.ShapeDtypeStruct((tokens, width), F32),
            jax.ShapeDtypeStruct((tokens, width), BF),
            jax.ShapeDtypeStruct((8, width), F32),
            jax.ShapeDtypeStruct((1, inner), F32),
        ],
        scratch_shapes=[
            pltpu.VMEM((tokens, width), F32),
            pltpu.VMEM((tokens, width), BF),
            pltpu.VMEM((tokens, width), BF),
            pltpu.VMEM((tokens, width), F32),
        ],
        compiler_params=pltpu.CompilerParams(vmem_limit_bytes=60 << 20),
        cost_estimate=pl.CostEstimate(
            flops=8 * tokens * width * inner, bytes_accessed=40 << 20, transcendentals=0
        ),
        name="mlp_backward",
    )(
        grad_tap,
        cotangent,
        out_tokens,
        normed,
        resid,
        attended,
        gain,
        tap_weight,
        out_weight,
        hidden,
        slope,
        fc1_weight,
        fc2_weight,
    )
    return outs


class Scatter:
    def __init__(self, bits, tokens, width, items):
        self.bits, self.tokens, self.width, self.items = bits, tokens, width, items
        self.orders = (tuple(range(bits - 1, -1, -1)), tuple(range(bits)))

    def scratch(self):
        slots = [pltpu.VMEM((2,) * self.bits + (self.tokens, self.width), BF)]
        for stage in range(self.bits):
            for _ in (0, 1):
                slots.append(
                    pltpu.VMEM(
                        (self.items,)
                        + (2,) * (self.bits - 1 - stage)
                        + (self.tokens // 2, self.width),
                        BF,
                    )
                )
        return slots + [
            pltpu.SemaphoreType.DMA((self.bits, 2)),
            pltpu.SemaphoreType.DMA((self.items, self.bits, 2)),
        ]

    def bind(self, slots):
        self.held = slots[0]
        self.landed = [(slots[1 + 2 * s], slots[2 + 2 * s]) for s in range(self.bits)]
        self.send_sem, self.recv_sem = slots[-2:]

    def place(self, half, stage, bit_value):
        index = [slice(None)] * self.bits
        for done in self.orders[half][:stage]:
            index[self.bits - 1 - done] = 0
        index[self.bits - 1 - self.orders[half][stage]] = bit_value
        size = self.tokens // 2
        return tuple(index) + (pl.ds(half * size, size),)

    def copy(self, item, stage, half):
        me, at = lax.axis_index("rows"), lax.axis_index("items")
        return pltpu.make_async_remote_copy(
            src_ref=self.held.at[self.place(half, stage, 1)],
            dst_ref=self.landed[stage][half].at[item],
            send_sem=self.send_sem.at[stage, half],
            recv_sem=self.recv_sem.at[item, stage, half],
            device_id=(at, flip(me, self.orders[half][stage])),
            device_id_type=MESH,
        )

    def start(self, item):
        for half in (0, 1):
            self.copy(item, 0, half).start()

    def advance(self, item, stage, finish):
        for half in (0, 1):
            self.copy(item, stage, half).wait_recv()
            at = self.place(half, stage, 0)
            if stage + 1 < self.bits:
                self.held[at] = add_low(self.held[at], self.landed[stage][half][item])
                self.copy(item, stage + 1, half).start()
            else:
                finish(
                    at[-1],
                    self.held[at].astype(F32) + self.landed[stage][half][item].astype(F32),
                )

    def drain(self, item):
        for stage in range(self.bits):
            for half in (0, 1):
                self.copy(item, stage, half).wait_send()


def attention_backward_kernel(
    valid_ref,
    q_ref,
    k_ref,
    v_ref,
    g_ref,
    o_ref,
    lse_ref,
    normed_ref,
    wq_ref,
    wk_ref,
    wv_ref,
    *refs,
    reducer,
    late,
    scatter,
    groups,
    items,
    kb,
    rounds,
    sources,
):
    early_sources = refs[:sources]
    grad_ref, sums_ref, early_out, late_out = refs[sources : sources + 4]
    slots = list(refs[sources + 4 :])
    q4, g4, acc, dkv, back, held = slots[:6]
    del slots[:6]
    early_slots = slots[: reducer.slots()]
    del slots[: reducer.slots()]
    late_slots = slots[: late.slots()]
    del slots[: late.slots()]
    reducer.bind(early_out, early_slots, sources=early_sources)
    late.bind(late_out, late_slots, held=held)
    scatter.bind(slots)
    step = pl.program_id(0)
    item, group = step // groups, step % groups
    t, n = q_ref.shape[1], k_ref.shape[1]
    width = back.shape[1]
    depth = width // (1 << reducer.row_bits)
    shares = shares_of(reducer.row_bits)
    me = lax.axis_index("rows")

    @pl.when(step == 0)
    def _():
        reducer.greet()
        reducer.begin()
        sums_ref[...] = jnp.zeros_like(sums_ref)

    q4[...] = spread_heads(q_ref[0] * jnp.asarray(HEAD_DIM**-0.5, BF))
    grads = spread_heads(g_ref[0])
    g4[...] = grads
    outs = jnp.concatenate([o_ref[0].astype(F32)] * HEADS_PER_GROUP, axis=0)
    product = grads.astype(F32) * outs
    high = product.astype(BF)
    low = (product - high.astype(F32)).astype(BF)
    ones = jnp.ones((8, GROUP), BF)
    dots = (mm(ones, high, NT) + mm(ones, low, NT))[:1]
    lse = lse_ref[0, 0, :1, :]
    acc[...] = jnp.zeros_like(acc)
    limit = valid_ref[item] * PC

    def turn(number):
        now = step * rounds + number
        reducer.step(now)
        late.step(now - ((items - 1) * groups + 1) * rounds)

    inner = n // kb
    each = rounds // inner

    def block_step(b, carry):
        at = pl.ds(pl.multiple_of(b * kb, kb), kb)
        keys, values = k_ref[0, at, :], v_ref[0, at, :]
        index = b * kb + lax.broadcasted_iota(jnp.int32, (kb, 1), 0)
        position = index + key_shift(index, n, t, me)
        bias = jnp.where(position < limit, 0.0, MASKED).astype(F32)
        scores = mm(keys, q4[...], NT)
        probs = jnp.exp2((scores * LOG2E + bias) - lse)
        grad_probs = mm(values, g4[...], NT)
        grad_scores = (probs * (grad_probs - dots)).astype(BF)
        dkv[at, pl.ds(GROUP, GROUP)] = mm(probs.astype(BF), g4[...]).astype(BF)
        dkv[at, pl.ds(0, GROUP)] = mm(grad_scores, q4[...]).astype(BF)
        acc[...] += mm(grad_scores, keys, TN)

        def rest(k, inner_carry):
            turn(b * each + k)
            return inner_carry

        lax.fori_loop(0, each, rest, 0)
        return carry

    lax.fori_loop(0, inner, block_step, 0)
    out = jnp.zeros((t, GROUP), F32)
    for h in range(HEADS_PER_GROUP):
        out = jnp.where(head_mask((t, GROUP), h), acc[pl.ds(h * t, t), :], out)
    dq = (out * HEAD_DIM**-0.5).astype(BF)

    for stage in range(scatter.bits):

        @pl.when((group == stage) & (item > 0))
        def _(stage=stage):
            def finish(rows, value):
                grad_ref[item - 1, rows, :] += value

            scatter.advance(item - 1, stage, finish)

    part = jnp.concatenate(
        [mm(normed_ref[0, pl.ds(0, t), :], dq, TN), mm(normed_ref[0], dkv[...], TN)], axis=1
    ).reshape(shares + (depth, width))
    before = held[group].astype(F32)
    held[group] = jnp.where(item == 0, part, before + part).astype(BF)
    sums_ref[group, pl.ds(0, 1), :] += jnp.sum(dq.astype(F32), axis=0, keepdims=True)
    sums_ref[group, pl.ds(1, 1), :] += jnp.sum(
        dkv[:, pl.ds(GROUP, GROUP)].astype(F32), axis=0, keepdims=True
    )

    @pl.when(item == items - 1)
    def _():
        late.begin_held(group)

    row_piece = n // 4
    both = jnp.concatenate([wk_ref[...], wv_ref[...]], axis=1)

    def project(k, carry):
        at = pl.ds(pl.multiple_of(k * row_piece, row_piece), row_piece)
        value = mm(dkv[at, :], both, NT)
        back[at, :] = jnp.where(group == 0, value, back[at, :] + value)
        return carry

    lax.fori_loop(0, 2, project, 0)

    @pl.when(step == items * groups - 1)
    def _():
        late.step((groups - 1) * rounds)

    lax.fori_loop(2, 4, project, 0)
    value = mm(dq, wq_ref[...], NT)
    grad_ref[item] = jnp.where(group == 0, value, grad_ref[item] + value)

    @pl.when(group == groups - 1)
    def _():
        @pl.when(item > 0)
        def _():
            scatter.drain(item - 1)

        for j in range(1 << scatter.bits):
            index = tuple(j >> b & 1 for b in range(scatter.bits - 1, -1, -1))
            scatter.held[index] = back[pl.ds(j * t, t), :].astype(BF)
        scatter.start(item)

    @pl.when(step == items * groups - 1)
    def _():
        start = ((items - 1) * groups + 1) * rounds

        last = items * groups * rounds

        def rest(now, carry):
            reducer.step(now)
            return carry

        def late_turn(k, carry):
            late.step(last - start + k * late.lag)
            return carry

        lax.fori_loop(last, max(last, reducer.steps), rest, 0)
        mark = 1

        for stage in range(scatter.bits):

            def finish(rows, value):
                grad_ref[items - 1, rows, :] += value

            lax.fori_loop(mark, 2 + 2 * stage, late_turn, 0)
            mark = 2 + 2 * stage
            scatter.advance(items - 1, stage, finish)
        lax.fori_loop(mark, late.phases, late_turn, 0)
        scatter.drain(items - 1)
        reducer.finish()
        late.finish()


def attention_backward(
    valid_rows, queries, keys, values, grads, outs, lse, normed, qkv_weight, packed, collective_id
):
    items, t, d = queries.shape
    n = keys.shape[1]
    groups = d // GROUP
    bits = axis_bits("rows")
    depth = d >> bits
    rows4 = HEADS_PER_GROUP * t
    rounds = 8
    reducer = Reducer(
        sum(a.shape[0] for a in packed), depth, d, bits, axis_bits("items"), 3, 9
    )
    late = Reducer(groups, depth, d, bits, axis_bits("items"), rounds, 8)
    scatter = Scatter(bits, t, d, items)
    query_spec = pl.BlockSpec((1, t, GROUP), lambda i: (i // groups, 0, i % groups))
    vmem = pl.BlockSpec(memory_space=pltpu.VMEM)

    def weight_spec(kind):
        return pl.BlockSpec((d, GROUP), lambda i: (0, kind * groups + i % groups))

    key_spec = pl.BlockSpec((1, n, GROUP), lambda i: (i // groups, 0, i % groups))

    outs = pl.pallas_call(
        functools.partial(
            attention_backward_kernel,
            reducer=reducer,
            late=late,
            scatter=scatter,
            groups=groups,
            items=items,
            kb=n // 4,
            rounds=rounds,
            sources=len(packed),
        ),
        grid=(items * groups,),
        in_specs=[
            pl.BlockSpec(memory_space=pltpu.SMEM),
            query_spec,
            key_spec,
            key_spec,
            query_spec,
            query_spec,
            pl.BlockSpec((1, 1, 8, rows4), lambda i: (i // groups, i % groups, 0, 0)),
            pl.BlockSpec((1, n, d), lambda i: (i // groups, 0, 0), pipeline_mode=pl.Buffered(1)),
            weight_spec(0),
            weight_spec(1),
            weight_spec(2),
        ]
        + [pl.BlockSpec(memory_space=pl.ANY)] * len(packed),
        out_specs=[vmem] * 2 + [pl.BlockSpec(memory_space=pl.ANY)] * 2,
        out_shape=[
            jax.ShapeDtypeStruct((items, t, d), F32),
            jax.ShapeDtypeStruct((groups, 8, GROUP), F32),
            reducer.out_shape(),
            late.out_shape(),
        ],
        scratch_shapes=[
            pltpu.VMEM((rows4, GROUP), BF),
            pltpu.VMEM((rows4, GROUP), BF),
            pltpu.VMEM((rows4, GROUP), F32),
            pltpu.VMEM((n, 2 * GROUP), BF),
            pltpu.VMEM((n, d), F32),
            pltpu.VMEM((groups,) + shares_of(bits) + (depth, d), BF),
        ]
        + reducer.scratch()
        + late.scratch()
        + scatter.scratch(),
        compiler_params=pltpu.CompilerParams(
            vmem_limit_bytes=63 << 20, collective_id=collective_id, has_side_effects=True
        ),
        cost_estimate=pl.CostEstimate(
            flops=100 * items * t * n * d,
            bytes_accessed=40 << 20,
            transcendentals=12 * items * t * n,
        ),
        name="attention_backward",
    )(
        valid_rows,
        queries,
        keys,
        values,
        grads,
        outs,
        lse,
        normed,
        qkv_weight,
        qkv_weight,
        qkv_weight,
        *packed,
    )
    return outs


def shards(
    tokens,
    valid_rows,
    dataset_ids,
    shift_flags,
    norm_gains,
    norm_biases,
    qkv_weight,
    qv_bias,
    out_weight,
    out_bias,
    fc1_weight,
    fc1_bias,
    fc2_weight,
    fc2_bias,
    tap_weight,
    tap_bias,
    conv_weights,
    conv_biases,
    table_gain,
    table_shift,
    token_cotangent,
    joined_cotangent,
):
    items_here, tok_here, width = tokens.shape
    rows_here = tok_here // PC
    channels = tap_weight.shape[1]
    row_index = lax.axis_index("rows")
    row_count = lax.axis_size("rows")
    last_index = row_count - 1

    flat_in = tokens.reshape(-1, width).astype(F32)
    queries, keys, values, attended, lses, normed_all = attention_forward(
        valid_rows,
        tokens,
        norm_gains[:1],
        norm_biases[:1],
        qkv_weight,
        qv_bias[None, :width],
        qv_bias[None, width:],
        5,
    )
    attended_flat = attended.reshape(-1, width)
    resid, normed_two, hidden, hidden_slope, output_low, tap_pre = mlp_forward(
        tokens.reshape(-1, width),
        attended_flat,
        out_weight,
        out_bias[None],
        norm_gains[1:2],
        norm_biases[1:2],
        fc1_weight,
        fc1_bias[None],
        fc2_weight,
        fc2_bias[None],
        tap_weight,
        tap_bias[None],
        tok_here,
    )
    grid_rows = row_index * rows_here + jnp.arange(rows_here, dtype=jnp.int32)
    row_valid = (grid_rows[None, :] < valid_rows[:, None]).astype(F32)
    token_valid = jnp.broadcast_to(
        row_valid[:, :, None], (items_here, rows_here, PC)
    ).reshape(-1, 1)
    field = (tap_pre * token_valid).reshape(items_here, rows_here, PC, channels)

    choose = (
        dataset_ids[:, None] == jnp.arange(table_gain.shape[0], dtype=jnp.int32)[None, :]
    ).astype(F32)
    flag_value = shift_flags.astype(F32)[:, None]
    gain_pick = jnp.dot(choose, table_gain, precision=highest)
    shift_pick = jnp.dot(choose, table_shift, precision=highest)
    factor = 1.0 + flag_value * (gain_pick - 1.0)
    offset = flag_value * shift_pick
    depth = width // row_count
    joined, grad_field, conv_grads, grad_conv_biases, table_sums = refine(
        field, conv_weights, conv_biases, factor, offset, joined_cotangent, depth
    )
    grad_table_gain = jnp.dot(choose.T, flag_value * table_sums[0], precision=highest)
    grad_table_shift = jnp.dot(choose.T, flag_value * table_sums[1], precision=highest)

    grad_tap = (grad_field[:, :, :PC].reshape(-1, channels) * token_valid).astype(BF)
    (
        tap_grads,
        out_grads,
        fc1_grads,
        fc2_grads,
        grad_resid,
        grad_attended,
        wide_sums,
        fc1_sums,
    ) = mlp_backward(
        grad_tap,
        token_cotangent.reshape(-1, width),
        output_low,
        normed_two,
        resid,
        attended_flat,
        norm_gains[1:2],
        tap_weight,
        out_weight,
        hidden,
        hidden_slope,
        fc1_weight,
        fc2_weight,
        tok_here,
    )
    shares = shares_of(axis_bits("rows"))
    fc2_grads = fc2_grads.reshape(fc2_grads.shape[:1] + shares + fc2_grads.shape[2:])
    grads_in, qkv_sums, early_sum, late_sum = attention_backward(
        valid_rows,
        queries,
        keys,
        values,
        grad_attended.reshape(tokens.shape),
        attended,
        lses,
        normed_all.reshape(keys.shape),
        qkv_weight,
        [conv_grads, tap_grads, fc2_grads, fc1_grads, out_grads],
        3,
    )
    grad_in_norm, grad_gain_one, grad_shift_one = norm_back(
        flat_in, norm_gains[0], grads_in.reshape(-1, width)
    )
    grad_tokens = (grad_resid + grad_in_norm).reshape(tokens.shape)

    groups = width // GROUP
    inner = fc1_weight.shape[1]
    kernels = conv_weights.shape[1]
    convs = conv_weights.shape[0]
    places = kernels // row_count // depth
    fc2_chunks = inner // row_count // depth
    blocks = inner // width
    table = [
        (conv, place * channels, channels, 0, conv, place * depth, 0)
        for conv in range(convs)
        for place in range(places)
    ]
    table += [(convs, 0, channels, 1, None, 0, 0)]
    first = convs + 1
    table += [(first + k, 0, width, 2, None, k * depth, 0) for k in range(fc2_chunks)]
    first += fc2_chunks
    table += [(first + k, 0, width, 3, None, 0, k * width) for k in range(blocks)]
    table += [(first + blocks, 0, width, 4, None, 0, 0)]
    share_conv, share_tap, share_fc2, share_fc1, share_out = unpack(
        early_sum,
        table,
        [
            (convs, kernels // row_count, channels),
            (depth, channels),
            (inner // row_count, width),
            (depth, inner),
            (depth, width),
        ],
    )
    (share_qkv,) = unpack(
        late_sum,
        [
            (group, kind * GROUP, GROUP, 0, None, 0, (kind * groups + group) * GROUP)
            for group in range(groups)
            for kind in range(3)
        ],
        [(depth, 3 * width)],
    )

    small = [
        jnp.stack([grad_gain_one, wide_sums[1]]),
        jnp.stack([grad_shift_one, wide_sums[2]]),
        jnp.concatenate([qkv_sums[:, 0].reshape(-1), qkv_sums[:, 1].reshape(-1)]),
        wide_sums[3],
        fc1_sums[0],
        wide_sums[0],
        wide_sums[4, :channels],
        grad_conv_biases,
        grad_table_gain,
        grad_table_shift,
    ]
    packed = jnp.concatenate(
        [
            array.reshape(row_count, -1)
            if array.ndim == 1
            else jnp.swapaxes(array.reshape(array.shape[0], row_count, -1), 0, 1).reshape(
                row_count, -1
            )
            for array in small
        ],
        axis=1,
    )
    packed = jnp.pad(packed, ((0, 0), (0, -packed.shape[1] % 1024)))
    summed = all_sum(packed.reshape(row_count, -1, 128), 4).reshape(-1)
    outs, place = [], 0
    for array in small:
        size = array.size // row_count
        piece = summed[place : place + size]
        place += size
        outs.append(piece if array.ndim == 1 else piece.reshape(array.shape[0], -1))
    (
        out_gains,
        out_shifts,
        out_qv,
        out_out,
        out_fc1,
        out_fc2,
        out_tap,
        out_conv,
        out_table_gain,
        out_table_shift,
    ) = outs
    return (
        output_low.reshape(tokens.shape),
        joined,
        grad_tokens,
        out_gains,
        out_shifts,
        share_qkv,
        out_qv,
        share_out,
        out_out,
        share_fc1,
        out_fc1,
        share_fc2,
        out_fc2,
        share_tap,
        out_tap,
        share_conv,
        out_conv,
        out_table_gain,
        out_table_shift,
    )


def solution(mesh):
    return jax.shard_map(
        shards,
        mesh=mesh,
        in_specs=(P("items", "rows", None), P("items"), P("items"), P("items"))
        + (P(),) * 16
        + (P("items", "rows", None), P("items", "rows", None, None)),
        out_specs=(
            P("items", "rows", None),
            P("items", "rows", None, None),
            P("items", "rows", None),
            P(None, "rows"),
            P(None, "rows"),
            P("rows", None),
            P("rows"),
            P("rows", None),
            P("rows"),
            P("rows", None),
            P("rows"),
            P("rows", None),
            P("rows"),
            P("rows", None),
            P("rows"),
            P(None, "rows", None),
            P(None, "rows"),
            P(None, "rows"),
            P(None, "rows"),
        ),
        check_vma=False,
    )
```
